32 devices in a mesh: row: 2 (over x), col: 8 (over z, y), img: 2 (over core).
Axes of the slice: x: 2, y: 2, z: 4, core: 2. Of those that a mesh axis runs over, the one named last changes fastest.
Arguments:
- x_in: bfloat16 [2, 64, 64, 1536], P('img', 'row', 'col'), may hold values from -6 to 6
- gate_in: bfloat16 [2, 64, 64, 1536], P('img', 'row', 'col'), may hold values from -6 to 6
- proj_bc: bfloat16 [2, 64, 64, 64], P('img', 'row', 'col'), may hold values from -3 to 3
- dt_raw: bfloat16 [2, 64, 64, 48], P('img', 'row', 'col'), may hold values from -3 to 3
- step_index: int32 [2], P('img'), may hold values from 0 to 999
- step_table: float32 [1000, 48], replicated, may hold values from -1.5 to 0.5
- rates: float32 [2, 24], replicated, may hold values from 0.0015625 to 0.1875, as said below
- skip: float32 [24], replicated, may hold values from 0.5 to 2
- norm_gain: float32 [1536], replicated, may hold values from 0.5 to 1.5
Outputs:
- mixed: bfloat16 [2, 64, 64, 1536], P('img', 'row', 'col')
The draws below stay inside these ranges and needn't reach their ends.
Inputs may be any that keep to these rules, and one draw needn't show every extreme that they name: rates of the row heads are given per column step and those of the column heads per row step.
All inputs are finite; a program needn't handle non-finite values.
Results may differ from the reference program's by a relative error of at most 0.0065.
Values may be sent and summed in bfloat16 or wider, within the bound.
No kernel may reach another device: no remote copies, remote signals or barrier semaphores. Data moves between devices by JAX's collectives and lax.ppermute only.
A program may use at most 128 MiB of HBM per device.

```python
import math
import jax
import jax.numpy as jnp
from jax import lax

HEADS = 24
HEAD = 64
STATE = 16
STEPS = 1000
INNER = 1536
BATCH = 2
H = 64
W = 64


def draw_rates(key, part):
    lengths = jnp.array([W, H], jnp.float32)[:, None]
    spread = jax.random.uniform(key, (2, HEADS), jnp.float32)
    lowest, highest = (0.3, 12.0)
    return jnp.exp(jnp.log(lowest) + spread * (jnp.log(highest) - jnp.log(lowest))) / lengths


def steps_of(rng, dims, shards, least, largest):
    def one(dim, blocks):
        heights = jax.random.uniform(jax.random.fold_in(jax.random.fold_in(rng, 6), dim), (blocks,), jnp.float32, least / len(shards), largest / len(shards))
        return jnp.repeat(jnp.exp(heights), dims[dim] // blocks).reshape((-1,) + (1,) * (len(dims) - dim - 1))

    level = one(*shards[0])
    for cut in shards[1:]:
        level = level * one(*cut)
    return level


def scatter_about(own_key, dims, scale, reach, pieces=(), dtype=jnp.bfloat16):
    loudness = steps_of(own_key, dims, pieces, -0.22, 0.18) if pieces else 1.0
    values = jax.random.normal(own_key, dims, jnp.float32) * scale * loudness
    return jnp.minimum(jnp.maximum(values, -reach), reach).astype(dtype)


def setup_inputs(seed: int = 0) -> dict:
    arg_keys = jax.random.split(jax.random.key(seed), 10)
    return {
        "x_in": scatter_about(arg_keys[0], (BATCH, H, W, INNER), 1.0, 6.0, ((0, 2), (1, 2), (2, 8))),
        "gate_in": scatter_about(arg_keys[1], (BATCH, H, W, INNER), 1.0, 6.0, ((0, 2), (1, 2), (2, 8))),
        "proj_bc": scatter_about(arg_keys[2], (BATCH, H, W, 4 * STATE), 0.5, 3.0, ((0, 2), (1, 2), (2, 8))),
        "dt_raw": scatter_about(arg_keys[3], (BATCH, H, W, 2 * HEADS), 0.5, 3.0, ((0, 2), (1, 2), (2, 8))),
        "step_index": jax.random.randint(arg_keys[4], (BATCH,), 0, STEPS).astype(jnp.int32),
        "step_table": jnp.clip(jax.random.uniform(arg_keys[5], (STEPS, 2 * HEADS), jnp.float32, -1.5, 0.5), -1.5, 0.5),
        "rates": draw_rates(jax.random.fold_in(arg_keys[9], 71), 0),
        "skip": jnp.clip(jnp.exp(jax.random.uniform(arg_keys[7], (HEADS,), jnp.float32, math.log(0.5), math.log(2.0))), 0.5, 2.0),
        "norm_gain": jnp.clip(1.0 + 0.1 * jax.random.normal(arg_keys[8], (INNER,), jnp.float32), 0.5, 1.5),
    }


def line_scan(inputs, decay_log, in_map, out_map):

    def advance(state_now, items):
        token_in, token_decay, token_b, token_c = items
        state_now = jnp.exp(token_decay)[:, :, None, None] * state_now + token_in[:, :, :, None] * token_b[:, None, None, :]
        result = jnp.einsum('lhpn,ln->lhp', state_now, token_c, precision=lax.Precision.HIGHEST)
        return (state_now, result)
    line_count = inputs.shape[0]
    start = jnp.zeros((line_count, HEADS, HEAD, STATE), jnp.float32)
    items = (jnp.moveaxis(inputs, 1, 0), jnp.moveaxis(decay_log, 1, 0), jnp.moveaxis(in_map, 1, 0), jnp.moveaxis(out_map, 1, 0))
    final, results = lax.scan(advance, start, items)
    return jnp.moveaxis(results, 0, 1)

def reference(x_in, gate_in, proj_bc, dt_raw, step_index, step_table, rates, skip, norm_gain):
    bias = step_table[step_index]
    step_size = jax.nn.softplus(dt_raw.astype(jnp.float32) + bias[:, None, None, :])
    decay_log = -rates.reshape(2 * HEADS) * step_size
    x_heads = x_in.astype(jnp.float32).reshape(BATCH, H, W, HEADS, HEAD)
    u_row = (step_size[..., :HEADS, None] * x_heads).astype(jnp.bfloat16)
    u_col = (step_size[..., HEADS:, None] * x_heads).astype(jnp.bfloat16)
    maps = proj_bc.astype(jnp.float32)
    y_row = line_scan(u_row.astype(jnp.float32).reshape(BATCH * H, W, HEADS, HEAD), decay_log[..., :HEADS].reshape(BATCH * H, W, HEADS), maps[..., :STATE].reshape(BATCH * H, W, STATE), maps[..., STATE:2 * STATE].reshape(BATCH * H, W, STATE))
    y_row = y_row.astype(jnp.bfloat16).reshape(BATCH, H, W, HEADS, HEAD)
    y_col = line_scan(jnp.swapaxes(u_col.astype(jnp.float32), 1, 2).reshape(BATCH * W, H, HEADS, HEAD), jnp.swapaxes(decay_log[..., HEADS:], 1, 2).reshape(BATCH * W, H, HEADS), jnp.swapaxes(maps[..., 2 * STATE:3 * STATE], 1, 2).reshape(BATCH * W, H, STATE), jnp.swapaxes(maps[..., 3 * STATE:], 1, 2).reshape(BATCH * W, H, STATE))
    y_col = jnp.swapaxes(y_col.astype(jnp.bfloat16).reshape(BATCH, W, H, HEADS, HEAD), 1, 2)
    gate = jax.nn.silu(gate_in.astype(jnp.float32).reshape(BATCH, H, W, HEADS, HEAD))
    mixed = (y_row.astype(jnp.float32) + y_col.astype(jnp.float32) + skip[:, None] * x_heads) * gate
    power = lax.optimization_barrier(jnp.mean(mixed * mixed, axis=(-2, -1), keepdims=True))
    normed = mixed * lax.rsqrt(power + 1e-05) * norm_gain.reshape(HEADS, HEAD)
    return normed.astype(jnp.bfloat16).reshape(BATCH, H, W, HEADS * HEAD)
```

```python
import functools

import jax
import jax.numpy as jnp
from jax import lax
from jax.experimental import pallas as pl
from jax.experimental.pallas import tpu as pltpu
from jax.sharding import PartitionSpec as P

LANES = 128
CHUNK = 512
F32 = jnp.float32
BF16 = jnp.bfloat16


def dot(a, b):
    return jnp.dot(a, b, preferred_element_type=F32)


def iota(shape, dim):
    return lax.broadcasted_iota(jnp.int32, shape, dim)


def parts(values, count):
    terms = []
    for _ in range(count):
        term = values.astype(BF16)
        terms.append(term)
        values = values - term.astype(F32)
    return jnp.concatenate(terms, axis=1)


def spread(pair, first_channel, channels, width):
    heads = pair.shape[1] // 2
    head_of = (first_channel + iota((2 * heads, channels), 1)) // width
    pick = (iota((2 * heads, channels), 0) % heads == head_of).astype(BF16)
    return dot(pair, pick)


def summed(mask, values):
    heads = values.shape[1]
    sums = dot(mask, parts(values, 3))
    return sums[:, :heads] + sums[:, heads : 2 * heads] + sums[:, 2 * heads :]


def step_sizes(raw, bias):
    shifted = raw.astype(F32) + bias
    return jnp.maximum(shifted, 0.0) + jnp.log1p(jnp.exp(-jnp.abs(shifted)))


def bias_row(index_ref, table_ref):
    return table_ref[pl.ds(index_ref[0] % 8, 1), :]


def row_prepare(index_ref, aux_ref, table_ref, rates_ref, mix, grow, fade, cols, lines, state):
    tokens = mix.shape[0]
    heads = fade.shape[1] // 2
    aux = aux_ref[...]
    steps = step_sizes(aux[:, :heads], bias_row(index_ref, table_ref)[:, :heads])
    decay = -rates_ref[0:1, :] * steps
    out, into = iota((tokens, tokens), 0), iota((tokens, tokens), 1)
    same = (out // cols) % lines == (into // cols) % lines
    lower = jnp.logical_and(same, out >= into)
    running = summed(lower.astype(BF16), decay)
    fade[...] = parts(jnp.exp(running), 2)
    grow[...] = parts(steps * jnp.exp(-running), 2)
    b = aux[:, heads : heads + state]
    c = aux[:, heads + state : heads + 2 * state]
    scores = lax.dot_general(c, b, (((1,), (1,)), ((), ())), preferred_element_type=F32)
    mix[...] = jnp.where(lower, scores, 0.0).astype(BF16)


def row_kernel(index_ref, x_ref, aux_ref, table_ref, rates_ref, y_ref, mix, grow, fade, *, cols, lines, state, width):
    step = pl.program_id(0)
    channels = x_ref.shape[1]

    @pl.when(step == 0)
    def _():
        row_prepare(index_ref, aux_ref, table_ref, rates_ref, mix, grow, fade, cols, lines, state)

    first = step * channels
    values = (x_ref[...].astype(F32) * spread(grow[...], first, channels, width)).astype(BF16)
    y_ref[...] = (dot(mix[...], values) * spread(fade[...], first, channels, width)).astype(BF16)


def col_running(index_ref, raw_ref, table_ref, rates_ref, lower, heads):
    steps = step_sizes(raw_ref[:, heads:], bias_row(index_ref, table_ref)[:, heads:])
    decay = -rates_ref[1:2, :] * steps
    return steps, decay, summed(lower, decay)


def widen(maps, cols, state):
    tokens = maps.shape[0]
    places = cols * state
    copy = (iota((state, places), 1) % state == iota((state, places), 0)).astype(BF16)
    own = iota((tokens, places), 1) // state == iota((tokens, places), 0) % cols
    return jnp.where(own, dot(maps, copy), 0.0).astype(BF16)


def state_kernel(index_ref, x_ref, raw_ref, maps_ref, table_ref, rates_ref, s_ref, into, grow, end, *, cols, state, width):
    step = pl.program_id(0)
    channels = x_ref.shape[1]
    tokens = x_ref.shape[0]
    heads = grow.shape[1] // 2

    @pl.when(step == 0)
    def _():
        a, b = iota((tokens, tokens), 0), iota((tokens, tokens), 1)
        lower = jnp.logical_and(a % cols == b % cols, a >= b).astype(BF16)
        steps, decay, running = col_running(index_ref, raw_ref, table_ref, rates_ref, lower, heads)
        grow[...] = parts(steps * jnp.exp(-running), 2)
        places = (cols * state, tokens)
        whole = (iota(places, 0) // state == iota(places, 1) % cols).astype(BF16)
        end[...] = parts(jnp.exp(summed(whole, decay)), 2)
        into[...] = widen(maps_ref[:, 2 * state : 3 * state], cols, state).astype(F32).T.astype(BF16)

    first = step * channels
    values = (x_ref[...].astype(F32) * spread(grow[...], first, channels, width)).astype(BF16)
    s_ref[...] = (dot(into[...], values) * spread(end[...], first, channels, width)).astype(BF16)


def final_kernel(
    index_ref, x_ref, gate_ref, row_ref, s_ref, raw_ref, maps_ref, table_ref, rates_ref, skip_ref, gain_ref,
    out_ref, mix, grow, fade, kept, power, *, cols, state, width
):
    step = pl.program_id(0)
    channels = x_ref.shape[1]
    tokens = x_ref.shape[0]
    heads = grow.shape[1] // 2

    @pl.when(step == 0)
    def _():
        a, b = iota((tokens, tokens), 0), iota((tokens, tokens), 1)
        lower = jnp.logical_and(a % cols == b % cols, a >= b)
        steps, decay, running = col_running(
            index_ref, raw_ref, table_ref, rates_ref, lower.astype(BF16), heads
        )
        fade[...] = parts(jnp.exp(running), 2)
        grow[...] = parts(steps * jnp.exp(-running), 2)
        b_map = maps_ref[:, 2 * state : 3 * state]
        c_map = maps_ref[:, 3 * state :]
        scores = lax.dot_general(c_map, b_map, (((1,), (1,)), ((), ())), preferred_element_type=F32)
        mix[:, :tokens] = jnp.where(lower, scores, 0.0).astype(BF16)
        mix[:, tokens:] = widen(c_map, cols, state)
        power[...] = jnp.zeros_like(power)

    first = step * channels
    x = x_ref[...].astype(F32)
    values = (x * spread(grow[...], first, channels, width)).astype(BF16)
    y_col = dot(mix[...], jnp.concatenate([values, s_ref[...]], axis=0))
    y_col = y_col * spread(fade[...], first, channels, width)
    gate = gate_ref[...].astype(F32)
    v = (row_ref[...].astype(F32) + y_col + skip_ref[...] * x) * (gate / (1.0 + jnp.exp(-gate)))
    kept[step] = v
    power[...] += jnp.sum(v * v, axis=1, keepdims=True)

    @pl.when(step == pl.num_programs(0) - 1)
    def _():
        count = kept.shape[0]
        scale = lax.rsqrt(power[:, 0:1] / (count * channels) + 1e-5)
        for i in range(count):
            part = pl.ds(i * channels, channels)
            out_ref[:, part] = (kept[i] * scale * gain_ref[:, part]).astype(BF16)


def call(kernel, grid, in_specs, out_specs, out_shape, scratch, cost):
    return pl.pallas_call(
        kernel,
        grid_spec=pltpu.PrefetchScalarGridSpec(
            num_scalar_prefetch=1,
            grid=grid,
            in_specs=in_specs,
            out_specs=out_specs,
            scratch_shapes=scratch,
        ),
        out_shape=out_shape,
        compiler_params=pltpu.CompilerParams(vmem_limit_bytes=32 * 1024 * 1024),
        cost_estimate=pl.CostEstimate(flops=cost[0], bytes_accessed=cost[1], transcendentals=0),
    )


def entering_states(ends, state_decay, axis, count):
    onward = [(i, i + 1) for i in range(count - 1)]
    if count == 1:
        return jnp.zeros_like(ends)
    entering = lax.ppermute(ends, axis, onward)
    for _ in range(count - 2):
        passed = (ends.astype(F32) + state_decay() * entering.astype(F32)).astype(BF16)
        entering = lax.ppermute(passed, axis, onward)
    return entering


def body(x_in, gate_in, proj_bc, dt_raw, step_index, step_table, rates, skip, norm_gain, *, row_count, col_count):
    images, tile_rows, tile_cols, channels = x_in.shape
    heads = skip.shape[0]
    width = channels // heads
    state = proj_bc.shape[-1] // 4
    tokens = images * tile_rows * tile_cols
    lines = images * tile_rows // col_count
    chunk = CHUNK
    steps = channels // chunk
    places = tile_cols * state

    x = x_in.reshape(tokens, channels)
    gate = gate_in.reshape(tokens, channels)
    maps = proj_bc.reshape(tokens, 4 * state)
    raw = dt_raw.reshape(tokens, 2 * heads)

    table_spec = pl.BlockSpec((8, 2 * heads), lambda i, index: (index[0] // 8, 0))
    whole = lambda shape: pl.BlockSpec(shape, lambda i, index: (0,) * len(shape))
    part = lambda rows: pl.BlockSpec((rows, chunk), lambda i, index: (0, i))
    pair = pltpu.VMEM((tokens, 2 * heads), BF16)

    aux = jnp.concatenate(
        [raw[:, :heads], maps[:, : 2 * state], jnp.zeros((tokens, LANES - heads - 2 * state), BF16)], axis=1
    )
    sent = jnp.concatenate([x, aux], axis=1).reshape(col_count, tokens // col_count, channels + LANES)
    got = lax.all_to_all(sent, "col", split_axis=0, concat_axis=0, tiled=True)
    got = got.reshape(tokens, channels + LANES)

    ends = call(
        functools.partial(state_kernel, cols=tile_cols, state=state, width=width),
        (steps,),
        [part(tokens), whole((tokens, 2 * heads)), whole((tokens, 4 * state)), table_spec, whole((2, heads))],
        part(places),
        jax.ShapeDtypeStruct((places, channels), BF16),
        [pltpu.VMEM((places, tokens), BF16), pair, pltpu.VMEM((places, 2 * heads), BF16)],
        (2 * places * tokens * channels, 2 * tokens * channels),
    )(step_index, x, raw, maps, step_table, rates)

    def state_decay():
        bias = lax.dynamic_slice_in_dim(step_table, step_index[0], 1, 0)[:, heads:]
        total = -rates[1] * jnp.sum(
            jax.nn.softplus(raw[:, heads:].astype(F32) + bias).reshape(tile_rows, tile_cols, heads), axis=0
        )
        return jnp.repeat(jnp.repeat(jnp.exp(total), state, axis=0), width, axis=1)

    entering = entering_states(ends, state_decay, "row", row_count)

    y_row = call(
        functools.partial(row_kernel, cols=tile_cols, lines=lines, state=state, width=width),
        (steps,),
        [
            part(tokens),
            pl.BlockSpec((tokens, LANES), lambda i, index: (0, channels // LANES)),
            table_spec,
            whole((2, heads)),
        ],
        part(tokens),
        jax.ShapeDtypeStruct((tokens, channels), BF16),
        [pltpu.VMEM((tokens, tokens), BF16), pair, pair],
        (2 * tokens * tokens * channels, 4 * tokens * channels),
    )(step_index, got, got, step_table, rates)
    y_row = lax.all_to_all(
        y_row.reshape(col_count, tokens // col_count, channels), "col", split_axis=0, concat_axis=0, tiled=True
    ).reshape(tokens, channels)

    mixed = call(
        functools.partial(final_kernel, cols=tile_cols, state=state, width=width),
        (steps,),
        [
            part(tokens),
            part(tokens),
            part(tokens),
            part(places),
            whole((tokens, 2 * heads)),
            whole((tokens, 4 * state)),
            table_spec,
            whole((2, heads)),
            pl.BlockSpec((1, chunk), lambda i, index: (0, i)),
            whole((1, channels)),
        ],
        whole((tokens, channels)),
        jax.ShapeDtypeStruct((tokens, channels), BF16),
        [
            pltpu.VMEM((tokens, tokens + places), BF16),
            pair,
            pair,
            pltpu.VMEM((steps, tokens, chunk), F32),
            pltpu.VMEM((tokens, LANES), F32),
        ],
        (2 * tokens * tokens * channels, 8 * tokens * channels),
    )(
        step_index, x, gate, y_row, entering, raw, maps, step_table, rates,
        jnp.repeat(skip, width).reshape(1, channels), norm_gain.reshape(1, channels),
    )
    return mixed.reshape(x_in.shape)


def solution(mesh):
    tile = P("img", "row", "col", None)
    return jax.shard_map(
        functools.partial(body, row_count=mesh.shape["row"], col_count=mesh.shape["col"]),
        mesh=mesh,
        in_specs=(tile, tile, tile, tile, P("img"), P(), P(), P(), P()),
        out_specs=tile,
        check_vma=False,
    )
```

```python
import functools

import jax
import jax.numpy as jnp
from jax import lax
from jax.experimental import pallas as pl
from jax.experimental.pallas import tpu as pltpu
from jax.sharding import PartitionSpec as P

LANES = 128
GROUP = 4
PIECES = 2
STRIP = 512
F32 = jnp.float32
BF16 = jnp.bfloat16


def dot(a, b):
    return jnp.dot(a, b, preferred_element_type=F32)


def iota(shape, dim):
    return lax.broadcasted_iota(jnp.int32, shape, dim)


def div(a, n):
    return lax.shift_right_logical(a, n.bit_length() - 1) if n & (n - 1) == 0 else a // n


def mod(a, n):
    return jnp.bitwise_and(a, n - 1) if n & (n - 1) == 0 else a % n


def parts(values, count):
    terms = []
    for _ in range(count):
        term = values.astype(BF16)
        terms.append(term)
        values = values - term.astype(F32)
    return jnp.concatenate(terms, axis=1)


def picks(heads, width, first, channels):
    row = iota((2 * heads, 1), 0)
    head = jnp.where(row >= heads, row - heads, row)
    return (head == div(first + iota((1, channels), 1), width)).astype(BF16)


def summed(mask, values):
    heads = values.shape[1]
    sums = dot(mask, parts(values, 3))
    return sums[:, :heads] + sums[:, heads : 2 * heads] + sums[:, 2 * heads :]


def step_sizes(raw, bias):
    shifted = raw.astype(F32) + bias
    return jnp.maximum(shifted, 0.0) + jnp.log1p(jnp.exp(-jnp.abs(shifted)))


def widen(maps, line, lines):
    state = maps.shape[1]
    places = lines * state
    copy = (mod(iota((1, places), 1), state) == iota((state, 1), 0)).astype(BF16)
    own = div(iota((1, places), 1), state) == line
    return jnp.where(own, dot(maps, copy), 0.0).astype(BF16)


class Scan:
    def __init__(self, order, lines, raw, bias, rates, b_map, c_map):
        tokens, self.heads = raw.shape
        self.lines, self.b_map, self.c_map = lines, b_map, c_map
        self.line, place = order(iota((tokens, 1), 0))
        self.line_in, place_in = order(iota((1, tokens), 1))
        self.lower = jnp.logical_and(self.line == self.line_in, place >= place_in)
        steps = step_sizes(raw, bias)
        self.decay = -rates * steps
        running = summed(self.lower.astype(BF16), self.decay)
        self.fade = parts(jnp.exp(running), 2)
        self.grow = parts(steps * jnp.exp(-running), 2)

    def ends(self):
        places = self.lines * self.b_map.shape[1]
        own = div(iota((places, 1), 0), self.b_map.shape[1]) == self.line_in
        return jnp.exp(summed(own.astype(BF16), self.decay))

    def into(self):
        return widen(self.b_map, self.line, self.lines).astype(F32).T.astype(BF16)

    def mix(self):
        scores = lax.dot_general(
            self.c_map, self.b_map, (((1,), (1,)), ((), ())), preferred_element_type=F32
        )
        within = jnp.where(self.lower, scores, 0.0).astype(BF16)
        return jnp.concatenate([within, widen(self.c_map, self.line, self.lines)], axis=1)


def column_order(cols):
    return lambda token: (mod(token, cols), div(token, cols))


def row_order(cols, lines, member):
    def order(token):
        source = jnp.bitwise_xor(div(token, cols * lines), member)
        return mod(div(token, cols), lines), source * cols + mod(token, cols)

    return order


def strips(channels):
    return [(first, min(STRIP, channels - first)) for first in range(0, channels, STRIP)]


def pack_kernel(index_ref, x_ref, raw_ref, maps_ref, table_ref, bias_ref, *sent, group, axis, heads, state):
    member = mod(lax.axis_index(axis), group)
    pieces = len(sent) // group
    share = x_ref.shape[0] // group
    rows = share // pieces
    channels = x_ref.shape[1]
    for s in range(group):
        for piece in range(pieces):
            first = pl.multiple_of(jnp.bitwise_xor(member, s) * share + piece * rows, rows)
            part = pl.ds(first, rows)
            out = sent[piece * group + s]
            out[:, :channels] = x_ref[part, :]
            used = heads + 2 * state
            out[:, channels : channels + heads] = raw_ref[part, :heads]
            out[:, channels + heads : channels + used] = maps_ref[part, : 2 * state]
            out[:, channels + used :] = jnp.zeros((rows, LANES - used), BF16)
    lanes = table_ref.shape[1]
    mine = iota(table_ref.shape, 1) == mod(index_ref[0], lanes)
    row = jnp.where(mine, table_ref[...], 0.0)
    ones = jnp.ones((8, lanes), BF16)
    total = jnp.zeros((8, row.shape[0]), F32)
    for _ in range(3):
        term = row.astype(BF16)
        row = row - term.astype(F32)
        total += lax.dot_general(ones, term, (((1,), (1,)), ((), ())), preferred_element_type=F32)
    bias_ref[...] = total


def row_scan(bias_ref, rates_ref, blocks, member, cols, heads, state):
    channels = blocks[0].shape[1] - LANES
    tokens = blocks[0].shape[0] * len(blocks)
    lines = tokens // (cols * len(blocks))
    aux = jnp.concatenate([block[:, channels:] for block in blocks], axis=0)
    return Scan(
        row_order(cols, lines, member),
        lines,
        aux[:, :heads],
        bias_ref[0:1, :heads],
        rates_ref[0:1, :],
        aux[:, heads : heads + state],
        aux[:, heads + state : heads + 2 * state],
    )


def col_scan(bias_ref, rates_ref, raw_ref, maps_ref, cols, heads, state):
    return Scan(
        column_order(cols),
        cols,
        raw_ref[:, heads:],
        bias_ref[0:1, heads:],
        rates_ref[1:2, :],
        maps_ref[:, 2 * state : 3 * state],
        maps_ref[:, 3 * state :],
    )


def write_state(scan, tokens_of, width, channels, s_ref, factor_ref):
    ends = scan.ends()
    if factor_ref:
        factor_ref[0][...] = ends
    ends = parts(ends, 2)
    into = scan.into()
    for first, count in strips(channels):
        pick = picks(scan.heads, width, first, count)
        values = (tokens_of(first, count) * dot(scan.grow, pick)).astype(BF16)
        s_ref[:, first : first + count] = (dot(into, values) * dot(ends, pick)).astype(BF16)


def row_state_kernel(bias_ref, rates_ref, *refs, group, axis, cols, heads, state, width):
    blocks, s_ref, factor_ref = refs[:group], refs[group], refs[group + 1 :]
    member = mod(lax.axis_index(axis), group)
    scan = row_scan(bias_ref, rates_ref, blocks, member, cols, heads, state)
    tokens_of = lambda first, count: jnp.concatenate(
        [block[:, first : first + count] for block in blocks], axis=0
    ).astype(F32)
    write_state(scan, tokens_of, width, s_ref.shape[1], s_ref, factor_ref)


def col_state_kernel(bias_ref, rates_ref, x_ref, raw_ref, maps_ref, s_ref, *factor_ref, cols, heads, state, width):
    scan = col_scan(bias_ref, rates_ref, raw_ref, maps_ref, cols, heads, state)
    tokens_of = lambda first, count: x_ref[:, first : first + count].astype(F32)
    write_state(scan, tokens_of, width, s_ref.shape[1], s_ref, factor_ref)


def row_out_kernel(bias_ref, rates_ref, s_ref, *refs, group, axis, cols, heads, state, width):
    blocks, outs = refs[:group], refs[group:]
    member = mod(lax.axis_index(axis), group)
    scan = row_scan(bias_ref, rates_ref, blocks, member, cols, heads, state)
    mix = scan.mix()
    rows = blocks[0].shape[0]
    for first, count in strips(s_ref.shape[1]):
        pick = picks(heads, width, first, count)
        part = slice(first, first + count)
        x = jnp.concatenate([block[:, part] for block in blocks], axis=0).astype(F32)
        values = (x * dot(scan.grow, pick)).astype(BF16)
        y = dot(mix, jnp.concatenate([values, s_ref[:, part]], axis=0)) * dot(scan.fade, pick)
        for s in range(group):
            outs[s][:, part] = y[s * rows : (s + 1) * rows].astype(BF16)


def col_out_kernel(bias_ref, rates_ref, s_ref, x_ref, raw_ref, maps_ref, skip_ref, w_ref, *, cols, heads, state, width):
    scan = col_scan(bias_ref, rates_ref, raw_ref, maps_ref, cols, heads, state)
    mix = scan.mix()
    for first, count in strips(s_ref.shape[1]):
        pick = picks(heads, width, first, count)
        part = slice(first, first + count)
        x = x_ref[:, part].astype(F32)
        values = (x * dot(scan.grow, pick)).astype(BF16)
        y = dot(mix, jnp.concatenate([values, s_ref[:, part]], axis=0)) * dot(scan.fade, pick)
        w_ref[:, part] = y + skip_ref[:, part] * x


def final_kernel(w_ref, gate_ref, gain_ref, *refs, group, axis):
    rows_of, out_ref = refs[:-1], refs[-1]
    pieces = len(rows_of) // group
    rows, channels = rows_of[0].shape
    member = mod(lax.axis_index(axis), group)
    for piece in range(pieces):
        for s in range(group):
            first = (jnp.bitwise_xor(member, s) * pieces + piece) * rows
            part = pl.ds(pl.multiple_of(first, rows), rows)
            gate = gate_ref[part, :].astype(F32)
            v = (rows_of[piece * group + s][...].astype(F32) + w_ref[part, :]) * (gate / (1.0 + jnp.exp(-gate)))
            power = jnp.sum(v * v, axis=1, keepdims=True) / channels
            out_ref[part, :] = (v * lax.rsqrt(power + 1e-5) * gain_ref[...]).astype(BF16)


def call(kernel, out_shape, flops, moved):
    return pl.pallas_call(
        kernel,
        out_shape=out_shape,
        compiler_params=pltpu.CompilerParams(vmem_limit_bytes=32 * 1024 * 1024),
        cost_estimate=pl.CostEstimate(flops=flops, bytes_accessed=moved, transcendentals=0),
    )


def entering_states(made, axis, size, stride, width):
    ends = made[0]
    onward = [(i, i + stride) for i in range(size - stride)]
    if not onward:
        return jnp.zeros_like(ends)
    entering = lax.ppermute(ends, axis, onward)
    for _ in range(size // stride - 2):
        factor = jnp.repeat(made[1], width, axis=1)
        entering = lax.ppermute(
            (ends.astype(F32) + factor * entering.astype(F32)).astype(BF16), axis, onward
        )
    return entering


def body(x_in, gate_in, proj_bc, dt_raw, step_index, step_table, rates, skip, norm_gain, *, row_count, col_count):
    _, tile_rows, cols, channels = x_in.shape
    heads = skip.shape[0]
    width = channels // heads
    state = proj_bc.shape[-1] // 4
    tokens = tile_rows * cols
    group = GROUP
    while col_count % group:
        group //= 2
    share = tokens // group // PIECES
    lines = share // cols

    x = x_in.reshape(tokens, channels)
    gate = gate_in.reshape(tokens, channels)
    maps = proj_bc.reshape(tokens, 4 * state)
    raw = dt_raw.reshape(tokens, 2 * heads)
    sizes = dict(cols=cols, heads=heads, state=state, width=width)
    shared = dict(group=group, axis="col")
    shape = jax.ShapeDtypeStruct

    full = lambda *dims: pl.BlockSpec(dims, lambda i, index: (0,) * len(dims))
    packed = pl.pallas_call(
        functools.partial(pack_kernel, heads=heads, state=state, **shared),
        grid_spec=pltpu.PrefetchScalarGridSpec(
            num_scalar_prefetch=1,
            grid=(1,),
            in_specs=[
                full(tokens, channels),
                full(tokens, 2 * heads),
                full(tokens, 4 * state),
                pl.BlockSpec((2 * heads, LANES), lambda i, index: (0, index[0] // LANES)),
            ],
            out_specs=[full(8, 2 * heads)] + [full(share, channels + LANES)] * (group * PIECES),
        ),
        out_shape=[shape((8, 2 * heads), F32)] + [shape((share, channels + LANES), BF16)] * (group * PIECES),
        compiler_params=pltpu.CompilerParams(vmem_limit_bytes=32 * 1024 * 1024),
        cost_estimate=pl.CostEstimate(flops=0, bytes_accessed=4 * tokens * channels, transcendentals=0),
    )(step_index, x, raw, maps, step_table.T)
    bias, packed = packed[0], packed[1:]

    def exchange(blocks):
        return [blocks[0]] + [
            lax.ppermute(blocks[s], "col", [(i, i ^ s) for i in range(col_count)]) for s in range(1, group)
        ]

    def state_shapes(places, count):
        return [shape((places, channels), BF16)] + [shape((places, heads), F32)] * (count > 2)

    got = [exchange(packed[piece * group : (piece + 1) * group]) for piece in range(PIECES)]

    col_made = call(
        functools.partial(col_state_kernel, **sizes),
        state_shapes(cols * state, row_count),
        2 * cols * state * tokens * channels,
        2 * tokens * channels,
    )(bias, rates, x, raw, maps)
    col_entering = entering_states(col_made, "row", row_count, 1, width)

    row_entering = []
    for piece in range(PIECES):
        made = call(
            functools.partial(row_state_kernel, **sizes, **shared),
            state_shapes(lines * state, col_count // group),
            2 * lines * state * group * share * channels,
            2 * group * share * channels,
        )(bias, rates, *got[piece])
        row_entering.append(entering_states(made, "col", col_count, group, width))

    w = call(
        functools.partial(col_out_kernel, **sizes),
        shape((tokens, channels), F32),
        2 * tokens * tokens * channels,
        8 * tokens * channels,
    )(bias, rates, col_entering, x, raw, maps, jnp.repeat(skip, width).reshape(1, channels))

    back = []
    for piece in range(PIECES):
        y_row = call(
            functools.partial(row_out_kernel, **sizes, **shared),
            [shape((share, channels), BF16)] * group,
            2 * (group * share) ** 2 * channels,
            4 * group * share * channels,
        )(bias, rates, row_entering[piece], *got[piece])
        back += exchange(y_row)

    mixed = call(
        functools.partial(final_kernel, **shared),
        shape((tokens, channels), BF16),
        10 * tokens * channels,
        10 * tokens * channels,
    )(w, gate, norm_gain.reshape(1, channels), *back)
    return mixed.reshape(x_in.shape)


def solution(mesh):
    tile = P("img", "row", "col", None)
    return jax.shard_map(
        functools.partial(body, row_count=mesh.shape["row"], col_count=mesh.shape["col"]),
        mesh=mesh,
        in_specs=(tile, tile, tile, tile, P("img"), P(), P(), P(), P()),
        out_specs=tile,
        check_vma=False,
    )
```

```python
import functools

import jax
import jax.numpy as jnp
from jax import lax
from jax.experimental import pallas as pl
from jax.experimental.pallas import tpu as pltpu
from jax.sharding import PartitionSpec as P

LANES = 128
GROUP = 4
PIECES = 2
STRIP = 512
F32 = jnp.float32
BF16 = jnp.bfloat16


def dot(a, b):
    return jnp.dot(a, b, preferred_element_type=F32)


def iota(shape, dim):
    return lax.broadcasted_iota(jnp.int32, shape, dim)


def div(a, n):
    return lax.shift_right_logical(a, n.bit_length() - 1) if n & (n - 1) == 0 else a // n


def mod(a, n):
    return jnp.bitwise_and(a, n - 1) if n & (n - 1) == 0 else a % n


def parts(values, count):
    terms = []
    for _ in range(count):
        term = values.astype(BF16)
        terms.append(term)
        values = values - term.astype(F32)
    return jnp.concatenate(terms, axis=1)


def picks(heads, width, first, channels):
    row = iota((2 * heads, 1), 0)
    head = jnp.where(row >= heads, row - heads, row)
    return (head == div(first + iota((1, channels), 1), width)).astype(BF16)


def summed(mask, values):
    heads = values.shape[1]
    sums = dot(mask, parts(values, 3))
    return sums[:, :heads] + sums[:, heads : 2 * heads] + sums[:, 2 * heads :]


def step_sizes(raw, bias):
    shifted = raw.astype(F32) + bias
    return jnp.maximum(shifted, 0.0) + jnp.log1p(jnp.exp(-jnp.abs(shifted)))


def widen(maps, line, lines):
    state = maps.shape[1]
    places = lines * state
    copy = (mod(iota((1, places), 1), state) == iota((state, 1), 0)).astype(BF16)
    own = div(iota((1, places), 1), state) == line
    return jnp.where(own, dot(maps, copy), 0.0).astype(BF16)


class Scan:
    def __init__(self, order, lines, raw, bias, rates, b_map, c_map):
        tokens, self.heads = raw.shape
        self.lines, self.b_map, self.c_map = lines, b_map, c_map
        self.line, place = order(iota((tokens, 1), 0))
        self.line_in, place_in = order(iota((1, tokens), 1))
        self.lower = jnp.logical_and(self.line == self.line_in, place >= place_in)
        steps = step_sizes(raw, bias)
        self.decay = -rates * steps
        running = summed(self.lower.astype(BF16), self.decay)
        self.fade = parts(jnp.exp(running), 2)
        self.grow = parts(steps * jnp.exp(-running), 2)

    def ends(self):
        places = self.lines * self.b_map.shape[1]
        own = div(iota((places, 1), 0), self.b_map.shape[1]) == self.line_in
        return jnp.exp(summed(own.astype(BF16), self.decay))

    def into(self):
        return widen(self.b_map, self.line, self.lines).astype(F32).T.astype(BF16)

    def mix(self):
        scores = lax.dot_general(
            self.c_map, self.b_map, (((1,), (1,)), ((), ())), preferred_element_type=F32
        )
        within = jnp.where(self.lower, scores, 0.0).astype(BF16)
        return jnp.concatenate([within, widen(self.c_map, self.line, self.lines)], axis=1)


def column_order(cols):
    return lambda token: (mod(token, cols), div(token, cols))


def row_order(cols, lines, member):
    def order(token):
        source = jnp.bitwise_xor(div(token, cols * lines), member)
        return mod(div(token, cols), lines), source * cols + mod(token, cols)

    return order


def strips(channels):
    return [(first, min(STRIP, channels - first)) for first in range(0, channels, STRIP)]


def pack_kernel(
    index_ref, x_ref, raw_ref, maps_ref, table_ref, rates_ref, params_ref, *refs, group, axis, heads, state
):
    sent, (raw, maps, table, rates, sems) = refs[:-5], refs[-5:]
    member = mod(lax.axis_index(axis), group)
    pieces = len(sent) // group
    share = x_ref.shape[0] // group
    rows = share // pieces
    channels = x_ref.shape[1]
    small = [(raw_ref, raw), (maps_ref, maps), (table_ref, table), (rates_ref, rates)]
    copies = [pltpu.make_async_copy(a, b, sems.at[i]) for i, (a, b) in enumerate(small)]
    places = []
    for piece in range(pieces):
        for s in range(group):
            first = pl.multiple_of(jnp.bitwise_xor(member, s) * share + piece * rows, rows)
            out = sent[piece * group + s]
            places.append((out, pl.ds(first, rows)))
            copies.append(
                pltpu.make_async_copy(
                    x_ref.at[pl.ds(first, rows), :], out.at[:, pl.ds(0, channels)], sems.at[len(copies)]
                )
            )
    for copy in copies:
        copy.start()
    for copy in copies[: len(small)]:
        copy.wait()
    used = heads + 2 * state
    for out, part in places:
        out[:, channels : channels + heads] = raw[part, :heads]
        out[:, channels + heads : channels + used] = maps[part, : 2 * state]
        out[:, channels + used :] = jnp.zeros((rows, LANES - used), BF16)
    row = jnp.where(iota(table.shape, 1) == index_ref[0], table[...], 0.0)
    ones = jnp.ones((8, table.shape[1]), BF16)
    bias = jnp.zeros((8, row.shape[0]), F32)
    for _ in range(3):
        term = row.astype(BF16)
        row = row - term.astype(F32)
        bias += lax.dot_general(ones, term, (((1,), (1,)), ((), ())), preferred_element_type=F32)
    params_ref[0:1, :] = bias[0:1, :]
    params_ref[1:2, :heads] = rates[0:1, :]
    params_ref[1:2, heads:] = rates[1:2, :]
    params_ref[2:, :] = jnp.zeros((6, 2 * heads), F32)
    for copy in copies[len(small) :]:
        copy.wait()


def row_scan(params_ref, blocks, member, cols, heads, state):
    channels = blocks[0].shape[1] - LANES
    tokens = blocks[0].shape[0] * len(blocks)
    lines = tokens // (cols * len(blocks))
    aux = jnp.concatenate([block[:, channels:] for block in blocks], axis=0)
    return Scan(
        row_order(cols, lines, member),
        lines,
        aux[:, :heads],
        params_ref[0:1, :heads],
        params_ref[1:2, :heads],
        aux[:, heads : heads + state],
        aux[:, heads + state : heads + 2 * state],
    )


def col_scan(params_ref, raw_ref, maps_ref, cols, heads, state):
    return Scan(
        column_order(cols),
        cols,
        raw_ref[:, heads:],
        params_ref[0:1, heads:],
        params_ref[1:2, heads:],
        maps_ref[:, 2 * state : 3 * state],
        maps_ref[:, 3 * state :],
    )


def write_state(scan, tokens_of, width, channels, s_ref, factor_ref):
    ends = scan.ends()
    if factor_ref:
        factor_ref[0][...] = ends
    ends = parts(ends, 2)
    into = scan.into()
    for first, count in strips(channels):
        pick = picks(scan.heads, width, first, count)
        values = (tokens_of(first, count) * dot(scan.grow, pick)).astype(BF16)
        s_ref[:, first : first + count] = (dot(into, values) * dot(ends, pick)).astype(BF16)


def row_state_kernel(params_ref, *refs, group, axis, cols, heads, state, width):
    blocks, s_ref, factor_ref = refs[:group], refs[group + 1], refs[group + 2 :]
    member = mod(lax.axis_index(axis), group)
    scan = row_scan(params_ref, blocks, member, cols, heads, state)
    tokens_of = lambda first, count: jnp.concatenate(
        [block[:, first : first + count] for block in blocks], axis=0
    ).astype(F32)
    write_state(scan, tokens_of, width, s_ref.shape[1], s_ref, factor_ref)


def col_state_kernel(params_ref, x_ref, raw_ref, maps_ref, _, s_ref, *factor_ref, cols, heads, state, width):
    scan = col_scan(params_ref, raw_ref, maps_ref, cols, heads, state)
    tokens_of = lambda first, count: x_ref[:, first : first + count].astype(F32)
    write_state(scan, tokens_of, width, s_ref.shape[1], s_ref, factor_ref)


def row_out_kernel(params_ref, s_ref, *refs, group, axis, cols, heads, state, width):
    blocks, outs = refs[:group], refs[group + 1 :]
    member = mod(lax.axis_index(axis), group)
    scan = row_scan(params_ref, blocks, member, cols, heads, state)
    mix = scan.mix()
    rows = blocks[0].shape[0]
    for first, count in strips(s_ref.shape[1]):
        pick = picks(heads, width, first, count)
        part = slice(first, first + count)
        x = jnp.concatenate([block[:, part] for block in blocks], axis=0).astype(F32)
        values = (x * dot(scan.grow, pick)).astype(BF16)
        y = dot(mix, jnp.concatenate([values, s_ref[:, part]], axis=0)) * dot(scan.fade, pick)
        for s in range(group):
            outs[s][:, part] = y[s * rows : (s + 1) * rows].astype(BF16)


def col_out_kernel(params_ref, s_ref, x_ref, raw_ref, maps_ref, skip_ref, w_ref, *, cols, heads, state, width):
    scan = col_scan(params_ref, raw_ref, maps_ref, cols, heads, state)
    mix = scan.mix()
    for first, count in strips(s_ref.shape[1]):
        pick = picks(heads, width, first, count)
        part = slice(first, first + count)
        x = x_ref[:, part].astype(F32)
        values = (x * dot(scan.grow, pick)).astype(BF16)
        y = dot(mix, jnp.concatenate([values, s_ref[:, part]], axis=0)) * dot(scan.fade, pick)
        w_ref[:, part] = y + skip_ref[:, part] * x


def final_kernel(w_ref, gate_ref, gain_ref, *refs, group, axis):
    rows_of, out_ref = refs[:-1], refs[-1]
    pieces = len(rows_of) // group
    rows, channels = rows_of[0].shape
    member = mod(lax.axis_index(axis), group)
    for piece in range(pieces):
        for s in range(group):
            first = (jnp.bitwise_xor(member, s) * pieces + piece) * rows
            part = pl.ds(pl.multiple_of(first, rows), rows)
            gate = gate_ref[part, :].astype(F32)
            v = (rows_of[piece * group + s][...].astype(F32) + w_ref[part, :]) * (gate / (1.0 + jnp.exp(-gate)))
            power = jnp.sum(v * v, axis=1, keepdims=True) / channels
            out_ref[part, :] = (v * lax.rsqrt(power + 1e-5) * gain_ref[...]).astype(BF16)


SMALL = pl.CostEstimate(flops=1024, bytes_accessed=1024, transcendentals=0)
LONG = pl.CostEstimate(flops=2 * 10**10, bytes_accessed=1024, transcendentals=0)


def call(kernel, out_shape, specs=None, cost=SMALL):
    more = {} if specs is None else dict(in_specs=[spec or pl.BlockSpec() for spec in specs])
    return pl.pallas_call(
        kernel,
        **more,
        out_shape=out_shape,
        compiler_params=pltpu.CompilerParams(vmem_limit_bytes=32 * 1024 * 1024),
        cost_estimate=cost,
    )


def entering_states(made, axis, size, stride, width):
    ends = made[0]
    onward = [(i, i + stride) for i in range(size - stride)]
    if not onward:
        return jnp.zeros_like(ends)
    entering = lax.ppermute(ends, axis, onward)
    for _ in range(size // stride - 2):
        factor = jnp.repeat(made[1], width, axis=1)
        entering = lax.ppermute(
            (ends.astype(F32) + factor * entering.astype(F32)).astype(BF16), axis, onward
        )
    return entering


def body(x_in, gate_in, proj_bc, dt_raw, step_index, step_table, rates, skip, norm_gain, *, row_count, col_count):
    _, tile_rows, cols, channels = x_in.shape
    heads = skip.shape[0]
    width = channels // heads
    state = proj_bc.shape[-1] // 4
    tokens = tile_rows * cols
    group = GROUP
    while col_count % group:
        group //= 2
    share = tokens // group // PIECES
    lines = share // cols

    x = x_in.reshape(tokens, channels)
    gate = gate_in.reshape(tokens, channels)
    maps = proj_bc.reshape(tokens, 4 * state)
    raw = dt_raw.reshape(tokens, 2 * heads)
    sizes = dict(cols=cols, heads=heads, state=state, width=width)
    shared = dict(group=group, axis="col")
    shape = jax.ShapeDtypeStruct

    any_spec = pl.BlockSpec(memory_space=pl.ANY)
    hbm_spec = pl.BlockSpec(memory_space=pltpu.HBM)
    full = lambda *dims: pl.BlockSpec(dims, lambda i, index: (0,) * len(dims))
    packed = pl.pallas_call(
        functools.partial(pack_kernel, heads=heads, state=state, **shared),
        grid_spec=pltpu.PrefetchScalarGridSpec(
            num_scalar_prefetch=1,
            grid=(1,),
            in_specs=[hbm_spec] * 5,
            out_specs=[full(8, 2 * heads)] + [full(share, channels + LANES)] * (group * PIECES),
            scratch_shapes=[
                pltpu.VMEM(raw.shape, BF16),
                pltpu.VMEM(maps.shape, BF16),
                pltpu.VMEM(step_table.shape[::-1], F32),
                pltpu.VMEM(rates.shape, F32),
                pltpu.SemaphoreType.DMA((4 + group * PIECES,)),
            ],
        ),
        out_shape=[pltpu.VMEM((8, 2 * heads), F32)] + [pltpu.VMEM((share, channels + LANES), BF16)] * (group * PIECES),
        compiler_params=pltpu.CompilerParams(vmem_limit_bytes=32 * 1024 * 1024),
        cost_estimate=SMALL,
    )(step_index, *[pltpu.with_memory_space_constraint(a, pltpu.HBM) for a in (x, raw, maps, step_table.T, rates)])
    params, packed = packed[0], packed[1:]

    def exchange(blocks):
        return [blocks[0]] + [
            lax.ppermute(blocks[s], "col", [(i, i ^ s) for i in range(col_count)]) for s in range(1, group)
        ]

    def state_shapes(places, count):
        return [shape((places, channels), BF16)] + [shape((places, heads), F32)] * (count > 2)

    got = [exchange(packed[piece * group : (piece + 1) * group]) for piece in range(PIECES)]

    row_entering = []
    row_made = params
    for piece in range(PIECES):
        made = call(
            functools.partial(row_state_kernel, **sizes, **shared),
            state_shapes(lines * state, col_count // group),
            specs=[None] * (1 + group) + [any_spec],
        )(params, *got[piece], row_made)
        row_made = made[0]
        row_entering.append(entering_states(made, "col", col_count, group, width))

    col_made = call(
        functools.partial(col_state_kernel, **sizes),
        state_shapes(cols * state, row_count),
            specs=[None] * 4 + [any_spec],
    )(params, x, raw, maps, row_made)
    col_entering = entering_states(col_made, "row", row_count, 1, width)

    w = call(
        functools.partial(col_out_kernel, **sizes),
        shape((tokens, channels), F32),
    )(params, col_entering, x, raw, maps, jnp.repeat(skip, width).reshape(1, channels))

    back = []
    y_row = [params]
    for piece in range(PIECES):
        y_row = call(
            functools.partial(row_out_kernel, **sizes, **shared),
            [shape((share, channels), BF16)] * group,
            specs=[None] * (2 + group) + [any_spec],
            cost=LONG if piece == PIECES - 1 else SMALL,
        )(params, row_entering[piece], *got[piece], y_row[0])
        back += exchange(y_row)

    mixed = call(
        functools.partial(final_kernel, **shared),
        shape((tokens, channels), BF16),
    )(w, gate, norm_gain.reshape(1, channels), *back)
    return mixed.reshape(x_in.shape)


def solution(mesh):
    tile = P("img", "row", "col", None)
    return jax.shard_map(
        functools.partial(body, row_count=mesh.shape["row"], col_count=mesh.shape["col"]),
        mesh=mesh,
        in_specs=(tile, tile, tile, tile, P("img"), P(), P(), P(), P()),
        out_specs=tile,
        check_vma=False,
    )
```

```python
import functools

import jax
import jax.numpy as jnp
from jax import lax
from jax.experimental import pallas as pl
from jax.experimental.pallas import tpu as pltpu
from jax.sharding import PartitionSpec as P

LANES = 128
GROUP = 4
PIECES = 2
STRIP = 512
F32 = jnp.float32
BF16 = jnp.bfloat16


def dot(a, b):
    return jnp.dot(a, b, preferred_element_type=F32)


def iota(shape, dim):
    return lax.broadcasted_iota(jnp.int32, shape, dim)


def div(a, n):
    return lax.shift_right_logical(a, n.bit_length() - 1) if n & (n - 1) == 0 else a // n


def mod(a, n):
    return jnp.bitwise_and(a, n - 1) if n & (n - 1) == 0 else a % n


def parts(values, count):
    terms = []
    for _ in range(count):
        term = values.astype(BF16)
        terms.append(term)
        values = values - term.astype(F32)
    return jnp.concatenate(terms, axis=1)


def picks(heads, width, first, channels):
    row = iota((2 * heads, 1), 0)
    head = jnp.where(row >= heads, row - heads, row)
    return (head == div(first + iota((1, channels), 1), width)).astype(BF16)


def summed(mask, values):
    heads = values.shape[1]
    sums = dot(mask, parts(values, 3))
    return sums[:, :heads] + sums[:, heads : 2 * heads] + sums[:, 2 * heads :]


def step_sizes(raw, bias):
    shifted = raw.astype(F32) + bias
    return jnp.maximum(shifted, 0.0) + jnp.log1p(jnp.exp(-jnp.abs(shifted)))


def widen(maps, line, lines):
    state = maps.shape[1]
    places = lines * state
    copy = (mod(iota((1, places), 1), state) == iota((state, 1), 0)).astype(BF16)
    own = div(iota((1, places), 1), state) == line
    return jnp.where(own, dot(maps, copy), 0.0).astype(BF16)


class Scan:
    def __init__(self, order, lines, raw, bias, rates, b_map, c_map):
        tokens, self.heads = raw.shape
        self.lines, self.b_map, self.c_map = lines, b_map, c_map
        self.line, place = order(iota((tokens, 1), 0))
        self.line_in, place_in = order(iota((1, tokens), 1))
        self.lower = jnp.logical_and(self.line == self.line_in, place >= place_in)
        steps = step_sizes(raw, bias)
        self.decay = -rates * steps
        running = summed(self.lower.astype(BF16), self.decay)
        self.fade = parts(jnp.exp(running), 2)
        self.grow = parts(steps * jnp.exp(-running), 2)

    def ends(self):
        places = self.lines * self.b_map.shape[1]
        own = div(iota((places, 1), 0), self.b_map.shape[1]) == self.line_in
        return jnp.exp(summed(own.astype(BF16), self.decay))

    def into(self):
        return widen(self.b_map, self.line, self.lines).astype(F32).T.astype(BF16)

    def mix(self):
        scores = lax.dot_general(
            self.c_map, self.b_map, (((1,), (1,)), ((), ())), preferred_element_type=F32
        )
        within = jnp.where(self.lower, scores, 0.0).astype(BF16)
        return jnp.concatenate([within, widen(self.c_map, self.line, self.lines)], axis=1)


def column_order(cols):
    return lambda token: (mod(token, cols), div(token, cols))


def row_order(cols, lines):
    def order(token):
        return mod(div(token, cols), lines), div(token, cols * lines) * cols + mod(token, cols)

    return order


def strips(channels):
    return [(first, min(STRIP, channels - first)) for first in range(0, channels, STRIP)]


def pack_kernel(index_ref, x_ref, raw_ref, maps_ref, table_ref, rates_ref, params_ref, *refs, group, heads, state):
    sent, (index, raw, maps, table, rates, sems) = refs[:-6], refs[-6:]
    share = x_ref.shape[0] // group
    rows = share // len(sent)
    channels = x_ref.shape[1]
    small = [(index_ref, index), (raw_ref, raw), (maps_ref, maps), (table_ref, table), (rates_ref, rates)]
    copies = [pltpu.make_async_copy(a, b, sems.at[i]) for i, (a, b) in enumerate(small)]
    places = []
    for piece in range(len(sent)):
        for member in range(group):
            source = pl.ds(member * share + piece * rows, rows)
            target = pl.ds(member * rows, rows)
            places.append((sent[piece], target, source))
            copies.append(
                pltpu.make_async_copy(
                    x_ref.at[source, :], sent[piece].at[target, pl.ds(0, channels)], sems.at[len(copies)]
                )
            )
    for copy in copies:
        copy.start()
    for copy in copies[: len(small)]:
        copy.wait()
    used = heads + 2 * state
    for out, target, source in places:
        out[target, channels : channels + heads] = raw[source, :heads]
        out[target, channels + heads : channels + used] = maps[source, : 2 * state]
        out[target, channels + used :] = jnp.zeros((rows, LANES - used), BF16)
    row = jnp.where(iota(table.shape, 1) == index[0], table[...], 0.0)
    ones = jnp.ones((8, table.shape[1]), BF16)
    bias = jnp.zeros((8, row.shape[0]), F32)
    for _ in range(3):
        term = row.astype(BF16)
        row = row - term.astype(F32)
        bias += lax.dot_general(ones, term, (((1,), (1,)), ((), ())), preferred_element_type=F32)
    params_ref[0:1, :] = bias[0:1, :]
    params_ref[1:2, :heads] = rates[0:1, :]
    params_ref[1:2, heads:] = rates[1:2, :]
    params_ref[2:, :] = jnp.zeros((6, 2 * heads), F32)
    for copy in copies[len(small) :]:
        copy.wait()


def row_scan(params_ref, got_ref, group, cols, heads, state):
    tokens = got_ref.shape[0]
    channels = got_ref.shape[1] - LANES
    lines = tokens // (cols * group)
    aux = got_ref[:, channels:]
    return Scan(
        row_order(cols, lines),
        lines,
        aux[:, :heads],
        params_ref[0:1, :heads],
        params_ref[1:2, :heads],
        aux[:, heads : heads + state],
        aux[:, heads + state : heads + 2 * state],
    )


def col_scan(params_ref, raw_ref, maps_ref, cols, heads, state):
    return Scan(
        column_order(cols),
        cols,
        raw_ref[:, heads:],
        params_ref[0:1, heads:],
        params_ref[1:2, heads:],
        maps_ref[:, 2 * state : 3 * state],
        maps_ref[:, 3 * state :],
    )


def write_state(scan, tokens_of, width, channels, s_ref, factor_ref):
    ends = scan.ends()
    if factor_ref:
        factor_ref[0][...] = ends
    ends = parts(ends, 2)
    into = scan.into()
    for first, count in strips(channels):
        pick = picks(scan.heads, width, first, count)
        values = (tokens_of(first, count) * dot(scan.grow, pick)).astype(BF16)
        s_ref[:, first : first + count] = (dot(into, values) * dot(ends, pick)).astype(BF16)


def row_state_kernel(params_ref, got_ref, _, s_ref, *factor_ref, group, cols, heads, state, width):
    scan = row_scan(params_ref, got_ref, group, cols, heads, state)
    tokens_of = lambda first, count: got_ref[:, first : first + count].astype(F32)
    write_state(scan, tokens_of, width, s_ref.shape[1], s_ref, factor_ref)


def col_state_kernel(params_ref, x_ref, raw_ref, maps_ref, _, s_ref, *factor_ref, cols, heads, state, width):
    scan = col_scan(params_ref, raw_ref, maps_ref, cols, heads, state)
    tokens_of = lambda first, count: x_ref[:, first : first + count].astype(F32)
    write_state(scan, tokens_of, width, s_ref.shape[1], s_ref, factor_ref)


def row_out_kernel(params_ref, s_ref, got_ref, _, y_ref, *, group, cols, heads, state, width):
    scan = row_scan(params_ref, got_ref, group, cols, heads, state)
    mix = scan.mix()
    for first, count in strips(s_ref.shape[1]):
        pick = picks(heads, width, first, count)
        part = slice(first, first + count)
        values = (got_ref[:, part].astype(F32) * dot(scan.grow, pick)).astype(BF16)
        y = dot(mix, jnp.concatenate([values, s_ref[:, part]], axis=0)) * dot(scan.fade, pick)
        y_ref[:, part] = y.astype(BF16)


def col_out_kernel(params_ref, s_ref, x_ref, raw_ref, maps_ref, gate_ref, skip_ref, w_ref, g_ref, *, cols, heads, state, width):
    scan = col_scan(params_ref, raw_ref, maps_ref, cols, heads, state)
    mix = scan.mix()
    for first, count in strips(s_ref.shape[1]):
        pick = picks(heads, width, first, count)
        part = slice(first, first + count)
        x = x_ref[:, part].astype(F32)
        values = (x * dot(scan.grow, pick)).astype(BF16)
        y = dot(mix, jnp.concatenate([values, s_ref[:, part]], axis=0)) * dot(scan.fade, pick)
        w_ref[:, part] = y + skip_ref[:, part] * x
        gate = gate_ref[:, part].astype(F32)
        g_ref[:, part] = gate / (1.0 + jnp.exp(-gate))


def final_kernel(w_ref, g_ref, gain_ref, *refs, group):
    back, out_ref = refs[:-1], refs[-1]
    rows = back[0].shape[0] // group
    channels = back[0].shape[1]
    for member in range(group):
        for piece in range(len(back)):
            first = (member * len(back) + piece) * rows
            part = slice(first, first + rows)
            row = back[piece][member * rows : (member + 1) * rows, :].astype(F32)
            v = (row + w_ref[part, :]) * g_ref[part, :]
            power = jnp.sum(v * v, axis=1, keepdims=True) / channels
            out_ref[part, :] = (v * lax.rsqrt(power + 1e-5) * gain_ref[...]).astype(BF16)


SMALL = pl.CostEstimate(flops=1024, bytes_accessed=1024, transcendentals=0)
LONG = pl.CostEstimate(flops=2 * 10**10, bytes_accessed=1024, transcendentals=0)


def call(kernel, out_shape, specs=None, cost=SMALL):
    more = {} if specs is None else dict(in_specs=[spec or pl.BlockSpec() for spec in specs])
    return pl.pallas_call(
        kernel,
        **more,
        out_shape=out_shape,
        compiler_params=pltpu.CompilerParams(vmem_limit_bytes=32 * 1024 * 1024),
        cost_estimate=cost,
    )


def entering_states(made, axis, size, stride, width):
    ends = made[0]
    onward = [(i, i + stride) for i in range(size - stride)]
    if not onward:
        return jnp.zeros_like(ends)
    entering = lax.ppermute(ends, axis, onward)
    for _ in range(size // stride - 2):
        factor = jnp.repeat(made[1], width, axis=1)
        entering = lax.ppermute(
            (ends.astype(F32) + factor * entering.astype(F32)).astype(BF16), axis, onward
        )
    return entering


def body(x_in, gate_in, proj_bc, dt_raw, step_index, step_table, rates, skip, norm_gain, *, row_count, col_count):
    _, tile_rows, cols, channels = x_in.shape
    heads = skip.shape[0]
    width = channels // heads
    state = proj_bc.shape[-1] // 4
    tokens = tile_rows * cols
    group = GROUP
    while col_count % group:
        group //= 2
    share = tokens // PIECES
    lines = share // group // cols
    groups = [list(range(i, i + group)) for i in range(0, col_count, group)]

    x = x_in.reshape(tokens, channels)
    gate = gate_in.reshape(tokens, channels)
    maps = proj_bc.reshape(tokens, 4 * state)
    raw = dt_raw.reshape(tokens, 2 * heads)
    sizes = dict(cols=cols, heads=heads, state=state, width=width)
    shape = jax.ShapeDtypeStruct

    any_spec = pl.BlockSpec(memory_space=pl.ANY)
    given = (step_index, x, raw, maps, step_table.T, rates)
    params, *packed = pl.pallas_call(
        functools.partial(pack_kernel, group=group, heads=heads, state=state),
        in_specs=[any_spec] + [pl.BlockSpec(memory_space=pltpu.HBM)] * (len(given) - 1),
        out_shape=[pltpu.VMEM((8, 2 * heads), F32)] + [pltpu.VMEM((share, channels + LANES), BF16)] * PIECES,
        scratch_shapes=[
            pltpu.SMEM(step_index.shape, jnp.int32),
            pltpu.VMEM(raw.shape, BF16),
            pltpu.VMEM(maps.shape, BF16),
            pltpu.VMEM(step_table.shape[::-1], F32),
            pltpu.VMEM(rates.shape, F32),
            pltpu.SemaphoreType.DMA((len(given) - 1 + group * PIECES,)),
        ],
        compiler_params=pltpu.CompilerParams(vmem_limit_bytes=32 * 1024 * 1024),
        cost_estimate=SMALL,
    )(given[0], *[pltpu.with_memory_space_constraint(a, pltpu.HBM) for a in given[1:]])

    def exchange(blocks):
        return lax.all_to_all(blocks, "col", split_axis=0, concat_axis=0, axis_index_groups=groups, tiled=True)

    def state_shapes(places, count):
        return [shape((places, channels), BF16)] + [shape((places, heads), F32)] * (count > 2)

    got = [exchange(blocks) for blocks in packed]

    row_entering = []
    row_made = params
    for piece in range(PIECES):
        made = call(
            functools.partial(row_state_kernel, group=group, **sizes),
            state_shapes(lines * state, col_count // group),
            specs=[None] * 2 + [any_spec],
        )(params, got[piece], row_made)
        row_made = made[0]
        row_entering.append(entering_states(made, "col", col_count, group, width))

    col_made = call(
        functools.partial(col_state_kernel, **sizes),
        state_shapes(cols * state, row_count),
        specs=[None] * 4 + [any_spec],
    )(params, x, raw, maps, row_made)
    col_entering = entering_states(col_made, "row", row_count, 1, width)

    w, silu = call(
        functools.partial(col_out_kernel, **sizes),
        [shape((tokens, channels), F32)] * 2,
    )(params, col_entering, x, raw, maps, gate, jnp.repeat(skip, width).reshape(1, channels))

    back = []
    y_row = params
    for piece in range(PIECES):
        y_row = call(
            functools.partial(row_out_kernel, group=group, **sizes),
            shape((share, channels), BF16),
            specs=[None] * 3 + [any_spec],
            cost=LONG if piece == PIECES - 1 else SMALL,
        )(params, row_entering[piece], got[piece], y_row)
        back.append(exchange(y_row))

    mixed = call(
        functools.partial(final_kernel, group=group),
        shape((tokens, channels), BF16),
    )(w, silu, norm_gain.reshape(1, channels), *back)
    return mixed.reshape(x_in.shape)


def solution(mesh):
    tile = P("img", "row", "col", None)
    return jax.shard_map(
        functools.partial(body, row_count=mesh.shape["row"], col_count=mesh.shape["col"]),
        mesh=mesh,
        in_specs=(tile, tile, tile, tile, P("img"), P(), P(), P(), P()),
        out_specs=tile,
        check_vma=False,
    )
```

```python
import functools

import jax
import jax.numpy as jnp
from jax import lax
from jax.experimental import pallas as pl
from jax.experimental.pallas import tpu as pltpu
from jax.sharding import PartitionSpec as P

LANES = 128
GROUP = 4
PIECES = 2
STRIP = 512
F32 = jnp.float32
BF16 = jnp.bfloat16


def dot(a, b):
    return jnp.dot(a, b, preferred_element_type=F32)


def iota(shape, dim):
    return lax.broadcasted_iota(jnp.int32, shape, dim)


def div(a, n):
    return lax.shift_right_logical(a, n.bit_length() - 1) if n & (n - 1) == 0 else a // n


def mod(a, n):
    return jnp.bitwise_and(a, n - 1) if n & (n - 1) == 0 else a % n


def parts(values, count):
    terms = []
    for _ in range(count):
        term = values.astype(BF16)
        terms.append(term)
        values = values - term.astype(F32)
    return jnp.concatenate(terms, axis=1)


def picks(heads, width, first, channels):
    row = iota((2 * heads, 1), 0)
    head = jnp.where(row >= heads, row - heads, row)
    return (head == div(first + iota((1, channels), 1), width)).astype(BF16)


def summed(mask, values):
    heads = values.shape[1]
    sums = dot(mask, parts(values, 3))
    return sums[:, :heads] + sums[:, heads : 2 * heads] + sums[:, 2 * heads :]


def step_sizes(raw, bias):
    shifted = raw.astype(F32) + bias
    return jnp.maximum(shifted, 0.0) + jnp.log1p(jnp.exp(-jnp.abs(shifted)))


def widen(maps, line, lines):
    state = maps.shape[1]
    places = lines * state
    copy = (mod(iota((1, places), 1), state) == iota((state, 1), 0)).astype(BF16)
    own = div(iota((1, places), 1), state) == line
    return jnp.where(own, dot(maps, copy), 0.0).astype(BF16)


class Scan:
    def __init__(self, order, lines, raw, bias, rates, b_map, c_map):
        tokens, self.heads = raw.shape
        self.lines, self.b_map, self.c_map = lines, b_map, c_map
        self.line, place = order(iota((tokens, 1), 0))
        self.line_in, place_in = order(iota((1, tokens), 1))
        self.lower = jnp.logical_and(self.line == self.line_in, place >= place_in)
        steps = step_sizes(raw, bias)
        self.decay = -rates * steps
        running = summed(self.lower.astype(BF16), self.decay)
        self.fade = parts(jnp.exp(running), 2)
        self.grow = parts(steps * jnp.exp(-running), 2)

    def ends(self):
        places = self.lines * self.b_map.shape[1]
        own = div(iota((places, 1), 0), self.b_map.shape[1]) == self.line_in
        return jnp.exp(summed(own.astype(BF16), self.decay))

    def into(self):
        return widen(self.b_map, self.line, self.lines).astype(F32).T.astype(BF16)

    def mix(self, follows):
        scores = lax.dot_general(
            self.c_map, self.b_map, (((1,), (1,)), ((), ())), preferred_element_type=F32
        )
        within = jnp.where(self.lower, scores, 0.0).astype(BF16)
        entering = widen(self.c_map, self.line, self.lines)
        return jnp.concatenate([within, jnp.where(follows, entering, 0)], axis=1)


def column_order(cols):
    return lambda token: (mod(token, cols), div(token, cols))


def row_order(cols, lines, member):
    def order(token):
        source = jnp.bitwise_xor(div(token, cols * lines), member)
        return mod(div(token, cols), lines), source * cols + mod(token, cols)

    return order


def strips(channels):
    return [(first, min(STRIP, channels - first)) for first in range(0, channels, STRIP)]


def pack_kernel(
    index_ref, x_ref, raw_ref, maps_ref, table_ref, rates_ref, params_ref, *refs, group, axis, heads, state
):
    sent, (raw, maps, table, rates, sems) = refs[:-5], refs[-5:]
    member = mod(lax.axis_index(axis), group)
    pieces = len(sent) // group
    share = x_ref.shape[0] // group
    rows = share // pieces
    channels = x_ref.shape[1]
    small = [(raw_ref, raw), (maps_ref, maps), (table_ref, table), (rates_ref, rates)]
    copies = [pltpu.make_async_copy(a, b, sems.at[i]) for i, (a, b) in enumerate(small)]
    places = []
    for piece in range(pieces):
        for s in range(group):
            first = pl.multiple_of(jnp.bitwise_xor(member, s) * share + piece * rows, rows)
            out = sent[piece * group + s]
            places.append((out, pl.ds(first, rows)))
            copies.append(
                pltpu.make_async_copy(
                    x_ref.at[pl.ds(first, rows), :], out.at[:, pl.ds(0, channels)], sems.at[len(copies)]
                )
            )
    for copy in copies:
        copy.start()
    for copy in copies[: len(small)]:
        copy.wait()
    used = heads + 2 * state
    for out, part in places:
        out[:, channels : channels + heads] = raw[part, :heads]
        out[:, channels + heads : channels + used] = maps[part, : 2 * state]
        out[:, channels + used :] = jnp.zeros((rows, LANES - used), BF16)
    row = jnp.where(iota(table.shape, 1) == index_ref[0], table[...], 0.0)
    ones = jnp.ones((8, table.shape[1]), BF16)
    bias = jnp.zeros((8, row.shape[0]), F32)
    for _ in range(3):
        term = row.astype(BF16)
        row = row - term.astype(F32)
        bias += lax.dot_general(ones, term, (((1,), (1,)), ((), ())), preferred_element_type=F32)
    params_ref[0:1, :] = bias[0:1, :]
    params_ref[1:2, :heads] = rates[0:1, :]
    params_ref[1:2, heads:] = rates[1:2, :]
    params_ref[2:, :] = jnp.zeros((6, 2 * heads), F32)
    for copy in copies[len(small) :]:
        copy.wait()


def row_scan(params_ref, blocks, member, cols, heads, state):
    channels = blocks[0].shape[1] - LANES
    tokens = blocks[0].shape[0] * len(blocks)
    lines = tokens // (cols * len(blocks))
    aux = jnp.concatenate([block[:, channels:] for block in blocks], axis=0)
    return Scan(
        row_order(cols, lines, member),
        lines,
        aux[:, :heads],
        params_ref[0:1, :heads],
        params_ref[1:2, :heads],
        aux[:, heads : heads + state],
        aux[:, heads + state : heads + 2 * state],
    )


def col_scan(params_ref, raw_ref, maps_ref, cols, heads, state):
    return Scan(
        column_order(cols),
        cols,
        raw_ref[:, heads:],
        params_ref[0:1, heads:],
        params_ref[1:2, heads:],
        maps_ref[:, 2 * state : 3 * state],
        maps_ref[:, 3 * state :],
    )


def write_state(scan, tokens_of, width, channels, s_ref, factor_ref):
    ends = scan.ends()
    if factor_ref:
        factor_ref[0][...] = ends
    ends = parts(ends, 2)
    into = scan.into()
    for first, count in strips(channels):
        pick = picks(scan.heads, width, first, count)
        values = (tokens_of(first, count) * dot(scan.grow, pick)).astype(BF16)
        s_ref[:, first : first + count] = (dot(into, values) * dot(ends, pick)).astype(BF16)


def row_state_kernel(params_ref, *refs, group, axis, cols, heads, state, width):
    blocks, s_ref, factor_ref = refs[:group], refs[group + 1], refs[group + 2 :]
    member = mod(lax.axis_index(axis), group)
    scan = row_scan(params_ref, blocks, member, cols, heads, state)
    tokens_of = lambda first, count: jnp.concatenate(
        [block[:, first : first + count] for block in blocks], axis=0
    ).astype(F32)
    write_state(scan, tokens_of, width, s_ref.shape[1], s_ref, factor_ref)


def col_state_kernel(params_ref, x_ref, raw_ref, maps_ref, _, s_ref, *factor_ref, cols, heads, state, width):
    scan = col_scan(params_ref, raw_ref, maps_ref, cols, heads, state)
    tokens_of = lambda first, count: x_ref[:, first : first + count].astype(F32)
    write_state(scan, tokens_of, width, s_ref.shape[1], s_ref, factor_ref)


def row_out_kernel(params_ref, s_ref, *refs, group, axis, cols, heads, state, width):
    blocks, outs = refs[:group], refs[group + 1 :]
    member = mod(lax.axis_index(axis), group)
    scan = row_scan(params_ref, blocks, member, cols, heads, state)
    mix = scan.mix(lax.axis_index(axis) >= group)
    rows = blocks[0].shape[0]
    for first, count in strips(s_ref.shape[1]):
        pick = picks(heads, width, first, count)
        part = slice(first, first + count)
        x = jnp.concatenate([block[:, part] for block in blocks], axis=0).astype(F32)
        values = (x * dot(scan.grow, pick)).astype(BF16)
        y = dot(mix, jnp.concatenate([values, s_ref[:, part]], axis=0)) * dot(scan.fade, pick)
        for s in range(group):
            outs[s][:, part] = y[s * rows : (s + 1) * rows].astype(BF16)


def col_out_kernel(params_ref, s_ref, x_ref, raw_ref, maps_ref, gate_ref, skip_ref, w_ref, g_ref, *, cols, heads, state, width):
    scan = col_scan(params_ref, raw_ref, maps_ref, cols, heads, state)
    mix = scan.mix(lax.axis_index("row") > 0)
    for first, count in strips(s_ref.shape[1]):
        pick = picks(heads, width, first, count)
        part = slice(first, first + count)
        x = x_ref[:, part].astype(F32)
        values = (x * dot(scan.grow, pick)).astype(BF16)
        y = dot(mix, jnp.concatenate([values, s_ref[:, part]], axis=0)) * dot(scan.fade, pick)
        w_ref[:, part] = y + skip_ref[:, part] * x
        gate = gate_ref[:, part].astype(F32)
        g_ref[:, part] = gate / (1.0 + jnp.exp(-gate))


def final_kernel(w_ref, g_ref, gain_ref, *refs, group, axis):
    rows_of, out_ref = refs[:-1], refs[-1]
    pieces = len(rows_of) // group
    rows, channels = rows_of[0].shape
    member = mod(lax.axis_index(axis), group)
    for piece in range(pieces):
        for s in range(group):
            first = (jnp.bitwise_xor(member, s) * pieces + piece) * rows
            part = pl.ds(pl.multiple_of(first, rows), rows)
            v = (rows_of[piece * group + s][...].astype(F32) + w_ref[part, :]) * g_ref[part, :]
            power = jnp.sum(v * v, axis=1, keepdims=True) / channels
            out_ref[part, :] = (v * lax.rsqrt(power + 1e-5) * gain_ref[...]).astype(BF16)


SMALL = pl.CostEstimate(flops=1024, bytes_accessed=1024, transcendentals=0)
LONG = pl.CostEstimate(flops=2 * 10**10, bytes_accessed=1024, transcendentals=0)


def call(kernel, out_shape, specs=None, cost=SMALL):
    more = {} if specs is None else dict(in_specs=[spec or pl.BlockSpec() for spec in specs])
    return pl.pallas_call(
        kernel,
        **more,
        out_shape=out_shape,
        compiler_params=pltpu.CompilerParams(vmem_limit_bytes=32 * 1024 * 1024),
        cost_estimate=cost,
    )


def entering_states(made, axis, size, stride, width):
    ends = made[0]
    if size == stride:
        return ends
    onward = [(i, (i + stride) % size) for i in range(size)]
    entering = lax.ppermute(ends, axis, onward)
    for _ in range(size // stride - 2):
        follows = (lax.axis_index(axis) >= stride).astype(F32)
        factor = follows * jnp.repeat(made[1], width, axis=1)
        entering = lax.ppermute(
            (ends.astype(F32) + factor * entering.astype(F32)).astype(BF16), axis, onward
        )
    return entering


def body(x_in, gate_in, proj_bc, dt_raw, step_index, step_table, rates, skip, norm_gain, *, row_count, col_count):
    _, tile_rows, cols, channels = x_in.shape
    heads = skip.shape[0]
    width = channels // heads
    state = proj_bc.shape[-1] // 4
    tokens = tile_rows * cols
    group = GROUP
    while col_count % group:
        group //= 2
    share = tokens // group // PIECES
    lines = share // cols

    x = x_in.reshape(tokens, channels)
    gate = gate_in.reshape(tokens, channels)
    maps = proj_bc.reshape(tokens, 4 * state)
    raw = dt_raw.reshape(tokens, 2 * heads)
    sizes = dict(cols=cols, heads=heads, state=state, width=width)
    shared = dict(group=group, axis="col")
    shape = jax.ShapeDtypeStruct

    any_spec = pl.BlockSpec(memory_space=pl.ANY)
    hbm_spec = pl.BlockSpec(memory_space=pltpu.HBM)
    full = lambda *dims: pl.BlockSpec(dims, lambda i, index: (0,) * len(dims))
    packed = pl.pallas_call(
        functools.partial(pack_kernel, heads=heads, state=state, **shared),
        grid_spec=pltpu.PrefetchScalarGridSpec(
            num_scalar_prefetch=1,
            grid=(1,),
            in_specs=[hbm_spec] * 5,
            out_specs=[full(8, 2 * heads)] + [full(share, channels + LANES)] * (group * PIECES),
            scratch_shapes=[
                pltpu.VMEM(raw.shape, BF16),
                pltpu.VMEM(maps.shape, BF16),
                pltpu.VMEM(step_table.shape[::-1], F32),
                pltpu.VMEM(rates.shape, F32),
                pltpu.SemaphoreType.DMA((4 + group * PIECES,)),
            ],
        ),
        out_shape=[pltpu.VMEM((8, 2 * heads), F32)] + [pltpu.VMEM((share, channels + LANES), BF16)] * (group * PIECES),
        compiler_params=pltpu.CompilerParams(vmem_limit_bytes=32 * 1024 * 1024),
        cost_estimate=SMALL,
    )(step_index, *[pltpu.with_memory_space_constraint(a, pltpu.HBM) for a in (x, raw, maps, step_table.T, rates)])
    params, packed = packed[0], packed[1:]

    def exchange(blocks):
        return [blocks[0]] + [
            lax.ppermute(blocks[s], "col", [(i, i ^ s) for i in range(col_count)]) for s in range(1, group)
        ]

    def state_shapes(places, count):
        return [shape((places, channels), BF16)] + [shape((places, heads), F32)] * (count > 2)

    got = [exchange(packed[piece * group : (piece + 1) * group]) for piece in range(PIECES)]

    row_entering = []
    row_made = params
    for piece in range(PIECES):
        made = call(
            functools.partial(row_state_kernel, **sizes, **shared),
            state_shapes(lines * state, col_count // group),
            specs=[None] * (1 + group) + [any_spec],
        )(params, *got[piece], row_made)
        row_made = made[0]
        row_entering.append(entering_states(made, "col", col_count, group, width))

    col_made = call(
        functools.partial(col_state_kernel, **sizes),
        state_shapes(cols * state, row_count),
            specs=[None] * 4 + [any_spec],
    )(params, x, raw, maps, row_made)
    col_entering = entering_states(col_made, "row", row_count, 1, width)

    w, silu = call(
        functools.partial(col_out_kernel, **sizes),
        [shape((tokens, channels), F32)] * 2,
    )(params, col_entering, x, raw, maps, gate, jnp.repeat(skip, width).reshape(1, channels))

    back = []
    y_row = [params]
    for piece in range(PIECES):
        y_row = call(
            functools.partial(row_out_kernel, **sizes, **shared),
            [shape((share, channels), BF16)] * group,
            specs=[None] * (2 + group) + [any_spec],
            cost=LONG if piece == PIECES - 1 else SMALL,
        )(params, row_entering[piece], *got[piece], y_row[0])
        back += exchange(y_row)

    mixed = call(
        functools.partial(final_kernel, **shared),
        shape((tokens, channels), BF16),
    )(w, silu, norm_gain.reshape(1, channels), *back)
    return mixed.reshape(x_in.shape)


def solution(mesh):
    tile = P("img", "row", "col", None)
    return jax.shard_map(
        functools.partial(body, row_count=mesh.shape["row"], col_count=mesh.shape["col"]),
        mesh=mesh,
        in_specs=(tile, tile, tile, tile, P("img"), P(), P(), P(), P()),
        out_specs=tile,
        check_vma=False,
    )
```

```python
import functools

import jax
import jax.numpy as jnp
from jax import lax
from jax.experimental import pallas as pl
from jax.experimental.pallas import tpu as pltpu
from jax.sharding import PartitionSpec as P

LANES = 128
GROUP = 4
PIECES = 2
STRIP = 512
F32 = jnp.float32
BF16 = jnp.bfloat16


def dot(a, b):
    return jnp.dot(a, b, preferred_element_type=F32)


def iota(shape, dim):
    return lax.broadcasted_iota(jnp.int32, shape, dim)


def div(a, n):
    return lax.shift_right_logical(a, n.bit_length() - 1) if n & (n - 1) == 0 else a // n


def mod(a, n):
    return jnp.bitwise_and(a, n - 1) if n & (n - 1) == 0 else a % n


def parts(values, count):
    terms = []
    for _ in range(count):
        term = values.astype(BF16)
        terms.append(term)
        values = values - term.astype(F32)
    return jnp.concatenate(terms, axis=1)


def picks(heads, width, first, channels):
    row = iota((2 * heads, 1), 0)
    head = jnp.where(row >= heads, row - heads, row)
    return (head == div(first + iota((1, channels), 1), width)).astype(BF16)


def summed(mask, values):
    heads = values.shape[1]
    sums = dot(mask, parts(values, 3))
    return sums[:, :heads] + sums[:, heads : 2 * heads] + sums[:, 2 * heads :]


def step_sizes(raw, bias):
    shifted = raw.astype(F32) + bias
    return jnp.maximum(shifted, 0.0) + jnp.log1p(jnp.exp(-jnp.abs(shifted)))


def widen(maps, line, lines):
    state = maps.shape[1]
    places = lines * state
    copy = (mod(iota((1, places), 1), state) == iota((state, 1), 0)).astype(BF16)
    own = div(iota((1, places), 1), state) == line
    return jnp.where(own, dot(maps, copy), 0.0).astype(BF16)


class Scan:
    def __init__(self, order, lines, raw, bias, rates, b_map, c_map):
        tokens, self.heads = raw.shape
        self.lines, self.b_map, self.c_map = lines, b_map, c_map
        self.line, place = order(iota((tokens, 1), 0))
        self.line_in, place_in = order(iota((1, tokens), 1))
        self.lower = jnp.logical_and(self.line == self.line_in, place >= place_in)
        steps = step_sizes(raw, bias)
        self.decay = -rates * steps
        running = summed(self.lower.astype(BF16), self.decay)
        self.fade = parts(jnp.exp(running), 2)
        self.grow = parts(steps * jnp.exp(-running), 2)

    def ends(self):
        places = self.lines * self.b_map.shape[1]
        own = div(iota((places, 1), 0), self.b_map.shape[1]) == self.line_in
        return jnp.exp(summed(own.astype(BF16), self.decay))

    def into(self):
        return widen(self.b_map, self.line, self.lines).astype(F32).T.astype(BF16)

    def mix(self, follows):
        scores = lax.dot_general(
            self.c_map, self.b_map, (((1,), (1,)), ((), ())), preferred_element_type=F32
        )
        within = jnp.where(self.lower, scores, 0.0).astype(BF16)
        entering = widen(self.c_map, self.line, self.lines)
        return jnp.concatenate([within, jnp.where(follows, entering, 0)], axis=1)


def column_order(cols):
    return lambda token: (mod(token, cols), div(token, cols))


def row_order(cols, lines, member):
    def order(token):
        source = jnp.bitwise_xor(div(token, cols * lines), member)
        return mod(div(token, cols), lines), source * cols + mod(token, cols)

    return order


def strips(channels):
    return [(first, min(STRIP, channels - first)) for first in range(0, channels, STRIP)]


def pack_places(sent, piece, pieces, share, axis):
    member = mod(lax.axis_index(axis), len(sent))
    rows = share // pieces
    return [
        (out, pl.ds(pl.multiple_of(jnp.bitwise_xor(member, s) * share + piece * rows, rows), rows))
        for s, out in enumerate(sent)
    ]


def pack_aux(places, raw, maps, channels, heads, state):
    used = heads + 2 * state
    for out, part in places:
        out[:, channels : channels + heads] = raw[part, :heads]
        out[:, channels + heads : channels + used] = maps[part, : 2 * state]
        out[:, channels + used :] = jnp.zeros((out.shape[0], LANES - used), BF16)


def first_pack_kernel(
    index_ref, x_ref, raw_ref, maps_ref, table_ref, rates_ref, params_ref, *refs, pieces, axis, heads, state
):
    sent, (raw, maps, table, rates, sems) = refs[:-5], refs[-5:]
    channels = x_ref.shape[1]
    places = pack_places(sent, 0, pieces, x_ref.shape[0] // len(sent), axis)
    moved = [(raw_ref, raw), (maps_ref, maps), (table_ref, table), (rates_ref, rates)]
    small = len(moved)
    moved += [(x_ref.at[part, :], out.at[:, pl.ds(0, channels)]) for out, part in places]
    copies = [pltpu.make_async_copy(a, b, sems.at[i]) for i, (a, b) in enumerate(moved)]
    for copy in copies:
        copy.start()
    for copy in copies[:small]:
        copy.wait()
    pack_aux(places, raw, maps, channels, heads, state)
    row = jnp.where(iota(table.shape, 1) == index_ref[0], table[...], 0.0)
    ones = jnp.ones((8, table.shape[1]), BF16)
    bias = jnp.zeros((8, row.shape[0]), F32)
    for _ in range(3):
        term = row.astype(BF16)
        row = row - term.astype(F32)
        bias += lax.dot_general(ones, term, (((1,), (1,)), ((), ())), preferred_element_type=F32)
    params_ref[0:1, :] = bias[0:1, :]
    params_ref[1:2, :heads] = rates[0:1, :]
    params_ref[1:2, heads:] = rates[1:2, :]
    params_ref[2:, :] = jnp.zeros((6, 2 * heads), F32)
    for copy in copies[small:]:
        copy.wait()


def pack_kernel(x_ref, raw_ref, maps_ref, _, *sent, piece, pieces, axis, heads, state):
    channels = x_ref.shape[1]
    places = pack_places(sent, piece, pieces, x_ref.shape[0] // len(sent), axis)
    for out, part in places:
        out[:, :channels] = x_ref[part, :]
    pack_aux(places, raw_ref, maps_ref, channels, heads, state)


def row_scan(params_ref, blocks, member, cols, heads, state):
    channels = blocks[0].shape[1] - LANES
    tokens = blocks[0].shape[0] * len(blocks)
    lines = tokens // (cols * len(blocks))
    aux = jnp.concatenate([block[:, channels:] for block in blocks], axis=0)
    return Scan(
        row_order(cols, lines, member),
        lines,
        aux[:, :heads],
        params_ref[0:1, :heads],
        params_ref[1:2, :heads],
        aux[:, heads : heads + state],
        aux[:, heads + state : heads + 2 * state],
    )


def col_scan(params_ref, raw_ref, maps_ref, cols, heads, state):
    return Scan(
        column_order(cols),
        cols,
        raw_ref[:, heads:],
        params_ref[0:1, heads:],
        params_ref[1:2, heads:],
        maps_ref[:, 2 * state : 3 * state],
        maps_ref[:, 3 * state :],
    )


def write_state(scan, tokens_of, width, channels, s_ref, factor_ref):
    ends = scan.ends()
    if factor_ref:
        factor_ref[0][...] = ends
    ends = parts(ends, 2)
    into = scan.into()
    for first, count in strips(channels):
        pick = picks(scan.heads, width, first, count)
        values = (tokens_of(first, count) * dot(scan.grow, pick)).astype(BF16)
        s_ref[:, first : first + count] = (dot(into, values) * dot(ends, pick)).astype(BF16)


def row_state_kernel(params_ref, *refs, group, axis, cols, heads, state, width):
    blocks, s_ref, factor_ref = refs[:group], refs[group + 1], refs[group + 2 :]
    member = mod(lax.axis_index(axis), group)
    scan = row_scan(params_ref, blocks, member, cols, heads, state)
    tokens_of = lambda first, count: jnp.concatenate(
        [block[:, first : first + count] for block in blocks], axis=0
    ).astype(F32)
    write_state(scan, tokens_of, width, s_ref.shape[1], s_ref, factor_ref)


def col_state_kernel(params_ref, x_ref, raw_ref, maps_ref, _, s_ref, *factor_ref, cols, heads, state, width):
    scan = col_scan(params_ref, raw_ref, maps_ref, cols, heads, state)
    tokens_of = lambda first, count: x_ref[:, first : first + count].astype(F32)
    write_state(scan, tokens_of, width, s_ref.shape[1], s_ref, factor_ref)


def row_out_kernel(params_ref, s_ref, *refs, group, axis, cols, heads, state, width):
    blocks, outs = refs[:group], refs[group + 1 :]
    member = mod(lax.axis_index(axis), group)
    scan = row_scan(params_ref, blocks, member, cols, heads, state)
    mix = scan.mix(lax.axis_index(axis) >= group)
    rows = blocks[0].shape[0]
    for first, count in strips(s_ref.shape[1]):
        pick = picks(heads, width, first, count)
        part = slice(first, first + count)
        x = jnp.concatenate([block[:, part] for block in blocks], axis=0).astype(F32)
        values = (x * dot(scan.grow, pick)).astype(BF16)
        y = dot(mix, jnp.concatenate([values, s_ref[:, part]], axis=0)) * dot(scan.fade, pick)
        for s in range(group):
            outs[s][:, part] = y[s * rows : (s + 1) * rows].astype(BF16)


def col_out_kernel(params_ref, s_ref, x_ref, raw_ref, maps_ref, gate_ref, skip_ref, w_ref, g_ref, *, cols, heads, state, width):
    scan = col_scan(params_ref, raw_ref, maps_ref, cols, heads, state)
    mix = scan.mix(lax.axis_index("row") > 0)
    for first, count in strips(s_ref.shape[1]):
        pick = picks(heads, width, first, count)
        part = slice(first, first + count)
        x = x_ref[:, part].astype(F32)
        values = (x * dot(scan.grow, pick)).astype(BF16)
        y = dot(mix, jnp.concatenate([values, s_ref[:, part]], axis=0)) * dot(scan.fade, pick)
        w_ref[:, part] = y + skip_ref[:, part] * x
        gate = gate_ref[:, part].astype(F32)
        g_ref[:, part] = gate / (1.0 + jnp.exp(-gate))


def final_kernel(w_ref, g_ref, gain_ref, *refs, group, axis):
    rows_of, out_ref = refs[:-1], refs[-1]
    pieces = len(rows_of) // group
    rows, channels = rows_of[0].shape
    member = mod(lax.axis_index(axis), group)
    for piece in range(pieces):
        for s in range(group):
            first = (jnp.bitwise_xor(member, s) * pieces + piece) * rows
            part = pl.ds(pl.multiple_of(first, rows), rows)
            v = (rows_of[piece * group + s][...].astype(F32) + w_ref[part, :]) * g_ref[part, :]
            power = jnp.sum(v * v, axis=1, keepdims=True) / channels
            out_ref[part, :] = (v * lax.rsqrt(power + 1e-5) * gain_ref[...]).astype(BF16)


SMALL = pl.CostEstimate(flops=1024, bytes_accessed=1024, transcendentals=0)
LONG = pl.CostEstimate(flops=2 * 10**10, bytes_accessed=1024, transcendentals=0)


def call(kernel, out_shape, specs=None, cost=SMALL):
    more = {} if specs is None else dict(in_specs=[spec or pl.BlockSpec() for spec in specs])
    return pl.pallas_call(
        kernel,
        **more,
        out_shape=out_shape,
        compiler_params=pltpu.CompilerParams(vmem_limit_bytes=32 * 1024 * 1024),
        cost_estimate=cost,
    )


def entering_states(made, axis, size, stride, width):
    ends = made[0]
    if size == stride:
        return ends
    onward = [(i, (i + stride) % size) for i in range(size)]
    entering = lax.ppermute(ends, axis, onward)
    for _ in range(size // stride - 2):
        follows = (lax.axis_index(axis) >= stride).astype(F32)
        factor = follows * jnp.repeat(made[1], width, axis=1)
        entering = lax.ppermute(
            (ends.astype(F32) + factor * entering.astype(F32)).astype(BF16), axis, onward
        )
    return entering


def body(x_in, gate_in, proj_bc, dt_raw, step_index, step_table, rates, skip, norm_gain, *, row_count, col_count):
    _, tile_rows, cols, channels = x_in.shape
    heads = skip.shape[0]
    width = channels // heads
    state = proj_bc.shape[-1] // 4
    tokens = tile_rows * cols
    group = GROUP
    while col_count % group:
        group //= 2
    share = tokens // group // PIECES
    lines = share // cols

    x = x_in.reshape(tokens, channels)
    gate = gate_in.reshape(tokens, channels)
    maps = proj_bc.reshape(tokens, 4 * state)
    raw = dt_raw.reshape(tokens, 2 * heads)
    sizes = dict(cols=cols, heads=heads, state=state, width=width)
    shared = dict(group=group, axis="col")
    shape = jax.ShapeDtypeStruct

    any_spec = pl.BlockSpec(memory_space=pl.ANY)
    hbm_spec = pl.BlockSpec(memory_space=pltpu.HBM)
    full = lambda *dims: pl.BlockSpec(dims, lambda i, index: (0,) * len(dims))
    block = shape((share, channels + LANES), BF16)
    given = [x, raw, maps, step_table.T, rates]
    params, *packed = pl.pallas_call(
        functools.partial(first_pack_kernel, pieces=PIECES, heads=heads, state=state, axis="col"),
        grid_spec=pltpu.PrefetchScalarGridSpec(
            num_scalar_prefetch=1,
            grid=(1,),
            in_specs=[hbm_spec] * len(given),
            out_specs=[full(8, 2 * heads)] + [full(*block.shape)] * group,
            scratch_shapes=[
                pltpu.VMEM(raw.shape, BF16),
                pltpu.VMEM(maps.shape, BF16),
                pltpu.VMEM(step_table.shape[::-1], F32),
                pltpu.VMEM(rates.shape, F32),
                pltpu.SemaphoreType.DMA((len(given) - 1 + group,)),
            ],
        ),
        out_shape=[pltpu.VMEM((8, 2 * heads), F32)] + [pltpu.VMEM(block.shape, BF16)] * group,
        compiler_params=pltpu.CompilerParams(vmem_limit_bytes=32 * 1024 * 1024),
        cost_estimate=SMALL,
    )(step_index, *[pltpu.with_memory_space_constraint(a, pltpu.HBM) for a in given])

    def exchange(blocks):
        got = {0: blocks[0]}
        for s in reversed(range(1, group)):
            got[s] = lax.ppermute(blocks[s], "col", [(i, i ^ s) for i in range(col_count)])
        return [got[s] for s in range(group)]

    def state_shapes(places, count):
        return [shape((places, channels), BF16)] + [shape((places, heads), F32)] * (count > 2)

    got = []
    row_entering = []
    for piece in range(PIECES):
        before = params
        if piece:
            packed = call(
                functools.partial(pack_kernel, piece=piece, pieces=PIECES, heads=heads, state=state, axis="col"),
                [block] * group,
                specs=[None] * 3 + [any_spec],
            )(x, raw, maps, made[0])
            before = packed[0]
        got.append(exchange(packed))
        if piece == PIECES - 1:
            col_made = call(
                functools.partial(col_state_kernel, **sizes),
                state_shapes(cols * state, row_count),
                specs=[None] * 4 + [any_spec],
                cost=LONG,
            )(params, x, raw, maps, before)
            col_entering = entering_states(col_made, "row", row_count, 1, width)
            before = col_made[0]
        made = call(
            functools.partial(row_state_kernel, **sizes, **shared),
            state_shapes(lines * state, col_count // group),
            specs=[None] * (1 + group) + [any_spec],
        )(params, *got[piece], before)
        row_entering.append(entering_states(made, "col", col_count, group, width))

    w, silu = call(
        functools.partial(col_out_kernel, **sizes),
        [shape((tokens, channels), F32)] * 2,
    )(params, col_entering, x, raw, maps, gate, jnp.repeat(skip, width).reshape(1, channels))

    back = []
    y_row = [params]
    for piece in range(PIECES):
        y_row = call(
            functools.partial(row_out_kernel, **sizes, **shared),
            [shape((share, channels), BF16)] * group,
            specs=[None] * (2 + group) + [any_spec],
            cost=LONG if piece == PIECES - 1 else SMALL,
        )(params, row_entering[piece], *got[piece], y_row[0])
        back += exchange(y_row)

    mixed = call(
        functools.partial(final_kernel, **shared),
        shape((tokens, channels), BF16),
    )(w, silu, norm_gain.reshape(1, channels), *back)
    return mixed.reshape(x_in.shape)


def solution(mesh):
    tile = P("img", "row", "col", None)
    return jax.shard_map(
        functools.partial(body, row_count=mesh.shape["row"], col_count=mesh.shape["col"]),
        mesh=mesh,
        in_specs=(tile, tile, tile, tile, P("img"), P(), P(), P(), P()),
        out_specs=tile,
        check_vma=False,
    )
```

```python
import functools

import jax
import jax.numpy as jnp
from jax import lax
from jax.experimental import pallas as pl
from jax.experimental.pallas import tpu as pltpu
from jax.sharding import PartitionSpec as P

LANES = 128
GROUP = 4
LATER = 4
STRIP = 512
F32 = jnp.float32
BF16 = jnp.bfloat16


def dot(a, b):
    return jnp.dot(a, b, preferred_element_type=F32)


def iota(shape, dim):
    return lax.broadcasted_iota(jnp.int32, shape, dim)


def div(a, n):
    return lax.shift_right_logical(a, n.bit_length() - 1) if n & (n - 1) == 0 else a // n


def mod(a, n):
    return jnp.bitwise_and(a, n - 1) if n & (n - 1) == 0 else a % n


def parts(values, count):
    terms = []
    for _ in range(count):
        term = values.astype(BF16)
        terms.append(term)
        values = values - term.astype(F32)
    return jnp.concatenate(terms, axis=1)


def picks(heads, width, first, channels):
    row = iota((2 * heads, 1), 0)
    head = jnp.where(row >= heads, row - heads, row)
    return (head == div(first + iota((1, channels), 1), width)).astype(BF16)


def summed(mask, values):
    heads = values.shape[1]
    sums = dot(mask, parts(values, 3))
    return sums[:, :heads] + sums[:, heads : 2 * heads] + sums[:, 2 * heads :]


def step_sizes(raw, bias):
    shifted = raw.astype(F32) + bias
    return jnp.maximum(shifted, 0.0) + jnp.log1p(jnp.exp(-jnp.abs(shifted)))


def widen(maps, line, lines):
    state = maps.shape[1]
    places = lines * state
    copy = (mod(iota((1, places), 1), state) == iota((state, 1), 0)).astype(BF16)
    own = div(iota((1, places), 1), state) == line
    return jnp.where(own, dot(maps, copy), 0.0).astype(BF16)


class Scan:
    def __init__(self, order, lines, raw, bias, rates, b_map, c_map):
        tokens, self.heads = raw.shape
        self.lines, self.b_map, self.c_map = lines, b_map, c_map
        self.line, place = order(iota((tokens, 1), 0))
        self.line_in, place_in = order(iota((1, tokens), 1))
        self.lower = jnp.logical_and(self.line == self.line_in, place >= place_in)
        steps = step_sizes(raw, bias)
        self.decay = -rates * steps
        running = summed(self.lower.astype(BF16), self.decay)
        self.fade = parts(jnp.exp(running), 2)
        self.grow = parts(steps * jnp.exp(-running), 2)

    def ends(self):
        places = self.lines * self.b_map.shape[1]
        own = div(iota((places, 1), 0), self.b_map.shape[1]) == self.line_in
        return jnp.exp(summed(own.astype(BF16), self.decay))

    def into(self):
        return widen(self.b_map, self.line, self.lines).astype(F32).T.astype(BF16)

    def mix(self, follows):
        scores = lax.dot_general(
            self.c_map, self.b_map, (((1,), (1,)), ((), ())), preferred_element_type=F32
        )
        within = jnp.where(self.lower, scores, 0.0).astype(BF16)
        entering = widen(self.c_map, self.line, self.lines)
        return jnp.concatenate([within, jnp.where(follows, entering, 0)], axis=1)


def column_order(cols):
    return lambda token: (mod(token, cols), div(token, cols))


def row_order(cols, lines, member):
    def order(token):
        source = jnp.bitwise_xor(div(token, cols * lines), member)
        return mod(div(token, cols), lines), source * cols + mod(token, cols)

    return order


def strips(channels):
    return [(first, min(STRIP, channels - first)) for first in range(0, channels, STRIP)]


def pack_kernel(
    x_ref, raw_ref, maps_ref, table_ref, rates_ref, raw, maps, table, rates, *refs, group, axis, heads, state
):
    sent, sems = refs[:-1], refs[-1]
    channels = x_ref.shape[1]
    share = x_ref.shape[0] // group
    member = mod(lax.axis_index(axis), group)
    moved = [(raw_ref, raw), (maps_ref, maps)]
    places = []
    offset = 0
    for i, out in enumerate(sent):
        rows = out.shape[0]
        first = jnp.bitwise_xor(member, i % group) * share + offset
        part = pl.ds(pl.multiple_of(first, 16), rows)
        places.append((out, part))
        moved.append((x_ref.at[part, :], out.at[:, pl.ds(0, channels)]))
        if i % group == group - 1:
            offset += rows
    moved += [(table_ref, table), (rates_ref, rates)]
    copies = [pltpu.make_async_copy(a, b, sems.at[i]) for i, (a, b) in enumerate(moved)]
    for copy in copies:
        copy.start()
    for copy in copies[:2]:
        copy.wait()
    used = heads + 2 * state
    for out, part in places:
        out[:, channels : channels + heads] = raw[part, :heads]
        out[:, channels + heads : channels + used] = maps[part, : 2 * state]
        out[:, channels + used :] = jnp.zeros((out.shape[0], LANES - used), BF16)
    for copy in copies[2:]:
        copy.wait()


def params_kernel(index_ref, table_ref, rates_ref, params_ref):
    heads = rates_ref.shape[1]
    row = jnp.where(iota(table_ref.shape, 1) == index_ref[0], table_ref[...], 0.0)
    ones = jnp.ones((8, table_ref.shape[1]), BF16)
    bias = jnp.zeros((8, row.shape[0]), F32)
    for _ in range(3):
        term = row.astype(BF16)
        row = row - term.astype(F32)
        bias += lax.dot_general(ones, term, (((1,), (1,)), ((), ())), preferred_element_type=F32)
    params_ref[0:1, :] = bias[0:1, :]
    params_ref[1:2, :heads] = rates_ref[0:1, :]
    params_ref[1:2, heads:] = rates_ref[1:2, :]
    params_ref[2:, :] = jnp.zeros((6, 2 * heads), F32)


def row_scan(params_ref, blocks, member, cols, heads, state):
    channels = blocks[0].shape[1] - LANES
    tokens = blocks[0].shape[0] * len(blocks)
    lines = tokens // (cols * len(blocks))
    aux = jnp.concatenate([block[:, channels:] for block in blocks], axis=0)
    return Scan(
        row_order(cols, lines, member),
        lines,
        aux[:, :heads],
        params_ref[0:1, :heads],
        params_ref[1:2, :heads],
        aux[:, heads : heads + state],
        aux[:, heads + state : heads + 2 * state],
    )


def col_scan(params_ref, raw_ref, maps_ref, cols, heads, state):
    return Scan(
        column_order(cols),
        cols,
        raw_ref[:, heads:],
        params_ref[0:1, heads:],
        params_ref[1:2, heads:],
        maps_ref[:, 2 * state : 3 * state],
        maps_ref[:, 3 * state :],
    )


def write_state(scan, tokens_of, width, channels, s_ref, factor_ref):
    ends = scan.ends()
    if factor_ref:
        factor_ref[0][...] = ends
    ends = parts(ends, 2)
    into = scan.into()
    for first, count in strips(channels):
        pick = picks(scan.heads, width, first, count)
        values = (tokens_of(first, count) * dot(scan.grow, pick)).astype(BF16)
        s_ref[:, first : first + count] = (dot(into, values) * dot(ends, pick)).astype(BF16)


def row_state_kernel(params_ref, *refs, group, axis, cols, heads, state, width):
    blocks, s_ref, factor_ref = refs[:group], refs[group + 1], refs[group + 2 :]
    member = mod(lax.axis_index(axis), group)
    scan = row_scan(params_ref, blocks, member, cols, heads, state)
    tokens_of = lambda first, count: jnp.concatenate(
        [block[:, first : first + count] for block in blocks], axis=0
    ).astype(F32)
    write_state(scan, tokens_of, width, s_ref.shape[1], s_ref, factor_ref)


def col_state_kernel(params_ref, x_ref, raw_ref, maps_ref, s_ref, *factor_ref, cols, heads, state, width):
    scan = col_scan(params_ref, raw_ref, maps_ref, cols, heads, state)
    tokens_of = lambda first, count: x_ref[:, first : first + count].astype(F32)
    write_state(scan, tokens_of, width, s_ref.shape[1], s_ref, factor_ref)


def row_out_kernel(params_ref, s_ref, *refs, group, axis, cols, heads, state, width):
    blocks, outs = refs[:group], refs[group + 1 :]
    member = mod(lax.axis_index(axis), group)
    scan = row_scan(params_ref, blocks, member, cols, heads, state)
    mix = scan.mix(lax.axis_index(axis) >= group)
    rows = blocks[0].shape[0]
    for first, count in strips(s_ref.shape[1]):
        pick = picks(heads, width, first, count)
        part = slice(first, first + count)
        x = jnp.concatenate([block[:, part] for block in blocks], axis=0).astype(F32)
        values = (x * dot(scan.grow, pick)).astype(BF16)
        y = dot(mix, jnp.concatenate([values, s_ref[:, part]], axis=0)) * dot(scan.fade, pick)
        for s in range(group):
            outs[s][:, part] = y[s * rows : (s + 1) * rows].astype(BF16)


def col_out_kernel(params_ref, s_ref, x_ref, raw_ref, maps_ref, gate_ref, skip_ref, w_ref, g_ref, *, cols, heads, state, width):
    scan = col_scan(params_ref, raw_ref, maps_ref, cols, heads, state)
    mix = scan.mix(lax.axis_index("row") > 0)
    for first, count in strips(s_ref.shape[1]):
        pick = picks(heads, width, first, count)
        part = slice(first, first + count)
        x = x_ref[:, part].astype(F32)
        values = (x * dot(scan.grow, pick)).astype(BF16)
        y = dot(mix, jnp.concatenate([values, s_ref[:, part]], axis=0)) * dot(scan.fade, pick)
        w_ref[:, part] = y + skip_ref[:, part] * x
        gate = gate_ref[:, part].astype(F32)
        g_ref[:, part] = gate / (1.0 + jnp.exp(-gate))


def final_kernel(w_ref, g_ref, gain_ref, *refs, group, axis, offset, share):
    blocks, (out_ref, made, sems) = refs[:group], refs[-3:]
    rows, channels = blocks[0].shape
    member = mod(lax.axis_index(axis), group)
    copies = []
    for s in range(group):
        part = pl.ds(pl.multiple_of(jnp.bitwise_xor(member, s) * share + offset, 16), rows)
        v = (blocks[s][...].astype(F32) + w_ref[part, :]) * g_ref[part, :]
        power = jnp.sum(v * v, axis=1, keepdims=True) / channels
        made[s] = (v * lax.rsqrt(power + 1e-5) * gain_ref[...]).astype(BF16)
        copies.append(pltpu.make_async_copy(made.at[s], out_ref.at[part, :], sems.at[s]))
        copies[-1].start()
    for copy in copies:
        copy.wait()


SMALL = pl.CostEstimate(flops=1024, bytes_accessed=1024, transcendentals=0)
LONG = pl.CostEstimate(flops=2 * 10**10, bytes_accessed=1024, transcendentals=0)


def call(kernel, out_shape, specs=None, cost=SMALL, **more):
    if specs is not None:
        more["in_specs"] = [spec or pl.BlockSpec() for spec in specs]
    return pl.pallas_call(
        kernel,
        out_shape=out_shape,
        compiler_params=pltpu.CompilerParams(vmem_limit_bytes=32 * 1024 * 1024),
        cost_estimate=cost,
        **more,
    )


def entering_states(made, axis, size, stride, width):
    ends = made[0]
    if size == stride:
        return ends
    onward = [(i, (i + stride) % size) for i in range(size)]
    entering = lax.ppermute(ends, axis, onward)
    for _ in range(size // stride - 2):
        follows = (lax.axis_index(axis) >= stride).astype(F32)
        factor = follows * jnp.repeat(made[1], width, axis=1)
        entering = lax.ppermute(
            (ends.astype(F32) + factor * entering.astype(F32)).astype(BF16), axis, onward
        )
    return entering


def body(x_in, gate_in, proj_bc, dt_raw, step_index, step_table, rates, skip, norm_gain, *, row_count, col_count):
    _, tile_rows, cols, channels = x_in.shape
    heads = skip.shape[0]
    width = channels // heads
    state = proj_bc.shape[-1] // 4
    tokens = tile_rows * cols
    group = GROUP
    while col_count % group:
        group //= 2
    share = tokens // group
    later = max(share // LATER, 16)
    pieces = [share - later, later]

    x = x_in.reshape(tokens, channels)
    gate = gate_in.reshape(tokens, channels)
    maps = proj_bc.reshape(tokens, 4 * state)
    raw = dt_raw.reshape(tokens, 2 * heads)
    sizes = dict(cols=cols, heads=heads, state=state, width=width)
    shared = dict(group=group, axis="col")
    shape = jax.ShapeDtypeStruct
    any_spec = pl.BlockSpec(memory_space=pl.ANY)

    given = [x, raw, maps, step_table.T, rates]
    raw, maps, table, rates, *packed = pl.pallas_call(
        functools.partial(pack_kernel, heads=heads, state=state, **shared),
        in_specs=[pl.BlockSpec(memory_space=pltpu.HBM)] * len(given),
        out_shape=[pltpu.VMEM(a.shape, a.dtype) for a in given[1:]]
        + [pltpu.VMEM((rows, channels + LANES), BF16) for rows in pieces for _ in range(group)],
        scratch_shapes=[pltpu.SemaphoreType.DMA((len(given) - 1 + group * len(pieces),))],
        compiler_params=pltpu.CompilerParams(vmem_limit_bytes=32 * 1024 * 1024),
        cost_estimate=SMALL,
    )(*[pltpu.with_memory_space_constraint(a, pltpu.HBM) for a in given])
    index, rates = lax.optimization_barrier((step_index, rates))
    params = pl.pallas_call(
        params_kernel,
        grid_spec=pltpu.PrefetchScalarGridSpec(
            num_scalar_prefetch=1,
            grid=(1,),
            in_specs=[
                pl.BlockSpec(table.shape, lambda i, index: (0, 0)),
                pl.BlockSpec(rates.shape, lambda i, index: (0, 0)),
            ],
            out_specs=pl.BlockSpec((8, 2 * heads), lambda i, index: (0, 0)),
        ),
        out_shape=shape((8, 2 * heads), F32),
        cost_estimate=SMALL,
    )(index, table, rates)

    def exchange(blocks):
        return [blocks[0]] + [
            lax.ppermute(blocks[s], "col", [(i, i ^ s) for i in range(col_count)]) for s in range(1, group)
        ]

    def state_shapes(places, count):
        return [shape((places, channels), BF16)] + [shape((places, heads), F32)] * (count > 2)

    got = [exchange(packed[i * group : (i + 1) * group]) for i in range(len(pieces))]
    col_made = call(
        functools.partial(col_state_kernel, **sizes),
        state_shapes(cols * state, row_count),
    )(params, x, raw, maps)
    col_entering = entering_states(col_made, "row", row_count, 1, width)
    row_entering = []
    before = col_made[0]
    for i, rows in enumerate(pieces):
        made = call(
            functools.partial(row_state_kernel, **sizes, **shared),
            state_shapes(rows // cols * state, col_count // group),
            specs=[None] * (1 + group) + [any_spec],
            cost=LONG if i else SMALL,
        )(params, *got[i], before)
        before = made[0]
        row_entering.append(entering_states(made, "col", col_count, group, width))

    w, silu = call(
        functools.partial(col_out_kernel, **sizes),
        [shape((tokens, channels), F32)] * 2,
    )(params, col_entering, x, raw, maps, gate, jnp.repeat(skip, width).reshape(1, channels))

    back = []
    before = w
    for i, rows in enumerate(pieces):
        y_row = call(
            functools.partial(row_out_kernel, **sizes, **shared),
            [shape((rows, channels), BF16)] * group,
            specs=[None] * (2 + group) + [any_spec],
            cost=LONG if i else SMALL,
        )(params, row_entering[i], *got[i], before)
        back.append(exchange(y_row))
        before = y_row[0]

    mixed = None
    for i, rows in enumerate(pieces):
        more = [] if mixed is None else [mixed]
        mixed = call(
            functools.partial(final_kernel, offset=sum(pieces[:i]), share=share, **shared),
            shape((tokens, channels), BF16),
            specs=[None] * (3 + group) + [any_spec] * len(more),
            out_specs=any_spec,
            scratch_shapes=[pltpu.VMEM((group, rows, channels), BF16), pltpu.SemaphoreType.DMA((group,))],
            input_output_aliases={3 + group: 0} if more else {},
        )(w, silu, norm_gain.reshape(1, channels), *back[i], *more)
    return mixed.reshape(x_in.shape)


def solution(mesh):
    tile = P("img", "row", "col", None)
    return jax.shard_map(
        functools.partial(body, row_count=mesh.shape["row"], col_count=mesh.shape["col"]),
        mesh=mesh,
        in_specs=(tile, tile, tile, tile, P("img"), P(), P(), P(), P()),
        out_specs=tile,
        check_vma=False,
    )
```

```python
import functools

import jax
import jax.numpy as jnp
from jax import lax
from jax.experimental import pallas as pl
from jax.experimental.pallas import tpu as pltpu
from jax.sharding import PartitionSpec as P

LANES = 128
GROUP = 4
LATER = 4
STRIP = 512
VMEM_LIMIT = 24 * 1024 * 1024
F32 = jnp.float32
BF16 = jnp.bfloat16


def dot(a, b):
    return jnp.dot(a, b, preferred_element_type=F32)


def iota(shape, dim):
    return lax.broadcasted_iota(jnp.int32, shape, dim)


def div(a, n):
    return lax.shift_right_logical(a, n.bit_length() - 1) if n & (n - 1) == 0 else a // n


def mod(a, n):
    return jnp.bitwise_and(a, n - 1) if n & (n - 1) == 0 else a % n


def parts(values, count):
    terms = []
    for _ in range(count):
        term = values.astype(BF16)
        terms.append(term)
        values = values - term.astype(F32)
    return jnp.concatenate(terms, axis=1)


def picks(heads, width, first, channels):
    row = iota((2 * heads, 1), 0)
    head = jnp.where(row >= heads, row - heads, row)
    return (head == div(first + iota((1, channels), 1), width)).astype(BF16)


def summed(mask, values):
    heads = values.shape[1]
    sums = dot(mask, parts(values, 3))
    return sums[:, :heads] + sums[:, heads : 2 * heads] + sums[:, 2 * heads :]


def step_sizes(raw, bias):
    shifted = raw.astype(F32) + bias
    return jnp.maximum(shifted, 0.0) + jnp.log1p(jnp.exp(-jnp.abs(shifted)))


def widen(maps, line, lines):
    state = maps.shape[1]
    places = lines * state
    copy = (mod(iota((1, places), 1), state) == iota((state, 1), 0)).astype(BF16)
    own = div(iota((1, places), 1), state) == line
    return jnp.where(own, dot(maps, copy), 0.0).astype(BF16)


class Scan:
    def __init__(self, order, lines, raw, bias, rates, b_map, c_map):
        tokens, self.heads = raw.shape
        self.lines, self.b_map, self.c_map = lines, b_map, c_map
        self.line, place = order(iota((tokens, 1), 0))
        self.line_in, place_in = order(iota((1, tokens), 1))
        self.lower = jnp.logical_and(self.line == self.line_in, place >= place_in)
        steps = step_sizes(raw, bias)
        self.decay = -rates * steps
        running = summed(self.lower.astype(BF16), self.decay)
        self.fade = parts(jnp.exp(running), 2)
        self.grow = parts(steps * jnp.exp(-running), 2)

    def ends(self):
        places = self.lines * self.b_map.shape[1]
        own = div(iota((places, 1), 0), self.b_map.shape[1]) == self.line_in
        return jnp.exp(summed(own.astype(BF16), self.decay))

    def into(self):
        return widen(self.b_map, self.line, self.lines).astype(F32).T.astype(BF16)

    def mix(self, follows):
        scores = lax.dot_general(
            self.c_map, self.b_map, (((1,), (1,)), ((), ())), preferred_element_type=F32
        )
        within = jnp.where(self.lower, scores, 0.0).astype(BF16)
        entering = widen(self.c_map, self.line, self.lines)
        return jnp.concatenate([within, jnp.where(follows, entering, 0)], axis=1)


def column_order(cols):
    return lambda token: (mod(token, cols), div(token, cols))


def row_order(cols, lines, member):
    def order(token):
        source = jnp.bitwise_xor(div(token, cols * lines), member)
        return mod(div(token, cols), lines), source * cols + mod(token, cols)

    return order


def strips(channels):
    return [(first, min(STRIP, channels - first)) for first in range(0, channels, STRIP)]


def pack_kernel(
    x_ref, raw_ref, maps_ref, table_ref, rates_ref, raw, maps, table, rates, *refs, group, axis, heads, state
):
    sent, sems = refs[:-1], refs[-1]
    channels = x_ref.shape[1]
    share = x_ref.shape[0] // group
    member = mod(lax.axis_index(axis), group)
    moved = [(raw_ref, raw), (maps_ref, maps)]
    places = []
    offset = 0
    for i, out in enumerate(sent):
        rows = out.shape[0]
        first = jnp.bitwise_xor(member, i % group) * share + offset
        part = pl.ds(pl.multiple_of(first, 16), rows)
        places.append((out, part))
        moved.append((x_ref.at[part, :], out.at[:, pl.ds(0, channels)]))
        if i % group == group - 1:
            offset += rows
    moved += [(table_ref, table), (rates_ref, rates)]
    copies = [pltpu.make_async_copy(a, b, sems.at[i]) for i, (a, b) in enumerate(moved)]
    for copy in copies:
        copy.start()
    for copy in copies[:2]:
        copy.wait()
    used = heads + 2 * state
    for out, part in places:
        out[:, channels : channels + heads] = raw[part, :heads]
        out[:, channels + heads : channels + used] = maps[part, : 2 * state]
        out[:, channels + used :] = jnp.zeros((out.shape[0], LANES - used), BF16)
    for copy in copies[2:]:
        copy.wait()


def params_kernel(index_ref, table_ref, rates_ref, params_ref):
    heads = rates_ref.shape[1]
    row = jnp.where(iota(table_ref.shape, 1) == index_ref[0], table_ref[...], 0.0)
    ones = jnp.ones((8, table_ref.shape[1]), BF16)
    bias = jnp.zeros((8, row.shape[0]), F32)
    for _ in range(3):
        term = row.astype(BF16)
        row = row - term.astype(F32)
        bias += lax.dot_general(ones, term, (((1,), (1,)), ((), ())), preferred_element_type=F32)
    params_ref[0:1, :] = bias[0:1, :]
    params_ref[1:2, :heads] = rates_ref[0:1, :]
    params_ref[1:2, heads:] = rates_ref[1:2, :]
    params_ref[2:, :] = jnp.zeros((6, 2 * heads), F32)


def row_scan(params_ref, blocks, member, cols, heads, state):
    channels = blocks[0].shape[1] - LANES
    tokens = blocks[0].shape[0] * len(blocks)
    lines = tokens // (cols * len(blocks))
    aux = jnp.concatenate([block[:, channels:] for block in blocks], axis=0)
    return Scan(
        row_order(cols, lines, member),
        lines,
        aux[:, :heads],
        params_ref[0:1, :heads],
        params_ref[1:2, :heads],
        aux[:, heads : heads + state],
        aux[:, heads + state : heads + 2 * state],
    )


def col_scan(params_ref, raw_ref, maps_ref, cols, heads, state):
    return Scan(
        column_order(cols),
        cols,
        raw_ref[:, heads:],
        params_ref[0:1, heads:],
        params_ref[1:2, heads:],
        maps_ref[:, 2 * state : 3 * state],
        maps_ref[:, 3 * state :],
    )


def write_state(scan, tokens_of, width, channels, s_ref, factor_ref):
    ends = scan.ends()
    if factor_ref:
        factor_ref[0][...] = ends
    ends = parts(ends, 2)
    into = scan.into()
    for first, count in strips(channels):
        pick = picks(scan.heads, width, first, count)
        values = (tokens_of(first, count) * dot(scan.grow, pick)).astype(BF16)
        s_ref[:, first : first + count] = (dot(into, values) * dot(ends, pick)).astype(BF16)


def row_state_kernel(params_ref, *refs, group, axis, cols, heads, state, width):
    blocks, s_ref, factor_ref = refs[:group], refs[group + 1], refs[group + 2 :]
    member = mod(lax.axis_index(axis), group)
    scan = row_scan(params_ref, blocks, member, cols, heads, state)
    tokens_of = lambda first, count: jnp.concatenate(
        [block[:, first : first + count] for block in blocks], axis=0
    ).astype(F32)
    write_state(scan, tokens_of, width, s_ref.shape[1], s_ref, factor_ref)


def col_state_kernel(params_ref, x_ref, raw_ref, maps_ref, s_ref, *factor_ref, cols, heads, state, width):
    scan = col_scan(params_ref, raw_ref, maps_ref, cols, heads, state)
    tokens_of = lambda first, count: x_ref[:, first : first + count].astype(F32)
    write_state(scan, tokens_of, width, s_ref.shape[1], s_ref, factor_ref)


def row_out_kernel(params_ref, s_ref, *refs, group, axis, cols, heads, state, width):
    blocks, outs = refs[:group], refs[group + 1 :]
    member = mod(lax.axis_index(axis), group)
    scan = row_scan(params_ref, blocks, member, cols, heads, state)
    mix = scan.mix(lax.axis_index(axis) >= group)
    rows = blocks[0].shape[0]
    for first, count in strips(s_ref.shape[1]):
        pick = picks(heads, width, first, count)
        part = slice(first, first + count)
        x = jnp.concatenate([block[:, part] for block in blocks], axis=0).astype(F32)
        values = (x * dot(scan.grow, pick)).astype(BF16)
        y = dot(mix, jnp.concatenate([values, s_ref[:, part]], axis=0)) * dot(scan.fade, pick)
        for s in range(group):
            outs[s][:, part] = y[s * rows : (s + 1) * rows].astype(BF16)


def col_out_kernel(params_ref, s_ref, x_ref, raw_ref, maps_ref, gate_ref, skip_ref, w_ref, g_ref, *, cols, heads, state, width):
    scan = col_scan(params_ref, raw_ref, maps_ref, cols, heads, state)
    mix = scan.mix(lax.axis_index("row") > 0)
    for first, count in strips(s_ref.shape[1]):
        pick = picks(heads, width, first, count)
        part = slice(first, first + count)
        x = x_ref[:, part].astype(F32)
        values = (x * dot(scan.grow, pick)).astype(BF16)
        y = dot(mix, jnp.concatenate([values, s_ref[:, part]], axis=0)) * dot(scan.fade, pick)
        w_ref[:, part] = y + skip_ref[:, part] * x
        gate = gate_ref[:, part].astype(F32)
        g_ref[:, part] = gate / (1.0 + jnp.exp(-gate))


def final_kernel(w_ref, g_ref, gain_ref, *refs, group, axis, offset, share):
    blocks, (out_ref, made, sems) = refs[:group], refs[-3:]
    rows, channels = blocks[0].shape
    member = mod(lax.axis_index(axis), group)
    copies = []
    for s in range(group):
        part = pl.ds(pl.multiple_of(jnp.bitwise_xor(member, s) * share + offset, 16), rows)
        v = (blocks[s][...].astype(F32) + w_ref[part, :]) * g_ref[part, :]
        power = jnp.sum(v * v, axis=1, keepdims=True) / channels
        made[s] = (v * lax.rsqrt(power + 1e-5) * gain_ref[...]).astype(BF16)
        copies.append(pltpu.make_async_copy(made.at[s], out_ref.at[part, :], sems.at[s]))
        copies[-1].start()
    for copy in copies:
        copy.wait()


SMALL = pl.CostEstimate(flops=1024, bytes_accessed=1024, transcendentals=0)
LONG = pl.CostEstimate(flops=2 * 10**10, bytes_accessed=1024, transcendentals=0)


def call(kernel, out_shape, specs=None, cost=SMALL, **more):
    if specs is not None:
        more["in_specs"] = [spec or pl.BlockSpec() for spec in specs]
    return pl.pallas_call(
        kernel,
        out_shape=out_shape,
        compiler_params=pltpu.CompilerParams(vmem_limit_bytes=VMEM_LIMIT),
        cost_estimate=cost,
        **more,
    )


def entering_states(made, axis, size, stride, width):
    ends = made[0]
    if size == stride:
        return ends
    onward = [(i, (i + stride) % size) for i in range(size)]
    entering = lax.ppermute(ends, axis, onward)
    for _ in range(size // stride - 2):
        follows = (lax.axis_index(axis) >= stride).astype(F32)
        factor = follows * jnp.repeat(made[1], width, axis=1)
        entering = lax.ppermute(
            (ends.astype(F32) + factor * entering.astype(F32)).astype(BF16), axis, onward
        )
    return entering


def body(x_in, gate_in, proj_bc, dt_raw, step_index, step_table, rates, skip, norm_gain, *, row_count, col_count):
    _, tile_rows, cols, channels = x_in.shape
    heads = skip.shape[0]
    width = channels // heads
    state = proj_bc.shape[-1] // 4
    tokens = tile_rows * cols
    group = GROUP
    while col_count % group:
        group //= 2
    share = tokens // group
    later = max(share // LATER, 16)
    pieces = [share - later, later]

    x = x_in.reshape(tokens, channels)
    gate = gate_in.reshape(tokens, channels)
    maps = proj_bc.reshape(tokens, 4 * state)
    raw = dt_raw.reshape(tokens, 2 * heads)
    sizes = dict(cols=cols, heads=heads, state=state, width=width)
    shared = dict(group=group, axis="col")
    shape = jax.ShapeDtypeStruct
    any_spec = pl.BlockSpec(memory_space=pl.ANY)

    given = [x, raw, maps, step_table.T, rates]
    raw, maps, table, rates, *packed = pl.pallas_call(
        functools.partial(pack_kernel, heads=heads, state=state, **shared),
        in_specs=[pl.BlockSpec(memory_space=pltpu.HBM)] * len(given),
        out_shape=[pltpu.VMEM(a.shape, a.dtype) for a in given[1:]]
        + [pltpu.VMEM((rows, channels + LANES), BF16) for rows in pieces for _ in range(group)],
        scratch_shapes=[pltpu.SemaphoreType.DMA((len(given) - 1 + group * len(pieces),))],
        compiler_params=pltpu.CompilerParams(vmem_limit_bytes=VMEM_LIMIT),
        cost_estimate=SMALL,
    )(*[pltpu.with_memory_space_constraint(a, pltpu.HBM) for a in given])
    index, rates = lax.optimization_barrier((step_index, rates))
    params = pl.pallas_call(
        params_kernel,
        grid_spec=pltpu.PrefetchScalarGridSpec(
            num_scalar_prefetch=1,
            grid=(1,),
            in_specs=[
                pl.BlockSpec(table.shape, lambda i, index: (0, 0)),
                pl.BlockSpec(rates.shape, lambda i, index: (0, 0)),
            ],
            out_specs=pl.BlockSpec((8, 2 * heads), lambda i, index: (0, 0)),
        ),
        out_shape=shape((8, 2 * heads), F32),
        compiler_params=pltpu.CompilerParams(vmem_limit_bytes=VMEM_LIMIT),
        cost_estimate=SMALL,
    )(index, table, rates)

    def exchange(blocks):
        return [blocks[0]] + [
            lax.ppermute(blocks[s], "col", [(i, i ^ s) for i in range(col_count)]) for s in range(1, group)
        ]

    def state_shapes(places, count):
        return [shape((places, channels), BF16)] + [shape((places, heads), F32)] * (count > 2)

    got = [exchange(packed[i * group : (i + 1) * group]) for i in range(len(pieces))]
    col_made = call(
        functools.partial(col_state_kernel, **sizes),
        state_shapes(cols * state, row_count),
    )(params, x, raw, maps)
    col_entering = entering_states(col_made, "row", row_count, 1, width)
    row_entering = []
    before = col_made[0]
    for i, rows in enumerate(pieces):
        made = call(
            functools.partial(row_state_kernel, **sizes, **shared),
            state_shapes(rows // cols * state, col_count // group),
            specs=[None] * (1 + group) + [any_spec],
            cost=LONG if i else SMALL,
        )(params, *got[i], before)
        before = made[0]
        row_entering.append(entering_states(made, "col", col_count, group, width))

    w, silu = call(
        functools.partial(col_out_kernel, **sizes),
        [shape((tokens, channels), F32)] * 2,
    )(params, col_entering, x, raw, maps, gate, jnp.repeat(skip, width).reshape(1, channels))

    back = []
    before = w
    for i, rows in enumerate(pieces):
        y_row = call(
            functools.partial(row_out_kernel, **sizes, **shared),
            [shape((rows, channels), BF16)] * group,
            specs=[None] * (2 + group) + [any_spec],
            cost=LONG if i else SMALL,
        )(params, row_entering[i], *got[i], before)
        back.append(exchange(y_row))
        before = y_row[0]

    mixed = None
    for i, rows in enumerate(pieces):
        more = [] if mixed is None else [mixed]
        mixed = call(
            functools.partial(final_kernel, offset=sum(pieces[:i]), share=share, **shared),
            shape((tokens, channels), BF16),
            specs=[None] * (3 + group) + [any_spec] * len(more),
            out_specs=any_spec,
            scratch_shapes=[pltpu.VMEM((group, rows, channels), BF16), pltpu.SemaphoreType.DMA((group,))],
            input_output_aliases={3 + group: 0} if more else {},
        )(w, silu, norm_gain.reshape(1, channels), *back[i], *more)
    return mixed.reshape(x_in.shape)


def solution(mesh):
    tile = P("img", "row", "col", None)
    return jax.shard_map(
        functools.partial(body, row_count=mesh.shape["row"], col_count=mesh.shape["col"]),
        mesh=mesh,
        in_specs=(tile, tile, tile, tile, P("img"), P(), P(), P(), P()),
        out_specs=tile,
        check_vma=False,
    )
```

```python
import functools

import jax
import jax.numpy as jnp
from jax import lax
from jax.experimental import pallas as pl
from jax.experimental.pallas import tpu as pltpu
from jax.sharding import PartitionSpec as P

LANES = 128
GROUP = 4
PIECES = ((4,), (4,))
STRIP = 512
VMEM_LIMIT = 24 * 1024 * 1024
F32 = jnp.float32
BF16 = jnp.bfloat16


def dot(a, b):
    return jnp.dot(a, b, preferred_element_type=F32)


def iota(shape, dim):
    return lax.broadcasted_iota(jnp.int32, shape, dim)


def div(a, n):
    return lax.shift_right_logical(a, n.bit_length() - 1) if n & (n - 1) == 0 else a // n


def mod(a, n):
    return jnp.bitwise_and(a, n - 1) if n & (n - 1) == 0 else a % n


def parts(values, count):
    terms = []
    for _ in range(count):
        term = values.astype(BF16)
        terms.append(term)
        values = values - term.astype(F32)
    return jnp.concatenate(terms, axis=1)


def picks(heads, width, first, channels):
    row = iota((2 * heads, 1), 0)
    head = jnp.where(row >= heads, row - heads, row)
    return (head == div(first + iota((1, channels), 1), width)).astype(BF16)


def summed(mask, values):
    heads = values.shape[1]
    sums = dot(mask, parts(values, 3))
    return sums[:, :heads] + sums[:, heads : 2 * heads] + sums[:, 2 * heads :]


def step_sizes(raw, bias):
    shifted = raw.astype(F32) + bias
    return jnp.maximum(shifted, 0.0) + jnp.log1p(jnp.exp(-jnp.abs(shifted)))


def widen(maps, line, lines):
    state = maps.shape[1]
    places = lines * state
    copy = (mod(iota((1, places), 1), state) == iota((state, 1), 0)).astype(BF16)
    own = div(iota((1, places), 1), state) == line
    return jnp.where(own, dot(maps, copy), 0.0).astype(BF16)


class Scan:
    def __init__(self, order, lines, raw, bias, rates, b_map, c_map):
        tokens, self.heads = raw.shape
        self.lines, self.b_map, self.c_map = lines, b_map, c_map
        self.line, place = order(iota((tokens, 1), 0))
        self.line_in, place_in = order(iota((1, tokens), 1))
        self.lower = jnp.logical_and(self.line == self.line_in, place >= place_in)
        steps = step_sizes(raw, bias)
        self.decay = -rates * steps
        running = summed(self.lower.astype(BF16), self.decay)
        self.fade = parts(jnp.exp(running), 2)
        self.grow = parts(steps * jnp.exp(-running), 2)

    def ends(self):
        places = self.lines * self.b_map.shape[1]
        own = div(iota((places, 1), 0), self.b_map.shape[1]) == self.line_in
        return jnp.exp(summed(own.astype(BF16), self.decay))

    def into(self):
        return widen(self.b_map, self.line, self.lines).astype(F32).T.astype(BF16)

    def mix(self, follows):
        scores = lax.dot_general(
            self.c_map, self.b_map, (((1,), (1,)), ((), ())), preferred_element_type=F32
        )
        within = jnp.where(self.lower, scores, 0.0).astype(BF16)
        entering = widen(self.c_map, self.line, self.lines)
        return jnp.concatenate([within, jnp.where(follows, entering, 0)], axis=1)


def column_order(cols):
    return lambda token: (mod(token, cols), div(token, cols))


def row_order(cols, lines, member):
    def order(token):
        source = jnp.bitwise_xor(div(token, cols * lines), member)
        return mod(div(token, cols), lines), source * cols + mod(token, cols)

    return order


def strips(channels):
    return [(first, min(STRIP, channels - first)) for first in range(0, channels, STRIP)]


def pack_kernel(
    x_ref, raw_ref, maps_ref, table_ref, rates_ref, raw, maps, table, rates, *refs, group, axis, heads, state
):
    sent, sems = refs[:-1], refs[-1]
    channels = x_ref.shape[1]
    share = x_ref.shape[0] // group
    member = mod(lax.axis_index(axis), group)
    moved = [(raw_ref, raw), (maps_ref, maps)]
    places = []
    offset = 0
    for i, out in enumerate(sent):
        rows = out.shape[0]
        first = jnp.bitwise_xor(member, i % group) * share + offset
        part = pl.ds(pl.multiple_of(first, 16), rows)
        places.append((out, part))
        moved.append((x_ref.at[part, :], out.at[:, pl.ds(0, channels)]))
        if i % group == group - 1:
            offset += rows
    moved += [(table_ref, table), (rates_ref, rates)]
    copies = [pltpu.make_async_copy(a, b, sems.at[i]) for i, (a, b) in enumerate(moved)]
    for copy in copies:
        copy.start()
    for copy in copies[:2]:
        copy.wait()
    used = heads + 2 * state
    for out, part in places:
        out[:, channels : channels + heads] = raw[part, :heads]
        out[:, channels + heads : channels + used] = maps[part, : 2 * state]
        out[:, channels + used :] = jnp.zeros((out.shape[0], LANES - used), BF16)
    for copy in copies[2:]:
        copy.wait()


def params_kernel(index_ref, table_ref, rates_ref, params_ref):
    heads = rates_ref.shape[1]
    row = jnp.where(iota(table_ref.shape, 1) == index_ref[0], table_ref[...], 0.0)
    ones = jnp.ones((8, table_ref.shape[1]), BF16)
    bias = jnp.zeros((8, row.shape[0]), F32)
    for _ in range(3):
        term = row.astype(BF16)
        row = row - term.astype(F32)
        bias += lax.dot_general(ones, term, (((1,), (1,)), ((), ())), preferred_element_type=F32)
    params_ref[0:1, :] = bias[0:1, :]
    params_ref[1:2, :heads] = rates_ref[0:1, :]
    params_ref[1:2, heads:] = rates_ref[1:2, :]
    params_ref[2:, :] = jnp.zeros((6, 2 * heads), F32)


def row_scan(params_ref, blocks, member, cols, heads, state):
    channels = blocks[0].shape[1] - LANES
    tokens = blocks[0].shape[0] * len(blocks)
    lines = tokens // (cols * len(blocks))
    aux = jnp.concatenate([block[:, channels:] for block in blocks], axis=0)
    return Scan(
        row_order(cols, lines, member),
        lines,
        aux[:, :heads],
        params_ref[0:1, :heads],
        params_ref[1:2, :heads],
        aux[:, heads : heads + state],
        aux[:, heads + state : heads + 2 * state],
    )


def col_scan(params_ref, raw_ref, maps_ref, cols, heads, state):
    return Scan(
        column_order(cols),
        cols,
        raw_ref[:, heads:],
        params_ref[0:1, heads:],
        params_ref[1:2, heads:],
        maps_ref[:, 2 * state : 3 * state],
        maps_ref[:, 3 * state :],
    )


def write_state(scan, tokens_of, width, channels, s_refs, factor_ref):
    ends = scan.ends()
    if factor_ref:
        factor_ref[0][...] = ends
    ends = parts(ends, 2)
    into = scan.into()
    for first, count in strips(channels):
        pick = picks(scan.heads, width, first, count)
        values = (tokens_of(first, count) * dot(scan.grow, pick)).astype(BF16)
        made = (dot(into, values) * dot(ends, pick)).astype(BF16)
        row = 0
        for s_ref in s_refs:
            s_ref[:, first : first + count] = made[row : row + s_ref.shape[0]]
            row += s_ref.shape[0]


def row_state_kernel(params_ref, *refs, group, count, axis, cols, heads, state, width):
    blocks, s_refs, factor_ref = refs[:group], refs[group + 1 : group + 1 + count], refs[group + 1 + count :]
    member = mod(lax.axis_index(axis), group)
    scan = row_scan(params_ref, [block[...] for block in blocks], member, cols, heads, state)
    tokens_of = lambda first, count: jnp.concatenate(
        [block[:, first : first + count] for block in blocks], axis=0
    ).astype(F32)
    write_state(scan, tokens_of, width, s_refs[0].shape[1], s_refs, factor_ref)


def col_state_kernel(params_ref, x_ref, raw_ref, maps_ref, _, s_ref, *factor_ref, cols, heads, state, width):
    scan = col_scan(params_ref, raw_ref, maps_ref, cols, heads, state)
    tokens_of = lambda first, count: x_ref[:, first : first + count].astype(F32)
    write_state(scan, tokens_of, width, s_ref.shape[1], [s_ref], factor_ref)


def row_out_kernel(params_ref, s_ref, *refs, group, offset, axis, cols, heads, state, width):
    blocks, outs = refs[:group], refs[group + 1 :]
    rows = outs[0].shape[0]
    mine = slice(offset, offset + rows)
    member = mod(lax.axis_index(axis), group)
    scan = row_scan(params_ref, [block[mine, :] for block in blocks], member, cols, heads, state)
    mix = scan.mix(lax.axis_index(axis) >= group)
    for first, count in strips(s_ref.shape[1]):
        pick = picks(heads, width, first, count)
        part = slice(first, first + count)
        x = jnp.concatenate([block[mine, part] for block in blocks], axis=0).astype(F32)
        values = (x * dot(scan.grow, pick)).astype(BF16)
        y = dot(mix, jnp.concatenate([values, s_ref[:, part]], axis=0)) * dot(scan.fade, pick)
        for s in range(group):
            outs[s][:, part] = y[s * rows : (s + 1) * rows].astype(BF16)


def col_out_kernel(params_ref, s_ref, x_ref, raw_ref, maps_ref, gate_ref, skip_ref, w_ref, g_ref, *, cols, heads, state, width):
    scan = col_scan(params_ref, raw_ref, maps_ref, cols, heads, state)
    mix = scan.mix(lax.axis_index("row") > 0)
    for first, count in strips(s_ref.shape[1]):
        pick = picks(heads, width, first, count)
        part = slice(first, first + count)
        x = x_ref[:, part].astype(F32)
        values = (x * dot(scan.grow, pick)).astype(BF16)
        y = dot(mix, jnp.concatenate([values, s_ref[:, part]], axis=0)) * dot(scan.fade, pick)
        w_ref[:, part] = y + skip_ref[:, part] * x
        gate = gate_ref[:, part].astype(F32)
        g_ref[:, part] = gate / (1.0 + jnp.exp(-gate))


def final_kernel(w_ref, g_ref, gain_ref, *refs, group, axis, offset, share):
    blocks, (out_ref, made, sems) = refs[:group], refs[-3:]
    rows, channels = blocks[0].shape
    member = mod(lax.axis_index(axis), group)
    copies = []
    for s in range(group):
        part = pl.ds(pl.multiple_of(jnp.bitwise_xor(member, s) * share + offset, 16), rows)
        v = (blocks[s][...].astype(F32) + w_ref[part, :]) * g_ref[part, :]
        power = jnp.sum(v * v, axis=1, keepdims=True) / channels
        made[s] = (v * lax.rsqrt(power + 1e-5) * gain_ref[...]).astype(BF16)
        copies.append(pltpu.make_async_copy(made.at[s], out_ref.at[part, :], sems.at[s]))
        copies[-1].start()
    for copy in copies:
        copy.wait()


def cost(micros):
    return pl.CostEstimate(flops=1024 + int(micros * 10**9), bytes_accessed=1024, transcendentals=0)


def call(kernel, out_shape, micros, specs=None, **more):
    if specs is not None:
        more["in_specs"] = [spec or pl.BlockSpec() for spec in specs]
    return pl.pallas_call(
        kernel,
        out_shape=out_shape,
        compiler_params=pltpu.CompilerParams(vmem_limit_bytes=VMEM_LIMIT),
        cost_estimate=cost(micros),
        **more,
    )


def entering_states(ends, factor, axis, size, stride, width):
    if size == stride:
        return ends
    onward = [(i, (i + stride) % size) for i in range(size)]
    entering = lax.ppermute(ends, axis, onward)
    for _ in range(size // stride - 2):
        follows = (lax.axis_index(axis) >= stride).astype(F32)
        decayed = follows * jnp.repeat(factor[0], width, axis=1) * entering.astype(F32)
        entering = lax.ppermute((ends.astype(F32) + decayed).astype(BF16), axis, onward)
    return entering


def body(x_in, gate_in, proj_bc, dt_raw, step_index, step_table, rates, skip, norm_gain, *, row_count, col_count):
    _, tile_rows, cols, channels = x_in.shape
    heads = skip.shape[0]
    width = channels // heads
    state = proj_bc.shape[-1] // 4
    tokens = tile_rows * cols
    group = GROUP
    while col_count % group:
        group //= 2
    share = tokens // group
    pieces = [[eighths * share // 8 for eighths in piece] for piece in PIECES]

    x = x_in.reshape(tokens, channels)
    gate = gate_in.reshape(tokens, channels)
    maps = proj_bc.reshape(tokens, 4 * state)
    raw = dt_raw.reshape(tokens, 2 * heads)
    sizes = dict(cols=cols, heads=heads, state=state, width=width)
    shared = dict(group=group, axis="col")
    shape = jax.ShapeDtypeStruct
    any_spec = pl.BlockSpec(memory_space=pl.ANY)

    given = [x, raw, maps, step_table.T, rates]
    raw, maps, table, rates, *packed = pl.pallas_call(
        functools.partial(pack_kernel, heads=heads, state=state, **shared),
        in_specs=[pl.BlockSpec(memory_space=pltpu.HBM)] * len(given),
        out_shape=[pltpu.VMEM(a.shape, a.dtype) for a in given[1:]]
        + [pltpu.VMEM((sum(piece), channels + LANES), BF16) for piece in pieces for _ in range(group)],
        scratch_shapes=[pltpu.SemaphoreType.DMA((len(given) - 1 + group * len(pieces),))],
        compiler_params=pltpu.CompilerParams(vmem_limit_bytes=VMEM_LIMIT),
        cost_estimate=cost(1),
    )(*[pltpu.with_memory_space_constraint(a, pltpu.HBM) for a in given])
    index, rates = lax.optimization_barrier((step_index, rates))
    params = pl.pallas_call(
        params_kernel,
        grid_spec=pltpu.PrefetchScalarGridSpec(
            num_scalar_prefetch=1,
            grid=(1,),
            in_specs=[
                pl.BlockSpec(table.shape, lambda i, index: (0, 0)),
                pl.BlockSpec(rates.shape, lambda i, index: (0, 0)),
            ],
            out_specs=pl.BlockSpec((8, 2 * heads), lambda i, index: (0, 0)),
        ),
        out_shape=shape((8, 2 * heads), F32),
        compiler_params=pltpu.CompilerParams(vmem_limit_bytes=VMEM_LIMIT),
        cost_estimate=cost(0),
    )(index, table, rates)

    def exchange(blocks):
        return [blocks[0]] + [
            lax.ppermute(blocks[s], "col", [(i, i ^ s) for i in range(col_count)]) for s in range(1, group)
        ]

    def state_shapes(places, count):
        states = [pltpu.VMEM((rows, channels), BF16) for rows in places]
        return states + [shape((sum(places), heads), F32)] * (count > 2)

    got = [exchange(packed[i * group : (i + 1) * group]) for i in range(len(pieces))]
    before = params
    parts_of = []
    for i, piece in enumerate(pieces):
        places = [rows // cols * state for rows in piece]
        made = call(
            functools.partial(row_state_kernel, count=len(piece), **sizes, **shared),
            state_shapes(places, col_count // group),
            0,
            specs=[None] * (1 + group) + [any_spec],
        )(params, *got[i], before)
        before = made[0]
        for j, rows in enumerate(piece):
            first = sum(places[:j])
            factor = [f[first : first + places[j]] for f in made[len(piece) :]]
            entering = entering_states(made[j], factor, "col", col_count, group, width)
            offset = sum(piece[:j])
            parts_of.append((i, offset, sum(map(sum, pieces[:i])) + offset, rows, entering))

    col_made = call(
        functools.partial(col_state_kernel, **sizes),
        state_shapes([cols * state], row_count),
        0,
        specs=[None] * 4 + [any_spec],
    )(params, x, raw, maps, before)
    col_entering = entering_states(col_made[0], col_made[1:], "row", row_count, 1, width)

    w, silu = call(
        functools.partial(col_out_kernel, **sizes),
        [pltpu.VMEM((tokens, channels), F32)] * 2,
        0,
    )(params, col_entering, x, raw, maps, gate, jnp.repeat(skip, width).reshape(1, channels))

    back = []
    before = params
    for i, offset, _, rows, entering in parts_of:
        y_row = call(
            functools.partial(row_out_kernel, offset=offset, **sizes, **shared),
            [pltpu.VMEM((rows, channels), BF16)] * group,
            20 if len(back) == len(parts_of) - 1 else 0,
            specs=[None] * (2 + group) + [any_spec],
        )(params, entering, *got[i], before)
        back.append(exchange(y_row))
        before = y_row[0]

    mixed = None
    for (_, _, first, rows, _), blocks in zip(parts_of, back):
        more = [] if mixed is None else [mixed]
        mixed = call(
            functools.partial(final_kernel, offset=first, share=share, **shared),
            shape((tokens, channels), BF16),
            0,
            specs=[None] * (3 + group) + [any_spec] * len(more),
            out_specs=any_spec,
            scratch_shapes=[pltpu.VMEM((group, rows, channels), BF16), pltpu.SemaphoreType.DMA((group,))],
            input_output_aliases={3 + group: 0} if more else {},
        )(w, silu, norm_gain.reshape(1, channels), *blocks, *more)
    return mixed.reshape(x_in.shape)


def solution(mesh):
    tile = P("img", "row", "col", None)
    return jax.shard_map(
        functools.partial(body, row_count=mesh.shape["row"], col_count=mesh.shape["col"]),
        mesh=mesh,
        in_specs=(tile, tile, tile, tile, P("img"), P(), P(), P(), P()),
        out_specs=tile,
        check_vma=False,
    )
```

```python
import functools

import jax
import jax.numpy as jnp
from jax import lax
from jax.experimental import pallas as pl
from jax.experimental.pallas import tpu as pltpu
from jax.sharding import PartitionSpec as P

LANES = 128
GROUP = 4
PIECES = ((4,), (4,))
STRIP = 512
VMEM_LIMIT = 24 * 1024 * 1024
F32 = jnp.float32
BF16 = jnp.bfloat16


def dot(a, b):
    return jnp.dot(a, b, preferred_element_type=F32)


def iota(shape, dim):
    return lax.broadcasted_iota(jnp.int32, shape, dim)


def div(a, n):
    return lax.shift_right_logical(a, n.bit_length() - 1) if n & (n - 1) == 0 else a // n


def mod(a, n):
    return jnp.bitwise_and(a, n - 1) if n & (n - 1) == 0 else a % n


def parts(values, count):
    terms = []
    for _ in range(count):
        term = values.astype(BF16)
        terms.append(term)
        values = values - term.astype(F32)
    return jnp.concatenate(terms, axis=1)


def picks(heads, width, first, channels):
    row = iota((2 * heads, 1), 0)
    head = jnp.where(row >= heads, row - heads, row)
    return (head == div(first + iota((1, channels), 1), width)).astype(BF16)


def summed(mask, values):
    heads = values.shape[1]
    sums = dot(mask, parts(values, 3))
    return sums[:, :heads] + sums[:, heads : 2 * heads] + sums[:, 2 * heads :]


def step_sizes(raw, bias):
    shifted = raw.astype(F32) + bias
    return jnp.maximum(shifted, 0.0) + jnp.log1p(jnp.exp(-jnp.abs(shifted)))


def widen(maps, line, lines):
    state = maps.shape[1]
    places = lines * state
    copy = (mod(iota((1, places), 1), state) == iota((state, 1), 0)).astype(BF16)
    own = div(iota((1, places), 1), state) == line
    return jnp.where(own, dot(maps, copy), 0.0).astype(BF16)


class Scan:
    def __init__(self, order, lines, raw, bias, rates, b_map, c_map):
        tokens, self.heads = raw.shape
        self.lines, self.b_map, self.c_map = lines, b_map, c_map
        self.line, place = order(iota((tokens, 1), 0))
        self.line_in, place_in = order(iota((1, tokens), 1))
        self.lower = jnp.logical_and(self.line == self.line_in, place >= place_in)
        steps = step_sizes(raw, bias)
        self.decay = -rates * steps
        running = summed(self.lower.astype(BF16), self.decay)
        self.fade = parts(jnp.exp(running), 2)
        self.grow = parts(steps * jnp.exp(-running), 2)

    def ends(self):
        places = self.lines * self.b_map.shape[1]
        own = div(iota((places, 1), 0), self.b_map.shape[1]) == self.line_in
        return jnp.exp(summed(own.astype(BF16), self.decay))

    def into(self):
        return widen(self.b_map, self.line, self.lines).astype(F32).T.astype(BF16)

    def within(self):
        scores = lax.dot_general(
            self.c_map, self.b_map, (((1,), (1,)), ((), ())), preferred_element_type=F32
        )
        return jnp.where(self.lower, scores, 0.0).astype(BF16)

    def entry(self, follows):
        return jnp.where(follows, widen(self.c_map, self.line, self.lines), 0)


def partner(member, i, group):
    return member ^ ((group - i) & (group - 1))


def column_order(cols):
    return lambda token: (mod(token, cols), div(token, cols))


def row_order(cols, lines, member, group):
    def order(token):
        source = partner(member, div(token, cols * lines), group)
        return mod(div(token, cols), lines), source * cols + mod(token, cols)

    return order


def strips(channels):
    return [(first, min(STRIP, channels - first)) for first in range(0, channels, STRIP)]


def pack_kernel(
    x_ref, raw_ref, maps_ref, table_ref, rates_ref, raw, maps, table, rates, *refs, group, axis, heads, state
):
    sent, sems = refs[:-1], refs[-1]
    channels = x_ref.shape[1]
    share = x_ref.shape[0] // group
    member = mod(lax.axis_index(axis), group)
    moved = [(raw_ref, raw), (maps_ref, maps)]
    places = []
    offset = 0
    for i, out in enumerate(sent):
        rows = out.shape[0]
        first = partner(member, i % group, group) * share + offset
        part = pl.ds(pl.multiple_of(first, 16), rows)
        places.append((out, part))
        moved.append((x_ref.at[part, :], out.at[:, pl.ds(0, channels)]))
        if i % group == group - 1:
            offset += rows
    moved += [(table_ref, table), (rates_ref, rates)]
    copies = [pltpu.make_async_copy(a, b, sems.at[i]) for i, (a, b) in enumerate(moved)]
    for copy in copies:
        copy.start()
    for copy in copies[:2]:
        copy.wait()
    used = heads + 2 * state
    for out, part in places:
        out[:, channels : channels + heads] = raw[part, :heads]
        out[:, channels + heads : channels + used] = maps[part, : 2 * state]
        out[:, channels + used :] = jnp.zeros((out.shape[0], LANES - used), BF16)
    for copy in copies[2:]:
        copy.wait()


def params_kernel(index_ref, table_ref, rates_ref, params_ref):
    heads = rates_ref.shape[1]
    row = jnp.where(iota(table_ref.shape, 1) == index_ref[0], table_ref[...], 0.0)
    ones = jnp.ones((8, table_ref.shape[1]), BF16)
    bias = jnp.zeros((8, row.shape[0]), F32)
    for _ in range(3):
        term = row.astype(BF16)
        row = row - term.astype(F32)
        bias += lax.dot_general(ones, term, (((1,), (1,)), ((), ())), preferred_element_type=F32)
    params_ref[0:1, :] = bias[0:1, :]
    params_ref[1:2, :heads] = rates_ref[0:1, :]
    params_ref[1:2, heads:] = rates_ref[1:2, :]
    params_ref[2:, :] = jnp.zeros((6, 2 * heads), F32)


def row_scan(params_ref, blocks, member, cols, heads, state):
    channels = blocks[0].shape[1] - LANES
    tokens = blocks[0].shape[0] * len(blocks)
    lines = tokens // (cols * len(blocks))
    aux = jnp.concatenate([block[:, channels:] for block in blocks], axis=0)
    return Scan(
        row_order(cols, lines, member, len(blocks)),
        lines,
        aux[:, :heads],
        params_ref[0:1, :heads],
        params_ref[1:2, :heads],
        aux[:, heads : heads + state],
        aux[:, heads + state : heads + 2 * state],
    )


def col_scan(params_ref, raw_ref, maps_ref, cols, heads, state):
    return Scan(
        column_order(cols),
        cols,
        raw_ref[:, heads:],
        params_ref[0:1, heads:],
        params_ref[1:2, heads:],
        maps_ref[:, 2 * state : 3 * state],
        maps_ref[:, 3 * state :],
    )


def write_state(scan, tokens_of, width, channels, s_refs, factor_ref):
    ends = scan.ends()
    if factor_ref:
        factor_ref[0][...] = ends
    ends = parts(ends, 2)
    into = scan.into()
    for first, count in strips(channels):
        pick = picks(scan.heads, width, first, count)
        values = (tokens_of(first, count) * dot(scan.grow, pick)).astype(BF16)
        made = (dot(into, values) * dot(ends, pick)).astype(BF16)
        row = 0
        for s_ref in s_refs:
            s_ref[:, first : first + count] = made[row : row + s_ref.shape[0]]
            row += s_ref.shape[0]


def row_state_kernel(params_ref, *refs, group, count, axis, cols, heads, state, width):
    blocks, s_refs, factor_ref = refs[:group], refs[group + 1 : group + 1 + count], refs[group + 1 + count :]
    member = mod(lax.axis_index(axis), group)
    scan = row_scan(params_ref, [block[...] for block in blocks], member, cols, heads, state)
    tokens_of = lambda first, count: jnp.concatenate(
        [block[:, first : first + count] for block in blocks], axis=0
    ).astype(F32)
    write_state(scan, tokens_of, width, s_refs[0].shape[1], s_refs, factor_ref)


def col_state_kernel(params_ref, x_ref, raw_ref, maps_ref, _, s_ref, *factor_ref, cols, heads, state, width):
    scan = col_scan(params_ref, raw_ref, maps_ref, cols, heads, state)
    tokens_of = lambda first, count: x_ref[:, first : first + count].astype(F32)
    write_state(scan, tokens_of, width, s_ref.shape[1], [s_ref], factor_ref)


def row_local_kernel(params_ref, *refs, group, offset, axis, cols, heads, state, width):
    blocks, (y_ref, fade_ref, entry_ref) = refs[:group], refs[group + 1 :]
    rows = y_ref.shape[0] // group
    mine = slice(offset, offset + rows)
    member = mod(lax.axis_index(axis), group)
    scan = row_scan(params_ref, [block[mine, :] for block in blocks], member, cols, heads, state)
    mix = scan.within()
    fade_ref[...] = scan.fade
    entry_ref[...] = scan.entry(lax.axis_index(axis) >= group)
    for first, count in strips(y_ref.shape[1]):
        pick = picks(heads, width, first, count)
        part = slice(first, first + count)
        x = jnp.concatenate([block[mine, part] for block in blocks], axis=0).astype(F32)
        values = (x * dot(scan.grow, pick)).astype(BF16)
        y_ref[:, part] = dot(mix, values) * dot(scan.fade, pick)


def row_out_kernel(s_ref, y_ref, fade_ref, entry_ref, _, *outs, heads, width):
    rows = outs[0].shape[0]
    for first, count in strips(s_ref.shape[1]):
        pick = picks(heads, width, first, count)
        part = slice(first, first + count)
        y = y_ref[:, part] + dot(entry_ref[...], s_ref[:, part]) * dot(fade_ref[...], pick)
        for i, out in enumerate(outs):
            out[:, part] = y[i * rows : (i + 1) * rows].astype(BF16)


def col_out_kernel(params_ref, s_ref, x_ref, raw_ref, maps_ref, gate_ref, skip_ref, w_ref, g_ref, *, cols, heads, state, width):
    scan = col_scan(params_ref, raw_ref, maps_ref, cols, heads, state)
    mix = jnp.concatenate([scan.within(), scan.entry(lax.axis_index("row") > 0)], axis=1)
    for first, count in strips(s_ref.shape[1]):
        pick = picks(heads, width, first, count)
        part = slice(first, first + count)
        x = x_ref[:, part].astype(F32)
        values = (x * dot(scan.grow, pick)).astype(BF16)
        y = dot(mix, jnp.concatenate([values, s_ref[:, part]], axis=0)) * dot(scan.fade, pick)
        w_ref[:, part] = y + skip_ref[:, part] * x
        gate = gate_ref[:, part].astype(F32)
        g_ref[:, part] = gate / (1.0 + jnp.exp(-gate))


def final_kernel(w_ref, g_ref, gain_ref, *refs, group, axis, offset, share):
    blocks, (out_ref, made, sems) = refs[:group], refs[-3:]
    rows, channels = blocks[0].shape
    member = mod(lax.axis_index(axis), group)
    copies = []
    for s in range(group):
        part = pl.ds(pl.multiple_of(partner(member, s, group) * share + offset, 16), rows)
        v = (blocks[s][...].astype(F32) + w_ref[part, :]) * g_ref[part, :]
        power = jnp.sum(v * v, axis=1, keepdims=True) / channels
        made[s] = (v * lax.rsqrt(power + 1e-5) * gain_ref[...]).astype(BF16)
        copies.append(pltpu.make_async_copy(made.at[s], out_ref.at[part, :], sems.at[s]))
        copies[-1].start()
    for copy in copies:
        copy.wait()


def cost(micros):
    return pl.CostEstimate(flops=1024 + int(micros * 10**9), bytes_accessed=1024, transcendentals=0)


def call(kernel, out_shape, micros, specs=None, **more):
    if specs is not None:
        more["in_specs"] = [spec or pl.BlockSpec() for spec in specs]
    return pl.pallas_call(
        kernel,
        out_shape=out_shape,
        compiler_params=pltpu.CompilerParams(vmem_limit_bytes=VMEM_LIMIT),
        cost_estimate=cost(micros),
        **more,
    )


def entering_states(ends, factor, axis, size, stride, width):
    if size == stride:
        return ends
    onward = [(i, (i + stride) % size) for i in range(size)]
    entering = lax.ppermute(ends, axis, onward)
    for _ in range(size // stride - 2):
        follows = (lax.axis_index(axis) >= stride).astype(F32)
        decayed = follows * jnp.repeat(factor[0], width, axis=1) * entering.astype(F32)
        entering = lax.ppermute((ends.astype(F32) + decayed).astype(BF16), axis, onward)
    return entering


def body(x_in, gate_in, proj_bc, dt_raw, step_index, step_table, rates, skip, norm_gain, *, row_count, col_count):
    _, tile_rows, cols, channels = x_in.shape
    heads = skip.shape[0]
    width = channels // heads
    state = proj_bc.shape[-1] // 4
    tokens = tile_rows * cols
    group = GROUP
    while col_count % group:
        group //= 2
    share = tokens // group
    pieces = [[eighths * share // 8 for eighths in piece] for piece in PIECES]

    x = x_in.reshape(tokens, channels)
    gate = gate_in.reshape(tokens, channels)
    maps = proj_bc.reshape(tokens, 4 * state)
    raw = dt_raw.reshape(tokens, 2 * heads)
    sizes = dict(cols=cols, heads=heads, state=state, width=width)
    shared = dict(group=group, axis="col")
    shape = jax.ShapeDtypeStruct
    any_spec = pl.BlockSpec(memory_space=pl.ANY)

    given = [x, raw, maps, step_table.T, rates]
    raw, maps, table, rates, *packed = pl.pallas_call(
        functools.partial(pack_kernel, heads=heads, state=state, **shared),
        in_specs=[pl.BlockSpec(memory_space=pltpu.HBM)] * len(given),
        out_shape=[pltpu.VMEM(a.shape, a.dtype) for a in given[1:]]
        + [pltpu.VMEM((sum(piece), channels + LANES), BF16) for piece in pieces for _ in range(group)],
        scratch_shapes=[pltpu.SemaphoreType.DMA((len(given) - 1 + group * len(pieces),))],
        compiler_params=pltpu.CompilerParams(vmem_limit_bytes=VMEM_LIMIT),
        cost_estimate=cost(1),
    )(*[pltpu.with_memory_space_constraint(a, pltpu.HBM) for a in given])
    index, rates = lax.optimization_barrier((step_index, rates))
    params = pl.pallas_call(
        params_kernel,
        grid_spec=pltpu.PrefetchScalarGridSpec(
            num_scalar_prefetch=1,
            grid=(1,),
            in_specs=[
                pl.BlockSpec(table.shape, lambda i, index: (0, 0)),
                pl.BlockSpec(rates.shape, lambda i, index: (0, 0)),
            ],
            out_specs=pl.BlockSpec((8, 2 * heads), lambda i, index: (0, 0)),
        ),
        out_shape=shape((8, 2 * heads), F32),
        compiler_params=pltpu.CompilerParams(vmem_limit_bytes=VMEM_LIMIT),
        cost_estimate=cost(0),
    )(index, table, rates)

    def exchange(blocks):
        return [blocks[0]] + [
            lax.ppermute(blocks[i], "col", [(at, partner(at, i, group)) for at in range(col_count)])
            for i in range(1, group)
        ]

    def state_shapes(places, count):
        states = [pltpu.VMEM((rows, channels), BF16) for rows in places]
        return states + [shape((sum(places), heads), F32)] * (count > 2)

    got = [exchange(packed[i * group : (i + 1) * group]) for i in range(len(pieces))]
    before = params
    parts_of = []
    for i, piece in enumerate(pieces):
        places = [rows // cols * state for rows in piece]
        made = call(
            functools.partial(row_state_kernel, count=len(piece), **sizes, **shared),
            state_shapes(places, col_count // group),
            0,
            specs=[None] * (1 + group) + [any_spec],
        )(params, *got[i], before)
        before = made[0]
        if i == 0:
            col_made = call(
                functools.partial(col_state_kernel, **sizes),
                state_shapes([cols * state], row_count),
                0,
                specs=[None] * 4 + [any_spec],
            )(params, x, raw, maps, before)
            col_entering = entering_states(col_made[0], col_made[1:], "row", row_count, 1, width)
            before = col_made[0]
        for j, rows in enumerate(piece):
            first = sum(places[:j])
            factor = [f[first : first + places[j]] for f in made[len(piece) :]]
            entering = entering_states(made[j], factor, "col", col_count, group, width)
            offset = sum(piece[:j])
            parts_of.append((i, offset, sum(map(sum, pieces[:i])) + offset, rows, entering))

    w, silu = call(
        functools.partial(col_out_kernel, **sizes),
        [pltpu.VMEM((tokens, channels), F32)] * 2,
        0,
    )(params, col_entering, x, raw, maps, gate, jnp.repeat(skip, width).reshape(1, channels))

    local = []
    for i, offset, _, rows, _ in parts_of:
        places = rows // cols * state
        local.append(
            call(
                functools.partial(row_local_kernel, offset=offset, **sizes, **shared),
                [
                    pltpu.VMEM((group * rows, channels), F32),
                    pltpu.VMEM((group * rows, 2 * heads), BF16),
                    pltpu.VMEM((group * rows, places), BF16),
                ],
                0,
                specs=[None] * (1 + group) + [any_spec],
            )(params, *got[i], before)
        )
    before = params

    back = []
    for (_, _, _, rows, entering), known in zip(parts_of, local):
        y_row = call(
            functools.partial(row_out_kernel, heads=heads, width=width),
            [pltpu.VMEM((rows, channels), BF16)] * group,
            20 if len(back) == len(parts_of) - 1 else 0,
            specs=[None] * 4 + [any_spec],
        )(entering, *known, before)
        back.append(exchange(y_row))
        before = y_row[0]

    mixed = None
    for (_, _, first, rows, _), blocks in zip(parts_of, back):
        more = [] if mixed is None else [mixed]
        mixed = call(
            functools.partial(final_kernel, offset=first, share=share, **shared),
            shape((tokens, channels), BF16),
            0,
            specs=[None] * (3 + group) + [any_spec] * len(more),
            out_specs=any_spec,
            scratch_shapes=[pltpu.VMEM((group, rows, channels), BF16), pltpu.SemaphoreType.DMA((group,))],
            input_output_aliases={3 + group: 0} if more else {},
        )(w, silu, norm_gain.reshape(1, channels), *blocks, *more)
    return mixed.reshape(x_in.shape)


def solution(mesh):
    tile = P("img", "row", "col", None)
    return jax.shard_map(
        functools.partial(body, row_count=mesh.shape["row"], col_count=mesh.shape["col"]),
        mesh=mesh,
        in_specs=(tile, tile, tile, tile, P("img"), P(), P(), P(), P()),
        out_specs=tile,
        check_vma=False,
    )
```

```python
import functools

import jax
import jax.numpy as jnp
from jax import lax
from jax.experimental import pallas as pl
from jax.experimental.pallas import tpu as pltpu
from jax.sharding import PartitionSpec as P

LANES = 128
GROUP = 4
PIECES = ((4,), (4,))
STRIP = 512
VMEM_LIMIT = 24 * 1024 * 1024
F32 = jnp.float32
BF16 = jnp.bfloat16


def dot(a, b):
    return jnp.dot(a, b, preferred_element_type=F32)


def iota(shape, dim):
    return lax.broadcasted_iota(jnp.int32, shape, dim)


def div(a, n):
    return lax.shift_right_logical(a, n.bit_length() - 1) if n & (n - 1) == 0 else a // n


def mod(a, n):
    return jnp.bitwise_and(a, n - 1) if n & (n - 1) == 0 else a % n


def parts(values, count):
    terms = []
    for _ in range(count):
        term = values.astype(BF16)
        terms.append(term)
        values = values - term.astype(F32)
    return jnp.concatenate(terms, axis=1)


def picks(heads, width, first, channels):
    row = iota((2 * heads, 1), 0)
    head = jnp.where(row >= heads, row - heads, row)
    return (head == div(first + iota((1, channels), 1), width)).astype(BF16)


def summed(mask, values):
    heads = values.shape[1]
    sums = dot(mask, parts(values, 3))
    return sums[:, :heads] + sums[:, heads : 2 * heads] + sums[:, 2 * heads :]


def step_sizes(raw, bias):
    shifted = raw.astype(F32) + bias
    return jnp.maximum(shifted, 0.0) + jnp.log1p(jnp.exp(-jnp.abs(shifted)))


def widen(maps, line, lines):
    state = maps.shape[1]
    places = lines * state
    copy = (mod(iota((1, places), 1), state) == iota((state, 1), 0)).astype(BF16)
    own = div(iota((1, places), 1), state) == line
    return jnp.where(own, dot(maps, copy), 0.0).astype(BF16)


class Scan:
    def __init__(self, order, lines, raw, bias, rates, b_map, c_map):
        tokens, self.heads = raw.shape
        self.lines, self.b_map, self.c_map = lines, b_map, c_map
        self.line, place = order(iota((tokens, 1), 0))
        self.line_in, place_in = order(iota((1, tokens), 1))
        self.lower = jnp.logical_and(self.line == self.line_in, place >= place_in)
        steps = step_sizes(raw, bias)
        self.decay = -rates * steps
        running = summed(self.lower.astype(BF16), self.decay)
        self.fade = parts(jnp.exp(running), 2)
        self.grow = parts(steps * jnp.exp(-running), 2)

    def ends(self):
        places = self.lines * self.b_map.shape[1]
        own = div(iota((places, 1), 0), self.b_map.shape[1]) == self.line_in
        return jnp.exp(summed(own.astype(BF16), self.decay))

    def into(self):
        return widen(self.b_map, self.line, self.lines).astype(F32).T.astype(BF16)

    def within(self):
        scores = lax.dot_general(
            self.c_map, self.b_map, (((1,), (1,)), ((), ())), preferred_element_type=F32
        )
        return jnp.where(self.lower, scores, 0.0).astype(BF16)

    def entry(self, follows):
        return jnp.where(follows, widen(self.c_map, self.line, self.lines), 0)


def partner(member, i, group):
    return member ^ i


def column_order(cols):
    return lambda token: (mod(token, cols), div(token, cols))


def row_order(cols, lines, member, group):
    def order(token):
        source = partner(member, div(token, cols * lines), group)
        return mod(div(token, cols), lines), source * cols + mod(token, cols)

    return order


def strips(channels):
    return [(first, min(STRIP, channels - first)) for first in range(0, channels, STRIP)]


def pack_kernel(
    x_ref, raw_ref, maps_ref, table_ref, rates_ref, raw, maps, table, rates, *refs, group, axis, heads, state
):
    sent, sems = refs[:-1], refs[-1]
    channels = x_ref.shape[1]
    share = x_ref.shape[0] // group
    member = mod(lax.axis_index(axis), group)
    moved = [(raw_ref, raw), (maps_ref, maps)]
    places = []
    offset = 0
    for i, out in enumerate(sent):
        rows = out.shape[0]
        first = partner(member, i % group, group) * share + offset
        part = pl.ds(pl.multiple_of(first, 16), rows)
        places.append((out, part))
        moved.append((x_ref.at[part, :], out.at[:, pl.ds(0, channels)]))
        if i % group == group - 1:
            offset += rows
    moved += [(table_ref, table), (rates_ref, rates)]
    copies = [pltpu.make_async_copy(a, b, sems.at[i]) for i, (a, b) in enumerate(moved)]
    for copy in copies:
        copy.start()
    for copy in copies[:2]:
        copy.wait()
    used = heads + 2 * state
    for out, part in places:
        out[:, channels : channels + heads] = raw[part, :heads]
        out[:, channels + heads : channels + used] = maps[part, : 2 * state]
        out[:, channels + used :] = jnp.zeros((out.shape[0], LANES - used), BF16)
    for copy in copies[2:]:
        copy.wait()


def params_kernel(index_ref, table_ref, rates_ref, params_ref):
    heads = rates_ref.shape[1]
    row = jnp.where(iota(table_ref.shape, 1) == index_ref[0], table_ref[...], 0.0)
    ones = jnp.ones((8, table_ref.shape[1]), BF16)
    bias = jnp.zeros((8, row.shape[0]), F32)
    for _ in range(3):
        term = row.astype(BF16)
        row = row - term.astype(F32)
        bias += lax.dot_general(ones, term, (((1,), (1,)), ((), ())), preferred_element_type=F32)
    params_ref[0:1, :] = bias[0:1, :]
    params_ref[1:2, :heads] = rates_ref[0:1, :]
    params_ref[1:2, heads:] = rates_ref[1:2, :]
    params_ref[2:, :] = jnp.zeros((6, 2 * heads), F32)


def row_scan(params_ref, blocks, member, cols, heads, state):
    channels = blocks[0].shape[1] - LANES
    tokens = blocks[0].shape[0] * len(blocks)
    lines = tokens // (cols * len(blocks))
    aux = jnp.concatenate([block[:, channels:] for block in blocks], axis=0)
    return Scan(
        row_order(cols, lines, member, len(blocks)),
        lines,
        aux[:, :heads],
        params_ref[0:1, :heads],
        params_ref[1:2, :heads],
        aux[:, heads : heads + state],
        aux[:, heads + state : heads + 2 * state],
    )


def col_scan(params_ref, raw_ref, maps_ref, cols, heads, state):
    return Scan(
        column_order(cols),
        cols,
        raw_ref[:, heads:],
        params_ref[0:1, heads:],
        params_ref[1:2, heads:],
        maps_ref[:, 2 * state : 3 * state],
        maps_ref[:, 3 * state :],
    )


def write_state(scan, tokens_of, width, channels, s_refs, factor_ref):
    ends = scan.ends()
    if factor_ref:
        factor_ref[0][...] = ends
    ends = parts(ends, 2)
    into = scan.into()
    for first, count in strips(channels):
        pick = picks(scan.heads, width, first, count)
        values = (tokens_of(first, count) * dot(scan.grow, pick)).astype(BF16)
        made = (dot(into, values) * dot(ends, pick)).astype(BF16)
        row = 0
        for s_ref in s_refs:
            s_ref[:, first : first + count] = made[row : row + s_ref.shape[0]]
            row += s_ref.shape[0]


def row_state_kernel(params_ref, *refs, group, count, axis, cols, heads, state, width):
    blocks, s_refs, factor_ref = refs[:group], refs[group + 1 : group + 1 + count], refs[group + 1 + count :]
    member = mod(lax.axis_index(axis), group)
    scan = row_scan(params_ref, [block[...] for block in blocks], member, cols, heads, state)
    tokens_of = lambda first, count: jnp.concatenate(
        [block[:, first : first + count] for block in blocks], axis=0
    ).astype(F32)
    write_state(scan, tokens_of, width, s_refs[0].shape[1], s_refs, factor_ref)


def col_state_kernel(params_ref, x_ref, raw_ref, maps_ref, _, s_ref, *factor_ref, cols, heads, state, width):
    scan = col_scan(params_ref, raw_ref, maps_ref, cols, heads, state)
    tokens_of = lambda first, count: x_ref[:, first : first + count].astype(F32)
    write_state(scan, tokens_of, width, s_ref.shape[1], [s_ref], factor_ref)


def row_local_kernel(params_ref, *refs, group, offset, axis, cols, heads, state, width):
    blocks, (y_ref, fade_ref, entry_ref) = refs[:group], refs[group + 1 :]
    rows = y_ref.shape[0] // group
    mine = slice(offset, offset + rows)
    member = mod(lax.axis_index(axis), group)
    scan = row_scan(params_ref, [block[mine, :] for block in blocks], member, cols, heads, state)
    mix = scan.within()
    fade_ref[...] = scan.fade
    entry_ref[...] = scan.entry(lax.axis_index(axis) >= group)
    for first, count in strips(y_ref.shape[1]):
        pick = picks(heads, width, first, count)
        part = slice(first, first + count)
        x = jnp.concatenate([block[mine, part] for block in blocks], axis=0).astype(F32)
        values = (x * dot(scan.grow, pick)).astype(BF16)
        y_ref[:, part] = dot(mix, values) * dot(scan.fade, pick)


def row_out_kernel(s_ref, y_ref, fade_ref, entry_ref, _, *outs, heads, width):
    rows = outs[0].shape[0]
    for first, count in strips(s_ref.shape[1]):
        pick = picks(heads, width, first, count)
        part = slice(first, first + count)
        y = y_ref[:, part] + dot(entry_ref[...], s_ref[:, part]) * dot(fade_ref[...], pick)
        for i, out in enumerate(outs):
            out[:, part] = y[i * rows : (i + 1) * rows].astype(BF16)


def col_out_kernel(params_ref, s_ref, x_ref, raw_ref, maps_ref, gate_ref, skip_ref, w_ref, g_ref, *, cols, heads, state, width):
    scan = col_scan(params_ref, raw_ref, maps_ref, cols, heads, state)
    mix = jnp.concatenate([scan.within(), scan.entry(lax.axis_index("row") > 0)], axis=1)
    for first, count in strips(s_ref.shape[1]):
        pick = picks(heads, width, first, count)
        part = slice(first, first + count)
        x = x_ref[:, part].astype(F32)
        values = (x * dot(scan.grow, pick)).astype(BF16)
        y = dot(mix, jnp.concatenate([values, s_ref[:, part]], axis=0)) * dot(scan.fade, pick)
        w_ref[:, part] = y + skip_ref[:, part] * x
        gate = gate_ref[:, part].astype(F32)
        g_ref[:, part] = gate / (1.0 + jnp.exp(-gate))


def final_kernel(w_ref, g_ref, gain_ref, *refs, group, axis, offset, share):
    blocks, (out_ref, made, sems) = refs[:group], refs[-3:]
    rows, channels = blocks[0].shape
    member = mod(lax.axis_index(axis), group)
    copies = []
    for s in range(group):
        part = pl.ds(pl.multiple_of(partner(member, s, group) * share + offset, 16), rows)
        v = (blocks[s][...].astype(F32) + w_ref[part, :]) * g_ref[part, :]
        power = jnp.sum(v * v, axis=1, keepdims=True) / channels
        made[s] = (v * lax.rsqrt(power + 1e-5) * gain_ref[...]).astype(BF16)
        copies.append(pltpu.make_async_copy(made.at[s], out_ref.at[part, :], sems.at[s]))
        copies[-1].start()
    for copy in copies:
        copy.wait()


def cost(micros):
    return pl.CostEstimate(flops=1024 + int(micros * 10**9), bytes_accessed=1024, transcendentals=0)


def call(kernel, out_shape, micros, specs=None, **more):
    if specs is not None:
        more["in_specs"] = [spec or pl.BlockSpec() for spec in specs]
    return pl.pallas_call(
        kernel,
        out_shape=out_shape,
        compiler_params=pltpu.CompilerParams(vmem_limit_bytes=VMEM_LIMIT),
        cost_estimate=cost(micros),
        **more,
    )


def entering_states(ends, factor, axis, size, stride, width):
    if size == stride:
        return ends
    onward = [(i, (i + stride) % size) for i in range(size)]
    entering = lax.ppermute(ends, axis, onward)
    for _ in range(size // stride - 2):
        follows = (lax.axis_index(axis) >= stride).astype(F32)
        decayed = follows * jnp.repeat(factor[0], width, axis=1) * entering.astype(F32)
        entering = lax.ppermute((ends.astype(F32) + decayed).astype(BF16), axis, onward)
    return entering


def body(x_in, gate_in, proj_bc, dt_raw, step_index, step_table, rates, skip, norm_gain, *, row_count, col_count):
    _, tile_rows, cols, channels = x_in.shape
    heads = skip.shape[0]
    width = channels // heads
    state = proj_bc.shape[-1] // 4
    tokens = tile_rows * cols
    group = GROUP
    while col_count % group:
        group //= 2
    share = tokens // group
    pieces = [[eighths * share // 8 for eighths in piece] for piece in PIECES]

    x = x_in.reshape(tokens, channels)
    gate = gate_in.reshape(tokens, channels)
    maps = proj_bc.reshape(tokens, 4 * state)
    raw = dt_raw.reshape(tokens, 2 * heads)
    sizes = dict(cols=cols, heads=heads, state=state, width=width)
    shared = dict(group=group, axis="col")
    shape = jax.ShapeDtypeStruct
    any_spec = pl.BlockSpec(memory_space=pl.ANY)

    given = [x, raw, maps, step_table.T, rates]
    raw, maps, table, rates, *packed = pl.pallas_call(
        functools.partial(pack_kernel, heads=heads, state=state, **shared),
        in_specs=[pl.BlockSpec(memory_space=pltpu.HBM)] * len(given),
        out_shape=[pltpu.VMEM(a.shape, a.dtype) for a in given[1:]]
        + [pltpu.VMEM((sum(piece), channels + LANES), BF16) for piece in pieces for _ in range(group)],
        scratch_shapes=[pltpu.SemaphoreType.DMA((len(given) - 1 + group * len(pieces),))],
        compiler_params=pltpu.CompilerParams(vmem_limit_bytes=VMEM_LIMIT),
        cost_estimate=cost(1),
    )(*[pltpu.with_memory_space_constraint(a, pltpu.HBM) for a in given])
    index, rates = lax.optimization_barrier((step_index, rates))
    params = pl.pallas_call(
        params_kernel,
        grid_spec=pltpu.PrefetchScalarGridSpec(
            num_scalar_prefetch=1,
            grid=(1,),
            in_specs=[
                pl.BlockSpec(table.shape, lambda i, index: (0, 0)),
                pl.BlockSpec(rates.shape, lambda i, index: (0, 0)),
            ],
            out_specs=pl.BlockSpec((8, 2 * heads), lambda i, index: (0, 0)),
        ),
        out_shape=shape((8, 2 * heads), F32),
        compiler_params=pltpu.CompilerParams(vmem_limit_bytes=VMEM_LIMIT),
        cost_estimate=cost(0),
    )(index, table, rates)

    def exchange(blocks):
        return [blocks[0]] + [
            lax.ppermute(blocks[i], "col", [(at, partner(at, i, group)) for at in range(col_count)])
            for i in range(1, group)
        ]

    def state_shapes(places, count):
        states = [pltpu.VMEM((rows, channels), BF16) for rows in places]
        return states + [shape((sum(places), heads), F32)] * (count > 2)

    got = [exchange(packed[i * group : (i + 1) * group]) for i in range(len(pieces))]
    before = params
    parts_of = []
    for i, piece in enumerate(pieces):
        places = [rows // cols * state for rows in piece]
        offsets = [sum(piece[:j]) for j in range(len(piece))]

        def of_own(before, i=i, piece=piece, places=places, offsets=offsets):
            known = []
            for offset, rows, count in zip(offsets, piece, places):
                known.append(
                    call(
                        functools.partial(row_local_kernel, offset=offset, **sizes, **shared),
                        [
                            pltpu.VMEM((group * rows, channels), F32),
                            pltpu.VMEM((group * rows, 2 * heads), BF16),
                            pltpu.VMEM((group * rows, count), BF16),
                        ],
                        5,
                        specs=[None] * (1 + group) + [any_spec],
                    )(params, *got[i], before)
                )
                before = known[-1][1]
            return known, before

        if i:
            known, before = of_own(before)
        made = call(
            functools.partial(row_state_kernel, count=len(piece), **sizes, **shared),
            state_shapes(places, col_count // group),
            0 if i else 0,
            specs=[None] * (1 + group) + [any_spec],
        )(params, *got[i], before)
        before = made[0]
        if i == 0:
            col_made = call(
                functools.partial(col_state_kernel, **sizes),
                state_shapes([cols * state], row_count),
                0,
                specs=[None] * 4 + [any_spec],
            )(params, x, raw, maps, before)
            col_entering = entering_states(col_made[0], col_made[1:], "row", row_count, 1, width)
            known, before = of_own(col_made[0])
        for j, rows in enumerate(piece):
            first = sum(places[:j])
            factor = [f[first : first + places[j]] for f in made[len(piece) :]]
            entering = entering_states(made[j], factor, "col", col_count, group, width)
            parts_of.append((sum(map(sum, pieces[:i])) + offsets[j], rows, known[j], entering))

    w, silu = call(
        functools.partial(col_out_kernel, **sizes),
        [pltpu.VMEM((tokens, channels), F32)] * 2,
        0,
    )(params, col_entering, x, raw, maps, gate, jnp.repeat(skip, width).reshape(1, channels))

    back = []
    before = w
    for _, rows, known, entering in parts_of:
        y_row = call(
            functools.partial(row_out_kernel, heads=heads, width=width),
            [pltpu.VMEM((rows, channels), BF16)] * group,
            20 if back else 0,
            specs=[None] * 4 + [any_spec],
        )(entering, *known, before)
        back.append(exchange(y_row))
        before = y_row[0]

    mixed = None
    for (first, rows, _, _), blocks in zip(parts_of, back):
        more = [] if mixed is None else [mixed]
        mixed = call(
            functools.partial(final_kernel, offset=first, share=share, **shared),
            shape((tokens, channels), BF16),
            0,
            specs=[None] * (3 + group) + [any_spec] * len(more),
            out_specs=any_spec,
            scratch_shapes=[pltpu.VMEM((group, rows, channels), BF16), pltpu.SemaphoreType.DMA((group,))],
            input_output_aliases={3 + group: 0} if more else {},
        )(w, silu, norm_gain.reshape(1, channels), *blocks, *more)
    return mixed.reshape(x_in.shape)


def solution(mesh):
    tile = P("img", "row", "col", None)
    return jax.shard_map(
        functools.partial(body, row_count=mesh.shape["row"], col_count=mesh.shape["col"]),
        mesh=mesh,
        in_specs=(tile, tile, tile, tile, P("img"), P(), P(), P(), P()),
        out_specs=tile,
        check_vma=False,
    )
```

```python
import functools

import jax
import jax.numpy as jnp
from jax import lax
from jax.experimental import pallas as pl
from jax.experimental.pallas import tpu as pltpu
from jax.sharding import PartitionSpec as P

LANES = 128
GROUP = 4
PIECES = ((4,), (4,))
STRIP = 512
VMEM_LIMIT = 16 * 1024 * 1024
F32 = jnp.float32
BF16 = jnp.bfloat16


def dot(a, b):
    return jnp.dot(a, b, preferred_element_type=F32)


def iota(shape, dim):
    return lax.broadcasted_iota(jnp.int32, shape, dim)


def div(a, n):
    return lax.shift_right_logical(a, n.bit_length() - 1) if n & (n - 1) == 0 else a // n


def mod(a, n):
    return jnp.bitwise_and(a, n - 1) if n & (n - 1) == 0 else a % n


def parts(values, count):
    terms = []
    for _ in range(count):
        term = values.astype(BF16)
        terms.append(term)
        values = values - term.astype(F32)
    return jnp.concatenate(terms, axis=1)


def picks(heads, width, first, channels):
    row = iota((2 * heads, 1), 0)
    head = jnp.where(row >= heads, row - heads, row)
    return (head == div(first + iota((1, channels), 1), width)).astype(BF16)


def summed(mask, values):
    heads = values.shape[1]
    sums = dot(mask, parts(values, 3))
    return sums[:, :heads] + sums[:, heads : 2 * heads] + sums[:, 2 * heads :]


def step_sizes(raw, bias):
    shifted = raw.astype(F32) + bias
    return jnp.maximum(shifted, 0.0) + jnp.log1p(jnp.exp(-jnp.abs(shifted)))


def widen(maps, line, lines):
    state = maps.shape[1]
    places = lines * state
    copy = (mod(iota((1, places), 1), state) == iota((state, 1), 0)).astype(BF16)
    own = div(iota((1, places), 1), state) == line
    return jnp.where(own, dot(maps, copy), 0.0).astype(BF16)


class Scan:
    def __init__(self, order, lines, raw, bias, rates, b_map, c_map):
        tokens, self.heads = raw.shape
        self.lines, self.b_map, self.c_map = lines, b_map, c_map
        self.line, place = order(iota((tokens, 1), 0))
        self.line_in, place_in = order(iota((1, tokens), 1))
        self.lower = jnp.logical_and(self.line == self.line_in, place >= place_in)
        steps = step_sizes(raw, bias)
        self.decay = -rates * steps
        running = summed(self.lower.astype(BF16), self.decay)
        self.fade = parts(jnp.exp(running), 2)
        self.grow = parts(steps * jnp.exp(-running), 2)

    def ends(self):
        places = self.lines * self.b_map.shape[1]
        own = div(iota((places, 1), 0), self.b_map.shape[1]) == self.line_in
        return jnp.exp(summed(own.astype(BF16), self.decay))

    def into(self):
        return widen(self.b_map, self.line, self.lines).astype(F32).T.astype(BF16)

    def within(self):
        scores = lax.dot_general(
            self.c_map, self.b_map, (((1,), (1,)), ((), ())), preferred_element_type=F32
        )
        return jnp.where(self.lower, scores, 0.0).astype(BF16)

    def entry(self, follows):
        return jnp.where(follows, widen(self.c_map, self.line, self.lines), 0)


def partner(member, i, group):
    return member ^ i


def column_order(cols):
    return lambda token: (mod(token, cols), div(token, cols))


def row_order(cols, lines, member, group):
    def order(token):
        source = partner(member, div(token, cols * lines), group)
        return mod(div(token, cols), lines), source * cols + mod(token, cols)

    return order


def strips(channels):
    return [(first, min(STRIP, channels - first)) for first in range(0, channels, STRIP)]


def pack_kernel(
    x_ref, raw_ref, maps_ref, table_ref, rates_ref, raw, maps, table, rates, *refs, group, axis, heads, state
):
    sent, sems = refs[:-1], refs[-1]
    channels = x_ref.shape[1]
    share = x_ref.shape[0] // group
    member = mod(lax.axis_index(axis), group)
    moved = [(raw_ref, raw), (maps_ref, maps)]
    places = []
    offset = 0
    for i, out in enumerate(sent):
        rows = out.shape[0]
        first = partner(member, i % group, group) * share + offset
        part = pl.ds(pl.multiple_of(first, 16), rows)
        places.append((out, part))
        moved.append((x_ref.at[part, :], out.at[:, pl.ds(0, channels)]))
        if i % group == group - 1:
            offset += rows
    moved += [(table_ref, table), (rates_ref, rates)]
    copies = [pltpu.make_async_copy(a, b, sems.at[i]) for i, (a, b) in enumerate(moved)]
    for copy in copies:
        copy.start()
    for copy in copies[:2]:
        copy.wait()
    used = heads + 2 * state
    for out, part in places:
        out[:, channels : channels + heads] = raw[part, :heads]
        out[:, channels + heads : channels + used] = maps[part, : 2 * state]
        out[:, channels + used :] = jnp.zeros((out.shape[0], LANES - used), BF16)
    for copy in copies[2:]:
        copy.wait()


def params_kernel(index_ref, table_ref, rates_ref, params_ref):
    heads = rates_ref.shape[1]
    row = jnp.where(iota(table_ref.shape, 1) == index_ref[0], table_ref[...], 0.0)
    ones = jnp.ones((8, table_ref.shape[1]), BF16)
    bias = jnp.zeros((8, row.shape[0]), F32)
    for _ in range(3):
        term = row.astype(BF16)
        row = row - term.astype(F32)
        bias += lax.dot_general(ones, term, (((1,), (1,)), ((), ())), preferred_element_type=F32)
    params_ref[0:1, :] = bias[0:1, :]
    params_ref[1:2, :heads] = rates_ref[0:1, :]
    params_ref[1:2, heads:] = rates_ref[1:2, :]
    params_ref[2:, :] = jnp.zeros((6, 2 * heads), F32)


def row_scan(params_ref, blocks, member, cols, heads, state):
    channels = blocks[0].shape[1] - LANES
    tokens = blocks[0].shape[0] * len(blocks)
    lines = tokens // (cols * len(blocks))
    aux = jnp.concatenate([block[:, channels:] for block in blocks], axis=0)
    return Scan(
        row_order(cols, lines, member, len(blocks)),
        lines,
        aux[:, :heads],
        params_ref[0:1, :heads],
        params_ref[1:2, :heads],
        aux[:, heads : heads + state],
        aux[:, heads + state : heads + 2 * state],
    )


def col_scan(params_ref, raw_ref, maps_ref, cols, heads, state):
    return Scan(
        column_order(cols),
        cols,
        raw_ref[:, heads:],
        params_ref[0:1, heads:],
        params_ref[1:2, heads:],
        maps_ref[:, 2 * state : 3 * state],
        maps_ref[:, 3 * state :],
    )


def write_state(scan, tokens_of, width, channels, s_refs, factor_ref):
    ends = scan.ends()
    if factor_ref:
        factor_ref[0][...] = ends
    ends = parts(ends, 2)
    into = scan.into()
    for first, count in strips(channels):
        pick = picks(scan.heads, width, first, count)
        values = (tokens_of(first, count) * dot(scan.grow, pick)).astype(BF16)
        made = (dot(into, values) * dot(ends, pick)).astype(BF16)
        row = 0
        for s_ref in s_refs:
            s_ref[:, first : first + count] = made[row : row + s_ref.shape[0]]
            row += s_ref.shape[0]


def row_state_kernel(params_ref, *refs, group, count, axis, cols, heads, state, width):
    blocks, s_refs, factor_ref = refs[:group], refs[group + 1 : group + 1 + count], refs[group + 1 + count :]
    member = mod(lax.axis_index(axis), group)
    scan = row_scan(params_ref, [block[...] for block in blocks], member, cols, heads, state)
    tokens_of = lambda first, count: jnp.concatenate(
        [block[:, first : first + count] for block in blocks], axis=0
    ).astype(F32)
    write_state(scan, tokens_of, width, s_refs[0].shape[1], s_refs, factor_ref)


def col_state_kernel(params_ref, x_ref, raw_ref, maps_ref, _, s_ref, *factor_ref, cols, heads, state, width):
    scan = col_scan(params_ref, raw_ref, maps_ref, cols, heads, state)
    tokens_of = lambda first, count: x_ref[:, first : first + count].astype(F32)
    write_state(scan, tokens_of, width, s_ref.shape[1], [s_ref], factor_ref)


def row_local_kernel(params_ref, *refs, group, offset, axis, cols, heads, state, width):
    blocks, (y_ref, fade_ref, entry_ref) = refs[:group], refs[group + 1 :]
    rows = y_ref.shape[0] // group
    mine = slice(offset, offset + rows)
    member = mod(lax.axis_index(axis), group)
    scan = row_scan(params_ref, [block[mine, :] for block in blocks], member, cols, heads, state)
    mix = scan.within()
    fade_ref[...] = scan.fade
    entry_ref[...] = scan.entry(lax.axis_index(axis) >= group)
    for first, count in strips(y_ref.shape[1]):
        pick = picks(heads, width, first, count)
        part = slice(first, first + count)
        x = jnp.concatenate([block[mine, part] for block in blocks], axis=0).astype(F32)
        values = (x * dot(scan.grow, pick)).astype(BF16)
        y_ref[:, part] = dot(mix, values) * dot(scan.fade, pick)


def row_out_kernel(s_ref, y_ref, fade_ref, entry_ref, _, *outs, heads, width):
    rows = outs[0].shape[0]
    for first, count in strips(s_ref.shape[1]):
        pick = picks(heads, width, first, count)
        part = slice(first, first + count)
        y = y_ref[:, part] + dot(entry_ref[...], s_ref[:, part]) * dot(fade_ref[...], pick)
        for i, out in enumerate(outs):
            out[:, part] = y[i * rows : (i + 1) * rows].astype(BF16)


def col_out_kernel(params_ref, s_ref, x_ref, raw_ref, maps_ref, gate_ref, skip_ref, w_ref, g_ref, *, cols, heads, state, width):
    scan = col_scan(params_ref, raw_ref, maps_ref, cols, heads, state)
    mix = jnp.concatenate([scan.within(), scan.entry(lax.axis_index("row") > 0)], axis=1)
    for first, count in strips(s_ref.shape[1]):
        pick = picks(heads, width, first, count)
        part = slice(first, first + count)
        x = x_ref[:, part].astype(F32)
        values = (x * dot(scan.grow, pick)).astype(BF16)
        y = dot(mix, jnp.concatenate([values, s_ref[:, part]], axis=0)) * dot(scan.fade, pick)
        w_ref[:, part] = y + skip_ref[:, part] * x
        gate = gate_ref[:, part].astype(F32)
        g_ref[:, part] = gate / (1.0 + jnp.exp(-gate))


def final_kernel(w_ref, g_ref, gain_ref, *refs, group, axis, offset, share):
    blocks, (out_ref, made, sems) = refs[:group], refs[-3:]
    rows, channels = blocks[0].shape
    member = mod(lax.axis_index(axis), group)
    copies = []
    for s in range(group):
        part = pl.ds(pl.multiple_of(partner(member, s, group) * share + offset, 16), rows)
        v = (blocks[s][...].astype(F32) + w_ref[part, :]) * g_ref[part, :]
        power = jnp.sum(v * v, axis=1, keepdims=True) / channels
        made[s] = (v * lax.rsqrt(power + 1e-5) * gain_ref[...]).astype(BF16)
        copies.append(pltpu.make_async_copy(made.at[s], out_ref.at[part, :], sems.at[s]))
        copies[-1].start()
    for copy in copies:
        copy.wait()


def cost(micros):
    return pl.CostEstimate(flops=1024 + int(micros * 10**9), bytes_accessed=1024, transcendentals=0)


def call(kernel, out_shape, micros, specs=None, **more):
    if specs is not None:
        more["in_specs"] = [spec or pl.BlockSpec() for spec in specs]
    return pl.pallas_call(
        kernel,
        out_shape=out_shape,
        compiler_params=pltpu.CompilerParams(vmem_limit_bytes=VMEM_LIMIT),
        cost_estimate=cost(micros),
        **more,
    )


def entering_states(ends, factor, axis, size, stride, width):
    if size == stride:
        return ends
    onward = [(i, (i + stride) % size) for i in range(size)]
    entering = lax.ppermute(ends, axis, onward)
    for _ in range(size // stride - 2):
        follows = (lax.axis_index(axis) >= stride).astype(F32)
        decayed = follows * jnp.repeat(factor[0], width, axis=1) * entering.astype(F32)
        entering = lax.ppermute((ends.astype(F32) + decayed).astype(BF16), axis, onward)
    return entering


def body(x_in, gate_in, proj_bc, dt_raw, step_index, step_table, rates, skip, norm_gain, *, row_count, col_count):
    _, tile_rows, cols, channels = x_in.shape
    heads = skip.shape[0]
    width = channels // heads
    state = proj_bc.shape[-1] // 4
    tokens = tile_rows * cols
    group = GROUP
    while col_count % group:
        group //= 2
    share = tokens // group
    pieces = [[eighths * share // 8 for eighths in piece] for piece in PIECES]

    x = x_in.reshape(tokens, channels)
    gate = gate_in.reshape(tokens, channels)
    maps = proj_bc.reshape(tokens, 4 * state)
    raw = dt_raw.reshape(tokens, 2 * heads)
    sizes = dict(cols=cols, heads=heads, state=state, width=width)
    shared = dict(group=group, axis="col")
    shape = jax.ShapeDtypeStruct
    any_spec = pl.BlockSpec(memory_space=pl.ANY)

    given = [x, raw, maps, step_table.T, rates]
    raw, maps, table, rates, *packed = pl.pallas_call(
        functools.partial(pack_kernel, heads=heads, state=state, **shared),
        in_specs=[pl.BlockSpec(memory_space=pltpu.HBM)] * len(given),
        out_shape=[pltpu.VMEM(a.shape, a.dtype) for a in given[1:]]
        + [pltpu.VMEM((sum(piece), channels + LANES), BF16) for piece in pieces for _ in range(group)],
        scratch_shapes=[pltpu.SemaphoreType.DMA((len(given) - 1 + group * len(pieces),))],
        compiler_params=pltpu.CompilerParams(vmem_limit_bytes=VMEM_LIMIT),
        cost_estimate=cost(1),
    )(*[pltpu.with_memory_space_constraint(a, pltpu.HBM) for a in given])
    index, rates = lax.optimization_barrier((step_index, rates))
    params = pl.pallas_call(
        params_kernel,
        grid_spec=pltpu.PrefetchScalarGridSpec(
            num_scalar_prefetch=1,
            grid=(1,),
            in_specs=[
                pl.BlockSpec(table.shape, lambda i, index: (0, 0)),
                pl.BlockSpec(rates.shape, lambda i, index: (0, 0)),
            ],
            out_specs=pl.BlockSpec((8, 2 * heads), lambda i, index: (0, 0)),
        ),
        out_shape=shape((8, 2 * heads), F32),
        compiler_params=pltpu.CompilerParams(vmem_limit_bytes=VMEM_LIMIT),
        cost_estimate=cost(0),
    )(index, table, rates)

    def exchange(blocks):
        return [blocks[0]] + [
            lax.ppermute(blocks[i], "col", [(at, partner(at, i, group)) for at in range(col_count)])
            for i in range(1, group)
        ]

    def state_shapes(places, count):
        states = [pltpu.VMEM((rows, channels), BF16) for rows in places]
        return states + [shape((sum(places), heads), F32)] * (count > 2)

    got = [exchange(packed[i * group : (i + 1) * group]) for i in range(len(pieces))]
    before = params
    parts_of = []
    for i, piece in enumerate(pieces):
        places = [rows // cols * state for rows in piece]
        offsets = [sum(piece[:j]) for j in range(len(piece))]

        def of_own(before, i=i, piece=piece, places=places, offsets=offsets):
            known = []
            for offset, rows, count in zip(offsets, piece, places):
                known.append(
                    call(
                        functools.partial(row_local_kernel, offset=offset, **sizes, **shared),
                        [
                            pltpu.VMEM((group * rows, channels), F32),
                            pltpu.VMEM((group * rows, 2 * heads), BF16),
                            pltpu.VMEM((group * rows, count), BF16),
                        ],
                        2,
                        specs=[None] * (1 + group) + [any_spec],
                    )(params, *got[i], before)
                )
                before = known[-1][1]
            return known, before

        if i:
            known, before = of_own(before)
        made = call(
            functools.partial(row_state_kernel, count=len(piece), **sizes, **shared),
            state_shapes(places, col_count // group),
            0 if i else 0,
            specs=[None] * (1 + group) + [any_spec],
        )(params, *got[i], before)
        before = made[0]
        if i == 0:
            col_made = call(
                functools.partial(col_state_kernel, **sizes),
                state_shapes([cols * state], row_count),
                0,
                specs=[None] * 4 + [any_spec],
            )(params, x, raw, maps, before)
            col_entering = entering_states(col_made[0], col_made[1:], "row", row_count, 1, width)
            known, before = of_own(col_made[0])
        for j, rows in enumerate(piece):
            first = sum(places[:j])
            factor = [f[first : first + places[j]] for f in made[len(piece) :]]
            entering = entering_states(made[j], factor, "col", col_count, group, width)
            parts_of.append((sum(map(sum, pieces[:i])) + offsets[j], rows, known[j], entering))

    w, silu = call(
        functools.partial(col_out_kernel, **sizes),
        [pltpu.VMEM((tokens, channels), F32)] * 2,
        0,
    )(params, col_entering, x, raw, maps, gate, jnp.repeat(skip, width).reshape(1, channels))

    back = []
    before = w
    for _, rows, known, entering in parts_of:
        y_row = call(
            functools.partial(row_out_kernel, heads=heads, width=width),
            [pltpu.VMEM((rows, channels), BF16)] * group,
            20 if back else 0,
            specs=[None] * 4 + [any_spec],
        )(entering, *known, before)
        back.append(exchange(y_row))
        before = y_row[0]

    mixed = None
    for (first, rows, _, _), blocks in zip(parts_of, back):
        more = [] if mixed is None else [mixed]
        mixed = call(
            functools.partial(final_kernel, offset=first, share=share, **shared),
            shape((tokens, channels), BF16),
            0,
            specs=[None] * (3 + group) + [any_spec] * len(more),
            out_specs=any_spec,
            scratch_shapes=[pltpu.VMEM((group, rows, channels), BF16), pltpu.SemaphoreType.DMA((group,))],
            input_output_aliases={3 + group: 0} if more else {},
        )(w, silu, norm_gain.reshape(1, channels), *blocks, *more)
    return mixed.reshape(x_in.shape)


def solution(mesh):
    tile = P("img", "row", "col", None)
    return jax.shard_map(
        functools.partial(body, row_count=mesh.shape["row"], col_count=mesh.shape["col"]),
        mesh=mesh,
        in_specs=(tile, tile, tile, tile, P("img"), P(), P(), P(), P()),
        out_specs=tile,
        check_vma=False,
    )
```

```python
import functools

import jax
import jax.numpy as jnp
from jax import lax
from jax.experimental import pallas as pl
from jax.experimental.pallas import tpu as pltpu
from jax.sharding import PartitionSpec as P

LANES = 128
GROUP = 4
PIECES = ((4,), (4,))
STRIP = 512
VMEM_LIMIT = 16 * 1024 * 1024
F32 = jnp.float32
BF16 = jnp.bfloat16


def dot(a, b):
    return jnp.dot(a, b, preferred_element_type=F32)


def iota(shape, dim):
    return lax.broadcasted_iota(jnp.int32, shape, dim)


def div(a, n):
    return lax.shift_right_logical(a, n.bit_length() - 1) if n & (n - 1) == 0 else a // n


def mod(a, n):
    return jnp.bitwise_and(a, n - 1) if n & (n - 1) == 0 else a % n


def parts(values, count):
    terms = []
    for _ in range(count):
        term = values.astype(BF16)
        terms.append(term)
        values = values - term.astype(F32)
    return jnp.concatenate(terms, axis=1)


def picks(heads, width, first, channels):
    row = iota((2 * heads, 1), 0)
    head = jnp.where(row >= heads, row - heads, row)
    return (head == div(first + iota((1, channels), 1), width)).astype(BF16)


def summed(mask, values):
    heads = values.shape[1]
    sums = dot(mask, parts(values, 3))
    return sums[:, :heads] + sums[:, heads : 2 * heads] + sums[:, 2 * heads :]


def step_sizes(raw, bias):
    shifted = raw.astype(F32) + bias
    return jnp.maximum(shifted, 0.0) + jnp.log1p(jnp.exp(-jnp.abs(shifted)))


def widen(maps, line, lines):
    state = maps.shape[1]
    places = lines * state
    copy = (mod(iota((1, places), 1), state) == iota((state, 1), 0)).astype(BF16)
    own = div(iota((1, places), 1), state) == line
    return jnp.where(own, dot(maps, copy), 0.0).astype(BF16)


class Scan:
    def __init__(self, order, lines, raw, bias, rates, b_map, c_map):
        tokens, self.heads = raw.shape
        self.lines, self.b_map, self.c_map = lines, b_map, c_map
        self.line, place = order(iota((tokens, 1), 0))
        self.line_in, place_in = order(iota((1, tokens), 1))
        self.lower = jnp.logical_and(self.line == self.line_in, place >= place_in)
        steps = step_sizes(raw, bias)
        self.decay = -rates * steps
        running = summed(self.lower.astype(BF16), self.decay)
        self.fade = parts(jnp.exp(running), 2)
        self.grow = parts(steps * jnp.exp(-running), 2)

    def ends(self):
        places = self.lines * self.b_map.shape[1]
        own = div(iota((places, 1), 0), self.b_map.shape[1]) == self.line_in
        return jnp.exp(summed(own.astype(BF16), self.decay))

    def into(self):
        return widen(self.b_map, self.line, self.lines).astype(F32).T.astype(BF16)

    def within(self):
        scores = lax.dot_general(
            self.c_map, self.b_map, (((1,), (1,)), ((), ())), preferred_element_type=F32
        )
        return jnp.where(self.lower, scores, 0.0).astype(BF16)

    def entry(self, follows):
        return jnp.where(follows, widen(self.c_map, self.line, self.lines), 0)


def partner(member, i, group):
    return member ^ i


def column_order(cols):
    return lambda token: (mod(token, cols), div(token, cols))


def row_order(cols, lines, member, group):
    def order(token):
        source = partner(member, div(token, cols * lines), group)
        return mod(div(token, cols), lines), source * cols + mod(token, cols)

    return order


def strips(channels):
    return [(first, min(STRIP, channels - first)) for first in range(0, channels, STRIP)]


def pack_kernel(
    x_ref, raw_ref, maps_ref, table_ref, rates_ref, raw, maps, table, rates, *refs, group, axis, heads, state
):
    sent, sems = refs[:-1], refs[-1]
    channels = x_ref.shape[1]
    share = x_ref.shape[0] // group
    member = mod(lax.axis_index(axis), group)
    moved = [(raw_ref, raw), (maps_ref, maps)]
    places = []
    offset = 0
    for i, out in enumerate(sent):
        rows = out.shape[0]
        first = partner(member, i % group, group) * share + offset
        part = pl.ds(pl.multiple_of(first, 16), rows)
        places.append((out, part))
        moved.append((x_ref.at[part, :], out.at[:, pl.ds(0, channels)]))
        if i % group == group - 1:
            offset += rows
    moved += [(table_ref, table), (rates_ref, rates)]
    copies = [pltpu.make_async_copy(a, b, sems.at[i]) for i, (a, b) in enumerate(moved)]
    for copy in copies:
        copy.start()
    for copy in copies[:2]:
        copy.wait()
    used = heads + 2 * state
    for out, part in places:
        out[:, channels : channels + heads] = raw[part, :heads]
        out[:, channels + heads : channels + used] = maps[part, : 2 * state]
        out[:, channels + used :] = jnp.zeros((out.shape[0], LANES - used), BF16)
    for copy in copies[2:]:
        copy.wait()


def params_kernel(index_ref, table_ref, rates_ref, params_ref):
    heads = rates_ref.shape[1]
    row = jnp.where(iota(table_ref.shape, 1) == index_ref[0], table_ref[...], 0.0)
    ones = jnp.ones((8, table_ref.shape[1]), BF16)
    bias = jnp.zeros((8, row.shape[0]), F32)
    for _ in range(3):
        term = row.astype(BF16)
        row = row - term.astype(F32)
        bias += lax.dot_general(ones, term, (((1,), (1,)), ((), ())), preferred_element_type=F32)
    params_ref[0:1, :] = bias[0:1, :]
    params_ref[1:2, :heads] = rates_ref[0:1, :]
    params_ref[1:2, heads:] = rates_ref[1:2, :]
    params_ref[2:, :] = jnp.zeros((6, 2 * heads), F32)


def row_scan(params_ref, blocks, member, cols, heads, state):
    channels = blocks[0].shape[1] - LANES
    tokens = blocks[0].shape[0] * len(blocks)
    lines = tokens // (cols * len(blocks))
    aux = jnp.concatenate([block[:, channels:] for block in blocks], axis=0)
    return Scan(
        row_order(cols, lines, member, len(blocks)),
        lines,
        aux[:, :heads],
        params_ref[0:1, :heads],
        params_ref[1:2, :heads],
        aux[:, heads : heads + state],
        aux[:, heads + state : heads + 2 * state],
    )


def col_scan(params_ref, raw_ref, maps_ref, cols, heads, state):
    return Scan(
        column_order(cols),
        cols,
        raw_ref[:, heads:],
        params_ref[0:1, heads:],
        params_ref[1:2, heads:],
        maps_ref[:, 2 * state : 3 * state],
        maps_ref[:, 3 * state :],
    )


def write_state(scan, tokens_of, width, channels, s_refs, factor_ref):
    ends = scan.ends()
    if factor_ref:
        factor_ref[0][...] = ends
    ends = parts(ends, 2)
    into = scan.into()
    for first, count in strips(channels):
        pick = picks(scan.heads, width, first, count)
        values = (tokens_of(first, count) * dot(scan.grow, pick)).astype(BF16)
        made = (dot(into, values) * dot(ends, pick)).astype(BF16)
        row = 0
        for s_ref in s_refs:
            s_ref[:, first : first + count] = made[row : row + s_ref.shape[0]]
            row += s_ref.shape[0]


def row_state_kernel(params_ref, *refs, group, count, axis, cols, heads, state, width):
    blocks, s_refs, factor_ref = refs[:group], refs[group + 1 : group + 1 + count], refs[group + 1 + count :]
    member = mod(lax.axis_index(axis), group)
    scan = row_scan(params_ref, [block[...] for block in blocks], member, cols, heads, state)
    tokens_of = lambda first, count: jnp.concatenate(
        [block[:, first : first + count] for block in blocks], axis=0
    ).astype(F32)
    write_state(scan, tokens_of, width, s_refs[0].shape[1], s_refs, factor_ref)


def col_state_kernel(params_ref, x_ref, raw_ref, maps_ref, _, s_ref, *factor_ref, cols, heads, state, width):
    scan = col_scan(params_ref, raw_ref, maps_ref, cols, heads, state)
    tokens_of = lambda first, count: x_ref[:, first : first + count].astype(F32)
    write_state(scan, tokens_of, width, s_ref.shape[1], [s_ref], factor_ref)


def row_local_kernel(params_ref, *refs, group, offset, axis, cols, heads, state, width):
    blocks, (y_ref, fade_ref, entry_ref) = refs[:group], refs[group + 1 :]
    rows = y_ref.shape[0] // group
    mine = slice(offset, offset + rows)
    member = mod(lax.axis_index(axis), group)
    scan = row_scan(params_ref, [block[mine, :] for block in blocks], member, cols, heads, state)
    mix = scan.within()
    fade_ref[...] = scan.fade
    entry_ref[...] = scan.entry(lax.axis_index(axis) >= group)
    for first, count in strips(y_ref.shape[1]):
        pick = picks(heads, width, first, count)
        part = slice(first, first + count)
        x = jnp.concatenate([block[mine, part] for block in blocks], axis=0).astype(F32)
        values = (x * dot(scan.grow, pick)).astype(BF16)
        y_ref[:, part] = dot(mix, values) * dot(scan.fade, pick)


def row_out_kernel(s_ref, y_ref, fade_ref, entry_ref, _, *outs, heads, width):
    rows = outs[0].shape[0]
    for first, count in strips(s_ref.shape[1]):
        pick = picks(heads, width, first, count)
        part = slice(first, first + count)
        y = y_ref[:, part] + dot(entry_ref[...], s_ref[:, part]) * dot(fade_ref[...], pick)
        for i, out in enumerate(outs):
            out[:, part] = y[i * rows : (i + 1) * rows].astype(BF16)


def col_out_kernel(params_ref, s_ref, x_ref, raw_ref, maps_ref, gate_ref, skip_ref, w_ref, g_ref, *, cols, heads, state, width):
    scan = col_scan(params_ref, raw_ref, maps_ref, cols, heads, state)
    mix = jnp.concatenate([scan.within(), scan.entry(lax.axis_index("row") > 0)], axis=1)
    skips = parts(jnp.broadcast_to(skip_ref[...], (8, heads)), 2)
    for first, count in strips(s_ref.shape[1]):
        pick = picks(heads, width, first, count)
        part = slice(first, first + count)
        x = x_ref[:, part].astype(F32)
        values = (x * dot(scan.grow, pick)).astype(BF16)
        y = dot(mix, jnp.concatenate([values, s_ref[:, part]], axis=0)) * dot(scan.fade, pick)
        w_ref[:, part] = y + dot(skips, pick)[0:1, :] * x
        gate = gate_ref[:, part].astype(F32)
        g_ref[:, part] = gate / (1.0 + jnp.exp(-gate))


def final_kernel(w_ref, g_ref, gain_ref, *refs, group, axis, offset, share):
    blocks, (out_ref, made, sems) = refs[:group], refs[-3:]
    rows, channels = blocks[0].shape
    member = mod(lax.axis_index(axis), group)
    copies = []
    for s in range(group):
        part = pl.ds(pl.multiple_of(partner(member, s, group) * share + offset, 16), rows)
        v = (blocks[s][...].astype(F32) + w_ref[part, :]) * g_ref[part, :]
        power = jnp.sum(v * v, axis=1, keepdims=True) / channels
        made[s] = (v * lax.rsqrt(power + 1e-5) * gain_ref[...]).astype(BF16)
        copies.append(pltpu.make_async_copy(made.at[s], out_ref.at[part, :], sems.at[s]))
        copies[-1].start()
    for copy in copies:
        copy.wait()


def cost(micros):
    return pl.CostEstimate(flops=1024 + int(micros * 10**9), bytes_accessed=1024, transcendentals=0)


def call(kernel, out_shape, micros, specs=None, **more):
    if specs is not None:
        more["in_specs"] = [spec or pl.BlockSpec() for spec in specs]
    return pl.pallas_call(
        kernel,
        out_shape=out_shape,
        compiler_params=pltpu.CompilerParams(vmem_limit_bytes=VMEM_LIMIT),
        cost_estimate=cost(micros),
        **more,
    )


def entering_states(ends, factor, axis, size, stride, width):
    if size == stride:
        return ends
    onward = [(i, (i + stride) % size) for i in range(size)]
    entering = lax.ppermute(ends, axis, onward)
    for _ in range(size // stride - 2):
        follows = (lax.axis_index(axis) >= stride).astype(F32)
        decayed = follows * jnp.repeat(factor[0], width, axis=1) * entering.astype(F32)
        entering = lax.ppermute((ends.astype(F32) + decayed).astype(BF16), axis, onward)
    return entering


def body(x_in, gate_in, proj_bc, dt_raw, step_index, step_table, rates, skip, norm_gain, *, row_count, col_count):
    _, tile_rows, cols, channels = x_in.shape
    heads = skip.shape[0]
    width = channels // heads
    state = proj_bc.shape[-1] // 4
    tokens = tile_rows * cols
    group = GROUP
    while col_count % group:
        group //= 2
    share = tokens // group
    pieces = [[eighths * share // 8 for eighths in piece] for piece in PIECES]

    x = x_in.reshape(tokens, channels)
    gate = gate_in.reshape(tokens, channels)
    maps = proj_bc.reshape(tokens, 4 * state)
    raw = dt_raw.reshape(tokens, 2 * heads)
    sizes = dict(cols=cols, heads=heads, state=state, width=width)
    shared = dict(group=group, axis="col")
    shape = jax.ShapeDtypeStruct
    any_spec = pl.BlockSpec(memory_space=pl.ANY)

    given = [x, raw, maps, step_table.T, rates]
    raw, maps, table, rates, *packed = pl.pallas_call(
        functools.partial(pack_kernel, heads=heads, state=state, **shared),
        in_specs=[pl.BlockSpec(memory_space=pltpu.HBM)] * len(given),
        out_shape=[pltpu.VMEM(a.shape, a.dtype) for a in given[1:]]
        + [pltpu.VMEM((sum(piece), channels + LANES), BF16) for piece in pieces for _ in range(group)],
        scratch_shapes=[pltpu.SemaphoreType.DMA((len(given) - 1 + group * len(pieces),))],
        compiler_params=pltpu.CompilerParams(vmem_limit_bytes=VMEM_LIMIT),
        cost_estimate=cost(1),
    )(*[pltpu.with_memory_space_constraint(a, pltpu.HBM) for a in given])
    index, rates = lax.optimization_barrier((step_index, rates))
    params = pl.pallas_call(
        params_kernel,
        grid_spec=pltpu.PrefetchScalarGridSpec(
            num_scalar_prefetch=1,
            grid=(1,),
            in_specs=[
                pl.BlockSpec(table.shape, lambda i, index: (0, 0)),
                pl.BlockSpec(rates.shape, lambda i, index: (0, 0)),
            ],
            out_specs=pl.BlockSpec((8, 2 * heads), lambda i, index: (0, 0)),
        ),
        out_shape=shape((8, 2 * heads), F32),
        compiler_params=pltpu.CompilerParams(vmem_limit_bytes=VMEM_LIMIT),
        cost_estimate=cost(0),
    )(index, table, rates)

    def exchange(blocks):
        return [blocks[0]] + [
            lax.ppermute(blocks[i], "col", [(at, partner(at, i, group)) for at in range(col_count)])
            for i in range(1, group)
        ]

    def state_shapes(places, count):
        states = [pltpu.VMEM((rows, channels), BF16) for rows in places]
        return states + [shape((sum(places), heads), F32)] * (count > 2)

    got = [exchange(packed[i * group : (i + 1) * group]) for i in range(len(pieces))]
    before = params
    parts_of = []
    for i, piece in enumerate(pieces):
        places = [rows // cols * state for rows in piece]
        offsets = [sum(piece[:j]) for j in range(len(piece))]

        def of_own(before, i=i, piece=piece, places=places, offsets=offsets):
            known = []
            for offset, rows, count in zip(offsets, piece, places):
                known.append(
                    call(
                        functools.partial(row_local_kernel, offset=offset, **sizes, **shared),
                        [
                            pltpu.VMEM((group * rows, channels), F32),
                            pltpu.VMEM((group * rows, 2 * heads), BF16),
                            pltpu.VMEM((group * rows, count), BF16),
                        ],
                        2,
                        specs=[None] * (1 + group) + [any_spec],
                    )(params, *got[i], before)
                )
                before = known[-1][1]
            return known, before

        if i:
            known, before = of_own(before)
        made = call(
            functools.partial(row_state_kernel, count=len(piece), **sizes, **shared),
            state_shapes(places, col_count // group),
            0 if i else 0,
            specs=[None] * (1 + group) + [any_spec],
        )(params, *got[i], before)
        before = made[0]
        if i == 0:
            col_made = call(
                functools.partial(col_state_kernel, **sizes),
                state_shapes([cols * state], row_count),
                0,
                specs=[None] * 4 + [any_spec],
            )(params, x, raw, maps, before)
            col_entering = entering_states(col_made[0], col_made[1:], "row", row_count, 1, width)
            known, before = of_own(col_made[0])
        for j, rows in enumerate(piece):
            first = sum(places[:j])
            factor = [f[first : first + places[j]] for f in made[len(piece) :]]
            entering = entering_states(made[j], factor, "col", col_count, group, width)
            parts_of.append((sum(map(sum, pieces[:i])) + offsets[j], rows, known[j], entering))

    w, silu = call(
        functools.partial(col_out_kernel, **sizes),
        [pltpu.VMEM((tokens, channels), F32)] * 2,
        0,
    )(params, col_entering, x, raw, maps, gate, skip.reshape(1, heads))

    back = []
    before = w
    for _, rows, known, entering in parts_of:
        y_row = call(
            functools.partial(row_out_kernel, heads=heads, width=width),
            [pltpu.VMEM((rows, channels), BF16)] * group,
            20 if back else 0,
            specs=[None] * 4 + [any_spec],
        )(entering, *known, before)
        back.append(exchange(y_row))
        before = y_row[0]

    mixed = None
    for (first, rows, _, _), blocks in zip(parts_of, back):
        more = [] if mixed is None else [mixed]
        mixed = call(
            functools.partial(final_kernel, offset=first, share=share, **shared),
            shape((tokens, channels), BF16),
            0,
            specs=[None] * (3 + group) + [any_spec] * len(more),
            out_specs=any_spec,
            scratch_shapes=[pltpu.VMEM((group, rows, channels), BF16), pltpu.SemaphoreType.DMA((group,))],
            input_output_aliases={3 + group: 0} if more else {},
        )(w, silu, norm_gain.reshape(1, channels), *blocks, *more)
    return mixed.reshape(x_in.shape)


def solution(mesh):
    tile = P("img", "row", "col", None)
    return jax.shard_map(
        functools.partial(body, row_count=mesh.shape["row"], col_count=mesh.shape["col"]),
        mesh=mesh,
        in_specs=(tile, tile, tile, tile, P("img"), P(), P(), P(), P()),
        out_specs=tile,
        check_vma=False,
    )
```

```python
import functools

import jax
import jax.numpy as jnp
from jax import lax
from jax.experimental import pallas as pl
from jax.experimental.pallas import tpu as pltpu
from jax.sharding import PartitionSpec as P

LANES = 128
GROUP = 4
PIECES = ((4,), (4,))
STRIP = 512
VMEM_LIMIT = 16 * 1024 * 1024
F32 = jnp.float32
BF16 = jnp.bfloat16


def dot(a, b):
    return jnp.dot(a, b, preferred_element_type=F32)


def iota(shape, dim):
    return lax.broadcasted_iota(jnp.int32, shape, dim)


def div(a, n):
    return lax.shift_right_logical(a, n.bit_length() - 1) if n & (n - 1) == 0 else a // n


def mod(a, n):
    return jnp.bitwise_and(a, n - 1) if n & (n - 1) == 0 else a % n


def parts(values, count):
    terms = []
    for _ in range(count):
        term = values.astype(BF16)
        terms.append(term)
        values = values - term.astype(F32)
    return jnp.concatenate(terms, axis=1)


def picks(heads, width, first, channels):
    row = iota((2 * heads, 1), 0)
    head = jnp.where(row >= heads, row - heads, row)
    return (head == div(first + iota((1, channels), 1), width)).astype(BF16)


def summed(mask, values):
    heads = values.shape[1]
    sums = dot(mask, parts(values, 3))
    return sums[:, :heads] + sums[:, heads : 2 * heads] + sums[:, 2 * heads :]


def step_sizes(raw, bias):
    shifted = raw.astype(F32) + bias
    return jnp.maximum(shifted, 0.0) + jnp.log1p(jnp.exp(-jnp.abs(shifted)))


def widen(maps, line, lines):
    state = maps.shape[1]
    places = lines * state
    copy = (mod(iota((1, places), 1), state) == iota((state, 1), 0)).astype(BF16)
    own = div(iota((1, places), 1), state) == line
    return jnp.where(own, dot(maps, copy), 0.0).astype(BF16)


class Scan:
    def __init__(self, order, lines, raw, bias, rates, b_map, c_map):
        tokens, self.heads = raw.shape
        self.lines, self.b_map, self.c_map = lines, b_map, c_map
        self.line, place = order(iota((tokens, 1), 0))
        self.line_in, place_in = order(iota((1, tokens), 1))
        self.lower = jnp.logical_and(self.line == self.line_in, place >= place_in)
        steps = step_sizes(raw, bias)
        self.decay = -rates * steps
        running = summed(self.lower.astype(BF16), self.decay)
        self.fade = parts(jnp.exp(running), 2)
        self.grow = parts(steps * jnp.exp(-running), 2)

    def ends(self):
        places = self.lines * self.b_map.shape[1]
        own = div(iota((places, 1), 0), self.b_map.shape[1]) == self.line_in
        return jnp.exp(summed(own.astype(BF16), self.decay))

    def into(self):
        return widen(self.b_map, self.line, self.lines).astype(F32).T.astype(BF16)

    def within(self):
        scores = lax.dot_general(
            self.c_map, self.b_map, (((1,), (1,)), ((), ())), preferred_element_type=F32
        )
        return jnp.where(self.lower, scores, 0.0).astype(BF16)

    def entry(self, follows):
        return jnp.where(follows, widen(self.c_map, self.line, self.lines), 0)


def partner(member, i, group):
    return member ^ i


def column_order(cols):
    return lambda token: (mod(token, cols), div(token, cols))


def row_order(cols, lines, member, group):
    def order(token):
        source = partner(member, div(token, cols * lines), group)
        return mod(div(token, cols), lines), source * cols + mod(token, cols)

    return order


def strips(channels):
    return [(first, min(STRIP, channels - first)) for first in range(0, channels, STRIP)]


def pack_kernel(
    x_ref, raw_ref, maps_ref, table_ref, rates_ref, raw, maps, table, rates, *refs, group, axis, heads, state
):
    sent, sems = refs[:-1], refs[-1]
    channels = x_ref.shape[1]
    share = x_ref.shape[0] // group
    member = mod(lax.axis_index(axis), group)
    moved = [(raw_ref, raw), (maps_ref, maps)]
    places = []
    offset = 0
    for i, out in enumerate(sent):
        rows = out.shape[0]
        first = partner(member, i % group, group) * share + offset
        part = pl.ds(pl.multiple_of(first, 16), rows)
        places.append((out, part))
        moved.append((x_ref.at[part, :], out.at[:, pl.ds(0, channels)]))
        if i % group == group - 1:
            offset += rows
    moved += [(table_ref, table), (rates_ref, rates)]
    copies = [pltpu.make_async_copy(a, b, sems.at[i]) for i, (a, b) in enumerate(moved)]
    for copy in copies:
        copy.start()
    for copy in copies[:2]:
        copy.wait()
    used = heads + 2 * state
    for out, part in places:
        out[:, channels : channels + heads] = raw[part, :heads]
        out[:, channels + heads : channels + used] = maps[part, : 2 * state]
        out[:, channels + used :] = jnp.zeros((out.shape[0], LANES - used), BF16)
    for copy in copies[2:]:
        copy.wait()


def params_kernel(index_ref, table_ref, rates_ref, params_ref):
    heads = rates_ref.shape[1]
    row = jnp.where(iota(table_ref.shape, 1) == index_ref[0], table_ref[...], 0.0)
    ones = jnp.ones((8, table_ref.shape[1]), BF16)
    bias = jnp.zeros((8, row.shape[0]), F32)
    for _ in range(3):
        term = row.astype(BF16)
        row = row - term.astype(F32)
        bias += lax.dot_general(ones, term, (((1,), (1,)), ((), ())), preferred_element_type=F32)
    params_ref[0:1, :] = bias[0:1, :]
    params_ref[1:2, :heads] = rates_ref[0:1, :]
    params_ref[1:2, heads:] = rates_ref[1:2, :]
    params_ref[2:, :] = jnp.zeros((6, 2 * heads), F32)


def row_scan(params_ref, blocks, member, cols, heads, state):
    channels = blocks[0].shape[1] - LANES
    tokens = blocks[0].shape[0] * len(blocks)
    lines = tokens // (cols * len(blocks))
    aux = jnp.concatenate([block[:, channels:] for block in blocks], axis=0)
    return Scan(
        row_order(cols, lines, member, len(blocks)),
        lines,
        aux[:, :heads],
        params_ref[0:1, :heads],
        params_ref[1:2, :heads],
        aux[:, heads : heads + state],
        aux[:, heads + state : heads + 2 * state],
    )


def col_scan(params_ref, raw_ref, maps_ref, cols, heads, state):
    return Scan(
        column_order(cols),
        cols,
        raw_ref[:, heads:],
        params_ref[0:1, heads:],
        params_ref[1:2, heads:],
        maps_ref[:, 2 * state : 3 * state],
        maps_ref[:, 3 * state :],
    )


def write_state(scan, tokens_of, width, channels, s_refs, factor_ref):
    ends = scan.ends()
    if factor_ref:
        factor_ref[0][...] = ends
    ends = parts(ends, 2)
    into = scan.into()
    for first, count in strips(channels):
        pick = picks(scan.heads, width, first, count)
        values = (tokens_of(first, count) * dot(scan.grow, pick)).astype(BF16)
        made = (dot(into, values) * dot(ends, pick)).astype(BF16)
        row = 0
        for s_ref in s_refs:
            s_ref[:, first : first + count] = made[row : row + s_ref.shape[0]]
            row += s_ref.shape[0]


def row_state_kernel(params_ref, *refs, group, count, axis, cols, heads, state, width):
    blocks, s_refs, factor_ref = refs[:group], refs[group + 1 : group + 1 + count], refs[group + 1 + count :]
    member = mod(lax.axis_index(axis), group)
    scan = row_scan(params_ref, [block[...] for block in blocks], member, cols, heads, state)
    tokens_of = lambda first, count: jnp.concatenate(
        [block[:, first : first + count] for block in blocks], axis=0
    ).astype(F32)
    write_state(scan, tokens_of, width, s_refs[0].shape[1], s_refs, factor_ref)


def col_state_kernel(params_ref, x_ref, raw_ref, maps_ref, _, s_ref, *factor_ref, cols, heads, state, width):
    scan = col_scan(params_ref, raw_ref, maps_ref, cols, heads, state)
    tokens_of = lambda first, count: x_ref[:, first : first + count].astype(F32)
    write_state(scan, tokens_of, width, s_ref.shape[1], [s_ref], factor_ref)


def row_local_kernel(params_ref, *refs, group, offset, axis, cols, heads, state, width):
    blocks, (y_ref, fade_ref, entry_ref) = refs[:group], refs[group + 1 :]
    rows = y_ref.shape[0] // group
    mine = slice(offset, offset + rows)
    member = mod(lax.axis_index(axis), group)
    scan = row_scan(params_ref, [block[mine, :] for block in blocks], member, cols, heads, state)
    mix = scan.within()
    fade_ref[...] = scan.fade
    entry_ref[...] = scan.entry(lax.axis_index(axis) >= group)
    for first, count in strips(y_ref.shape[1]):
        pick = picks(heads, width, first, count)
        part = slice(first, first + count)
        x = jnp.concatenate([block[mine, part] for block in blocks], axis=0).astype(F32)
        values = (x * dot(scan.grow, pick)).astype(BF16)
        y_ref[:, part] = dot(mix, values) * dot(scan.fade, pick)


def row_out_kernel(s_ref, y_ref, fade_ref, entry_ref, _, *outs, heads, width):
    rows = outs[0].shape[0]
    for first, count in strips(s_ref.shape[1]):
        pick = picks(heads, width, first, count)
        part = slice(first, first + count)
        y = y_ref[:, part] + dot(entry_ref[...], s_ref[:, part]) * dot(fade_ref[...], pick)
        for i, out in enumerate(outs):
            out[:, part] = y[i * rows : (i + 1) * rows].astype(BF16)


def col_local_kernel(
    params_ref, x_ref, raw_ref, maps_ref, gate_ref, skip_ref, _, y_ref, g_ref, fade_ref, entry_ref,
    *, cols, heads, state, width
):
    scan = col_scan(params_ref, raw_ref, maps_ref, cols, heads, state)
    mix = scan.within()
    fade_ref[...] = scan.fade
    entry_ref[...] = scan.entry(lax.axis_index("row") > 0)
    skips = parts(jnp.broadcast_to(skip_ref[...], (8, heads)), 2)
    for first, count in strips(x_ref.shape[1]):
        pick = picks(heads, width, first, count)
        part = slice(first, first + count)
        x = x_ref[:, part].astype(F32)
        values = (x * dot(scan.grow, pick)).astype(BF16)
        y_ref[:, part] = dot(mix, values) * dot(scan.fade, pick) + dot(skips, pick)[0:1, :] * x
        gate = gate_ref[:, part].astype(F32)
        g_ref[:, part] = gate / (1.0 + jnp.exp(-gate))


def col_out_kernel(s_ref, y_ref, fade_ref, entry_ref, w_ref, *, heads, width):
    for first, count in strips(s_ref.shape[1]):
        pick = picks(heads, width, first, count)
        part = slice(first, first + count)
        w_ref[:, part] = y_ref[:, part] + dot(entry_ref[...], s_ref[:, part]) * dot(fade_ref[...], pick)


def final_kernel(w_ref, g_ref, gain_ref, *refs, group, axis, offset, share):
    blocks, (out_ref, made, sems) = refs[:group], refs[-3:]
    rows, channels = blocks[0].shape
    member = mod(lax.axis_index(axis), group)
    copies = []
    for s in range(group):
        part = pl.ds(pl.multiple_of(partner(member, s, group) * share + offset, 16), rows)
        v = (blocks[s][...].astype(F32) + w_ref[part, :]) * g_ref[part, :]
        power = jnp.sum(v * v, axis=1, keepdims=True) / channels
        made[s] = (v * lax.rsqrt(power + 1e-5) * gain_ref[...]).astype(BF16)
        copies.append(pltpu.make_async_copy(made.at[s], out_ref.at[part, :], sems.at[s]))
        copies[-1].start()
    for copy in copies:
        copy.wait()


def cost(micros):
    return pl.CostEstimate(flops=1024 + int(micros * 10**9), bytes_accessed=1024, transcendentals=0)


def call(kernel, out_shape, micros, specs=None, **more):
    if specs is not None:
        more["in_specs"] = [spec or pl.BlockSpec() for spec in specs]
    return pl.pallas_call(
        kernel,
        out_shape=out_shape,
        compiler_params=pltpu.CompilerParams(vmem_limit_bytes=VMEM_LIMIT),
        cost_estimate=cost(micros),
        **more,
    )


def entering_states(ends, factor, axis, size, stride, width):
    if size == stride:
        return ends
    onward = [(i, (i + stride) % size) for i in range(size)]
    entering = lax.ppermute(ends, axis, onward)
    for _ in range(size // stride - 2):
        follows = (lax.axis_index(axis) >= stride).astype(F32)
        decayed = follows * jnp.repeat(factor[0], width, axis=1) * entering.astype(F32)
        entering = lax.ppermute((ends.astype(F32) + decayed).astype(BF16), axis, onward)
    return entering


def body(x_in, gate_in, proj_bc, dt_raw, step_index, step_table, rates, skip, norm_gain, *, row_count, col_count):
    _, tile_rows, cols, channels = x_in.shape
    heads = skip.shape[0]
    width = channels // heads
    state = proj_bc.shape[-1] // 4
    tokens = tile_rows * cols
    group = GROUP
    while col_count % group:
        group //= 2
    share = tokens // group
    pieces = [[eighths * share // 8 for eighths in piece] for piece in PIECES]

    x = x_in.reshape(tokens, channels)
    gate = gate_in.reshape(tokens, channels)
    maps = proj_bc.reshape(tokens, 4 * state)
    raw = dt_raw.reshape(tokens, 2 * heads)
    sizes = dict(cols=cols, heads=heads, state=state, width=width)
    shared = dict(group=group, axis="col")
    shape = jax.ShapeDtypeStruct
    any_spec = pl.BlockSpec(memory_space=pl.ANY)

    given = [x, raw, maps, step_table.T, rates]
    raw, maps, table, rates, *packed = pl.pallas_call(
        functools.partial(pack_kernel, heads=heads, state=state, **shared),
        in_specs=[pl.BlockSpec(memory_space=pltpu.HBM)] * len(given),
        out_shape=[pltpu.VMEM(a.shape, a.dtype) for a in given[1:]]
        + [pltpu.VMEM((sum(piece), channels + LANES), BF16) for piece in pieces for _ in range(group)],
        scratch_shapes=[pltpu.SemaphoreType.DMA((len(given) - 1 + group * len(pieces),))],
        compiler_params=pltpu.CompilerParams(vmem_limit_bytes=VMEM_LIMIT),
        cost_estimate=cost(1),
    )(*[pltpu.with_memory_space_constraint(a, pltpu.HBM) for a in given])
    index, rates = lax.optimization_barrier((step_index, rates))
    params = pl.pallas_call(
        params_kernel,
        grid_spec=pltpu.PrefetchScalarGridSpec(
            num_scalar_prefetch=1,
            grid=(1,),
            in_specs=[
                pl.BlockSpec(table.shape, lambda i, index: (0, 0)),
                pl.BlockSpec(rates.shape, lambda i, index: (0, 0)),
            ],
            out_specs=pl.BlockSpec((8, 2 * heads), lambda i, index: (0, 0)),
        ),
        out_shape=shape((8, 2 * heads), F32),
        compiler_params=pltpu.CompilerParams(vmem_limit_bytes=VMEM_LIMIT),
        cost_estimate=cost(0),
    )(index, table, rates)

    def exchange(blocks):
        return [blocks[0]] + [
            lax.ppermute(blocks[i], "col", [(at, partner(at, i, group)) for at in range(col_count)])
            for i in range(1, group)
        ]

    def state_shapes(places, count):
        states = [pltpu.VMEM((rows, channels), BF16) for rows in places]
        return states + [shape((sum(places), heads), F32)] * (count > 2)

    got = [exchange(packed[i * group : (i + 1) * group]) for i in range(len(pieces))]
    before = params
    parts_of = []
    for i, piece in enumerate(pieces):
        places = [rows // cols * state for rows in piece]
        offsets = [sum(piece[:j]) for j in range(len(piece))]

        def of_own(before, i=i, piece=piece, places=places, offsets=offsets):
            known = []
            for offset, rows, count in zip(offsets, piece, places):
                known.append(
                    call(
                        functools.partial(row_local_kernel, offset=offset, **sizes, **shared),
                        [
                            pltpu.VMEM((group * rows, channels), F32),
                            pltpu.VMEM((group * rows, 2 * heads), BF16),
                            pltpu.VMEM((group * rows, count), BF16),
                        ],
                        2,
                        specs=[None] * (1 + group) + [any_spec],
                    )(params, *got[i], before)
                )
                before = known[-1][1]
            return known, before

        if i:
            known, before = of_own(before)
        made = call(
            functools.partial(row_state_kernel, count=len(piece), **sizes, **shared),
            state_shapes(places, col_count // group),
            0 if i else 0,
            specs=[None] * (1 + group) + [any_spec],
        )(params, *got[i], before)
        before = made[0]
        if i == 0:
            col_made = call(
                functools.partial(col_state_kernel, **sizes),
                state_shapes([cols * state], row_count),
                0,
                specs=[None] * 4 + [any_spec],
            )(params, x, raw, maps, before)
            col_entering = entering_states(col_made[0], col_made[1:], "row", row_count, 1, width)
            known, before = of_own(col_made[0])
        for j, rows in enumerate(piece):
            first = sum(places[:j])
            factor = [f[first : first + places[j]] for f in made[len(piece) :]]
            entering = entering_states(made[j], factor, "col", col_count, group, width)
            parts_of.append((sum(map(sum, pieces[:i])) + offsets[j], rows, known[j], entering))

    y_col, silu, *known = call(
        functools.partial(col_local_kernel, **sizes),
        [
            pltpu.VMEM((tokens, channels), F32),
            pltpu.VMEM((tokens, channels), F32),
            pltpu.VMEM((tokens, 2 * heads), BF16),
            pltpu.VMEM((tokens, cols * state), BF16),
        ],
        0,
        specs=[None] * 6 + [any_spec],
    )(params, x, raw, maps, gate, skip.reshape(1, heads), before)
    w = call(
        functools.partial(col_out_kernel, heads=heads, width=width),
        pltpu.VMEM((tokens, channels), F32),
        0,
    )(col_entering, y_col, *known)

    back = []
    before = y_col
    for _, rows, known, entering in parts_of:
        y_row = call(
            functools.partial(row_out_kernel, heads=heads, width=width),
            [pltpu.VMEM((rows, channels), BF16)] * group,
            0,
            specs=[None] * 4 + [any_spec],
        )(entering, *known, before)
        back.append(exchange(y_row))
        before = y_row[0]

    mixed = None
    for (first, rows, _, _), blocks in zip(parts_of, back):
        more = [] if mixed is None else [mixed]
        mixed = call(
            functools.partial(final_kernel, offset=first, share=share, **shared),
            shape((tokens, channels), BF16),
            0,
            specs=[None] * (3 + group) + [any_spec] * len(more),
            out_specs=any_spec,
            scratch_shapes=[pltpu.VMEM((group, rows, channels), BF16), pltpu.SemaphoreType.DMA((group,))],
            input_output_aliases={3 + group: 0} if more else {},
        )(w, silu, norm_gain.reshape(1, channels), *blocks, *more)
    return mixed.reshape(x_in.shape)


def solution(mesh):
    tile = P("img", "row", "col", None)
    return jax.shard_map(
        functools.partial(body, row_count=mesh.shape["row"], col_count=mesh.shape["col"]),
        mesh=mesh,
        in_specs=(tile, tile, tile, tile, P("img"), P(), P(), P(), P()),
        out_specs=tile,
        check_vma=False,
    )
```

```python
import functools

import jax
import jax.numpy as jnp
from jax import lax
from jax.experimental import pallas as pl
from jax.experimental.pallas import tpu as pltpu
from jax.sharding import PartitionSpec as P

LANES = 128
GROUP = 4
PIECES = ((4,), (4,))
STRIP = 512
VMEM_LIMIT = 16 * 1024 * 1024
F32 = jnp.float32
BF16 = jnp.bfloat16


def dot(a, b):
    return jnp.dot(a, b, preferred_element_type=F32)


def iota(shape, dim):
    return lax.broadcasted_iota(jnp.int32, shape, dim)


def div(a, n):
    return lax.shift_right_logical(a, n.bit_length() - 1) if n & (n - 1) == 0 else a // n


def mod(a, n):
    return jnp.bitwise_and(a, n - 1) if n & (n - 1) == 0 else a % n


def parts(values, count):
    terms = []
    for _ in range(count):
        term = values.astype(BF16)
        terms.append(term)
        values = values - term.astype(F32)
    return jnp.concatenate(terms, axis=1)


def picks(heads, width, first, channels):
    row = iota((2 * heads, 1), 0)
    head = jnp.where(row >= heads, row - heads, row)
    return (head == div(first + iota((1, channels), 1), width)).astype(BF16)


def summed(mask, values):
    heads = values.shape[1]
    sums = dot(mask, parts(values, 3))
    return sums[:, :heads] + sums[:, heads : 2 * heads] + sums[:, 2 * heads :]


def step_sizes(raw, bias):
    shifted = raw.astype(F32) + bias
    return jnp.maximum(shifted, 0.0) + jnp.log1p(jnp.exp(-jnp.abs(shifted)))


def widen(maps, line, lines):
    state = maps.shape[1]
    places = lines * state
    copy = (mod(iota((1, places), 1), state) == iota((state, 1), 0)).astype(BF16)
    own = div(iota((1, places), 1), state) == line
    return jnp.where(own, dot(maps, copy), 0.0).astype(BF16)


class Scan:
    def __init__(self, order, lines, raw, bias, rates, b_map, c_map):
        tokens, self.heads = raw.shape
        self.lines, self.b_map, self.c_map = lines, b_map, c_map
        self.line, place = order(iota((tokens, 1), 0))
        self.line_in, place_in = order(iota((1, tokens), 1))
        self.lower = jnp.logical_and(self.line == self.line_in, place >= place_in)
        steps = step_sizes(raw, bias)
        self.decay = -rates * steps
        running = summed(self.lower.astype(BF16), self.decay)
        self.fade = parts(jnp.exp(running), 2)
        self.grow = parts(steps * jnp.exp(-running), 2)

    def ends(self):
        places = self.lines * self.b_map.shape[1]
        own = div(iota((places, 1), 0), self.b_map.shape[1]) == self.line_in
        return jnp.exp(summed(own.astype(BF16), self.decay))

    def into(self):
        return widen(self.b_map, self.line, self.lines).astype(F32).T.astype(BF16)

    def within(self):
        scores = lax.dot_general(
            self.c_map, self.b_map, (((1,), (1,)), ((), ())), preferred_element_type=F32
        )
        return jnp.where(self.lower, scores, 0.0).astype(BF16)

    def entry(self, follows):
        return jnp.where(follows, widen(self.c_map, self.line, self.lines), 0)


def partner(member, i, group):
    return member ^ i


def column_order(cols):
    return lambda token: (mod(token, cols), div(token, cols))


def row_order(cols, lines, member, group):
    def order(token):
        source = partner(member, div(token, cols * lines), group)
        return mod(div(token, cols), lines), source * cols + mod(token, cols)

    return order


def strips(channels):
    return [(first, min(STRIP, channels - first)) for first in range(0, channels, STRIP)]


def pack_kernel(
    x_ref, raw_ref, maps_ref, table_ref, rates_ref, raw, maps, table, rates, *refs, group, axis, heads, state
):
    sent, sems = refs[:-1], refs[-1]
    channels = x_ref.shape[1]
    share = x_ref.shape[0] // group
    member = mod(lax.axis_index(axis), group)
    moved = [(raw_ref, raw), (maps_ref, maps)]
    places = []
    offset = 0
    for i, out in enumerate(sent):
        rows = out.shape[0]
        first = partner(member, i % group, group) * share + offset
        part = pl.ds(pl.multiple_of(first, 16), rows)
        places.append((out, part))
        moved.append((x_ref.at[part, :], out.at[:, pl.ds(0, channels)]))
        if i % group == group - 1:
            offset += rows
    moved += [(table_ref, table), (rates_ref, rates)]
    copies = [pltpu.make_async_copy(a, b, sems.at[i]) for i, (a, b) in enumerate(moved)]
    for copy in copies:
        copy.start()
    for copy in copies[:2]:
        copy.wait()
    used = heads + 2 * state
    for out, part in places:
        out[:, channels : channels + heads] = raw[part, :heads]
        out[:, channels + heads : channels + used] = maps[part, : 2 * state]
        out[:, channels + used :] = jnp.zeros((out.shape[0], LANES - used), BF16)
    for copy in copies[2:]:
        copy.wait()


def params_kernel(index_ref, table_ref, rates_ref, params_ref):
    heads = rates_ref.shape[1]
    row = jnp.where(iota(table_ref.shape, 1) == index_ref[0], table_ref[...], 0.0)
    ones = jnp.ones((8, table_ref.shape[1]), BF16)
    bias = jnp.zeros((8, row.shape[0]), F32)
    for _ in range(3):
        term = row.astype(BF16)
        row = row - term.astype(F32)
        bias += lax.dot_general(ones, term, (((1,), (1,)), ((), ())), preferred_element_type=F32)
    params_ref[0:1, :] = bias[0:1, :]
    params_ref[1:2, :heads] = rates_ref[0:1, :]
    params_ref[1:2, heads:] = rates_ref[1:2, :]
    params_ref[2:, :] = jnp.zeros((6, 2 * heads), F32)


def row_scan(params_ref, blocks, member, cols, heads, state):
    channels = blocks[0].shape[1] - LANES
    tokens = blocks[0].shape[0] * len(blocks)
    lines = tokens // (cols * len(blocks))
    aux = jnp.concatenate([block[:, channels:] for block in blocks], axis=0)
    return Scan(
        row_order(cols, lines, member, len(blocks)),
        lines,
        aux[:, :heads],
        params_ref[0:1, :heads],
        params_ref[1:2, :heads],
        aux[:, heads : heads + state],
        aux[:, heads + state : heads + 2 * state],
    )


def col_scan(params_ref, raw_ref, maps_ref, cols, heads, state):
    return Scan(
        column_order(cols),
        cols,
        raw_ref[:, heads:],
        params_ref[0:1, heads:],
        params_ref[1:2, heads:],
        maps_ref[:, 2 * state : 3 * state],
        maps_ref[:, 3 * state :],
    )


def write_state(scan, tokens_of, width, channels, s_refs, factor_ref):
    ends = scan.ends()
    if factor_ref:
        factor_ref[0][...] = ends
    ends = parts(ends, 2)
    into = scan.into()
    for first, count in strips(channels):
        pick = picks(scan.heads, width, first, count)
        values = (tokens_of(first, count) * dot(scan.grow, pick)).astype(BF16)
        made = (dot(into, values) * dot(ends, pick)).astype(BF16)
        row = 0
        for s_ref in s_refs:
            s_ref[:, first : first + count] = made[row : row + s_ref.shape[0]]
            row += s_ref.shape[0]


def row_state_kernel(params_ref, *refs, group, count, axis, cols, heads, state, width):
    blocks, s_refs, factor_ref = refs[:group], refs[group + 1 : group + 1 + count], refs[group + 1 + count :]
    member = mod(lax.axis_index(axis), group)
    scan = row_scan(params_ref, [block[...] for block in blocks], member, cols, heads, state)
    tokens_of = lambda first, count: jnp.concatenate(
        [block[:, first : first + count] for block in blocks], axis=0
    ).astype(F32)
    write_state(scan, tokens_of, width, s_refs[0].shape[1], s_refs, factor_ref)


def col_state_kernel(params_ref, x_ref, raw_ref, maps_ref, _, s_ref, *factor_ref, cols, heads, state, width):
    scan = col_scan(params_ref, raw_ref, maps_ref, cols, heads, state)
    tokens_of = lambda first, count: x_ref[:, first : first + count].astype(F32)
    write_state(scan, tokens_of, width, s_ref.shape[1], [s_ref], factor_ref)


def row_local_kernel(params_ref, *refs, group, offset, axis, cols, heads, state, width):
    blocks, (y_ref, fade_ref, entry_ref) = refs[:group], refs[group + 1 :]
    rows = y_ref.shape[0] // group
    mine = slice(offset, offset + rows)
    member = mod(lax.axis_index(axis), group)
    scan = row_scan(params_ref, [block[mine, :] for block in blocks], member, cols, heads, state)
    mix = scan.within()
    fade_ref[...] = scan.fade
    entry_ref[...] = scan.entry(lax.axis_index(axis) >= group)
    for first, count in strips(y_ref.shape[1]):
        pick = picks(heads, width, first, count)
        part = slice(first, first + count)
        x = jnp.concatenate([block[mine, part] for block in blocks], axis=0).astype(F32)
        values = (x * dot(scan.grow, pick)).astype(BF16)
        y_ref[:, part] = dot(mix, values) * dot(scan.fade, pick)


def row_out_kernel(s_ref, y_ref, fade_ref, entry_ref, _, *outs, heads, width):
    rows = outs[0].shape[0]
    for first, count in strips(s_ref.shape[1]):
        pick = picks(heads, width, first, count)
        part = slice(first, first + count)
        y = y_ref[:, part] + dot(entry_ref[...], s_ref[:, part]) * dot(fade_ref[...], pick)
        for i, out in enumerate(outs):
            out[:, part] = y[i * rows : (i + 1) * rows].astype(BF16)


def col_local_kernel(
    params_ref, x_ref, raw_ref, maps_ref, gate_ref, skip_ref, _, y_ref, g_ref, fade_ref, entry_ref,
    *, cols, heads, state, width
):
    scan = col_scan(params_ref, raw_ref, maps_ref, cols, heads, state)
    mix = scan.within()
    fade_ref[...] = scan.fade
    entry_ref[...] = scan.entry(lax.axis_index("row") > 0)
    skips = parts(jnp.broadcast_to(skip_ref[...], (8, heads)), 2)
    for first, count in strips(x_ref.shape[1]):
        pick = picks(heads, width, first, count)
        part = slice(first, first + count)
        x = x_ref[:, part].astype(F32)
        values = (x * dot(scan.grow, pick)).astype(BF16)
        y_ref[:, part] = dot(mix, values) * dot(scan.fade, pick) + dot(skips, pick)[0:1, :] * x
        gate = gate_ref[:, part].astype(F32)
        g_ref[:, part] = gate / (1.0 + jnp.exp(-gate))


def col_out_kernel(s_ref, y_ref, fade_ref, entry_ref, w_ref, *, heads, width):
    for first, count in strips(s_ref.shape[1]):
        pick = picks(heads, width, first, count)
        part = slice(first, first + count)
        w_ref[:, part] = y_ref[:, part] + dot(entry_ref[...], s_ref[:, part]) * dot(fade_ref[...], pick)


def final_kernel(w_ref, g_ref, gain_ref, *refs, group, axis, offset, share):
    blocks, (out_ref, made, sems) = refs[:group], refs[-3:]
    rows, channels = blocks[0].shape
    member = mod(lax.axis_index(axis), group)
    copies = []
    for s in range(group):
        part = pl.ds(pl.multiple_of(partner(member, s, group) * share + offset, 16), rows)
        v = (blocks[s][...].astype(F32) + w_ref[part, :]) * g_ref[part, :]
        power = jnp.sum(v * v, axis=1, keepdims=True) / channels
        made[s] = (v * lax.rsqrt(power + 1e-5) * gain_ref[...]).astype(BF16)
        copies.append(pltpu.make_async_copy(made.at[s], out_ref.at[part, :], sems.at[s]))
        copies[-1].start()
    for copy in copies:
        copy.wait()


def cost(micros):
    return pl.CostEstimate(flops=1024 + int(micros * 10**9), bytes_accessed=1024, transcendentals=0)


def call(kernel, out_shape, micros, specs=None, **more):
    if specs is not None:
        more["in_specs"] = [spec or pl.BlockSpec() for spec in specs]
    return pl.pallas_call(
        kernel,
        out_shape=out_shape,
        compiler_params=pltpu.CompilerParams(vmem_limit_bytes=VMEM_LIMIT),
        cost_estimate=cost(micros),
        **more,
    )


def entering_states(ends, factor, axis, size, stride, width):
    if size == stride:
        return ends
    onward = [(i, (i + stride) % size) for i in range(size)]
    entering = lax.ppermute(ends, axis, onward)
    for _ in range(size // stride - 2):
        follows = (lax.axis_index(axis) >= stride).astype(F32)
        decayed = follows * jnp.repeat(factor[0], width, axis=1) * entering.astype(F32)
        entering = lax.ppermute((ends.astype(F32) + decayed).astype(BF16), axis, onward)
    return entering


def body(x_in, gate_in, proj_bc, dt_raw, step_index, step_table, rates, skip, norm_gain, *, row_count, col_count):
    _, tile_rows, cols, channels = x_in.shape
    heads = skip.shape[0]
    width = channels // heads
    state = proj_bc.shape[-1] // 4
    tokens = tile_rows * cols
    group = GROUP
    while col_count % group:
        group //= 2
    share = tokens // group
    pieces = [[eighths * share // 8 for eighths in piece] for piece in PIECES]

    x = x_in.reshape(tokens, channels)
    gate = gate_in.reshape(tokens, channels)
    maps = proj_bc.reshape(tokens, 4 * state)
    raw = dt_raw.reshape(tokens, 2 * heads)
    sizes = dict(cols=cols, heads=heads, state=state, width=width)
    shared = dict(group=group, axis="col")
    shape = jax.ShapeDtypeStruct
    any_spec = pl.BlockSpec(memory_space=pl.ANY)

    given = [x, raw, maps, step_table.T, rates]
    raw, maps, table, rates, *packed = pl.pallas_call(
        functools.partial(pack_kernel, heads=heads, state=state, **shared),
        in_specs=[pl.BlockSpec(memory_space=pltpu.HBM)] * len(given),
        out_shape=[pltpu.VMEM(a.shape, a.dtype) for a in given[1:]]
        + [pltpu.VMEM((sum(piece), channels + LANES), BF16) for piece in pieces for _ in range(group)],
        scratch_shapes=[pltpu.SemaphoreType.DMA((len(given) - 1 + group * len(pieces),))],
        compiler_params=pltpu.CompilerParams(vmem_limit_bytes=VMEM_LIMIT),
        cost_estimate=cost(1),
    )(*[pltpu.with_memory_space_constraint(a, pltpu.HBM) for a in given])
    index, rates = lax.optimization_barrier((step_index, rates))
    params = pl.pallas_call(
        params_kernel,
        grid_spec=pltpu.PrefetchScalarGridSpec(
            num_scalar_prefetch=1,
            grid=(1,),
            in_specs=[
                pl.BlockSpec(table.shape, lambda i, index: (0, 0)),
                pl.BlockSpec(rates.shape, lambda i, index: (0, 0)),
            ],
            out_specs=pl.BlockSpec((8, 2 * heads), lambda i, index: (0, 0)),
        ),
        out_shape=shape((8, 2 * heads), F32),
        compiler_params=pltpu.CompilerParams(vmem_limit_bytes=VMEM_LIMIT),
        cost_estimate=cost(0),
    )(index, table, rates)

    def exchange(blocks):
        return [blocks[0]] + [
            lax.ppermute(blocks[i], "col", [(at, partner(at, i, group)) for at in range(col_count)])
            for i in range(1, group)
        ]

    def state_shapes(places, count):
        states = [pltpu.VMEM((rows, channels), BF16) for rows in places]
        return states + [shape((sum(places), heads), F32)] * (count > 2)

    got = [exchange(packed[i * group : (i + 1) * group]) for i in range(len(pieces))]
    before = params
    parts_of = []
    for i, piece in enumerate(pieces):
        places = [rows // cols * state for rows in piece]
        offsets = [sum(piece[:j]) for j in range(len(piece))]

        def of_own(before, i=i, piece=piece, places=places, offsets=offsets):
            known = []
            for offset, rows, count in zip(offsets, piece, places):
                known.append(
                    call(
                        functools.partial(row_local_kernel, offset=offset, **sizes, **shared),
                        [
                            pltpu.VMEM((group * rows, channels), F32),
                            pltpu.VMEM((group * rows, 2 * heads), BF16),
                            pltpu.VMEM((group * rows, count), BF16),
                        ],
                        2,
                        specs=[None] * (1 + group) + [any_spec],
                    )(params, *got[i], before)
                )
                before = known[-1][1]
            return known, before

        if i:
            known, before = of_own(before)
        made = call(
            functools.partial(row_state_kernel, count=len(piece), **sizes, **shared),
            state_shapes(places, col_count // group),
            0 if i else 0,
            specs=[None] * (1 + group) + [any_spec],
        )(params, *got[i], before)
        before = made[0]
        if i == 0:
            col_made = call(
                functools.partial(col_state_kernel, **sizes),
                state_shapes([cols * state], row_count),
                0,
                specs=[None] * 4 + [any_spec],
            )(params, x, raw, maps, before)
            col_entering = entering_states(col_made[0], col_made[1:], "row", row_count, 1, width)
            known, before = of_own(col_made[0])
        for j, rows in enumerate(piece):
            first = sum(places[:j])
            factor = [f[first : first + places[j]] for f in made[len(piece) :]]
            entering = entering_states(made[j], factor, "col", col_count, group, width)
            parts_of.append((sum(map(sum, pieces[:i])) + offsets[j], rows, known[j], entering))

    y_col, silu, *known = call(
        functools.partial(col_local_kernel, **sizes),
        [
            pltpu.VMEM((tokens, channels), F32),
            pltpu.VMEM((tokens, channels), F32),
            pltpu.VMEM((tokens, 2 * heads), BF16),
            pltpu.VMEM((tokens, cols * state), BF16),
        ],
        0,
        specs=[None] * 6 + [any_spec],
    )(params, x, raw, maps, gate, skip.reshape(1, heads), before)
    w = call(
        functools.partial(col_out_kernel, heads=heads, width=width),
        pltpu.VMEM((tokens, channels), F32),
        0,
    )(col_entering, y_col, *known)

    back = []
    before = y_col
    for _, rows, known, entering in parts_of:
        y_row = call(
            functools.partial(row_out_kernel, heads=heads, width=width),
            [pltpu.VMEM((rows, channels), BF16)] * group,
            0,
            specs=[None] * 4 + [any_spec],
        )(entering, *known, before)
        back.append(exchange(y_row))
        before = col_entering

    mixed = None
    for (first, rows, _, _), blocks in zip(parts_of, back):
        more = [] if mixed is None else [mixed]
        mixed = call(
            functools.partial(final_kernel, offset=first, share=share, **shared),
            shape((tokens, channels), BF16),
            0,
            specs=[None] * (3 + group) + [any_spec] * len(more),
            out_specs=any_spec,
            scratch_shapes=[pltpu.VMEM((group, rows, channels), BF16), pltpu.SemaphoreType.DMA((group,))],
            input_output_aliases={3 + group: 0} if more else {},
        )(w, silu, norm_gain.reshape(1, channels), *blocks, *more)
    return mixed.reshape(x_in.shape)


def solution(mesh):
    tile = P("img", "row", "col", None)
    return jax.shard_map(
        functools.partial(body, row_count=mesh.shape["row"], col_count=mesh.shape["col"]),
        mesh=mesh,
        in_specs=(tile, tile, tile, tile, P("img"), P(), P(), P(), P()),
        out_specs=tile,
        check_vma=False,
    )
```

```python
import functools

import jax
import jax.numpy as jnp
from jax import lax
from jax.experimental import pallas as pl
from jax.experimental.pallas import tpu as pltpu
from jax.sharding import PartitionSpec as P

LANES = 128
GROUP = 4
PIECES = ((4,), (4,))
STRIP = 512
VMEM_LIMIT = 16 * 1024 * 1024
F32 = jnp.float32
BF16 = jnp.bfloat16


def dot(a, b):
    return jnp.dot(a, b, preferred_element_type=F32)


def iota(shape, dim):
    return lax.broadcasted_iota(jnp.int32, shape, dim)


def div(a, n):
    return lax.shift_right_logical(a, n.bit_length() - 1) if n & (n - 1) == 0 else a // n


def mod(a, n):
    return jnp.bitwise_and(a, n - 1) if n & (n - 1) == 0 else a % n


def parts(values, count):
    terms = []
    for _ in range(count):
        term = values.astype(BF16)
        terms.append(term)
        values = values - term.astype(F32)
    return jnp.concatenate(terms, axis=1)


def picks(heads, width, first, channels):
    row = iota((2 * heads, 1), 0)
    head = jnp.where(row >= heads, row - heads, row)
    return (head == div(first + iota((1, channels), 1), width)).astype(BF16)


def summed(mask, values):
    heads = values.shape[1]
    sums = dot(mask, parts(values, 3))
    return sums[:, :heads] + sums[:, heads : 2 * heads] + sums[:, 2 * heads :]


def step_sizes(raw, bias):
    shifted = raw.astype(F32) + bias
    return jnp.maximum(shifted, 0.0) + jnp.log1p(jnp.exp(-jnp.abs(shifted)))


def widen(maps, line, lines):
    state = maps.shape[1]
    places = lines * state
    copy = (mod(iota((1, places), 1), state) == iota((state, 1), 0)).astype(BF16)
    own = div(iota((1, places), 1), state) == line
    return jnp.where(own, dot(maps, copy), 0.0).astype(BF16)


class Scan:
    def __init__(self, order, lines, raw, bias, rates, b_map, c_map):
        tokens, self.heads = raw.shape
        self.lines, self.b_map, self.c_map = lines, b_map, c_map
        self.line, place = order(iota((tokens, 1), 0))
        self.line_in, place_in = order(iota((1, tokens), 1))
        self.lower = jnp.logical_and(self.line == self.line_in, place >= place_in)
        steps = step_sizes(raw, bias)
        self.decay = -rates * steps
        running = summed(self.lower.astype(BF16), self.decay)
        self.fade = parts(jnp.exp(running), 2)
        self.grow = parts(steps * jnp.exp(-running), 2)

    def ends(self):
        places = self.lines * self.b_map.shape[1]
        own = div(iota((places, 1), 0), self.b_map.shape[1]) == self.line_in
        return jnp.exp(summed(own.astype(BF16), self.decay))

    def into(self):
        return widen(self.b_map, self.line, self.lines).astype(F32).T.astype(BF16)

    def within(self):
        scores = lax.dot_general(
            self.c_map, self.b_map, (((1,), (1,)), ((), ())), preferred_element_type=F32
        )
        return jnp.where(self.lower, scores, 0.0).astype(BF16)

    def entry(self, follows):
        return jnp.where(follows, widen(self.c_map, self.line, self.lines), 0)


def partner(member, i, group):
    return member ^ i


def column_order(cols):
    return lambda token: (mod(token, cols), div(token, cols))


def row_order(cols, lines, member, group):
    def order(token):
        source = partner(member, div(token, cols * lines), group)
        return mod(div(token, cols), lines), source * cols + mod(token, cols)

    return order


def strips(channels):
    return [(first, min(STRIP, channels - first)) for first in range(0, channels, STRIP)]


def pack_places(sent, x_ref, offset, axis):
    group = len(sent)
    share = x_ref.shape[0] // group
    member = mod(lax.axis_index(axis), group)
    return [
        (out, pl.ds(pl.multiple_of(partner(member, i, group) * share + offset, 16), out.shape[0]))
        for i, out in enumerate(sent)
    ]


def pack_aux(places, raw, maps, channels, heads, state):
    used = heads + 2 * state
    for out, part in places:
        out[:, channels : channels + heads] = raw[part, :heads]
        out[:, channels + heads : channels + used] = maps[part, : 2 * state]
        out[:, channels + used :] = jnp.zeros((out.shape[0], LANES - used), BF16)


def first_pack_kernel(
    x_ref, raw_ref, maps_ref, table_ref, rates_ref, raw, maps, table, rates, *refs, offset, axis, heads, state
):
    sent, sems = refs[:-1], refs[-1]
    channels = x_ref.shape[1]
    places = pack_places(sent, x_ref, offset, axis)
    moved = [(raw_ref, raw), (maps_ref, maps)]
    moved += [(x_ref.at[part, :], out.at[:, pl.ds(0, channels)]) for out, part in places]
    moved += [(table_ref, table), (rates_ref, rates)]
    copies = [pltpu.make_async_copy(a, b, sems.at[i]) for i, (a, b) in enumerate(moved)]
    for copy in copies:
        copy.start()
    for copy in copies[:2]:
        copy.wait()
    pack_aux(places, raw, maps, channels, heads, state)
    for copy in copies[2:]:
        copy.wait()


def pack_kernel(x_ref, raw_ref, maps_ref, *sent, offset, axis, heads, state):
    channels = x_ref.shape[1]
    places = pack_places(sent, x_ref, offset, axis)
    for out, part in places:
        out[:, :channels] = x_ref[part, :]
    pack_aux(places, raw_ref, maps_ref, channels, heads, state)


def params_kernel(index_ref, table_ref, rates_ref, params_ref):
    heads = rates_ref.shape[1]
    row = jnp.where(iota(table_ref.shape, 1) == index_ref[0], table_ref[...], 0.0)
    ones = jnp.ones((8, table_ref.shape[1]), BF16)
    bias = jnp.zeros((8, row.shape[0]), F32)
    for _ in range(3):
        term = row.astype(BF16)
        row = row - term.astype(F32)
        bias += lax.dot_general(ones, term, (((1,), (1,)), ((), ())), preferred_element_type=F32)
    params_ref[0:1, :] = bias[0:1, :]
    params_ref[1:2, :heads] = rates_ref[0:1, :]
    params_ref[1:2, heads:] = rates_ref[1:2, :]
    params_ref[2:, :] = jnp.zeros((6, 2 * heads), F32)


def row_scan(params_ref, blocks, member, cols, heads, state):
    channels = blocks[0].shape[1] - LANES
    tokens = blocks[0].shape[0] * len(blocks)
    lines = tokens // (cols * len(blocks))
    aux = jnp.concatenate([block[:, channels:] for block in blocks], axis=0)
    return Scan(
        row_order(cols, lines, member, len(blocks)),
        lines,
        aux[:, :heads],
        params_ref[0:1, :heads],
        params_ref[1:2, :heads],
        aux[:, heads : heads + state],
        aux[:, heads + state : heads + 2 * state],
    )


def col_scan(params_ref, raw_ref, maps_ref, cols, heads, state):
    return Scan(
        column_order(cols),
        cols,
        raw_ref[:, heads:],
        params_ref[0:1, heads:],
        params_ref[1:2, heads:],
        maps_ref[:, 2 * state : 3 * state],
        maps_ref[:, 3 * state :],
    )


def write_state(scan, tokens_of, width, channels, s_refs, factor_ref):
    ends = scan.ends()
    if factor_ref:
        factor_ref[0][...] = ends
    ends = parts(ends, 2)
    into = scan.into()
    for first, count in strips(channels):
        pick = picks(scan.heads, width, first, count)
        values = (tokens_of(first, count) * dot(scan.grow, pick)).astype(BF16)
        made = (dot(into, values) * dot(ends, pick)).astype(BF16)
        row = 0
        for s_ref in s_refs:
            s_ref[:, first : first + count] = made[row : row + s_ref.shape[0]]
            row += s_ref.shape[0]


def row_state_kernel(params_ref, *refs, group, count, axis, cols, heads, state, width):
    blocks, s_refs, factor_ref = refs[:group], refs[group + 1 : group + 1 + count], refs[group + 1 + count :]
    member = mod(lax.axis_index(axis), group)
    scan = row_scan(params_ref, [block[...] for block in blocks], member, cols, heads, state)
    tokens_of = lambda first, count: jnp.concatenate(
        [block[:, first : first + count] for block in blocks], axis=0
    ).astype(F32)
    write_state(scan, tokens_of, width, s_refs[0].shape[1], s_refs, factor_ref)


def col_state_kernel(params_ref, x_ref, raw_ref, maps_ref, _, s_ref, *factor_ref, cols, heads, state, width):
    scan = col_scan(params_ref, raw_ref, maps_ref, cols, heads, state)
    tokens_of = lambda first, count: x_ref[:, first : first + count].astype(F32)
    write_state(scan, tokens_of, width, s_ref.shape[1], [s_ref], factor_ref)


def row_local_kernel(params_ref, *refs, group, offset, axis, cols, heads, state, width):
    blocks, (y_ref, fade_ref, entry_ref) = refs[:group], refs[group + 1 :]
    rows = y_ref.shape[0] // group
    mine = slice(offset, offset + rows)
    member = mod(lax.axis_index(axis), group)
    scan = row_scan(params_ref, [block[mine, :] for block in blocks], member, cols, heads, state)
    mix = scan.within()
    fade_ref[...] = scan.fade
    entry_ref[...] = scan.entry(lax.axis_index(axis) >= group)
    for first, count in strips(y_ref.shape[1]):
        pick = picks(heads, width, first, count)
        part = slice(first, first + count)
        x = jnp.concatenate([block[mine, part] for block in blocks], axis=0).astype(F32)
        values = (x * dot(scan.grow, pick)).astype(BF16)
        y_ref[:, part] = dot(mix, values) * dot(scan.fade, pick)


def row_out_kernel(s_ref, y_ref, fade_ref, entry_ref, _, *outs, heads, width):
    rows = outs[0].shape[0]
    for first, count in strips(s_ref.shape[1]):
        pick = picks(heads, width, first, count)
        part = slice(first, first + count)
        y = y_ref[:, part] + dot(entry_ref[...], s_ref[:, part]) * dot(fade_ref[...], pick)
        for i, out in enumerate(outs):
            out[:, part] = y[i * rows : (i + 1) * rows].astype(BF16)


def col_local_kernel(
    params_ref, x_ref, raw_ref, maps_ref, gate_ref, skip_ref, _, y_ref, g_ref, fade_ref, entry_ref,
    *, cols, heads, state, width
):
    scan = col_scan(params_ref, raw_ref, maps_ref, cols, heads, state)
    mix = scan.within()
    fade_ref[...] = scan.fade
    entry_ref[...] = scan.entry(lax.axis_index("row") > 0)
    skips = parts(jnp.broadcast_to(skip_ref[...], (8, heads)), 2)
    for first, count in strips(x_ref.shape[1]):
        pick = picks(heads, width, first, count)
        part = slice(first, first + count)
        x = x_ref[:, part].astype(F32)
        values = (x * dot(scan.grow, pick)).astype(BF16)
        y_ref[:, part] = dot(mix, values) * dot(scan.fade, pick) + dot(skips, pick)[0:1, :] * x
        gate = gate_ref[:, part].astype(F32)
        g_ref[:, part] = gate / (1.0 + jnp.exp(-gate))


def col_out_kernel(s_ref, y_ref, fade_ref, entry_ref, w_ref, *, heads, width):
    for first, count in strips(s_ref.shape[1]):
        pick = picks(heads, width, first, count)
        part = slice(first, first + count)
        w_ref[:, part] = y_ref[:, part] + dot(entry_ref[...], s_ref[:, part]) * dot(fade_ref[...], pick)


def final_kernel(w_ref, g_ref, gain_ref, *refs, which, offset, group, axis, share):
    blocks, (out_ref, made, sems) = refs[-3 - len(which) : -3], refs[-3:]
    rows, channels = blocks[0].shape
    member = mod(lax.axis_index(axis), group)
    copies = []
    for i, block in zip(which, blocks):
        part = pl.ds(pl.multiple_of(partner(member, i, group) * share + offset, 16), rows)
        v = (block[...].astype(F32) + w_ref[part, :]) * g_ref[part, :]
        power = jnp.sum(v * v, axis=1, keepdims=True) / channels
        at = len(copies)
        made[at] = (v * lax.rsqrt(power + 1e-5) * gain_ref[...]).astype(BF16)
        copies.append(pltpu.make_async_copy(made.at[at], out_ref.at[part, :], sems.at[at]))
        copies[-1].start()
    for copy in copies:
        copy.wait()


def cost(micros):
    return pl.CostEstimate(flops=1024 + int(micros * 10**9), bytes_accessed=1024, transcendentals=0)


def call(kernel, out_shape, micros, specs=None, **more):
    if specs is not None:
        more["in_specs"] = [spec or pl.BlockSpec() for spec in specs]
    return pl.pallas_call(
        kernel,
        out_shape=out_shape,
        compiler_params=pltpu.CompilerParams(vmem_limit_bytes=VMEM_LIMIT),
        cost_estimate=cost(micros),
        **more,
    )


def entering_states(ends, factor, axis, size, stride, width):
    if size == stride:
        return ends
    onward = [(i, (i + stride) % size) for i in range(size)]
    entering = lax.ppermute(ends, axis, onward)
    for _ in range(size // stride - 2):
        follows = (lax.axis_index(axis) >= stride).astype(F32)
        decayed = follows * jnp.repeat(factor[0], width, axis=1) * entering.astype(F32)
        entering = lax.ppermute((ends.astype(F32) + decayed).astype(BF16), axis, onward)
    return entering


def body(x_in, gate_in, proj_bc, dt_raw, step_index, step_table, rates, skip, norm_gain, *, row_count, col_count):
    _, tile_rows, cols, channels = x_in.shape
    heads = skip.shape[0]
    width = channels // heads
    state = proj_bc.shape[-1] // 4
    tokens = tile_rows * cols
    group = GROUP
    while col_count % group:
        group //= 2
    share = tokens // group
    pieces = [[eighths * share // 8 for eighths in piece] for piece in PIECES]

    x = x_in.reshape(tokens, channels)
    gate = gate_in.reshape(tokens, channels)
    maps = proj_bc.reshape(tokens, 4 * state)
    raw = dt_raw.reshape(tokens, 2 * heads)
    sizes = dict(cols=cols, heads=heads, state=state, width=width)
    shared = dict(group=group, axis="col")
    shape = jax.ShapeDtypeStruct
    any_spec = pl.BlockSpec(memory_space=pl.ANY)

    given = [x, raw, maps, step_table.T, rates]
    blocks_of = lambda piece: [pltpu.VMEM((sum(piece), channels + LANES), BF16)] * group
    packing = dict(axis="col", heads=heads, state=state)
    raw, maps, table, rates, *packed = call(
        functools.partial(first_pack_kernel, offset=0, **packing),
        [pltpu.VMEM(a.shape, a.dtype) for a in given[1:]] + blocks_of(pieces[0]),
        0,
        specs=[pl.BlockSpec(memory_space=pltpu.HBM)] * len(given),
        scratch_shapes=[pltpu.SemaphoreType.DMA((len(given) - 1 + group,))],
    )(*[pltpu.with_memory_space_constraint(a, pltpu.HBM) for a in given])
    for i in range(1, len(pieces)):
        packed += call(
            functools.partial(pack_kernel, offset=sum(map(sum, pieces[:i])), **packing),
            blocks_of(pieces[i]),
            0,
        )(x, raw, maps)
    index, rates = lax.optimization_barrier((step_index, rates))
    params = pl.pallas_call(
        params_kernel,
        grid_spec=pltpu.PrefetchScalarGridSpec(
            num_scalar_prefetch=1,
            grid=(1,),
            in_specs=[
                pl.BlockSpec(table.shape, lambda i, index: (0, 0)),
                pl.BlockSpec(rates.shape, lambda i, index: (0, 0)),
            ],
            out_specs=pl.BlockSpec((8, 2 * heads), lambda i, index: (0, 0)),
        ),
        out_shape=shape((8, 2 * heads), F32),
        compiler_params=pltpu.CompilerParams(vmem_limit_bytes=VMEM_LIMIT),
        cost_estimate=cost(0),
    )(index, table, rates)

    def exchange(blocks):
        return [blocks[0]] + [
            lax.ppermute(blocks[i], "col", [(at, partner(at, i, group)) for at in range(col_count)])
            for i in range(1, group)
        ]

    def state_shapes(places, count):
        states = [pltpu.VMEM((rows, channels), BF16) for rows in places]
        return states + [shape((sum(places), heads), F32)] * (count > 2)

    got = [exchange(packed[i * group : (i + 1) * group]) for i in range(len(pieces))]
    before = params
    parts_of = []
    for i, piece in enumerate(pieces):
        places = [rows // cols * state for rows in piece]
        offsets = [sum(piece[:j]) for j in range(len(piece))]

        def of_own(before, i=i, piece=piece, places=places, offsets=offsets):
            known = []
            for offset, rows, count in zip(offsets, piece, places):
                known.append(
                    call(
                        functools.partial(row_local_kernel, offset=offset, **sizes, **shared),
                        [
                            pltpu.VMEM((group * rows, channels), F32),
                            pltpu.VMEM((group * rows, 2 * heads), BF16),
                            pltpu.VMEM((group * rows, count), BF16),
                        ],
                        2,
                        specs=[None] * (1 + group) + [any_spec],
                    )(params, *got[i], before)
                )
                before = known[-1][1]
            return known, before

        if i:
            known, before = of_own(before)
        made = call(
            functools.partial(row_state_kernel, count=len(piece), **sizes, **shared),
            state_shapes(places, col_count // group),
            0 if i else 0,
            specs=[None] * (1 + group) + [any_spec],
        )(params, *got[i], before)
        before = made[0]
        if i == 0:
            col_made = call(
                functools.partial(col_state_kernel, **sizes),
                state_shapes([cols * state], row_count),
                0,
                specs=[None] * 4 + [any_spec],
            )(params, x, raw, maps, before)
            col_entering = entering_states(col_made[0], col_made[1:], "row", row_count, 1, width)
            known, before = of_own(col_made[0])
        for j, rows in enumerate(piece):
            first = sum(places[:j])
            factor = [f[first : first + places[j]] for f in made[len(piece) :]]
            entering = entering_states(made[j], factor, "col", col_count, group, width)
            parts_of.append((sum(map(sum, pieces[:i])) + offsets[j], rows, known[j], entering))

    y_col, silu, *known = call(
        functools.partial(col_local_kernel, **sizes),
        [
            pltpu.VMEM((tokens, channels), F32),
            pltpu.VMEM((tokens, channels), F32),
            pltpu.VMEM((tokens, 2 * heads), BF16),
            pltpu.VMEM((tokens, cols * state), BF16),
        ],
        0,
        specs=[None] * 6 + [any_spec],
    )(params, x, raw, maps, gate, skip.reshape(1, heads), before)
    w = call(
        functools.partial(col_out_kernel, heads=heads, width=width),
        pltpu.VMEM((tokens, channels), F32),
        0,
    )(col_entering, y_col, *known)

    back = []
    before = y_col
    for _, rows, known, entering in parts_of:
        y_row = call(
            functools.partial(row_out_kernel, heads=heads, width=width),
            [pltpu.VMEM((rows, channels), BF16)] * group,
            0,
            specs=[None] * 4 + [any_spec],
        )(entering, *known, before)
        back.append(exchange(y_row))
        before = col_entering

    order = list(range(group))
    stages = [(i, order) for i in range(len(parts_of) - 1)]
    stages += [(len(parts_of) - 1, order[:1] + order[:1:-1]), (len(parts_of) - 1, order[1:2])]
    mixed = None
    for i, which in stages:
        first, rows = parts_of[i][:2]
        more = [] if mixed is None else [mixed]
        mixed = call(
            functools.partial(final_kernel, which=which, offset=first, share=share, **shared),
            shape((tokens, channels), BF16),
            0,
            specs=[None] * 3 + [any_spec] * len(more) + [None] * len(which),
            out_specs=any_spec,
            scratch_shapes=[
                pltpu.VMEM((len(which), rows, channels), BF16),
                pltpu.SemaphoreType.DMA((len(which),)),
            ],
            input_output_aliases={3: 0} if more else {},
        )(w, silu, norm_gain.reshape(1, channels), *more, *[back[i][j] for j in which])
    return mixed.reshape(x_in.shape)


def solution(mesh):
    tile = P("img", "row", "col", None)
    return jax.shard_map(
        functools.partial(body, row_count=mesh.shape["row"], col_count=mesh.shape["col"]),
        mesh=mesh,
        in_specs=(tile, tile, tile, tile, P("img"), P(), P(), P(), P()),
        out_specs=tile,
        check_vma=False,
    )
```

```python
import functools

import jax
import jax.numpy as jnp
from jax import lax
from jax.experimental import pallas as pl
from jax.experimental.pallas import tpu as pltpu
from jax.sharding import PartitionSpec as P

LANES = 128
GROUP = 4
PIECES = ((4,), (4,))
STRIP = 512
VMEM_LIMIT = 16 * 1024 * 1024
F32 = jnp.float32
BF16 = jnp.bfloat16


def dot(a, b):
    return jnp.dot(a, b, preferred_element_type=F32)


def iota(shape, dim):
    return lax.broadcasted_iota(jnp.int32, shape, dim)


def div(a, n):
    return lax.shift_right_logical(a, n.bit_length() - 1) if n & (n - 1) == 0 else a // n


def mod(a, n):
    return jnp.bitwise_and(a, n - 1) if n & (n - 1) == 0 else a % n


def parts(values, count):
    terms = []
    for _ in range(count):
        term = values.astype(BF16)
        terms.append(term)
        values = values - term.astype(F32)
    return jnp.concatenate(terms, axis=1)


def picks(heads, width, first, channels):
    row = iota((2 * heads, 1), 0)
    head = jnp.where(row >= heads, row - heads, row)
    return (head == div(first + iota((1, channels), 1), width)).astype(BF16)


def summed(mask, values):
    heads = values.shape[1]
    sums = dot(mask, parts(values, 3))
    return sums[:, :heads] + sums[:, heads : 2 * heads] + sums[:, 2 * heads :]


def step_sizes(raw, bias):
    shifted = raw.astype(F32) + bias
    return jnp.maximum(shifted, 0.0) + jnp.log1p(jnp.exp(-jnp.abs(shifted)))


def widen(maps, line, lines):
    state = maps.shape[1]
    places = lines * state
    copy = (mod(iota((1, places), 1), state) == iota((state, 1), 0)).astype(BF16)
    own = div(iota((1, places), 1), state) == line
    return jnp.where(own, dot(maps, copy), 0.0).astype(BF16)


class Scan:
    def __init__(self, order, lines, raw, bias, rates, b_map, c_map):
        tokens, self.heads = raw.shape
        self.lines, self.b_map, self.c_map = lines, b_map, c_map
        self.line, place = order(iota((tokens, 1), 0))
        self.line_in, place_in = order(iota((1, tokens), 1))
        self.lower = jnp.logical_and(self.line == self.line_in, place >= place_in)
        steps = step_sizes(raw, bias)
        self.decay = -rates * steps
        running = summed(self.lower.astype(BF16), self.decay)
        self.fade = parts(jnp.exp(running), 2)
        self.grow = parts(steps * jnp.exp(-running), 2)

    def ends(self):
        places = self.lines * self.b_map.shape[1]
        own = div(iota((places, 1), 0), self.b_map.shape[1]) == self.line_in
        return jnp.exp(summed(own.astype(BF16), self.decay))

    def into(self):
        return widen(self.b_map, self.line, self.lines).astype(F32).T.astype(BF16)

    def within(self):
        scores = lax.dot_general(
            self.c_map, self.b_map, (((1,), (1,)), ((), ())), preferred_element_type=F32
        )
        return jnp.where(self.lower, scores, 0.0).astype(BF16)

    def entry(self, follows):
        return jnp.where(follows, widen(self.c_map, self.line, self.lines), 0)


def partner(member, i, group):
    return member ^ i


def column_order(cols):
    return lambda token: (mod(token, cols), div(token, cols))


def row_order(cols, lines, member, group):
    def order(token):
        source = partner(member, div(token, cols * lines), group)
        return mod(div(token, cols), lines), source * cols + mod(token, cols)

    return order


def strips(channels):
    return [(first, min(STRIP, channels - first)) for first in range(0, channels, STRIP)]


def pack_kernel(
    x_ref, raw_ref, maps_ref, table_ref, rates_ref, raw, maps, table, rates, *refs, group, axis, heads, state
):
    sent, sems = refs[:-1], refs[-1]
    channels = x_ref.shape[1]
    share = x_ref.shape[0] // group
    member = mod(lax.axis_index(axis), group)
    moved = [(raw_ref, raw), (maps_ref, maps)]
    places = []
    offset = 0
    for i, out in enumerate(sent):
        rows = out.shape[0]
        first = partner(member, i % group, group) * share + offset
        part = pl.ds(pl.multiple_of(first, 16), rows)
        places.append((out, part))
        moved.append((x_ref.at[part, :], out.at[:, pl.ds(0, channels)]))
        if i % group == group - 1:
            offset += rows
    moved += [(table_ref, table), (rates_ref, rates)]
    copies = [pltpu.make_async_copy(a, b, sems.at[i]) for i, (a, b) in enumerate(moved)]
    for copy in copies:
        copy.start()
    for copy in copies[:2]:
        copy.wait()
    used = heads + 2 * state
    for out, part in places:
        out[:, channels : channels + heads] = raw[part, :heads]
        out[:, channels + heads : channels + used] = maps[part, : 2 * state]
        out[:, channels + used :] = jnp.zeros((out.shape[0], LANES - used), BF16)
    for copy in copies[2:]:
        copy.wait()


def params_kernel(index_ref, table_ref, rates_ref, params_ref):
    heads = rates_ref.shape[1]
    row = jnp.where(iota(table_ref.shape, 1) == index_ref[0], table_ref[...], 0.0)
    ones = jnp.ones((8, table_ref.shape[1]), BF16)
    bias = jnp.zeros((8, row.shape[0]), F32)
    for _ in range(3):
        term = row.astype(BF16)
        row = row - term.astype(F32)
        bias += lax.dot_general(ones, term, (((1,), (1,)), ((), ())), preferred_element_type=F32)
    params_ref[0:1, :] = bias[0:1, :]
    params_ref[1:2, :heads] = rates_ref[0:1, :]
    params_ref[1:2, heads:] = rates_ref[1:2, :]
    params_ref[2:, :] = jnp.zeros((6, 2 * heads), F32)


def row_scan(params_ref, blocks, member, cols, heads, state):
    channels = blocks[0].shape[1] - LANES
    tokens = blocks[0].shape[0] * len(blocks)
    lines = tokens // (cols * len(blocks))
    aux = jnp.concatenate([block[:, channels:] for block in blocks], axis=0)
    return Scan(
        row_order(cols, lines, member, len(blocks)),
        lines,
        aux[:, :heads],
        params_ref[0:1, :heads],
        params_ref[1:2, :heads],
        aux[:, heads : heads + state],
        aux[:, heads + state : heads + 2 * state],
    )


def col_scan(params_ref, raw_ref, maps_ref, cols, heads, state):
    return Scan(
        column_order(cols),
        cols,
        raw_ref[:, heads:],
        params_ref[0:1, heads:],
        params_ref[1:2, heads:],
        maps_ref[:, 2 * state : 3 * state],
        maps_ref[:, 3 * state :],
    )


def write_state(scan, tokens_of, width, channels, s_refs, factor_ref):
    ends = scan.ends()
    if factor_ref:
        factor_ref[0][...] = ends
    ends = parts(ends, 2)
    into = scan.into()
    for first, count in strips(channels):
        pick = picks(scan.heads, width, first, count)
        values = (tokens_of(first, count) * dot(scan.grow, pick)).astype(BF16)
        made = (dot(into, values) * dot(ends, pick)).astype(BF16)
        row = 0
        for s_ref in s_refs:
            s_ref[:, first : first + count] = made[row : row + s_ref.shape[0]]
            row += s_ref.shape[0]


def row_state_kernel(params_ref, *refs, group, count, axis, cols, heads, state, width):
    blocks, s_refs, factor_ref = refs[:group], refs[group + 1 : group + 1 + count], refs[group + 1 + count :]
    member = mod(lax.axis_index(axis), group)
    scan = row_scan(params_ref, [block[...] for block in blocks], member, cols, heads, state)
    tokens_of = lambda first, count: jnp.concatenate(
        [block[:, first : first + count] for block in blocks], axis=0
    ).astype(F32)
    write_state(scan, tokens_of, width, s_refs[0].shape[1], s_refs, factor_ref)


def col_state_kernel(params_ref, x_ref, raw_ref, maps_ref, _, s_ref, *factor_ref, cols, heads, state, width):
    scan = col_scan(params_ref, raw_ref, maps_ref, cols, heads, state)
    tokens_of = lambda first, count: x_ref[:, first : first + count].astype(F32)
    write_state(scan, tokens_of, width, s_ref.shape[1], [s_ref], factor_ref)


def row_local_kernel(params_ref, *refs, group, offset, axis, cols, heads, state, width):
    blocks, (y_ref, fade_ref, entry_ref) = refs[:group], refs[group + 1 :]
    rows = y_ref.shape[0] // group
    mine = slice(offset, offset + rows)
    member = mod(lax.axis_index(axis), group)
    scan = row_scan(params_ref, [block[mine, :] for block in blocks], member, cols, heads, state)
    mix = scan.within()
    fade_ref[...] = scan.fade
    entry_ref[...] = scan.entry(lax.axis_index(axis) >= group)
    for first, count in strips(y_ref.shape[1]):
        pick = picks(heads, width, first, count)
        part = slice(first, first + count)
        x = jnp.concatenate([block[mine, part] for block in blocks], axis=0).astype(F32)
        values = (x * dot(scan.grow, pick)).astype(BF16)
        y_ref[:, part] = dot(mix, values) * dot(scan.fade, pick)


def row_out_kernel(s_ref, y_ref, fade_ref, entry_ref, _, *outs, heads, width):
    rows = outs[0].shape[0]
    for first, count in strips(s_ref.shape[1]):
        pick = picks(heads, width, first, count)
        part = slice(first, first + count)
        y = y_ref[:, part] + dot(entry_ref[...], s_ref[:, part]) * dot(fade_ref[...], pick)
        for i, out in enumerate(outs):
            out[:, part] = y[i * rows : (i + 1) * rows].astype(BF16)


def col_local_kernel(
    params_ref, x_ref, raw_ref, maps_ref, gate_ref, skip_ref, _, y_ref, g_ref, fade_ref, entry_ref,
    *, cols, heads, state, width
):
    scan = col_scan(params_ref, raw_ref, maps_ref, cols, heads, state)
    mix = scan.within()
    fade_ref[...] = scan.fade
    entry_ref[...] = scan.entry(lax.axis_index("row") > 0)
    skips = parts(jnp.broadcast_to(skip_ref[...], (8, heads)), 2)
    for first, count in strips(x_ref.shape[1]):
        pick = picks(heads, width, first, count)
        part = slice(first, first + count)
        x = x_ref[:, part].astype(F32)
        values = (x * dot(scan.grow, pick)).astype(BF16)
        y_ref[:, part] = dot(mix, values) * dot(scan.fade, pick) + dot(skips, pick)[0:1, :] * x
        gate = gate_ref[:, part].astype(F32)
        g_ref[:, part] = gate / (1.0 + jnp.exp(-gate))


def col_out_kernel(s_ref, y_ref, fade_ref, entry_ref, w_ref, *, heads, width):
    for first, count in strips(s_ref.shape[1]):
        pick = picks(heads, width, first, count)
        part = slice(first, first + count)
        w_ref[:, part] = y_ref[:, part] + dot(entry_ref[...], s_ref[:, part]) * dot(fade_ref[...], pick)


def final_kernel(w_ref, g_ref, gain_ref, *refs, which, offset, group, axis, share):
    blocks, (out_ref, made, sems) = refs[-3 - len(which) : -3], refs[-3:]
    rows, channels = blocks[0].shape
    member = mod(lax.axis_index(axis), group)
    copies = []
    for i, block in zip(which, blocks):
        part = pl.ds(pl.multiple_of(partner(member, i, group) * share + offset, 16), rows)
        v = (block[...].astype(F32) + w_ref[part, :]) * g_ref[part, :]
        power = jnp.sum(v * v, axis=1, keepdims=True) / channels
        at = len(copies)
        made[at] = (v * lax.rsqrt(power + 1e-5) * gain_ref[...]).astype(BF16)
        copies.append(pltpu.make_async_copy(made.at[at], out_ref.at[part, :], sems.at[at]))
        copies[-1].start()
    for copy in copies:
        copy.wait()


def cost(micros):
    return pl.CostEstimate(flops=1024 + int(micros * 10**9), bytes_accessed=1024, transcendentals=0)


def call(kernel, out_shape, micros, specs=None, **more):
    if specs is not None:
        more["in_specs"] = [spec or pl.BlockSpec() for spec in specs]
    return pl.pallas_call(
        kernel,
        out_shape=out_shape,
        compiler_params=pltpu.CompilerParams(vmem_limit_bytes=VMEM_LIMIT),
        cost_estimate=cost(micros),
        **more,
    )


def entering_states(ends, factor, axis, size, stride, width):
    if size == stride:
        return ends
    onward = [(i, (i + stride) % size) for i in range(size)]
    entering = lax.ppermute(ends, axis, onward)
    for _ in range(size // stride - 2):
        follows = (lax.axis_index(axis) >= stride).astype(F32)
        decayed = follows * jnp.repeat(factor[0], width, axis=1) * entering.astype(F32)
        entering = lax.ppermute((ends.astype(F32) + decayed).astype(BF16), axis, onward)
    return entering


def body(x_in, gate_in, proj_bc, dt_raw, step_index, step_table, rates, skip, norm_gain, *, row_count, col_count):
    _, tile_rows, cols, channels = x_in.shape
    heads = skip.shape[0]
    width = channels // heads
    state = proj_bc.shape[-1] // 4
    tokens = tile_rows * cols
    group = GROUP
    while col_count % group:
        group //= 2
    share = tokens // group
    pieces = [[eighths * share // 8 for eighths in piece] for piece in PIECES]

    x = x_in.reshape(tokens, channels)
    gate = gate_in.reshape(tokens, channels)
    maps = proj_bc.reshape(tokens, 4 * state)
    raw = dt_raw.reshape(tokens, 2 * heads)
    sizes = dict(cols=cols, heads=heads, state=state, width=width)
    shared = dict(group=group, axis="col")
    shape = jax.ShapeDtypeStruct
    any_spec = pl.BlockSpec(memory_space=pl.ANY)

    given = [x, raw, maps, step_table.T, rates]
    raw, maps, table, rates, *packed = pl.pallas_call(
        functools.partial(pack_kernel, heads=heads, state=state, **shared),
        in_specs=[pl.BlockSpec(memory_space=pltpu.HBM)] * len(given),
        out_shape=[pltpu.VMEM(a.shape, a.dtype) for a in given[1:]]
        + [pltpu.VMEM((sum(piece), channels + LANES), BF16) for piece in pieces for _ in range(group)],
        scratch_shapes=[pltpu.SemaphoreType.DMA((len(given) - 1 + group * len(pieces),))],
        compiler_params=pltpu.CompilerParams(vmem_limit_bytes=VMEM_LIMIT),
        cost_estimate=cost(1),
    )(*[pltpu.with_memory_space_constraint(a, pltpu.HBM) for a in given])
    index, rates = lax.optimization_barrier((step_index, rates))
    params = pl.pallas_call(
        params_kernel,
        grid_spec=pltpu.PrefetchScalarGridSpec(
            num_scalar_prefetch=1,
            grid=(1,),
            in_specs=[
                pl.BlockSpec(table.shape, lambda i, index: (0, 0)),
                pl.BlockSpec(rates.shape, lambda i, index: (0, 0)),
            ],
            out_specs=pl.BlockSpec((8, 2 * heads), lambda i, index: (0, 0)),
        ),
        out_shape=shape((8, 2 * heads), F32),
        compiler_params=pltpu.CompilerParams(vmem_limit_bytes=VMEM_LIMIT),
        cost_estimate=cost(0),
    )(index, table, rates)

    def exchange(blocks):
        return [blocks[0]] + [
            lax.ppermute(blocks[i], "col", [(at, partner(at, i, group)) for at in range(col_count)])
            for i in range(1, group)
        ]

    def state_shapes(places, count):
        states = [pltpu.VMEM((rows, channels), BF16) for rows in places]
        return states + [shape((sum(places), heads), F32)] * (count > 2)

    got = [exchange(packed[i * group : (i + 1) * group]) for i in range(len(pieces))]
    before = params
    parts_of = []
    for i, piece in enumerate(pieces):
        places = [rows // cols * state for rows in piece]
        offsets = [sum(piece[:j]) for j in range(len(piece))]

        def of_own(before, i=i, piece=piece, places=places, offsets=offsets):
            known = []
            for offset, rows, count in zip(offsets, piece, places):
                known.append(
                    call(
                        functools.partial(row_local_kernel, offset=offset, **sizes, **shared),
                        [
                            pltpu.VMEM((group * rows, channels), F32),
                            pltpu.VMEM((group * rows, 2 * heads), BF16),
                            pltpu.VMEM((group * rows, count), BF16),
                        ],
                        2,
                        specs=[None] * (1 + group) + [any_spec],
                    )(params, *got[i], before)
                )
                before = known[-1][1]
            return known, before

        if i:
            known, before = of_own(before)
        made = call(
            functools.partial(row_state_kernel, count=len(piece), **sizes, **shared),
            state_shapes(places, col_count // group),
            0 if i else 0,
            specs=[None] * (1 + group) + [any_spec],
        )(params, *got[i], before)
        before = made[0]
        if i == 0:
            col_made = call(
                functools.partial(col_state_kernel, **sizes),
                state_shapes([cols * state], row_count),
                0,
                specs=[None] * 4 + [any_spec],
            )(params, x, raw, maps, before)
            col_entering = entering_states(col_made[0], col_made[1:], "row", row_count, 1, width)
            known, before = of_own(col_made[0])
        for j, rows in enumerate(piece):
            first = sum(places[:j])
            factor = [f[first : first + places[j]] for f in made[len(piece) :]]
            entering = entering_states(made[j], factor, "col", col_count, group, width)
            parts_of.append((sum(map(sum, pieces[:i])) + offsets[j], rows, known[j], entering))

    y_col, silu, *known = call(
        functools.partial(col_local_kernel, **sizes),
        [
            pltpu.VMEM((tokens, channels), F32),
            pltpu.VMEM((tokens, channels), F32),
            pltpu.VMEM((tokens, 2 * heads), BF16),
            pltpu.VMEM((tokens, cols * state), BF16),
        ],
        0,
        specs=[None] * 6 + [any_spec],
    )(params, x, raw, maps, gate, skip.reshape(1, heads), before)
    w = call(
        functools.partial(col_out_kernel, heads=heads, width=width),
        pltpu.VMEM((tokens, channels), F32),
        0,
    )(col_entering, y_col, *known)

    back = []
    before = y_col
    for _, rows, known, entering in parts_of:
        y_row = call(
            functools.partial(row_out_kernel, heads=heads, width=width),
            [pltpu.VMEM((rows, channels), BF16)] * group,
            0,
            specs=[None] * 4 + [any_spec],
        )(entering, *known, before)
        back.append(exchange(y_row))
        before = col_entering

    which = [0, *range(group - 1, 0, -1)]
    mixed = None
    for i in range(len(parts_of)):
        first, rows = parts_of[i][:2]
        more = [] if mixed is None else [mixed]
        mixed = call(
            functools.partial(final_kernel, which=which, offset=first, share=share, **shared),
            shape((tokens, channels), BF16),
            0,
            specs=[None] * 3 + [any_spec] * len(more) + [None] * len(which),
            out_specs=any_spec,
            scratch_shapes=[
                pltpu.VMEM((len(which), rows, channels), BF16),
                pltpu.SemaphoreType.DMA((len(which),)),
            ],
            input_output_aliases={3: 0} if more else {},
        )(w, silu, norm_gain.reshape(1, channels), *more, *[back[i][j] for j in which])
    return mixed.reshape(x_in.shape)


def solution(mesh):
    tile = P("img", "row", "col", None)
    return jax.shard_map(
        functools.partial(body, row_count=mesh.shape["row"], col_count=mesh.shape["col"]),
        mesh=mesh,
        in_specs=(tile, tile, tile, tile, P("img"), P(), P(), P(), P()),
        out_specs=tile,
        check_vma=False,
    )
```

```python
import functools

import jax
import jax.numpy as jnp
from jax import lax
from jax.experimental import pallas as pl
from jax.experimental.pallas import tpu as pltpu
from jax.sharding import PartitionSpec as P

LANES = 128
GROUP = 4
PIECES = ((4,), (4,))
STRIP = 512
VMEM_LIMIT = 16 * 1024 * 1024
F32 = jnp.float32
BF16 = jnp.bfloat16


def dot(a, b):
    return jnp.dot(a, b, preferred_element_type=F32)


def iota(shape, dim):
    return lax.broadcasted_iota(jnp.int32, shape, dim)


def div(a, n):
    return lax.shift_right_logical(a, n.bit_length() - 1) if n & (n - 1) == 0 else a // n


def mod(a, n):
    return jnp.bitwise_and(a, n - 1) if n & (n - 1) == 0 else a % n


def parts(values, count):
    terms = []
    for _ in range(count):
        term = values.astype(BF16)
        terms.append(term)
        values = values - term.astype(F32)
    return jnp.concatenate(terms, axis=1)


def picks(heads, width, first, channels):
    row = iota((2 * heads, 1), 0)
    head = jnp.where(row >= heads, row - heads, row)
    return (head == div(first + iota((1, channels), 1), width)).astype(BF16)


def summed(mask, values):
    heads = values.shape[1]
    sums = dot(mask, parts(values, 3))
    return sums[:, :heads] + sums[:, heads : 2 * heads] + sums[:, 2 * heads :]


def step_sizes(raw, bias):
    shifted = raw.astype(F32) + bias
    return jnp.maximum(shifted, 0.0) + jnp.log1p(jnp.exp(-jnp.abs(shifted)))


def widen(maps, line, lines):
    state = maps.shape[1]
    places = lines * state
    copy = (mod(iota((1, places), 1), state) == iota((state, 1), 0)).astype(BF16)
    own = div(iota((1, places), 1), state) == line
    return jnp.where(own, dot(maps, copy), 0.0).astype(BF16)


class Scan:
    def __init__(self, order, lines, raw, bias, rates, b_map, c_map):
        tokens, self.heads = raw.shape
        self.lines, self.b_map, self.c_map = lines, b_map, c_map
        self.line, place = order(iota((tokens, 1), 0))
        self.line_in, place_in = order(iota((1, tokens), 1))
        self.lower = jnp.logical_and(self.line == self.line_in, place >= place_in)
        steps = step_sizes(raw, bias)
        self.decay = -rates * steps
        running = summed(self.lower.astype(BF16), self.decay)
        self.fade = parts(jnp.exp(running), 2)
        self.grow = parts(steps * jnp.exp(-running), 2)

    def ends(self):
        places = self.lines * self.b_map.shape[1]
        own = div(iota((places, 1), 0), self.b_map.shape[1]) == self.line_in
        return jnp.exp(summed(own.astype(BF16), self.decay))

    def into(self):
        return widen(self.b_map, self.line, self.lines).astype(F32).T.astype(BF16)

    def within(self):
        scores = lax.dot_general(
            self.c_map, self.b_map, (((1,), (1,)), ((), ())), preferred_element_type=F32
        )
        return jnp.where(self.lower, scores, 0.0).astype(BF16)

    def entry(self, follows):
        return jnp.where(follows, widen(self.c_map, self.line, self.lines), 0)


def partner(member, i, group):
    return member ^ i


def column_order(cols):
    return lambda token: (mod(token, cols), div(token, cols))


def row_order(cols, lines, member, group):
    def order(token):
        source = partner(member, div(token, cols * lines), group)
        return mod(div(token, cols), lines), source * cols + mod(token, cols)

    return order


def strips(channels):
    return [(first, min(STRIP, channels - first)) for first in range(0, channels, STRIP)]


def pack_kernel(
    x_ref, raw_ref, maps_ref, table_ref, rates_ref, raw, maps, table, rates, *refs, group, axis, heads, state
):
    sent, sems = refs[:-1], refs[-1]
    channels = x_ref.shape[1]
    share = x_ref.shape[0] // group
    member = mod(lax.axis_index(axis), group)
    moved = [(raw_ref, raw), (maps_ref, maps)]
    places = []
    offset = 0
    for i, out in enumerate(sent):
        rows = out.shape[0]
        first = partner(member, i % group, group) * share + offset
        part = pl.ds(pl.multiple_of(first, 16), rows)
        places.append((out, part))
        moved.append((x_ref.at[part, :], out.at[:, pl.ds(0, channels)]))
        if i % group == group - 1:
            offset += rows
    moved += [(table_ref, table), (rates_ref, rates)]
    copies = [pltpu.make_async_copy(a, b, sems.at[i]) for i, (a, b) in enumerate(moved)]
    for copy in copies:
        copy.start()
    for copy in copies[:2]:
        copy.wait()
    used = heads + 2 * state
    for out, part in places:
        out[:, channels : channels + heads] = raw[part, :heads]
        out[:, channels + heads : channels + used] = maps[part, : 2 * state]
        out[:, channels + used :] = jnp.zeros((out.shape[0], LANES - used), BF16)
    for copy in copies[2:]:
        copy.wait()


def params_kernel(index_ref, table_ref, rates_ref, params_ref):
    heads = rates_ref.shape[1]
    row = jnp.where(iota(table_ref.shape, 1) == index_ref[0], table_ref[...], 0.0)
    ones = jnp.ones((8, table_ref.shape[1]), BF16)
    bias = jnp.zeros((8, row.shape[0]), F32)
    for _ in range(3):
        term = row.astype(BF16)
        row = row - term.astype(F32)
        bias += lax.dot_general(ones, term, (((1,), (1,)), ((), ())), preferred_element_type=F32)
    params_ref[0:1, :] = bias[0:1, :]
    params_ref[1:2, :heads] = rates_ref[0:1, :]
    params_ref[1:2, heads:] = rates_ref[1:2, :]
    params_ref[2:, :] = jnp.zeros((6, 2 * heads), F32)


def row_scan(params_ref, blocks, member, cols, heads, state):
    channels = blocks[0].shape[1] - LANES
    tokens = blocks[0].shape[0] * len(blocks)
    lines = tokens // (cols * len(blocks))
    aux = jnp.concatenate([block[:, channels:] for block in blocks], axis=0)
    return Scan(
        row_order(cols, lines, member, len(blocks)),
        lines,
        aux[:, :heads],
        params_ref[0:1, :heads],
        params_ref[1:2, :heads],
        aux[:, heads : heads + state],
        aux[:, heads + state : heads + 2 * state],
    )


def col_scan(params_ref, raw_ref, maps_ref, cols, heads, state):
    return Scan(
        column_order(cols),
        cols,
        raw_ref[:, heads:],
        params_ref[0:1, heads:],
        params_ref[1:2, heads:],
        maps_ref[:, 2 * state : 3 * state],
        maps_ref[:, 3 * state :],
    )


def write_state(scan, tokens_of, width, channels, s_refs, factor_ref):
    ends = scan.ends()
    if factor_ref:
        factor_ref[0][...] = ends
    ends = parts(ends, 2)
    into = scan.into()
    for first, count in strips(channels):
        pick = picks(scan.heads, width, first, count)
        values = (tokens_of(first, count) * dot(scan.grow, pick)).astype(BF16)
        made = (dot(into, values) * dot(ends, pick)).astype(BF16)
        row = 0
        for s_ref in s_refs:
            s_ref[:, first : first + count] = made[row : row + s_ref.shape[0]]
            row += s_ref.shape[0]


def row_state_kernel(params_ref, *refs, group, count, axis, cols, heads, state, width):
    blocks, s_refs, factor_ref = refs[:group], refs[group + 1 : group + 1 + count], refs[group + 1 + count :]
    member = mod(lax.axis_index(axis), group)
    scan = row_scan(params_ref, [block[...] for block in blocks], member, cols, heads, state)
    tokens_of = lambda first, count: jnp.concatenate(
        [block[:, first : first + count] for block in blocks], axis=0
    ).astype(F32)
    write_state(scan, tokens_of, width, s_refs[0].shape[1], s_refs, factor_ref)


def col_state_kernel(params_ref, x_ref, raw_ref, maps_ref, _, s_ref, *factor_ref, cols, heads, state, width):
    scan = col_scan(params_ref, raw_ref, maps_ref, cols, heads, state)
    tokens_of = lambda first, count: x_ref[:, first : first + count].astype(F32)
    write_state(scan, tokens_of, width, s_ref.shape[1], [s_ref], factor_ref)


def row_local_kernel(params_ref, *refs, group, offset, axis, cols, heads, state, width):
    blocks, (y_ref, fade_ref, entry_ref) = refs[:group], refs[group + 1 :]
    rows = y_ref.shape[0] // group
    mine = slice(offset, offset + rows)
    member = mod(lax.axis_index(axis), group)
    scan = row_scan(params_ref, [block[mine, :] for block in blocks], member, cols, heads, state)
    mix = scan.within()
    fade_ref[...] = scan.fade
    entry_ref[...] = scan.entry(lax.axis_index(axis) >= group)
    for first, count in strips(y_ref.shape[1]):
        pick = picks(heads, width, first, count)
        part = slice(first, first + count)
        x = jnp.concatenate([block[mine, part] for block in blocks], axis=0).astype(F32)
        values = (x * dot(scan.grow, pick)).astype(BF16)
        y_ref[:, part] = dot(mix, values) * dot(scan.fade, pick)


def row_out_kernel(s_ref, y_ref, fade_ref, entry_ref, _, *outs, heads, width):
    rows = outs[0].shape[0]
    for first, count in strips(s_ref.shape[1]):
        pick = picks(heads, width, first, count)
        part = slice(first, first + count)
        y = y_ref[:, part] + dot(entry_ref[...], s_ref[:, part]) * dot(fade_ref[...], pick)
        for i, out in enumerate(outs):
            out[:, part] = y[i * rows : (i + 1) * rows].astype(BF16)


def col_local_kernel(
    params_ref, x_ref, raw_ref, maps_ref, gate_ref, skip_ref, _, y_ref, g_ref, fade_ref, entry_ref,
    *, cols, heads, state, width
):
    scan = col_scan(params_ref, raw_ref, maps_ref, cols, heads, state)
    mix = scan.within()
    fade_ref[...] = scan.fade
    entry_ref[...] = scan.entry(lax.axis_index("row") > 0)
    skips = parts(jnp.broadcast_to(skip_ref[...], (8, heads)), 2)
    for first, count in strips(x_ref.shape[1]):
        pick = picks(heads, width, first, count)
        part = slice(first, first + count)
        x = x_ref[:, part].astype(F32)
        values = (x * dot(scan.grow, pick)).astype(BF16)
        y_ref[:, part] = dot(mix, values) * dot(scan.fade, pick) + dot(skips, pick)[0:1, :] * x
        gate = gate_ref[:, part].astype(F32)
        g_ref[:, part] = gate / (1.0 + jnp.exp(-gate))


def col_out_kernel(s_ref, y_ref, fade_ref, entry_ref, w_ref, *, heads, width):
    for first, count in strips(s_ref.shape[1]):
        pick = picks(heads, width, first, count)
        part = slice(first, first + count)
        w_ref[:, part] = y_ref[:, part] + dot(entry_ref[...], s_ref[:, part]) * dot(fade_ref[...], pick)


def final_kernel(w_ref, g_ref, gain_ref, *refs, which, offset, group, axis, share):
    blocks, (out_ref, made, sems) = refs[-3 - len(which) : -3], refs[-3:]
    rows, channels = blocks[0].shape
    member = mod(lax.axis_index(axis), group)
    copies = []
    for i, block in zip(which, blocks):
        part = pl.ds(pl.multiple_of(partner(member, i, group) * share + offset, 16), rows)
        v = (block[...].astype(F32) + w_ref[part, :]) * g_ref[part, :]
        power = jnp.sum(v * v, axis=1, keepdims=True) / channels
        at = len(copies)
        made[at] = (v * lax.rsqrt(power + 1e-5) * gain_ref[...]).astype(BF16)
        copies.append(pltpu.make_async_copy(made.at[at], out_ref.at[part, :], sems.at[at]))
        copies[-1].start()
    for copy in copies:
        copy.wait()


def cost(micros):
    return pl.CostEstimate(flops=1024 + int(micros * 10**9), bytes_accessed=1024, transcendentals=0)


def call(kernel, out_shape, micros, specs=None, **more):
    if specs is not None:
        more["in_specs"] = [spec or pl.BlockSpec() for spec in specs]
    return pl.pallas_call(
        kernel,
        out_shape=out_shape,
        compiler_params=pltpu.CompilerParams(vmem_limit_bytes=VMEM_LIMIT),
        cost_estimate=cost(micros),
        **more,
    )


def entering_states(ends, factor, axis, size, stride, width):
    if size == stride:
        return ends
    onward = [(i, (i + stride) % size) for i in range(size)]
    entering = lax.ppermute(ends, axis, onward)
    for _ in range(size // stride - 2):
        follows = (lax.axis_index(axis) >= stride).astype(F32)
        decayed = follows * jnp.repeat(factor[0], width, axis=1) * entering.astype(F32)
        entering = lax.ppermute((ends.astype(F32) + decayed).astype(BF16), axis, onward)
    return entering


def body(x_in, gate_in, proj_bc, dt_raw, step_index, step_table, rates, skip, norm_gain, *, row_count, col_count):
    _, tile_rows, cols, channels = x_in.shape
    heads = skip.shape[0]
    width = channels // heads
    state = proj_bc.shape[-1] // 4
    tokens = tile_rows * cols
    group = GROUP
    while col_count % group:
        group //= 2
    share = tokens // group
    pieces = [[eighths * share // 8 for eighths in piece] for piece in PIECES]

    x = x_in.reshape(tokens, channels)
    gate = gate_in.reshape(tokens, channels)
    maps = proj_bc.reshape(tokens, 4 * state)
    raw = dt_raw.reshape(tokens, 2 * heads)
    sizes = dict(cols=cols, heads=heads, state=state, width=width)
    shared = dict(group=group, axis="col")
    shape = jax.ShapeDtypeStruct
    any_spec = pl.BlockSpec(memory_space=pl.ANY)

    given = [x, raw, maps, step_table.T, rates]
    raw, maps, table, rates, *packed = pl.pallas_call(
        functools.partial(pack_kernel, heads=heads, state=state, **shared),
        in_specs=[pl.BlockSpec(memory_space=pltpu.HBM)] * len(given),
        out_shape=[pltpu.VMEM(a.shape, a.dtype) for a in given[1:]]
        + [pltpu.VMEM((sum(piece), channels + LANES), BF16) for piece in pieces for _ in range(group)],
        scratch_shapes=[pltpu.SemaphoreType.DMA((len(given) - 1 + group * len(pieces),))],
        compiler_params=pltpu.CompilerParams(vmem_limit_bytes=VMEM_LIMIT),
        cost_estimate=cost(1),
    )(*[pltpu.with_memory_space_constraint(a, pltpu.HBM) for a in given])
    index, rates = lax.optimization_barrier((step_index, rates))
    params = pl.pallas_call(
        params_kernel,
        grid_spec=pltpu.PrefetchScalarGridSpec(
            num_scalar_prefetch=1,
            grid=(1,),
            in_specs=[
                pl.BlockSpec(table.shape, lambda i, index: (0, 0)),
                pl.BlockSpec(rates.shape, lambda i, index: (0, 0)),
            ],
            out_specs=pl.BlockSpec((8, 2 * heads), lambda i, index: (0, 0)),
        ),
        out_shape=shape((8, 2 * heads), F32),
        compiler_params=pltpu.CompilerParams(vmem_limit_bytes=VMEM_LIMIT),
        cost_estimate=cost(0),
    )(index, table, rates)

    def exchange(blocks):
        return [blocks[0]] + [
            lax.ppermute(blocks[i], "col", [(at, partner(at, i, group)) for at in range(col_count)])
            for i in range(1, group)
        ]

    def state_shapes(places, count):
        states = [pltpu.VMEM((rows, channels), BF16) for rows in places]
        return states + [shape((sum(places), heads), F32)] * (count > 2)

    got = [exchange(packed[i * group : (i + 1) * group]) for i in range(len(pieces))]

    def own_rows(i, before):
        known = []
        for j, rows in enumerate(pieces[i]):
            known.append(
                call(
                    functools.partial(row_local_kernel, offset=sum(pieces[i][:j]), **sizes, **shared),
                    [
                        pltpu.VMEM((group * rows, channels), F32),
                        pltpu.VMEM((group * rows, 2 * heads), BF16),
                        pltpu.VMEM((group * rows, rows // cols * state), BF16),
                    ],
                    2,
                    specs=[None] * (1 + group) + [any_spec],
                )(params, *got[i], before)
            )
            before = known[-1][1]
        return known, before

    def row_states(i, before):
        places = [rows // cols * state for rows in pieces[i]]
        made = call(
            functools.partial(row_state_kernel, count=len(places), **sizes, **shared),
            state_shapes(places, col_count // group),
            0,
            specs=[None] * (1 + group) + [any_spec],
        )(params, *got[i], before)
        entering = []
        for j, count in enumerate(places):
            first = sum(places[:j])
            factor = [f[first : first + count] for f in made[len(places) :]]
            entering.append(entering_states(made[j], factor, "col", col_count, group, width))
        return entering, made[0]

    known, entering = [None] * len(pieces), [None] * len(pieces)
    entering[0], before = row_states(0, params)
    col_made = call(
        functools.partial(col_state_kernel, **sizes),
        state_shapes([cols * state], row_count),
        0,
        specs=[None] * 4 + [any_spec],
    )(params, x, raw, maps, before)
    col_entering = entering_states(col_made[0], col_made[1:], "row", row_count, 1, width)
    before = col_made[0]
    y_col, silu, *col_known = call(
        functools.partial(col_local_kernel, **sizes),
        [
            pltpu.VMEM((tokens, channels), F32),
            pltpu.VMEM((tokens, channels), F32),
            pltpu.VMEM((tokens, 2 * heads), BF16),
            pltpu.VMEM((tokens, cols * state), BF16),
        ],
        2,
        specs=[None] * 6 + [any_spec],
    )(params, x, raw, maps, gate, skip.reshape(1, heads), before)
    before = y_col
    for i in range(1, len(pieces)):
        known[i], before = own_rows(i, before)
        entering[i], before = row_states(i, before)
    known[0], before = own_rows(0, before)
    w = call(
        functools.partial(col_out_kernel, heads=heads, width=width),
        pltpu.VMEM((tokens, channels), F32),
        0,
    )(col_entering, y_col, *col_known)
    parts_of = []
    for i, piece in enumerate(pieces):
        for j, rows in enumerate(piece):
            first = sum(map(sum, pieces[:i])) + sum(piece[:j])
            parts_of.append((first, rows, known[i][j], entering[i][j]))

    back = []
    for _, rows, known, entering in parts_of:
        y_row = call(
            functools.partial(row_out_kernel, heads=heads, width=width),
            [pltpu.VMEM((rows, channels), BF16)] * group,
            0,
            specs=[None] * 4 + [any_spec],
        )(entering, *known, before)
        back.append(exchange(y_row))
        before = col_entering

    which = [0, *range(group - 1, 0, -1)]
    mixed = None
    for i in range(len(parts_of)):
        first, rows = parts_of[i][:2]
        more = [] if mixed is None else [mixed]
        mixed = call(
            functools.partial(final_kernel, which=which, offset=first, share=share, **shared),
            shape((tokens, channels), BF16),
            0,
            specs=[None] * 3 + [any_spec] * len(more) + [None] * len(which),
            out_specs=any_spec,
            scratch_shapes=[
                pltpu.VMEM((len(which), rows, channels), BF16),
                pltpu.SemaphoreType.DMA((len(which),)),
            ],
            input_output_aliases={3: 0} if more else {},
        )(w, silu, norm_gain.reshape(1, channels), *more, *[back[i][j] for j in which])
    return mixed.reshape(x_in.shape)


def solution(mesh):
    tile = P("img", "row", "col", None)
    return jax.shard_map(
        functools.partial(body, row_count=mesh.shape["row"], col_count=mesh.shape["col"]),
        mesh=mesh,
        in_specs=(tile, tile, tile, tile, P("img"), P(), P(), P(), P()),
        out_specs=tile,
        check_vma=False,
    )
```

```python
import functools

import jax
import jax.numpy as jnp
from jax import lax
from jax.experimental import pallas as pl
from jax.experimental.pallas import tpu as pltpu
from jax.sharding import PartitionSpec as P

LANES = 128
GROUP = 4
PIECES = ((4,), (4,))
STRIP = 512
VMEM_LIMIT = 16 * 1024 * 1024
F32 = jnp.float32
BF16 = jnp.bfloat16


def dot(a, b):
    return jnp.dot(a, b, preferred_element_type=F32)


def iota(shape, dim):
    return lax.broadcasted_iota(jnp.int32, shape, dim)


def div(a, n):
    return lax.shift_right_logical(a, n.bit_length() - 1) if n & (n - 1) == 0 else a // n


def mod(a, n):
    return jnp.bitwise_and(a, n - 1) if n & (n - 1) == 0 else a % n


def parts(values, count):
    terms = []
    for _ in range(count):
        term = values.astype(BF16)
        terms.append(term)
        values = values - term.astype(F32)
    return jnp.concatenate(terms, axis=1)


def picks(heads, width, first, channels):
    row = iota((2 * heads, 1), 0)
    head = jnp.where(row >= heads, row - heads, row)
    return (head == div(first + iota((1, channels), 1), width)).astype(BF16)


def summed(mask, values):
    heads = values.shape[1]
    sums = dot(mask, parts(values, 3))
    return sums[:, :heads] + sums[:, heads : 2 * heads] + sums[:, 2 * heads :]


def step_sizes(raw, bias):
    shifted = raw.astype(F32) + bias
    return jnp.maximum(shifted, 0.0) + jnp.log1p(jnp.exp(-jnp.abs(shifted)))


def widen(maps, line, lines):
    state = maps.shape[1]
    places = lines * state
    copy = (mod(iota((1, places), 1), state) == iota((state, 1), 0)).astype(BF16)
    own = div(iota((1, places), 1), state) == line
    return jnp.where(own, dot(maps, copy), 0.0).astype(BF16)


class Scan:
    def __init__(self, order, lines, raw, bias, rates, b_map, c_map):
        tokens, self.heads = raw.shape
        self.lines, self.b_map, self.c_map = lines, b_map, c_map
        self.line, place = order(iota((tokens, 1), 0))
        self.line_in, place_in = order(iota((1, tokens), 1))
        self.lower = jnp.logical_and(self.line == self.line_in, place >= place_in)
        steps = step_sizes(raw, bias)
        self.decay = -rates * steps
        running = summed(self.lower.astype(BF16), self.decay)
        self.fade = parts(jnp.exp(running), 2)
        self.grow = parts(steps * jnp.exp(-running), 2)

    def ends(self):
        places = self.lines * self.b_map.shape[1]
        own = div(iota((places, 1), 0), self.b_map.shape[1]) == self.line_in
        return jnp.exp(summed(own.astype(BF16), self.decay))

    def into(self):
        return widen(self.b_map, self.line, self.lines).astype(F32).T.astype(BF16)

    def within(self):
        scores = lax.dot_general(
            self.c_map, self.b_map, (((1,), (1,)), ((), ())), preferred_element_type=F32
        )
        return jnp.where(self.lower, scores, 0.0).astype(BF16)

    def entry(self, follows):
        return jnp.where(follows, widen(self.c_map, self.line, self.lines), 0)


def partner(member, i, group):
    return member ^ i


def column_order(cols):
    return lambda token: (mod(token, cols), div(token, cols))


def row_order(cols, lines, member, group):
    def order(token):
        source = partner(member, div(token, cols * lines), group)
        return mod(div(token, cols), lines), source * cols + mod(token, cols)

    return order


def strips(channels):
    return [(first, min(STRIP, channels - first)) for first in range(0, channels, STRIP)]


def pack_kernel(
    x_ref, raw_ref, maps_ref, table_ref, rates_ref, raw, maps, table, rates, *refs, group, axis, heads, state
):
    sent, sems = refs[:-1], refs[-1]
    channels = x_ref.shape[1]
    share = x_ref.shape[0] // group
    member = mod(lax.axis_index(axis), group)
    moved = [(raw_ref, raw), (maps_ref, maps)]
    places = []
    offset = 0
    for i, out in enumerate(sent):
        rows = out.shape[0]
        first = partner(member, i % group, group) * share + offset
        part = pl.ds(pl.multiple_of(first, 16), rows)
        places.append((out, part))
        moved.append((x_ref.at[part, :], out.at[:, pl.ds(0, channels)]))
        if i % group == group - 1:
            offset += rows
    moved += [(table_ref, table), (rates_ref, rates)]
    copies = [pltpu.make_async_copy(a, b, sems.at[i]) for i, (a, b) in enumerate(moved)]
    for copy in copies:
        copy.start()
    for copy in copies[:2]:
        copy.wait()
    used = heads + 2 * state
    for out, part in places:
        out[:, channels : channels + heads] = raw[part, :heads]
        out[:, channels + heads : channels + used] = maps[part, : 2 * state]
        out[:, channels + used :] = jnp.zeros((out.shape[0], LANES - used), BF16)
    for copy in copies[2:]:
        copy.wait()


def params_kernel(index_ref, table_ref, rates_ref, params_ref):
    heads = rates_ref.shape[1]
    row = jnp.where(iota(table_ref.shape, 1) == index_ref[0], table_ref[...], 0.0)
    ones = jnp.ones((8, table_ref.shape[1]), BF16)
    bias = jnp.zeros((8, row.shape[0]), F32)
    for _ in range(3):
        term = row.astype(BF16)
        row = row - term.astype(F32)
        bias += lax.dot_general(ones, term, (((1,), (1,)), ((), ())), preferred_element_type=F32)
    params_ref[0:1, :] = bias[0:1, :]
    params_ref[1:2, :heads] = rates_ref[0:1, :]
    params_ref[1:2, heads:] = rates_ref[1:2, :]
    params_ref[2:, :] = jnp.zeros((6, 2 * heads), F32)


def row_scan(params_ref, blocks, member, cols, heads, state):
    channels = blocks[0].shape[1] - LANES
    tokens = blocks[0].shape[0] * len(blocks)
    lines = tokens // (cols * len(blocks))
    aux = jnp.concatenate([block[:, channels:] for block in blocks], axis=0)
    return Scan(
        row_order(cols, lines, member, len(blocks)),
        lines,
        aux[:, :heads],
        params_ref[0:1, :heads],
        params_ref[1:2, :heads],
        aux[:, heads : heads + state],
        aux[:, heads + state : heads + 2 * state],
    )


def col_scan(params_ref, raw_ref, maps_ref, cols, heads, state):
    return Scan(
        column_order(cols),
        cols,
        raw_ref[:, heads:],
        params_ref[0:1, heads:],
        params_ref[1:2, heads:],
        maps_ref[:, 2 * state : 3 * state],
        maps_ref[:, 3 * state :],
    )


def write_state(scan, tokens_of, width, channels, s_refs, factor_ref):
    ends = scan.ends()
    if factor_ref:
        factor_ref[0][...] = ends
    ends = parts(ends, 2)
    into = scan.into()
    for first, count in strips(channels):
        pick = picks(scan.heads, width, first, count)
        values = (tokens_of(first, count) * dot(scan.grow, pick)).astype(BF16)
        made = (dot(into, values) * dot(ends, pick)).astype(BF16)
        row = 0
        for s_ref in s_refs:
            s_ref[:, first : first + count] = made[row : row + s_ref.shape[0]]
            row += s_ref.shape[0]


def row_state_kernel(params_ref, *refs, group, count, axis, cols, heads, state, width):
    blocks, s_refs, factor_ref = refs[:group], refs[group + 1 : group + 1 + count], refs[group + 1 + count :]
    member = mod(lax.axis_index(axis), group)
    scan = row_scan(params_ref, [block[...] for block in blocks], member, cols, heads, state)
    tokens_of = lambda first, count: jnp.concatenate(
        [block[:, first : first + count] for block in blocks], axis=0
    ).astype(F32)
    write_state(scan, tokens_of, width, s_refs[0].shape[1], s_refs, factor_ref)


def col_state_kernel(params_ref, x_ref, raw_ref, maps_ref, _, s_ref, *factor_ref, cols, heads, state, width):
    scan = col_scan(params_ref, raw_ref, maps_ref, cols, heads, state)
    tokens_of = lambda first, count: x_ref[:, first : first + count].astype(F32)
    write_state(scan, tokens_of, width, s_ref.shape[1], [s_ref], factor_ref)


def row_local_kernel(params_ref, *refs, group, offset, axis, cols, heads, state, width):
    blocks, (y_ref, fade_ref, entry_ref) = refs[:group], refs[group + 1 :]
    rows = y_ref.shape[0] // group
    mine = slice(offset, offset + rows)
    member = mod(lax.axis_index(axis), group)
    scan = row_scan(params_ref, [block[mine, :] for block in blocks], member, cols, heads, state)
    mix = scan.within()
    fade_ref[...] = scan.fade
    entry_ref[...] = scan.entry(lax.axis_index(axis) >= group)
    for first, count in strips(y_ref.shape[1]):
        pick = picks(heads, width, first, count)
        part = slice(first, first + count)
        x = jnp.concatenate([block[mine, part] for block in blocks], axis=0).astype(F32)
        values = (x * dot(scan.grow, pick)).astype(BF16)
        y_ref[:, part] = dot(mix, values) * dot(scan.fade, pick)


def row_out_kernel(s_ref, y_ref, fade_ref, entry_ref, _, *outs, heads, width):
    rows = outs[0].shape[0]
    for first, count in strips(s_ref.shape[1]):
        pick = picks(heads, width, first, count)
        part = slice(first, first + count)
        y = y_ref[:, part] + dot(entry_ref[...], s_ref[:, part]) * dot(fade_ref[...], pick)
        for i, out in enumerate(outs):
            out[:, part] = y[i * rows : (i + 1) * rows].astype(BF16)


def col_local_kernel(
    params_ref, x_ref, raw_ref, maps_ref, gate_ref, skip_ref, _, y_ref, g_ref, fade_ref, entry_ref,
    *, cols, heads, state, width
):
    scan = col_scan(params_ref, raw_ref, maps_ref, cols, heads, state)
    mix = scan.within()
    fade_ref[...] = scan.fade
    entry_ref[...] = scan.entry(lax.axis_index("row") > 0)
    skips = parts(jnp.broadcast_to(skip_ref[...], (8, heads)), 2)
    for first, count in strips(x_ref.shape[1]):
        pick = picks(heads, width, first, count)
        part = slice(first, first + count)
        x = x_ref[:, part].astype(F32)
        values = (x * dot(scan.grow, pick)).astype(BF16)
        y_ref[:, part] = dot(mix, values) * dot(scan.fade, pick) + dot(skips, pick)[0:1, :] * x
        gate = gate_ref[:, part].astype(F32)
        g_ref[:, part] = gate / (1.0 + jnp.exp(-gate))


def col_out_kernel(s_ref, y_ref, fade_ref, entry_ref, w_ref, *, heads, width):
    for first, count in strips(s_ref.shape[1]):
        pick = picks(heads, width, first, count)
        part = slice(first, first + count)
        w_ref[:, part] = y_ref[:, part] + dot(entry_ref[...], s_ref[:, part]) * dot(fade_ref[...], pick)


def final_kernel(w_ref, g_ref, gain_ref, *refs, which, offset, group, axis, share):
    blocks, (out_ref, made, sems) = refs[-3 - len(which) : -3], refs[-3:]
    rows, channels = blocks[0].shape
    member = mod(lax.axis_index(axis), group)
    copies = []
    for i, block in zip(which, blocks):
        part = pl.ds(pl.multiple_of(partner(member, i, group) * share + offset, 16), rows)
        v = (block[...].astype(F32) + w_ref[part, :]) * g_ref[part, :]
        power = jnp.sum(v * v, axis=1, keepdims=True) / channels
        at = len(copies)
        made[at] = (v * lax.rsqrt(power + 1e-5) * gain_ref[...]).astype(BF16)
        copies.append(pltpu.make_async_copy(made.at[at], out_ref.at[part, :], sems.at[at]))
        copies[-1].start()
    for copy in copies:
        copy.wait()


def cost(micros):
    return pl.CostEstimate(flops=1024 + int(micros * 10**9), bytes_accessed=1024, transcendentals=0)


def call(kernel, out_shape, micros, specs=None, **more):
    if specs is not None:
        more["in_specs"] = [spec or pl.BlockSpec() for spec in specs]
    return pl.pallas_call(
        kernel,
        out_shape=out_shape,
        compiler_params=pltpu.CompilerParams(vmem_limit_bytes=VMEM_LIMIT),
        cost_estimate=cost(micros),
        **more,
    )


def entering_states(ends, factor, axis, size, stride, width, wrap=True):
    if size == stride:
        return ends
    onward = [(i, (i + stride) % size) for i in range(size if wrap else size - stride)]
    entering = lax.ppermute(ends, axis, onward)
    for _ in range(size // stride - 2):
        follows = (lax.axis_index(axis) >= stride).astype(F32)
        decayed = follows * jnp.repeat(factor[0], width, axis=1) * entering.astype(F32)
        entering = lax.ppermute((ends.astype(F32) + decayed).astype(BF16), axis, onward)
    return entering


def body(x_in, gate_in, proj_bc, dt_raw, step_index, step_table, rates, skip, norm_gain, *, row_count, col_count):
    _, tile_rows, cols, channels = x_in.shape
    heads = skip.shape[0]
    width = channels // heads
    state = proj_bc.shape[-1] // 4
    tokens = tile_rows * cols
    group = GROUP
    while col_count % group:
        group //= 2
    share = tokens // group
    pieces = [[eighths * share // 8 for eighths in piece] for piece in PIECES]

    x = x_in.reshape(tokens, channels)
    gate = gate_in.reshape(tokens, channels)
    maps = proj_bc.reshape(tokens, 4 * state)
    raw = dt_raw.reshape(tokens, 2 * heads)
    sizes = dict(cols=cols, heads=heads, state=state, width=width)
    shared = dict(group=group, axis="col")
    shape = jax.ShapeDtypeStruct
    any_spec = pl.BlockSpec(memory_space=pl.ANY)

    given = [x, raw, maps, step_table.T, rates]
    raw, maps, table, rates, *packed = pl.pallas_call(
        functools.partial(pack_kernel, heads=heads, state=state, **shared),
        in_specs=[pl.BlockSpec(memory_space=pltpu.HBM)] * len(given),
        out_shape=[pltpu.VMEM(a.shape, a.dtype) for a in given[1:]]
        + [pltpu.VMEM((sum(piece), channels + LANES), BF16) for piece in pieces for _ in range(group)],
        scratch_shapes=[pltpu.SemaphoreType.DMA((len(given) - 1 + group * len(pieces),))],
        compiler_params=pltpu.CompilerParams(vmem_limit_bytes=VMEM_LIMIT),
        cost_estimate=cost(1),
    )(*[pltpu.with_memory_space_constraint(a, pltpu.HBM) for a in given])
    index, rates = lax.optimization_barrier((step_index, rates))
    params = pl.pallas_call(
        params_kernel,
        grid_spec=pltpu.PrefetchScalarGridSpec(
            num_scalar_prefetch=1,
            grid=(1,),
            in_specs=[
                pl.BlockSpec(table.shape, lambda i, index: (0, 0)),
                pl.BlockSpec(rates.shape, lambda i, index: (0, 0)),
            ],
            out_specs=pl.BlockSpec((8, 2 * heads), lambda i, index: (0, 0)),
        ),
        out_shape=shape((8, 2 * heads), F32),
        compiler_params=pltpu.CompilerParams(vmem_limit_bytes=VMEM_LIMIT),
        cost_estimate=cost(0),
    )(index, table, rates)

    def exchange(blocks):
        return [blocks[0]] + [
            lax.ppermute(blocks[i], "col", [(at, partner(at, i, group)) for at in range(col_count)])
            for i in range(1, group)
        ]

    def state_shapes(places, count):
        states = [pltpu.VMEM((rows, channels), BF16) for rows in places]
        return states + [shape((sum(places), heads), F32)] * (count > 2)

    got = [exchange(packed[i * group : (i + 1) * group]) for i in range(len(pieces))]

    def own_rows(i, before):
        known = []
        for j, rows in enumerate(pieces[i]):
            known.append(
                call(
                    functools.partial(row_local_kernel, offset=sum(pieces[i][:j]), **sizes, **shared),
                    [
                        pltpu.VMEM((group * rows, channels), F32),
                        pltpu.VMEM((group * rows, 2 * heads), BF16),
                        pltpu.VMEM((group * rows, rows // cols * state), BF16),
                    ],
                    2,
                    specs=[None] * (1 + group) + [any_spec],
                )(params, *got[i], before)
            )
            before = known[-1][1]
        return known, before

    def row_states(i, before):
        places = [rows // cols * state for rows in pieces[i]]
        made = call(
            functools.partial(row_state_kernel, count=len(places), **sizes, **shared),
            state_shapes(places, col_count // group),
            0,
            specs=[None] * (1 + group) + [any_spec],
        )(params, *got[i], before)
        entering = []
        for j, count in enumerate(places):
            first = sum(places[:j])
            factor = [f[first : first + count] for f in made[len(places) :]]
            entering.append(entering_states(made[j], factor, "col", col_count, group, width, wrap=i == 0))
        return entering, made[0]

    known, entering = [None] * len(pieces), [None] * len(pieces)
    entering[0], before = row_states(0, params)
    col_made = call(
        functools.partial(col_state_kernel, **sizes),
        state_shapes([cols * state], row_count),
        0,
        specs=[None] * 4 + [any_spec],
    )(params, x, raw, maps, before)
    col_entering = entering_states(col_made[0], col_made[1:], "row", row_count, 1, width)
    before = col_made[0]
    y_col, silu, *col_known = call(
        functools.partial(col_local_kernel, **sizes),
        [
            pltpu.VMEM((tokens, channels), F32),
            pltpu.VMEM((tokens, channels), F32),
            pltpu.VMEM((tokens, 2 * heads), BF16),
            pltpu.VMEM((tokens, cols * state), BF16),
        ],
        2,
        specs=[None] * 6 + [any_spec],
    )(params, x, raw, maps, gate, skip.reshape(1, heads), before)
    before = y_col
    for i in range(1, len(pieces)):
        known[i], before = own_rows(i, before)
        entering[i], before = row_states(i, before)
    known[0], before = own_rows(0, before)
    w = call(
        functools.partial(col_out_kernel, heads=heads, width=width),
        pltpu.VMEM((tokens, channels), F32),
        0,
    )(col_entering, y_col, *col_known)
    parts_of = []
    for i, piece in enumerate(pieces):
        for j, rows in enumerate(piece):
            first = sum(map(sum, pieces[:i])) + sum(piece[:j])
            parts_of.append((first, rows, known[i][j], entering[i][j]))

    back = []
    for _, rows, known, entering in parts_of:
        y_row = call(
            functools.partial(row_out_kernel, heads=heads, width=width),
            [pltpu.VMEM((rows, channels), BF16)] * group,
            0,
            specs=[None] * 4 + [any_spec],
        )(entering, *known, before)
        back.append(exchange(y_row))
        before = col_entering

    which = [0, *range(group - 1, 0, -1)]
    mixed = None
    for i in range(len(parts_of)):
        first, rows = parts_of[i][:2]
        more = [] if mixed is None else [mixed]
        mixed = call(
            functools.partial(final_kernel, which=which, offset=first, share=share, **shared),
            shape((tokens, channels), BF16),
            0,
            specs=[None] * 3 + [any_spec] * len(more) + [None] * len(which),
            out_specs=any_spec,
            scratch_shapes=[
                pltpu.VMEM((len(which), rows, channels), BF16),
                pltpu.SemaphoreType.DMA((len(which),)),
            ],
            input_output_aliases={3: 0} if more else {},
        )(w, silu, norm_gain.reshape(1, channels), *more, *[back[i][j] for j in which])
    return mixed.reshape(x_in.shape)


def solution(mesh):
    tile = P("img", "row", "col", None)
    return jax.shard_map(
        functools.partial(body, row_count=mesh.shape["row"], col_count=mesh.shape["col"]),
        mesh=mesh,
        in_specs=(tile, tile, tile, tile, P("img"), P(), P(), P(), P()),
        out_specs=tile,
        check_vma=False,
    )
```

```python
import functools

import jax
import jax.numpy as jnp
from jax import lax
from jax.experimental import pallas as pl
from jax.experimental.pallas import tpu as pltpu
from jax.sharding import PartitionSpec as P

LANES = 128
GROUP = 4
PIECES = ((4,), (4,))
STRIP = 512
VMEM_LIMIT = 16 * 1024 * 1024
F32 = jnp.float32
BF16 = jnp.bfloat16


def dot(a, b):
    return jnp.dot(a, b, preferred_element_type=F32)


def iota(shape, dim):
    return lax.broadcasted_iota(jnp.int32, shape, dim)


def div(a, n):
    return lax.shift_right_logical(a, n.bit_length() - 1) if n & (n - 1) == 0 else a // n


def mod(a, n):
    return jnp.bitwise_and(a, n - 1) if n & (n - 1) == 0 else a % n


def parts(values, count):
    terms = []
    for _ in range(count):
        term = values.astype(BF16)
        terms.append(term)
        values = values - term.astype(F32)
    return jnp.concatenate(terms, axis=1)


def picks(heads, width, first, channels):
    row = iota((2 * heads, 1), 0)
    head = jnp.where(row >= heads, row - heads, row)
    return (head == div(first + iota((1, channels), 1), width)).astype(BF16)


def summed(mask, values):
    heads = values.shape[1]
    sums = dot(mask, parts(values, 3))
    return sums[:, :heads] + sums[:, heads : 2 * heads] + sums[:, 2 * heads :]


def step_sizes(raw, bias):
    shifted = raw.astype(F32) + bias
    return jnp.maximum(shifted, 0.0) + jnp.log1p(jnp.exp(-jnp.abs(shifted)))


def widen(maps, line, lines):
    state = maps.shape[1]
    places = lines * state
    copy = (mod(iota((1, places), 1), state) == iota((state, 1), 0)).astype(BF16)
    own = div(iota((1, places), 1), state) == line
    return jnp.where(own, dot(maps, copy), 0.0).astype(BF16)


class Scan:
    def __init__(self, order, lines, raw, bias, rates, b_map, c_map):
        tokens, self.heads = raw.shape
        self.lines, self.b_map, self.c_map = lines, b_map, c_map
        self.line, place = order(iota((tokens, 1), 0))
        self.line_in, place_in = order(iota((1, tokens), 1))
        self.lower = jnp.logical_and(self.line == self.line_in, place >= place_in)
        steps = step_sizes(raw, bias)
        self.decay = -rates * steps
        running = summed(self.lower.astype(BF16), self.decay)
        self.fade = parts(jnp.exp(running), 2)
        self.grow = parts(steps * jnp.exp(-running), 2)

    def ends(self):
        places = self.lines * self.b_map.shape[1]
        own = div(iota((places, 1), 0), self.b_map.shape[1]) == self.line_in
        return jnp.exp(summed(own.astype(BF16), self.decay))

    def into(self):
        return widen(self.b_map, self.line, self.lines).astype(F32).T.astype(BF16)

    def within(self):
        scores = lax.dot_general(
            self.c_map, self.b_map, (((1,), (1,)), ((), ())), preferred_element_type=F32
        )
        return jnp.where(self.lower, scores, 0.0).astype(BF16)

    def entry(self, follows):
        return jnp.where(follows, widen(self.c_map, self.line, self.lines), 0)


def partner(member, i, group):
    return member ^ i


def column_order(cols):
    return lambda token: (mod(token, cols), div(token, cols))


def row_order(cols, lines, member, group):
    def order(token):
        source = partner(member, div(token, cols * lines), group)
        return mod(div(token, cols), lines), source * cols + mod(token, cols)

    return order


def strips(channels):
    return [(first, min(STRIP, channels - first)) for first in range(0, channels, STRIP)]


def pack_kernel(
    x_ref, raw_ref, maps_ref, table_ref, rates_ref, raw, maps, table, rates, *refs, group, axis, heads, state
):
    sent, sems = refs[:-1], refs[-1]
    channels = x_ref.shape[1]
    share = x_ref.shape[0] // group
    member = mod(lax.axis_index(axis), group)
    moved = [(raw_ref, raw), (maps_ref, maps)]
    places = []
    offset = 0
    for i, out in enumerate(sent):
        rows = out.shape[0]
        first = partner(member, i % group, group) * share + offset
        part = pl.ds(pl.multiple_of(first, 16), rows)
        places.append((out, part))
        moved.append((x_ref.at[part, :], out.at[:, pl.ds(0, channels)]))
        if i % group == group - 1:
            offset += rows
    moved += [(table_ref, table), (rates_ref, rates)]
    copies = [pltpu.make_async_copy(a, b, sems.at[i]) for i, (a, b) in enumerate(moved)]
    for copy in copies:
        copy.start()
    for copy in copies[:2]:
        copy.wait()
    used = heads + 2 * state
    for out, part in places:
        out[:, channels : channels + heads] = raw[part, :heads]
        out[:, channels + heads : channels + used] = maps[part, : 2 * state]
        out[:, channels + used :] = jnp.zeros((out.shape[0], LANES - used), BF16)
    for copy in copies[2:]:
        copy.wait()


def params_kernel(index_ref, table_ref, rates_ref, params_ref):
    heads = rates_ref.shape[1]
    row = jnp.where(iota(table_ref.shape, 1) == index_ref[0], table_ref[...], 0.0)
    ones = jnp.ones((8, table_ref.shape[1]), BF16)
    bias = jnp.zeros((8, row.shape[0]), F32)
    for _ in range(3):
        term = row.astype(BF16)
        row = row - term.astype(F32)
        bias += lax.dot_general(ones, term, (((1,), (1,)), ((), ())), preferred_element_type=F32)
    params_ref[0:1, :] = bias[0:1, :]
    params_ref[1:2, :heads] = rates_ref[0:1, :]
    params_ref[1:2, heads:] = rates_ref[1:2, :]
    params_ref[2:, :] = jnp.zeros((6, 2 * heads), F32)


def row_scan(params_ref, blocks, member, cols, heads, state):
    channels = blocks[0].shape[1] - LANES
    tokens = blocks[0].shape[0] * len(blocks)
    lines = tokens // (cols * len(blocks))
    aux = jnp.concatenate([block[:, channels:] for block in blocks], axis=0)
    return Scan(
        row_order(cols, lines, member, len(blocks)),
        lines,
        aux[:, :heads],
        params_ref[0:1, :heads],
        params_ref[1:2, :heads],
        aux[:, heads : heads + state],
        aux[:, heads + state : heads + 2 * state],
    )


def col_scan(params_ref, raw_ref, maps_ref, cols, heads, state):
    return Scan(
        column_order(cols),
        cols,
        raw_ref[:, heads:],
        params_ref[0:1, heads:],
        params_ref[1:2, heads:],
        maps_ref[:, 2 * state : 3 * state],
        maps_ref[:, 3 * state :],
    )


def write_state(scan, tokens_of, width, channels, s_refs, factor_ref):
    ends = scan.ends()
    if factor_ref:
        factor_ref[0][...] = ends
    ends = parts(ends, 2)
    into = scan.into()
    for first, count in strips(channels):
        pick = picks(scan.heads, width, first, count)
        values = (tokens_of(first, count) * dot(scan.grow, pick)).astype(BF16)
        made = (dot(into, values) * dot(ends, pick)).astype(BF16)
        row = 0
        for s_ref in s_refs:
            s_ref[:, first : first + count] = made[row : row + s_ref.shape[0]]
            row += s_ref.shape[0]


def row_state_kernel(params_ref, *refs, group, count, axis, cols, heads, state, width):
    blocks, s_refs, factor_ref = refs[:group], refs[group + 1 : group + 1 + count], refs[group + 1 + count :]
    member = mod(lax.axis_index(axis), group)
    scan = row_scan(params_ref, [block[...] for block in blocks], member, cols, heads, state)
    tokens_of = lambda first, count: jnp.concatenate(
        [block[:, first : first + count] for block in blocks], axis=0
    ).astype(F32)
    write_state(scan, tokens_of, width, s_refs[0].shape[1], s_refs, factor_ref)


def col_state_kernel(params_ref, x_ref, raw_ref, maps_ref, _, s_ref, *factor_ref, cols, heads, state, width):
    scan = col_scan(params_ref, raw_ref, maps_ref, cols, heads, state)
    tokens_of = lambda first, count: x_ref[:, first : first + count].astype(F32)
    write_state(scan, tokens_of, width, s_ref.shape[1], [s_ref], factor_ref)


def row_local_kernel(params_ref, *refs, group, offset, axis, cols, heads, state, width):
    blocks, (y_ref, fade_ref, entry_ref) = refs[:group], refs[group + 1 :]
    rows = y_ref.shape[0] // group
    mine = slice(offset, offset + rows)
    member = mod(lax.axis_index(axis), group)
    scan = row_scan(params_ref, [block[mine, :] for block in blocks], member, cols, heads, state)
    mix = scan.within()
    fade_ref[...] = scan.fade
    entry_ref[...] = scan.entry(lax.axis_index(axis) >= group)
    for first, count in strips(y_ref.shape[1]):
        pick = picks(heads, width, first, count)
        part = slice(first, first + count)
        x = jnp.concatenate([block[mine, part] for block in blocks], axis=0).astype(F32)
        values = (x * dot(scan.grow, pick)).astype(BF16)
        y_ref[:, part] = dot(mix, values) * dot(scan.fade, pick)


def row_out_kernel(s_ref, y_ref, fade_ref, entry_ref, _, *outs, heads, width):
    rows = outs[0].shape[0]
    for first, count in strips(s_ref.shape[1]):
        pick = picks(heads, width, first, count)
        part = slice(first, first + count)
        y = y_ref[:, part] + dot(entry_ref[...], s_ref[:, part]) * dot(fade_ref[...], pick)
        for i, out in enumerate(outs):
            out[:, part] = y[i * rows : (i + 1) * rows].astype(BF16)


def col_local_kernel(
    params_ref, x_ref, raw_ref, maps_ref, gate_ref, skip_ref, _, y_ref, g_ref, fade_ref, entry_ref,
    *, cols, heads, state, width
):
    scan = col_scan(params_ref, raw_ref, maps_ref, cols, heads, state)
    mix = scan.within()
    fade_ref[...] = scan.fade
    entry_ref[...] = scan.entry(lax.axis_index("row") > 0)
    skips = parts(jnp.broadcast_to(skip_ref[...], (8, heads)), 2)
    for first, count in strips(x_ref.shape[1]):
        pick = picks(heads, width, first, count)
        part = slice(first, first + count)
        x = x_ref[:, part].astype(F32)
        values = (x * dot(scan.grow, pick)).astype(BF16)
        y_ref[:, part] = dot(mix, values) * dot(scan.fade, pick) + dot(skips, pick)[0:1, :] * x
        gate = gate_ref[:, part].astype(F32)
        g_ref[:, part] = gate / (1.0 + jnp.exp(-gate))


def col_out_kernel(s_ref, y_ref, fade_ref, entry_ref, w_ref, *, heads, width):
    for first, count in strips(s_ref.shape[1]):
        pick = picks(heads, width, first, count)
        part = slice(first, first + count)
        w_ref[:, part] = y_ref[:, part] + dot(entry_ref[...], s_ref[:, part]) * dot(fade_ref[...], pick)


def final_kernel(w_ref, g_ref, gain_ref, *refs, which, offset, group, axis, share):
    blocks, (out_ref, made, sems) = refs[-3 - len(which) : -3], refs[-3:]
    rows, channels = blocks[0].shape
    member = mod(lax.axis_index(axis), group)
    copies = []
    for i, block in zip(which, blocks):
        part = pl.ds(pl.multiple_of(partner(member, i, group) * share + offset, 16), rows)
        v = (block[...].astype(F32) + w_ref[part, :]) * g_ref[part, :]
        power = jnp.sum(v * v, axis=1, keepdims=True) / channels
        at = len(copies)
        made[at] = (v * lax.rsqrt(power + 1e-5) * gain_ref[...]).astype(BF16)
        copies.append(pltpu.make_async_copy(made.at[at], out_ref.at[part, :], sems.at[at]))
        copies[-1].start()
    for copy in copies:
        copy.wait()


def cost(micros):
    return pl.CostEstimate(flops=1024 + int(micros * 10**9), bytes_accessed=1024, transcendentals=0)


def call(kernel, out_shape, micros, specs=None, **more):
    if specs is not None:
        more["in_specs"] = [spec or pl.BlockSpec() for spec in specs]
    return pl.pallas_call(
        kernel,
        out_shape=out_shape,
        compiler_params=pltpu.CompilerParams(vmem_limit_bytes=VMEM_LIMIT),
        cost_estimate=cost(micros),
        **more,
    )


def entering_states(ends, factor, axis, size, stride, width, wrap=True):
    if size == stride:
        return ends
    onward = [(i, (i + stride) % size) for i in range(size if wrap else size - stride)]
    entering = lax.ppermute(ends, axis, onward)
    for _ in range(size // stride - 2):
        follows = (lax.axis_index(axis) >= stride).astype(F32)
        decayed = follows * jnp.repeat(factor[0], width, axis=1) * entering.astype(F32)
        entering = lax.ppermute((ends.astype(F32) + decayed).astype(BF16), axis, onward)
    return entering


def body(x_in, gate_in, proj_bc, dt_raw, step_index, step_table, rates, skip, norm_gain, *, row_count, col_count):
    _, tile_rows, cols, channels = x_in.shape
    heads = skip.shape[0]
    width = channels // heads
    state = proj_bc.shape[-1] // 4
    tokens = tile_rows * cols
    group = GROUP
    while col_count % group:
        group //= 2
    share = tokens // group
    pieces = [[eighths * share // 8 for eighths in piece] for piece in PIECES]

    x = x_in.reshape(tokens, channels)
    gate = gate_in.reshape(tokens, channels)
    maps = proj_bc.reshape(tokens, 4 * state)
    raw = dt_raw.reshape(tokens, 2 * heads)
    sizes = dict(cols=cols, heads=heads, state=state, width=width)
    shared = dict(group=group, axis="col")
    shape = jax.ShapeDtypeStruct
    any_spec = pl.BlockSpec(memory_space=pl.ANY)

    given = [x, raw, maps, step_table.T, rates]
    raw, maps, table, rates, *packed = pl.pallas_call(
        functools.partial(pack_kernel, heads=heads, state=state, **shared),
        in_specs=[pl.BlockSpec(memory_space=pltpu.HBM)] * len(given),
        out_shape=[pltpu.VMEM(a.shape, a.dtype) for a in given[1:]]
        + [pltpu.VMEM((sum(piece), channels + LANES), BF16) for piece in pieces for _ in range(group)],
        scratch_shapes=[pltpu.SemaphoreType.DMA((len(given) - 1 + group * len(pieces),))],
        compiler_params=pltpu.CompilerParams(vmem_limit_bytes=VMEM_LIMIT),
        cost_estimate=cost(1),
    )(*[pltpu.with_memory_space_constraint(a, pltpu.HBM) for a in given])
    index, rates = lax.optimization_barrier((step_index, rates))
    params = pl.pallas_call(
        params_kernel,
        grid_spec=pltpu.PrefetchScalarGridSpec(
            num_scalar_prefetch=1,
            grid=(1,),
            in_specs=[
                pl.BlockSpec(table.shape, lambda i, index: (0, 0)),
                pl.BlockSpec(rates.shape, lambda i, index: (0, 0)),
            ],
            out_specs=pl.BlockSpec((8, 2 * heads), lambda i, index: (0, 0)),
        ),
        out_shape=shape((8, 2 * heads), F32),
        compiler_params=pltpu.CompilerParams(vmem_limit_bytes=VMEM_LIMIT),
        cost_estimate=cost(0),
    )(index, table, rates)

    def exchange(blocks):
        return [blocks[0]] + [
            lax.ppermute(blocks[i], "col", [(at, partner(at, i, group)) for at in range(col_count)])
            for i in range(1, group)
        ]

    def state_shapes(places, count):
        states = [pltpu.VMEM((rows, channels), BF16) for rows in places]
        return states + [shape((sum(places), heads), F32)] * (count > 2)

    got = [exchange(packed[i * group : (i + 1) * group]) for i in range(len(pieces))]

    def own_rows(i, before):
        known = []
        for j, rows in enumerate(pieces[i]):
            known.append(
                call(
                    functools.partial(row_local_kernel, offset=sum(pieces[i][:j]), **sizes, **shared),
                    [
                        pltpu.VMEM((group * rows, channels), F32),
                        pltpu.VMEM((group * rows, 2 * heads), BF16),
                        pltpu.VMEM((group * rows, rows // cols * state), BF16),
                    ],
                    2,
                    specs=[None] * (1 + group) + [any_spec],
                )(params, *got[i], before)
            )
            before = known[-1][1]
        return known, before

    def row_states(i, before):
        places = [rows // cols * state for rows in pieces[i]]
        made = call(
            functools.partial(row_state_kernel, count=len(places), **sizes, **shared),
            state_shapes(places, col_count // group),
            0,
            specs=[None] * (1 + group) + [any_spec],
        )(params, *got[i], before)
        entering = []
        for j, count in enumerate(places):
            first = sum(places[:j])
            factor = [f[first : first + count] for f in made[len(places) :]]
            entering.append(entering_states(made[j], factor, "col", col_count, group, width, wrap=i == 0))
        return entering, made[0]

    known, entering = [None] * len(pieces), [None] * len(pieces)
    entering[0], before = row_states(0, params)
    col_made = call(
        functools.partial(col_state_kernel, **sizes),
        state_shapes([cols * state], row_count),
        0,
        specs=[None] * 4 + [any_spec],
    )(params, x, raw, maps, before)
    col_entering = entering_states(col_made[0], col_made[1:], "row", row_count, 1, width)
    before = col_made[0]
    known[0], before = own_rows(0, before)
    for i in range(1, len(pieces)):
        known[i], before = own_rows(i, before)
        entering[i], before = row_states(i, before)
    y_col, silu, *col_known = call(
        functools.partial(col_local_kernel, **sizes),
        [
            pltpu.VMEM((tokens, channels), F32),
            pltpu.VMEM((tokens, channels), F32),
            pltpu.VMEM((tokens, 2 * heads), BF16),
            pltpu.VMEM((tokens, cols * state), BF16),
        ],
        2,
        specs=[None] * 6 + [any_spec],
    )(params, x, raw, maps, gate, skip.reshape(1, heads), before)
    w = call(
        functools.partial(col_out_kernel, heads=heads, width=width),
        pltpu.VMEM((tokens, channels), F32),
        0,
    )(col_entering, y_col, *col_known)
    parts_of = []
    for i, piece in enumerate(pieces):
        for j, rows in enumerate(piece):
            first = sum(map(sum, pieces[:i])) + sum(piece[:j])
            parts_of.append((first, rows, known[i][j], entering[i][j]))

    back = []
    before = y_col
    for _, rows, known, entering in parts_of:
        y_row = call(
            functools.partial(row_out_kernel, heads=heads, width=width),
            [pltpu.VMEM((rows, channels), BF16)] * group,
            0,
            specs=[None] * 4 + [any_spec],
        )(entering, *known, before)
        back.append(exchange(y_row))
        before = col_entering

    which = [0, *range(group - 1, 0, -1)]
    mixed = None
    for i in range(len(parts_of)):
        first, rows = parts_of[i][:2]
        more = [] if mixed is None else [mixed]
        mixed = call(
            functools.partial(final_kernel, which=which, offset=first, share=share, **shared),
            shape((tokens, channels), BF16),
            0,
            specs=[None] * 3 + [any_spec] * len(more) + [None] * len(which),
            out_specs=any_spec,
            scratch_shapes=[
                pltpu.VMEM((len(which), rows, channels), BF16),
                pltpu.SemaphoreType.DMA((len(which),)),
            ],
            input_output_aliases={3: 0} if more else {},
        )(w, silu, norm_gain.reshape(1, channels), *more, *[back[i][j] for j in which])
    return mixed.reshape(x_in.shape)


def solution(mesh):
    tile = P("img", "row", "col", None)
    return jax.shard_map(
        functools.partial(body, row_count=mesh.shape["row"], col_count=mesh.shape["col"]),
        mesh=mesh,
        in_specs=(tile, tile, tile, tile, P("img"), P(), P(), P(), P()),
        out_specs=tile,
        check_vma=False,
    )
```

```python
import functools

import jax
import jax.numpy as jnp
from jax import lax
from jax.experimental import pallas as pl
from jax.experimental.pallas import tpu as pltpu
from jax.sharding import PartitionSpec as P

LANES = 128
GROUP = 4
PIECES = ((4,), (4,))
STRIP = 512
VMEM_LIMIT = 16 * 1024 * 1024
F32 = jnp.float32
BF16 = jnp.bfloat16


def dot(a, b):
    return jnp.dot(a, b, preferred_element_type=F32)


def iota(shape, dim):
    return lax.broadcasted_iota(jnp.int32, shape, dim)


def div(a, n):
    return lax.shift_right_logical(a, n.bit_length() - 1) if n & (n - 1) == 0 else a // n


def mod(a, n):
    return jnp.bitwise_and(a, n - 1) if n & (n - 1) == 0 else a % n


def parts(values, count):
    terms = []
    for _ in range(count):
        term = values.astype(BF16)
        terms.append(term)
        values = values - term.astype(F32)
    return jnp.concatenate(terms, axis=1)


def picks(heads, width, first, channels):
    row = iota((2 * heads, 1), 0)
    head = jnp.where(row >= heads, row - heads, row)
    return (head == div(first + iota((1, channels), 1), width)).astype(BF16)


def summed(mask, values):
    heads = values.shape[1]
    sums = dot(mask, parts(values, 3))
    return sums[:, :heads] + sums[:, heads : 2 * heads] + sums[:, 2 * heads :]


def step_sizes(raw, bias):
    shifted = raw.astype(F32) + bias
    return jnp.maximum(shifted, 0.0) + jnp.log1p(jnp.exp(-jnp.abs(shifted)))


def widen(maps, line, lines):
    state = maps.shape[1]
    places = lines * state
    copy = (mod(iota((1, places), 1), state) == iota((state, 1), 0)).astype(BF16)
    own = div(iota((1, places), 1), state) == line
    return jnp.where(own, dot(maps, copy), 0.0).astype(BF16)


class Scan:
    def __init__(self, order, lines, raw, bias, rates, b_map, c_map):
        tokens, self.heads = raw.shape
        self.lines, self.b_map, self.c_map = lines, b_map, c_map
        self.line, place = order(iota((tokens, 1), 0))
        self.line_in, place_in = order(iota((1, tokens), 1))
        self.lower = jnp.logical_and(self.line == self.line_in, place >= place_in)
        steps = step_sizes(raw, bias)
        self.decay = -rates * steps
        running = summed(self.lower.astype(BF16), self.decay)
        self.fade = parts(jnp.exp(running), 2)
        self.grow = parts(steps * jnp.exp(-running), 2)

    def ends(self):
        places = self.lines * self.b_map.shape[1]
        own = div(iota((places, 1), 0), self.b_map.shape[1]) == self.line_in
        return jnp.exp(summed(own.astype(BF16), self.decay))

    def into(self):
        return widen(self.b_map, self.line, self.lines).astype(F32).T.astype(BF16)

    def within(self):
        scores = lax.dot_general(
            self.c_map, self.b_map, (((1,), (1,)), ((), ())), preferred_element_type=F32
        )
        return jnp.where(self.lower, scores, 0.0).astype(BF16)

    def entry(self, follows):
        return jnp.where(follows, widen(self.c_map, self.line, self.lines), 0)


def partner(member, i, group):
    return member ^ i


def column_order(cols):
    return lambda token: (mod(token, cols), div(token, cols))


def row_order(cols, lines, member, group):
    def order(token):
        source = partner(member, div(token, cols * lines), group)
        return mod(div(token, cols), lines), source * cols + mod(token, cols)

    return order


def strips(channels):
    return [(first, min(STRIP, channels - first)) for first in range(0, channels, STRIP)]


def pack_kernel(
    x_ref, raw_ref, maps_ref, table_ref, rates_ref, raw, maps, table, rates, *refs, group, axis, heads, state
):
    sent, sems = refs[:-1], refs[-1]
    channels = x_ref.shape[1]
    share = x_ref.shape[0] // group
    member = mod(lax.axis_index(axis), group)
    moved = [(raw_ref, raw), (maps_ref, maps)]
    places = []
    offset = 0
    for i, out in enumerate(sent):
        rows = out.shape[0]
        first = partner(member, i % group, group) * share + offset
        part = pl.ds(pl.multiple_of(first, 16), rows)
        places.append((out, part))
        moved.append((x_ref.at[part, :], out.at[:, pl.ds(0, channels)]))
        if i % group == group - 1:
            offset += rows
    moved += [(table_ref, table), (rates_ref, rates)]
    copies = [pltpu.make_async_copy(a, b, sems.at[i]) for i, (a, b) in enumerate(moved)]
    for copy in copies:
        copy.start()
    for copy in copies[:2]:
        copy.wait()
    used = heads + 2 * state
    for out, part in places:
        out[:, channels : channels + heads] = raw[part, :heads]
        out[:, channels + heads : channels + used] = maps[part, : 2 * state]
        out[:, channels + used :] = jnp.zeros((out.shape[0], LANES - used), BF16)
    for copy in copies[2:]:
        copy.wait()


def params_kernel(index_ref, table_ref, rates_ref, params_ref):
    heads = rates_ref.shape[1]
    row = jnp.where(iota(table_ref.shape, 1) == index_ref[0], table_ref[...], 0.0)
    ones = jnp.ones((8, table_ref.shape[1]), BF16)
    bias = jnp.zeros((8, row.shape[0]), F32)
    for _ in range(3):
        term = row.astype(BF16)
        row = row - term.astype(F32)
        bias += lax.dot_general(ones, term, (((1,), (1,)), ((), ())), preferred_element_type=F32)
    params_ref[0:1, :] = bias[0:1, :]
    params_ref[1:2, :heads] = rates_ref[0:1, :]
    params_ref[1:2, heads:] = rates_ref[1:2, :]
    params_ref[2:, :] = jnp.zeros((6, 2 * heads), F32)


def row_scan(params_ref, blocks, member, cols, heads, state):
    channels = blocks[0].shape[1] - LANES
    tokens = blocks[0].shape[0] * len(blocks)
    lines = tokens // (cols * len(blocks))
    aux = jnp.concatenate([block[:, channels:] for block in blocks], axis=0)
    return Scan(
        row_order(cols, lines, member, len(blocks)),
        lines,
        aux[:, :heads],
        params_ref[0:1, :heads],
        params_ref[1:2, :heads],
        aux[:, heads : heads + state],
        aux[:, heads + state : heads + 2 * state],
    )


def col_scan(params_ref, raw_ref, maps_ref, cols, heads, state):
    return Scan(
        column_order(cols),
        cols,
        raw_ref[:, heads:],
        params_ref[0:1, heads:],
        params_ref[1:2, heads:],
        maps_ref[:, 2 * state : 3 * state],
        maps_ref[:, 3 * state :],
    )


def write_state(scan, tokens_of, width, channels, s_refs, factor_ref):
    ends = scan.ends()
    if factor_ref:
        factor_ref[0][...] = ends
    ends = parts(ends, 2)
    into = scan.into()
    for first, count in strips(channels):
        pick = picks(scan.heads, width, first, count)
        values = (tokens_of(first, count) * dot(scan.grow, pick)).astype(BF16)
        made = (dot(into, values) * dot(ends, pick)).astype(BF16)
        row = 0
        for s_ref in s_refs:
            s_ref[:, first : first + count] = made[row : row + s_ref.shape[0]]
            row += s_ref.shape[0]


def row_state_kernel(params_ref, *refs, group, count, axis, cols, heads, state, width):
    blocks, s_refs, factor_ref = refs[:group], refs[group + 1 : group + 1 + count], refs[group + 1 + count :]
    member = mod(lax.axis_index(axis), group)
    scan = row_scan(params_ref, [block[...] for block in blocks], member, cols, heads, state)
    tokens_of = lambda first, count: jnp.concatenate(
        [block[:, first : first + count] for block in blocks], axis=0
    ).astype(F32)
    write_state(scan, tokens_of, width, s_refs[0].shape[1], s_refs, factor_ref)


def col_state_kernel(params_ref, x_ref, raw_ref, maps_ref, _, s_ref, *factor_ref, cols, heads, state, width):
    scan = col_scan(params_ref, raw_ref, maps_ref, cols, heads, state)
    tokens_of = lambda first, count: x_ref[:, first : first + count].astype(F32)
    write_state(scan, tokens_of, width, s_ref.shape[1], [s_ref], factor_ref)


def row_local_kernel(params_ref, *refs, group, offset, axis, cols, heads, state, width):
    blocks, (y_ref, fade_ref, entry_ref) = refs[:group], refs[group + 1 :]
    rows = y_ref.shape[0] // group
    mine = slice(offset, offset + rows)
    member = mod(lax.axis_index(axis), group)
    scan = row_scan(params_ref, [block[mine, :] for block in blocks], member, cols, heads, state)
    mix = scan.within()
    fade_ref[...] = scan.fade
    entry_ref[...] = scan.entry(lax.axis_index(axis) >= group)
    for first, count in strips(y_ref.shape[1]):
        pick = picks(heads, width, first, count)
        part = slice(first, first + count)
        x = jnp.concatenate([block[mine, part] for block in blocks], axis=0).astype(F32)
        values = (x * dot(scan.grow, pick)).astype(BF16)
        y_ref[:, part] = dot(mix, values) * dot(scan.fade, pick)


def row_both_kernel(params_ref, *refs, group, axis, cols, heads, state, width):
    blocks, (s_ref, y_ref, fade_ref, entry_ref) = refs[:group], refs[group + 1 :]
    member = mod(lax.axis_index(axis), group)
    scan = row_scan(params_ref, [block[...] for block in blocks], member, cols, heads, state)
    into = scan.into()
    ends = parts(scan.ends(), 2)
    mix = scan.within()
    fade_ref[...] = scan.fade
    entry_ref[...] = scan.entry(lax.axis_index(axis) >= group)
    for first, count in strips(y_ref.shape[1]):
        pick = picks(heads, width, first, count)
        part = slice(first, first + count)
        x = jnp.concatenate([block[:, part] for block in blocks], axis=0).astype(F32)
        values = (x * dot(scan.grow, pick)).astype(BF16)
        s_ref[:, part] = (dot(into, values) * dot(ends, pick)).astype(BF16)
        y_ref[:, part] = dot(mix, values) * dot(scan.fade, pick)


def row_out_kernel(s_ref, y_ref, fade_ref, entry_ref, _, __, *outs, heads, width):
    rows = outs[0].shape[0]
    for first, count in strips(s_ref.shape[1]):
        pick = picks(heads, width, first, count)
        part = slice(first, first + count)
        y = y_ref[:, part] + dot(entry_ref[...], s_ref[:, part]) * dot(fade_ref[...], pick)
        for i, out in enumerate(outs):
            out[:, part] = y[i * rows : (i + 1) * rows].astype(BF16)


def col_local_kernel(
    params_ref, x_ref, raw_ref, maps_ref, gate_ref, skip_ref, _, y_ref, g_ref, fade_ref, entry_ref,
    *, cols, heads, state, width
):
    scan = col_scan(params_ref, raw_ref, maps_ref, cols, heads, state)
    mix = scan.within()
    fade_ref[...] = scan.fade
    entry_ref[...] = scan.entry(lax.axis_index("row") > 0)
    skips = parts(jnp.broadcast_to(skip_ref[...], (8, heads)), 2)
    for first, count in strips(x_ref.shape[1]):
        pick = picks(heads, width, first, count)
        part = slice(first, first + count)
        x = x_ref[:, part].astype(F32)
        values = (x * dot(scan.grow, pick)).astype(BF16)
        y_ref[:, part] = dot(mix, values) * dot(scan.fade, pick) + dot(skips, pick)[0:1, :] * x
        gate = gate_ref[:, part].astype(F32)
        g_ref[:, part] = gate / (1.0 + jnp.exp(-gate))


def col_out_kernel(s_ref, y_ref, fade_ref, entry_ref, w_ref, *, heads, width):
    for first, count in strips(s_ref.shape[1]):
        pick = picks(heads, width, first, count)
        part = slice(first, first + count)
        w_ref[:, part] = y_ref[:, part] + dot(entry_ref[...], s_ref[:, part]) * dot(fade_ref[...], pick)


def final_kernel(w_ref, g_ref, gain_ref, *refs, which, offset, group, axis, share):
    blocks, (out_ref, made, sems) = refs[-3 - len(which) : -3], refs[-3:]
    rows, channels = blocks[0].shape
    member = mod(lax.axis_index(axis), group)
    copies = []
    for i, block in zip(which, blocks):
        part = pl.ds(pl.multiple_of(partner(member, i, group) * share + offset, 16), rows)
        v = (block[...].astype(F32) + w_ref[part, :]) * g_ref[part, :]
        power = jnp.sum(v * v, axis=1, keepdims=True) / channels
        at = len(copies)
        made[at] = (v * lax.rsqrt(power + 1e-5) * gain_ref[...]).astype(BF16)
        copies.append(pltpu.make_async_copy(made.at[at], out_ref.at[part, :], sems.at[at]))
        copies[-1].start()
    for copy in copies:
        copy.wait()


def cost(micros):
    return pl.CostEstimate(flops=1024 + int(micros * 10**9), bytes_accessed=1024, transcendentals=0)


def call(kernel, out_shape, micros, specs=None, **more):
    if specs is not None:
        more["in_specs"] = [spec or pl.BlockSpec() for spec in specs]
    return pl.pallas_call(
        kernel,
        out_shape=out_shape,
        compiler_params=pltpu.CompilerParams(vmem_limit_bytes=VMEM_LIMIT),
        cost_estimate=cost(micros),
        **more,
    )


def entering_states(ends, factor, axis, size, stride, width, wrap=True):
    if size == stride:
        return ends
    onward = [(i, (i + stride) % size) for i in range(size if wrap else size - stride)]
    entering = lax.ppermute(ends, axis, onward)
    for _ in range(size // stride - 2):
        follows = (lax.axis_index(axis) >= stride).astype(F32)
        decayed = follows * jnp.repeat(factor[0], width, axis=1) * entering.astype(F32)
        entering = lax.ppermute((ends.astype(F32) + decayed).astype(BF16), axis, onward)
    return entering


def body(x_in, gate_in, proj_bc, dt_raw, step_index, step_table, rates, skip, norm_gain, *, row_count, col_count):
    _, tile_rows, cols, channels = x_in.shape
    heads = skip.shape[0]
    width = channels // heads
    state = proj_bc.shape[-1] // 4
    tokens = tile_rows * cols
    group = GROUP
    while col_count % group:
        group //= 2
    share = tokens // group
    pieces = [[eighths * share // 8 for eighths in piece] for piece in PIECES]

    x = x_in.reshape(tokens, channels)
    gate = gate_in.reshape(tokens, channels)
    maps = proj_bc.reshape(tokens, 4 * state)
    raw = dt_raw.reshape(tokens, 2 * heads)
    sizes = dict(cols=cols, heads=heads, state=state, width=width)
    shared = dict(group=group, axis="col")
    shape = jax.ShapeDtypeStruct
    any_spec = pl.BlockSpec(memory_space=pl.ANY)

    given = [x, raw, maps, step_table.T, rates]
    raw, maps, table, rates, *packed = pl.pallas_call(
        functools.partial(pack_kernel, heads=heads, state=state, **shared),
        in_specs=[pl.BlockSpec(memory_space=pltpu.HBM)] * len(given),
        out_shape=[pltpu.VMEM(a.shape, a.dtype) for a in given[1:]]
        + [pltpu.VMEM((sum(piece), channels + LANES), BF16) for piece in pieces for _ in range(group)],
        scratch_shapes=[pltpu.SemaphoreType.DMA((len(given) - 1 + group * len(pieces),))],
        compiler_params=pltpu.CompilerParams(vmem_limit_bytes=VMEM_LIMIT),
        cost_estimate=cost(1),
    )(*[pltpu.with_memory_space_constraint(a, pltpu.HBM) for a in given])
    index, rates = lax.optimization_barrier((step_index, rates))
    params = pl.pallas_call(
        params_kernel,
        grid_spec=pltpu.PrefetchScalarGridSpec(
            num_scalar_prefetch=1,
            grid=(1,),
            in_specs=[
                pl.BlockSpec(table.shape, lambda i, index: (0, 0)),
                pl.BlockSpec(rates.shape, lambda i, index: (0, 0)),
            ],
            out_specs=pl.BlockSpec((8, 2 * heads), lambda i, index: (0, 0)),
        ),
        out_shape=shape((8, 2 * heads), F32),
        compiler_params=pltpu.CompilerParams(vmem_limit_bytes=VMEM_LIMIT),
        cost_estimate=cost(0),
    )(index, table, rates)

    def exchange(blocks):
        return [blocks[0]] + [
            lax.ppermute(blocks[i], "col", [(at, partner(at, i, group)) for at in range(col_count)])
            for i in range(1, group)
        ]

    def state_shapes(places, count):
        states = [pltpu.VMEM((rows, channels), BF16) for rows in places]
        return states + [shape((sum(places), heads), F32)] * (count > 2)

    got = [exchange(packed[i * group : (i + 1) * group]) for i in range(len(pieces))]

    def own_rows(i, before):
        known = []
        for j, rows in enumerate(pieces[i]):
            known.append(
                call(
                    functools.partial(row_local_kernel, offset=sum(pieces[i][:j]), **sizes, **shared),
                    [
                        pltpu.VMEM((group * rows, channels), F32),
                        pltpu.VMEM((group * rows, 2 * heads), BF16),
                        pltpu.VMEM((group * rows, rows // cols * state), BF16),
                    ],
                    2,
                    specs=[None] * (1 + group) + [any_spec],
                )(params, *got[i], before)
            )
            before = known[-1][1]
        return known, before

    def row_states(i, before):
        places = [rows // cols * state for rows in pieces[i]]
        made = call(
            functools.partial(row_state_kernel, count=len(places), **sizes, **shared),
            state_shapes(places, col_count // group),
            0,
            specs=[None] * (1 + group) + [any_spec],
        )(params, *got[i], before)
        entering = []
        for j, count in enumerate(places):
            first = sum(places[:j])
            factor = [f[first : first + count] for f in made[len(places) :]]
            entering.append(entering_states(made[j], factor, "col", col_count, group, width, wrap=i == 0))
        return entering, made[0]

    known, entering = [None] * len(pieces), [None] * len(pieces)
    entering[0], before = row_states(0, params)
    col_made = call(
        functools.partial(col_state_kernel, **sizes),
        state_shapes([cols * state], row_count),
        0,
        specs=[None] * 4 + [any_spec],
    )(params, x, raw, maps, before)
    col_entering = entering_states(col_made[0], col_made[1:], "row", row_count, 1, width)
    before = col_made[0]
    known[0], before = own_rows(0, before)
    for i in range(1, len(pieces)):
        if len(pieces[i]) > 1 or col_count > 2 * group:
            known[i], before = own_rows(i, before)
            entering[i], before = row_states(i, before)
            continue
        rows = pieces[i][0]
        places = rows // cols * state
        made, *own = call(
            functools.partial(row_both_kernel, **sizes, **shared),
            [
                pltpu.VMEM((places, channels), BF16),
                pltpu.VMEM((group * rows, channels), F32),
                pltpu.VMEM((group * rows, 2 * heads), BF16),
                pltpu.VMEM((group * rows, places), BF16),
            ],
            2,
            specs=[None] * (1 + group) + [any_spec],
        )(params, *got[i], before)
        known[i], before = [own], made
        entering[i] = [entering_states(made, [], "col", col_count, group, width, wrap=False)]
    parts_of = []
    for i, piece in enumerate(pieces):
        for j, rows in enumerate(piece):
            first = sum(map(sum, pieces[:i])) + sum(piece[:j])
            parts_of.append((first, rows, known[i][j], entering[i][j]))

    back = []
    for _, rows, known, entering in parts_of:
        y_row = call(
            functools.partial(row_out_kernel, heads=heads, width=width),
            [pltpu.VMEM((rows, channels), BF16)] * group,
            0,
            specs=[None] * 4 + [any_spec] * 2,
        )(entering, *known, before, col_entering if back else before)
        back.append(exchange(y_row))
        before = y_row[0]
        if len(back) > 1:
            continue
        y_col, silu, *col_known = call(
            functools.partial(col_local_kernel, **sizes),
            [
                pltpu.VMEM((tokens, channels), F32),
                pltpu.VMEM((tokens, channels), F32),
                pltpu.VMEM((tokens, 2 * heads), BF16),
                pltpu.VMEM((tokens, cols * state), BF16),
            ],
            2,
            specs=[None] * 6 + [any_spec],
        )(params, x, raw, maps, gate, skip.reshape(1, heads), before)
        w = call(
            functools.partial(col_out_kernel, heads=heads, width=width),
            pltpu.VMEM((tokens, channels), F32),
            0,
        )(col_entering, y_col, *col_known)
        before = y_col

    which = [0, *range(group - 1, 0, -1)]
    mixed = None
    for i in range(len(parts_of)):
        first, rows = parts_of[i][:2]
        more = [] if mixed is None else [mixed]
        mixed = call(
            functools.partial(final_kernel, which=which, offset=first, share=share, **shared),
            shape((tokens, channels), BF16),
            0,
            specs=[None] * 3 + [any_spec] * len(more) + [None] * len(which),
            out_specs=any_spec,
            scratch_shapes=[
                pltpu.VMEM((len(which), rows, channels), BF16),
                pltpu.SemaphoreType.DMA((len(which),)),
            ],
            input_output_aliases={3: 0} if more else {},
        )(w, silu, norm_gain.reshape(1, channels), *more, *[back[i][j] for j in which])
    return mixed.reshape(x_in.shape)


def solution(mesh):
    tile = P("img", "row", "col", None)
    return jax.shard_map(
        functools.partial(body, row_count=mesh.shape["row"], col_count=mesh.shape["col"]),
        mesh=mesh,
        in_specs=(tile, tile, tile, tile, P("img"), P(), P(), P(), P()),
        out_specs=tile,
        check_vma=False,
    )
```

```python
import functools

import jax
import jax.numpy as jnp
from jax import lax
from jax.experimental import pallas as pl
from jax.experimental.pallas import tpu as pltpu
from jax.sharding import PartitionSpec as P

LANES = 128
GROUP = 4
PIECES = ((4,), (4,))
STRIP = 512
VMEM_LIMIT = 16 * 1024 * 1024
F32 = jnp.float32
BF16 = jnp.bfloat16


def dot(a, b):
    return jnp.dot(a, b, preferred_element_type=F32)


def iota(shape, dim):
    return lax.broadcasted_iota(jnp.int32, shape, dim)


def div(a, n):
    return lax.shift_right_logical(a, n.bit_length() - 1) if n & (n - 1) == 0 else a // n


def mod(a, n):
    return jnp.bitwise_and(a, n - 1) if n & (n - 1) == 0 else a % n


def parts(values, count):
    terms = []
    for _ in range(count):
        term = values.astype(BF16)
        terms.append(term)
        values = values - term.astype(F32)
    return jnp.concatenate(terms, axis=1)


def picks(heads, width, first, channels):
    row = iota((2 * heads, 1), 0)
    head = jnp.where(row >= heads, row - heads, row)
    return (head == div(first + iota((1, channels), 1), width)).astype(BF16)


def summed(mask, values):
    heads = values.shape[1]
    sums = dot(mask, parts(values, 3))
    return sums[:, :heads] + sums[:, heads : 2 * heads] + sums[:, 2 * heads :]


def step_sizes(raw, bias):
    shifted = raw.astype(F32) + bias
    return jnp.maximum(shifted, 0.0) + jnp.log1p(jnp.exp(-jnp.abs(shifted)))


def widen(maps, line, lines):
    state = maps.shape[1]
    places = lines * state
    copy = (mod(iota((1, places), 1), state) == iota((state, 1), 0)).astype(BF16)
    own = div(iota((1, places), 1), state) == line
    return jnp.where(own, dot(maps, copy), 0.0).astype(BF16)


class Scan:
    def __init__(self, order, lines, raw, bias, rates, b_map, c_map):
        tokens, self.heads = raw.shape
        self.lines, self.b_map, self.c_map = lines, b_map, c_map
        self.line, place = order(iota((tokens, 1), 0))
        self.line_in, place_in = order(iota((1, tokens), 1))
        self.lower = jnp.logical_and(self.line == self.line_in, place >= place_in)
        steps = step_sizes(raw, bias)
        self.decay = -rates * steps
        running = summed(self.lower.astype(BF16), self.decay)
        self.fade = parts(jnp.exp(running), 2)
        self.grow = parts(steps * jnp.exp(-running), 2)

    def ends(self):
        places = self.lines * self.b_map.shape[1]
        own = div(iota((places, 1), 0), self.b_map.shape[1]) == self.line_in
        return jnp.exp(summed(own.astype(BF16), self.decay))

    def into(self):
        return widen(self.b_map, self.line, self.lines).astype(F32).T.astype(BF16)

    def within(self):
        scores = lax.dot_general(
            self.c_map, self.b_map, (((1,), (1,)), ((), ())), preferred_element_type=F32
        )
        return jnp.where(self.lower, scores, 0.0).astype(BF16)

    def entry(self, follows):
        return jnp.where(follows, widen(self.c_map, self.line, self.lines), 0)


def partner(member, i, group):
    return member ^ i


def column_order(cols):
    return lambda token: (mod(token, cols), div(token, cols))


def row_order(cols, lines, member, group):
    def order(token):
        source = partner(member, div(token, cols * lines), group)
        return mod(div(token, cols), lines), source * cols + mod(token, cols)

    return order


def strips(channels):
    return [(first, min(STRIP, channels - first)) for first in range(0, channels, STRIP)]


def pack_kernel(
    x_ref, raw_ref, maps_ref, table_ref, rates_ref, raw, maps, table, rates, *refs, group, axis, heads, state
):
    sent, sems = refs[:-1], refs[-1]
    channels = x_ref.shape[1]
    share = x_ref.shape[0] // group
    member = mod(lax.axis_index(axis), group)
    moved = [(raw_ref, raw), (maps_ref, maps)]
    places = []
    offset = 0
    for i, out in enumerate(sent):
        rows = out.shape[0]
        first = partner(member, i % group, group) * share + offset
        part = pl.ds(pl.multiple_of(first, 16), rows)
        places.append((out, part))
        moved.append((x_ref.at[part, :], out.at[:, pl.ds(0, channels)]))
        if i % group == group - 1:
            offset += rows
    moved += [(table_ref, table), (rates_ref, rates)]
    copies = [pltpu.make_async_copy(a, b, sems.at[i]) for i, (a, b) in enumerate(moved)]
    for copy in copies:
        copy.start()
    for copy in copies[:2]:
        copy.wait()
    used = heads + 2 * state
    for out, part in places:
        out[:, channels : channels + heads] = raw[part, :heads]
        out[:, channels + heads : channels + used] = maps[part, : 2 * state]
        out[:, channels + used :] = jnp.zeros((out.shape[0], LANES - used), BF16)
    for copy in copies[2:]:
        copy.wait()


def params_kernel(index_ref, table_ref, rates_ref, params_ref):
    heads = rates_ref.shape[1]
    row = jnp.where(iota(table_ref.shape, 1) == index_ref[0], table_ref[...], 0.0)
    ones = jnp.ones((8, table_ref.shape[1]), BF16)
    bias = jnp.zeros((8, row.shape[0]), F32)
    for _ in range(3):
        term = row.astype(BF16)
        row = row - term.astype(F32)
        bias += lax.dot_general(ones, term, (((1,), (1,)), ((), ())), preferred_element_type=F32)
    params_ref[0:1, :] = bias[0:1, :]
    params_ref[1:2, :heads] = rates_ref[0:1, :]
    params_ref[1:2, heads:] = rates_ref[1:2, :]
    params_ref[2:, :] = jnp.zeros((6, 2 * heads), F32)


def row_scan(params_ref, blocks, member, cols, heads, state):
    channels = blocks[0].shape[1] - LANES
    tokens = blocks[0].shape[0] * len(blocks)
    lines = tokens // (cols * len(blocks))
    aux = jnp.concatenate([block[:, channels:] for block in blocks], axis=0)
    return Scan(
        row_order(cols, lines, member, len(blocks)),
        lines,
        aux[:, :heads],
        params_ref[0:1, :heads],
        params_ref[1:2, :heads],
        aux[:, heads : heads + state],
        aux[:, heads + state : heads + 2 * state],
    )


def col_scan(params_ref, raw_ref, maps_ref, cols, heads, state):
    return Scan(
        column_order(cols),
        cols,
        raw_ref[:, heads:],
        params_ref[0:1, heads:],
        params_ref[1:2, heads:],
        maps_ref[:, 2 * state : 3 * state],
        maps_ref[:, 3 * state :],
    )


def write_state(scan, tokens_of, width, channels, s_refs, factor_ref):
    ends = scan.ends()
    if factor_ref:
        factor_ref[0][...] = ends
    ends = parts(ends, 2)
    into = scan.into()
    for first, count in strips(channels):
        pick = picks(scan.heads, width, first, count)
        values = (tokens_of(first, count) * dot(scan.grow, pick)).astype(BF16)
        made = (dot(into, values) * dot(ends, pick)).astype(BF16)
        row = 0
        for s_ref in s_refs:
            s_ref[:, first : first + count] = made[row : row + s_ref.shape[0]]
            row += s_ref.shape[0]


def row_state_kernel(params_ref, *refs, group, count, axis, cols, heads, state, width):
    blocks, s_refs, factor_ref = refs[:group], refs[group + 1 : group + 1 + count], refs[group + 1 + count :]
    member = mod(lax.axis_index(axis), group)
    scan = row_scan(params_ref, [block[...] for block in blocks], member, cols, heads, state)
    tokens_of = lambda first, count: jnp.concatenate(
        [block[:, first : first + count] for block in blocks], axis=0
    ).astype(F32)
    write_state(scan, tokens_of, width, s_refs[0].shape[1], s_refs, factor_ref)


def col_state_kernel(params_ref, x_ref, raw_ref, maps_ref, _, s_ref, *factor_ref, cols, heads, state, width):
    scan = col_scan(params_ref, raw_ref, maps_ref, cols, heads, state)
    tokens_of = lambda first, count: x_ref[:, first : first + count].astype(F32)
    write_state(scan, tokens_of, width, s_ref.shape[1], [s_ref], factor_ref)


def row_local_kernel(params_ref, *refs, group, offset, axis, cols, heads, state, width):
    blocks, (y_ref, fade_ref, entry_ref) = refs[:group], refs[group + 1 :]
    rows = y_ref.shape[0] // group
    mine = slice(offset, offset + rows)
    member = mod(lax.axis_index(axis), group)
    scan = row_scan(params_ref, [block[mine, :] for block in blocks], member, cols, heads, state)
    mix = scan.within()
    fade_ref[...] = scan.fade
    entry_ref[...] = scan.entry(lax.axis_index(axis) >= group)
    for first, count in strips(y_ref.shape[1]):
        pick = picks(heads, width, first, count)
        part = slice(first, first + count)
        x = jnp.concatenate([block[mine, part] for block in blocks], axis=0).astype(F32)
        values = (x * dot(scan.grow, pick)).astype(BF16)
        y_ref[:, part] = dot(mix, values) * dot(scan.fade, pick)


def row_both_kernel(params_ref, *refs, group, axis, cols, heads, state, width):
    blocks, (s_ref, y_ref, fade_ref, entry_ref) = refs[:group], refs[group + 1 :]
    member = mod(lax.axis_index(axis), group)
    scan = row_scan(params_ref, [block[...] for block in blocks], member, cols, heads, state)
    into = scan.into()
    ends = parts(scan.ends(), 2)
    mix = scan.within()
    fade_ref[...] = scan.fade
    entry_ref[...] = scan.entry(lax.axis_index(axis) >= group)
    for first, count in strips(y_ref.shape[1]):
        pick = picks(heads, width, first, count)
        part = slice(first, first + count)
        x = jnp.concatenate([block[:, part] for block in blocks], axis=0).astype(F32)
        values = (x * dot(scan.grow, pick)).astype(BF16)
        s_ref[:, part] = (dot(into, values) * dot(ends, pick)).astype(BF16)
        y_ref[:, part] = dot(mix, values) * dot(scan.fade, pick)


def row_out_kernel(s_ref, y_ref, fade_ref, entry_ref, _, __, *outs, heads, width):
    rows = outs[0].shape[0]
    for first, count in strips(s_ref.shape[1]):
        pick = picks(heads, width, first, count)
        part = slice(first, first + count)
        y = y_ref[:, part] + dot(entry_ref[...], s_ref[:, part]) * dot(fade_ref[...], pick)
        for i, out in enumerate(outs):
            out[:, part] = y[i * rows : (i + 1) * rows].astype(BF16)


def col_local_kernel(
    params_ref, x_ref, raw_ref, maps_ref, gate_ref, skip_ref, _, y_ref, g_ref, fade_ref, entry_ref,
    *, cols, heads, state, width
):
    scan = col_scan(params_ref, raw_ref, maps_ref, cols, heads, state)
    mix = scan.within()
    fade_ref[...] = scan.fade
    entry_ref[...] = scan.entry(lax.axis_index("row") > 0)
    skips = parts(jnp.broadcast_to(skip_ref[...], (8, heads)), 2)
    for first, count in strips(x_ref.shape[1]):
        pick = picks(heads, width, first, count)
        part = slice(first, first + count)
        x = x_ref[:, part].astype(F32)
        values = (x * dot(scan.grow, pick)).astype(BF16)
        y_ref[:, part] = dot(mix, values) * dot(scan.fade, pick) + dot(skips, pick)[0:1, :] * x
        gate = gate_ref[:, part].astype(F32)
        g_ref[:, part] = gate / (1.0 + jnp.exp(-gate))


def col_out_kernel(s_ref, y_ref, fade_ref, entry_ref, w_ref, *, heads, width):
    for first, count in strips(s_ref.shape[1]):
        pick = picks(heads, width, first, count)
        part = slice(first, first + count)
        w_ref[:, part] = y_ref[:, part] + dot(entry_ref[...], s_ref[:, part]) * dot(fade_ref[...], pick)


def final_kernel(w_ref, g_ref, gain_ref, *refs, which, offset, group, axis, share):
    blocks, (out_ref, made, sems) = refs[-3 - len(which) : -3], refs[-3:]
    rows, channels = blocks[0].shape
    member = mod(lax.axis_index(axis), group)
    copies = []
    for i, block in zip(which, blocks):
        part = pl.ds(pl.multiple_of(partner(member, i, group) * share + offset, 16), rows)
        v = (block[...].astype(F32) + w_ref[part, :]) * g_ref[part, :]
        power = jnp.sum(v * v, axis=1, keepdims=True) / channels
        at = len(copies)
        made[at] = (v * lax.rsqrt(power + 1e-5) * gain_ref[...]).astype(BF16)
        copies.append(pltpu.make_async_copy(made.at[at], out_ref.at[part, :], sems.at[at]))
        copies[-1].start()
    for copy in copies:
        copy.wait()


def cost(micros):
    return pl.CostEstimate(flops=1024 + int(micros * 10**9), bytes_accessed=1024, transcendentals=0)


def call(kernel, out_shape, micros, specs=None, **more):
    if specs is not None:
        more["in_specs"] = [spec or pl.BlockSpec() for spec in specs]
    return pl.pallas_call(
        kernel,
        out_shape=out_shape,
        compiler_params=pltpu.CompilerParams(vmem_limit_bytes=VMEM_LIMIT),
        cost_estimate=cost(micros),
        **more,
    )


def entering_states(ends, factor, axis, size, stride, width, wrap=True):
    if size == stride:
        return ends
    onward = [(i, (i + stride) % size) for i in range(size if wrap else size - stride)]
    entering = lax.ppermute(ends, axis, onward)
    for _ in range(size // stride - 2):
        follows = (lax.axis_index(axis) >= stride).astype(F32)
        decayed = follows * jnp.repeat(factor[0], width, axis=1) * entering.astype(F32)
        entering = lax.ppermute((ends.astype(F32) + decayed).astype(BF16), axis, onward)
    return entering


def body(x_in, gate_in, proj_bc, dt_raw, step_index, step_table, rates, skip, norm_gain, *, row_count, col_count):
    _, tile_rows, cols, channels = x_in.shape
    heads = skip.shape[0]
    width = channels // heads
    state = proj_bc.shape[-1] // 4
    tokens = tile_rows * cols
    group = GROUP
    while col_count % group:
        group //= 2
    share = tokens // group
    pieces = [[eighths * share // 8 for eighths in piece] for piece in PIECES]

    x = x_in.reshape(tokens, channels)
    gate = gate_in.reshape(tokens, channels)
    maps = proj_bc.reshape(tokens, 4 * state)
    raw = dt_raw.reshape(tokens, 2 * heads)
    sizes = dict(cols=cols, heads=heads, state=state, width=width)
    shared = dict(group=group, axis="col")
    shape = jax.ShapeDtypeStruct
    any_spec = pl.BlockSpec(memory_space=pl.ANY)

    given = [x, raw, maps, step_table.T, rates]
    raw, maps, table, rates, *packed = pl.pallas_call(
        functools.partial(pack_kernel, heads=heads, state=state, **shared),
        in_specs=[pl.BlockSpec(memory_space=pltpu.HBM)] * len(given),
        out_shape=[pltpu.VMEM(a.shape, a.dtype) for a in given[1:]]
        + [pltpu.VMEM((sum(piece), channels + LANES), BF16) for piece in pieces for _ in range(group)],
        scratch_shapes=[pltpu.SemaphoreType.DMA((len(given) - 1 + group * len(pieces),))],
        compiler_params=pltpu.CompilerParams(vmem_limit_bytes=VMEM_LIMIT),
        cost_estimate=cost(1),
    )(*[pltpu.with_memory_space_constraint(a, pltpu.HBM) for a in given])
    index, rates = lax.optimization_barrier((step_index, rates))
    params = pl.pallas_call(
        params_kernel,
        grid_spec=pltpu.PrefetchScalarGridSpec(
            num_scalar_prefetch=1,
            grid=(1,),
            in_specs=[
                pl.BlockSpec(table.shape, lambda i, index: (0, 0)),
                pl.BlockSpec(rates.shape, lambda i, index: (0, 0)),
            ],
            out_specs=pl.BlockSpec((8, 2 * heads), lambda i, index: (0, 0)),
        ),
        out_shape=shape((8, 2 * heads), F32),
        compiler_params=pltpu.CompilerParams(vmem_limit_bytes=VMEM_LIMIT),
        cost_estimate=cost(0),
    )(index, table, rates)

    def exchange(blocks):
        return [blocks[0]] + [
            lax.ppermute(blocks[i], "col", [(at, partner(at, i, group)) for at in range(col_count)])
            for i in range(1, group)
        ]

    def state_shapes(places, count):
        states = [pltpu.VMEM((rows, channels), BF16) for rows in places]
        return states + [shape((sum(places), heads), F32)] * (count > 2)

    got = [exchange(packed[i * group : (i + 1) * group]) for i in range(len(pieces))]

    def own_rows(i, before):
        known = []
        for j, rows in enumerate(pieces[i]):
            known.append(
                call(
                    functools.partial(row_local_kernel, offset=sum(pieces[i][:j]), **sizes, **shared),
                    [
                        pltpu.VMEM((group * rows, channels), F32),
                        pltpu.VMEM((group * rows, 2 * heads), BF16),
                        pltpu.VMEM((group * rows, rows // cols * state), BF16),
                    ],
                    2,
                    specs=[None] * (1 + group) + [any_spec],
                )(params, *got[i], before)
            )
            before = known[-1][1]
        return known, before

    def row_states(i, before):
        places = [rows // cols * state for rows in pieces[i]]
        made = call(
            functools.partial(row_state_kernel, count=len(places), **sizes, **shared),
            state_shapes(places, col_count // group),
            0,
            specs=[None] * (1 + group) + [any_spec],
        )(params, *got[i], before)
        entering = []
        for j, count in enumerate(places):
            first = sum(places[:j])
            factor = [f[first : first + count] for f in made[len(places) :]]
            entering.append(entering_states(made[j], factor, "col", col_count, group, width, wrap=i == 0))
        return entering, made[0]

    known, entering = [None] * len(pieces), [None] * len(pieces)
    entering[0], before = row_states(0, params)
    col_made = call(
        functools.partial(col_state_kernel, **sizes),
        state_shapes([cols * state], row_count),
        0,
        specs=[None] * 4 + [any_spec],
    )(params, x, raw, maps, before)
    col_entering = entering_states(col_made[0], col_made[1:], "row", row_count, 1, width)
    before = col_made[0]
    y_col, silu, *col_known = call(
        functools.partial(col_local_kernel, **sizes),
        [
            pltpu.VMEM((tokens, channels), F32),
            pltpu.VMEM((tokens, channels), F32),
            pltpu.VMEM((tokens, 2 * heads), BF16),
            pltpu.VMEM((tokens, cols * state), BF16),
        ],
        2,
        specs=[None] * 6 + [any_spec],
    )(params, x, raw, maps, gate, skip.reshape(1, heads), before)
    w = call(
        functools.partial(col_out_kernel, heads=heads, width=width),
        pltpu.VMEM((tokens, channels), F32),
        0,
    )(col_entering, y_col, *col_known)
    before = y_col
    for i in range(1, len(pieces)):
        if len(pieces[i]) > 1 or col_count > 2 * group:
            known[i], before = own_rows(i, before)
            entering[i], before = row_states(i, before)
            continue
        rows = pieces[i][0]
        places = rows // cols * state
        made, *own = call(
            functools.partial(row_both_kernel, **sizes, **shared),
            [
                pltpu.VMEM((places, channels), BF16),
                pltpu.VMEM((group * rows, channels), F32),
                pltpu.VMEM((group * rows, 2 * heads), BF16),
                pltpu.VMEM((group * rows, places), BF16),
            ],
            2,
            specs=[None] * (1 + group) + [any_spec],
        )(params, *got[i], before)
        known[i], before = [own], made
        entering[i] = [entering_states(made, [], "col", col_count, group, width, wrap=False)]
    known[0], before = own_rows(0, before)
    parts_of = []
    for i, piece in enumerate(pieces):
        for j, rows in enumerate(piece):
            first = sum(map(sum, pieces[:i])) + sum(piece[:j])
            parts_of.append((first, rows, known[i][j], entering[i][j]))

    back = []
    for _, rows, known, entering in parts_of:
        y_row = call(
            functools.partial(row_out_kernel, heads=heads, width=width),
            [pltpu.VMEM((rows, channels), BF16)] * group,
            0,
            specs=[None] * 4 + [any_spec] * 2,
        )(entering, *known, before, col_entering if back else before)
        back.append(exchange(y_row))
        before = y_row[0]

    which = [0, *range(group - 1, 0, -1)]
    mixed = None
    for i in range(len(parts_of)):
        first, rows = parts_of[i][:2]
        more = [] if mixed is None else [mixed]
        mixed = call(
            functools.partial(final_kernel, which=which, offset=first, share=share, **shared),
            shape((tokens, channels), BF16),
            0,
            specs=[None] * 3 + [any_spec] * len(more) + [None] * len(which),
            out_specs=any_spec,
            scratch_shapes=[
                pltpu.VMEM((len(which), rows, channels), BF16),
                pltpu.SemaphoreType.DMA((len(which),)),
            ],
            input_output_aliases={3: 0} if more else {},
        )(w, silu, norm_gain.reshape(1, channels), *more, *[back[i][j] for j in which])
    return mixed.reshape(x_in.shape)


def solution(mesh):
    tile = P("img", "row", "col", None)
    return jax.shard_map(
        functools.partial(body, row_count=mesh.shape["row"], col_count=mesh.shape["col"]),
        mesh=mesh,
        in_specs=(tile, tile, tile, tile, P("img"), P(), P(), P(), P()),
        out_specs=tile,
        check_vma=False,
    )
```

```python
import functools

import jax
import jax.numpy as jnp
from jax import lax
from jax.experimental import pallas as pl
from jax.experimental.pallas import tpu as pltpu
from jax.sharding import PartitionSpec as P

LANES = 128
GROUP = 4
PIECES = ((4,), (4,))
STRIP = 512
VMEM_LIMIT = 16 * 1024 * 1024
F32 = jnp.float32
BF16 = jnp.bfloat16


def dot(a, b):
    return jnp.dot(a, b, preferred_element_type=F32)


def iota(shape, dim):
    return lax.broadcasted_iota(jnp.int32, shape, dim)


def div(a, n):
    return lax.shift_right_logical(a, n.bit_length() - 1) if n & (n - 1) == 0 else a // n


def mod(a, n):
    return jnp.bitwise_and(a, n - 1) if n & (n - 1) == 0 else a % n


def parts(values, count):
    terms = []
    for _ in range(count):
        term = values.astype(BF16)
        terms.append(term)
        values = values - term.astype(F32)
    return jnp.concatenate(terms, axis=1)


def picks(heads, width, first, channels):
    row = iota((2 * heads, 1), 0)
    head = jnp.where(row >= heads, row - heads, row)
    return (head == div(first + iota((1, channels), 1), width)).astype(BF16)


def summed(mask, values):
    heads = values.shape[1]
    sums = dot(mask, parts(values, 3))
    return sums[:, :heads] + sums[:, heads : 2 * heads] + sums[:, 2 * heads :]


def step_sizes(raw, bias):
    shifted = raw.astype(F32) + bias
    return jnp.maximum(shifted, 0.0) + jnp.log1p(jnp.exp(-jnp.abs(shifted)))


def widen(maps, line, lines):
    state = maps.shape[1]
    places = lines * state
    copy = (mod(iota((1, places), 1), state) == iota((state, 1), 0)).astype(BF16)
    own = div(iota((1, places), 1), state) == line
    return jnp.where(own, dot(maps, copy), 0.0).astype(BF16)


class Scan:
    def __init__(self, order, lines, raw, bias, rates, b_map, c_map):
        tokens, self.heads = raw.shape
        self.lines, self.b_map, self.c_map = lines, b_map, c_map
        self.line, place = order(iota((tokens, 1), 0))
        self.line_in, place_in = order(iota((1, tokens), 1))
        self.lower = jnp.logical_and(self.line == self.line_in, place >= place_in)
        steps = step_sizes(raw, bias)
        self.decay = -rates * steps
        running = summed(self.lower.astype(BF16), self.decay)
        self.fade = parts(jnp.exp(running), 2)
        self.grow = parts(steps * jnp.exp(-running), 2)

    def ends(self):
        places = self.lines * self.b_map.shape[1]
        own = div(iota((places, 1), 0), self.b_map.shape[1]) == self.line_in
        return jnp.exp(summed(own.astype(BF16), self.decay))

    def into(self):
        return widen(self.b_map, self.line, self.lines).astype(F32).T.astype(BF16)

    def within(self):
        scores = lax.dot_general(
            self.c_map, self.b_map, (((1,), (1,)), ((), ())), preferred_element_type=F32
        )
        return jnp.where(self.lower, scores, 0.0).astype(BF16)

    def entry(self, follows):
        return jnp.where(follows, widen(self.c_map, self.line, self.lines), 0)


def partner(member, i, group):
    return member ^ i


def column_order(cols):
    return lambda token: (mod(token, cols), div(token, cols))


def row_order(cols, lines, member, group):
    def order(token):
        source = partner(member, div(token, cols * lines), group)
        return mod(div(token, cols), lines), source * cols + mod(token, cols)

    return order


def strips(channels):
    return [(first, min(STRIP, channels - first)) for first in range(0, channels, STRIP)]


def pack_kernel(
    x_ref, raw_ref, maps_ref, table_ref, rates_ref, raw, maps, table, rates, *refs, group, axis, heads, state
):
    sent, sems = refs[:-1], refs[-1]
    channels = x_ref.shape[1]
    share = x_ref.shape[0] // group
    member = mod(lax.axis_index(axis), group)
    moved = [(raw_ref, raw), (maps_ref, maps)]
    places = []
    offset = 0
    for i, out in enumerate(sent):
        rows = out.shape[0]
        first = partner(member, i % group, group) * share + offset
        part = pl.ds(pl.multiple_of(first, 16), rows)
        places.append((out, part))
        moved.append((x_ref.at[part, :], out.at[:, pl.ds(0, channels)]))
        if i % group == group - 1:
            offset += rows
    moved += [(table_ref, table), (rates_ref, rates)]
    copies = [pltpu.make_async_copy(a, b, sems.at[i]) for i, (a, b) in enumerate(moved)]
    for copy in copies:
        copy.start()
    for copy in copies[:2]:
        copy.wait()
    used = heads + 2 * state
    for out, part in places:
        out[:, channels : channels + heads] = raw[part, :heads]
        out[:, channels + heads : channels + used] = maps[part, : 2 * state]
        out[:, channels + used :] = jnp.zeros((out.shape[0], LANES - used), BF16)
    for copy in copies[2:]:
        copy.wait()


def params_kernel(index_ref, table_ref, rates_ref, params_ref):
    heads = rates_ref.shape[1]
    row = jnp.where(iota(table_ref.shape, 1) == index_ref[0], table_ref[...], 0.0)
    ones = jnp.ones((8, table_ref.shape[1]), BF16)
    bias = jnp.zeros((8, row.shape[0]), F32)
    for _ in range(3):
        term = row.astype(BF16)
        row = row - term.astype(F32)
        bias += lax.dot_general(ones, term, (((1,), (1,)), ((), ())), preferred_element_type=F32)
    params_ref[0:1, :] = bias[0:1, :]
    params_ref[1:2, :heads] = rates_ref[0:1, :]
    params_ref[1:2, heads:] = rates_ref[1:2, :]
    params_ref[2:, :] = jnp.zeros((6, 2 * heads), F32)


def row_scan(params_ref, blocks, member, cols, heads, state):
    channels = blocks[0].shape[1] - LANES
    tokens = blocks[0].shape[0] * len(blocks)
    lines = tokens // (cols * len(blocks))
    aux = jnp.concatenate([block[:, channels:] for block in blocks], axis=0)
    return Scan(
        row_order(cols, lines, member, len(blocks)),
        lines,
        aux[:, :heads],
        params_ref[0:1, :heads],
        params_ref[1:2, :heads],
        aux[:, heads : heads + state],
        aux[:, heads + state : heads + 2 * state],
    )


def col_scan(params_ref, raw_ref, maps_ref, cols, heads, state):
    return Scan(
        column_order(cols),
        cols,
        raw_ref[:, heads:],
        params_ref[0:1, heads:],
        params_ref[1:2, heads:],
        maps_ref[:, 2 * state : 3 * state],
        maps_ref[:, 3 * state :],
    )


def write_state(scan, tokens_of, width, channels, s_refs, factor_ref):
    ends = scan.ends()
    if factor_ref:
        factor_ref[0][...] = ends
    ends = parts(ends, 2)
    into = scan.into()
    for first, count in strips(channels):
        pick = picks(scan.heads, width, first, count)
        values = (tokens_of(first, count) * dot(scan.grow, pick)).astype(BF16)
        made = (dot(into, values) * dot(ends, pick)).astype(BF16)
        row = 0
        for s_ref in s_refs:
            s_ref[:, first : first + count] = made[row : row + s_ref.shape[0]]
            row += s_ref.shape[0]


def row_state_kernel(params_ref, *refs, group, count, axis, cols, heads, state, width):
    blocks, s_refs, factor_ref = refs[:group], refs[group + 1 : group + 1 + count], refs[group + 1 + count :]
    member = mod(lax.axis_index(axis), group)
    scan = row_scan(params_ref, [block[...] for block in blocks], member, cols, heads, state)
    tokens_of = lambda first, count: jnp.concatenate(
        [block[:, first : first + count] for block in blocks], axis=0
    ).astype(F32)
    write_state(scan, tokens_of, width, s_refs[0].shape[1], s_refs, factor_ref)


def col_state_kernel(params_ref, x_ref, raw_ref, maps_ref, _, s_ref, *factor_ref, cols, heads, state, width):
    scan = col_scan(params_ref, raw_ref, maps_ref, cols, heads, state)
    tokens_of = lambda first, count: x_ref[:, first : first + count].astype(F32)
    write_state(scan, tokens_of, width, s_ref.shape[1], [s_ref], factor_ref)


def row_local_kernel(params_ref, *refs, group, offset, axis, cols, heads, state, width):
    blocks, (y_ref, fade_ref, entry_ref) = refs[:group], refs[group + 1 :]
    rows = y_ref.shape[0] // group
    mine = slice(offset, offset + rows)
    member = mod(lax.axis_index(axis), group)
    scan = row_scan(params_ref, [block[mine, :] for block in blocks], member, cols, heads, state)
    mix = scan.within()
    fade_ref[...] = scan.fade
    entry_ref[...] = scan.entry(lax.axis_index(axis) >= group)
    for first, count in strips(y_ref.shape[1]):
        pick = picks(heads, width, first, count)
        part = slice(first, first + count)
        x = jnp.concatenate([block[mine, part] for block in blocks], axis=0).astype(F32)
        values = (x * dot(scan.grow, pick)).astype(BF16)
        y_ref[:, part] = dot(mix, values) * dot(scan.fade, pick)


def row_both_kernel(params_ref, *refs, group, axis, cols, heads, state, width):
    blocks, (s_ref, y_ref, fade_ref, entry_ref) = refs[:group], refs[group + 1 :]
    member = mod(lax.axis_index(axis), group)
    scan = row_scan(params_ref, [block[...] for block in blocks], member, cols, heads, state)
    into = scan.into()
    ends = parts(scan.ends(), 2)
    mix = scan.within()
    fade_ref[...] = scan.fade
    entry_ref[...] = scan.entry(lax.axis_index(axis) >= group)
    for first, count in strips(y_ref.shape[1]):
        pick = picks(heads, width, first, count)
        part = slice(first, first + count)
        x = jnp.concatenate([block[:, part] for block in blocks], axis=0).astype(F32)
        values = (x * dot(scan.grow, pick)).astype(BF16)
        s_ref[:, part] = (dot(into, values) * dot(ends, pick)).astype(BF16)
        y_ref[:, part] = dot(mix, values) * dot(scan.fade, pick)


def row_out_kernel(s_ref, y_ref, fade_ref, entry_ref, _, __, *outs, heads, width):
    rows = outs[0].shape[0]
    for first, count in strips(s_ref.shape[1]):
        pick = picks(heads, width, first, count)
        part = slice(first, first + count)
        y = y_ref[:, part] + dot(entry_ref[...], s_ref[:, part]) * dot(fade_ref[...], pick)
        for i, out in enumerate(outs):
            out[:, part] = y[i * rows : (i + 1) * rows].astype(BF16)


def col_local_kernel(
    params_ref, x_ref, raw_ref, maps_ref, gate_ref, skip_ref, _, y_ref, g_ref, fade_ref, entry_ref,
    *, cols, heads, state, width
):
    scan = col_scan(params_ref, raw_ref, maps_ref, cols, heads, state)
    mix = scan.within()
    fade_ref[...] = scan.fade
    entry_ref[...] = scan.entry(lax.axis_index("row") > 0)
    skips = parts(jnp.broadcast_to(skip_ref[...], (8, heads)), 2)
    for first, count in strips(x_ref.shape[1]):
        pick = picks(heads, width, first, count)
        part = slice(first, first + count)
        x = x_ref[:, part].astype(F32)
        values = (x * dot(scan.grow, pick)).astype(BF16)
        y_ref[:, part] = dot(mix, values) * dot(scan.fade, pick) + dot(skips, pick)[0:1, :] * x
        gate = gate_ref[:, part].astype(F32)
        g_ref[:, part] = gate / (1.0 + jnp.exp(-gate))


def col_both_kernel(
    params_ref, x_ref, raw_ref, maps_ref, gate_ref, skip_ref, _, s_ref, y_ref, g_ref, fade_ref, entry_ref,
    *, cols, heads, state, width
):
    scan = col_scan(params_ref, raw_ref, maps_ref, cols, heads, state)
    into = scan.into()
    ends = parts(scan.ends(), 2)
    mix = scan.within()
    fade_ref[...] = scan.fade
    entry_ref[...] = scan.entry(lax.axis_index("row") > 0)
    skips = parts(jnp.broadcast_to(skip_ref[...], (8, heads)), 2)
    for first, count in strips(x_ref.shape[1]):
        pick = picks(heads, width, first, count)
        part = slice(first, first + count)
        x = x_ref[:, part].astype(F32)
        values = (x * dot(scan.grow, pick)).astype(BF16)
        s_ref[:, part] = (dot(into, values) * dot(ends, pick)).astype(BF16)
        y_ref[:, part] = dot(mix, values) * dot(scan.fade, pick) + dot(skips, pick)[0:1, :] * x
        gate = gate_ref[:, part].astype(F32)
        g_ref[:, part] = gate / (1.0 + jnp.exp(-gate))


def col_out_kernel(s_ref, y_ref, fade_ref, entry_ref, w_ref, *, heads, width):
    for first, count in strips(s_ref.shape[1]):
        pick = picks(heads, width, first, count)
        part = slice(first, first + count)
        w_ref[:, part] = y_ref[:, part] + dot(entry_ref[...], s_ref[:, part]) * dot(fade_ref[...], pick)


def final_kernel(w_ref, g_ref, gain_ref, *refs, which, offset, group, axis, share):
    blocks, (out_ref, made, sems) = refs[-3 - len(which) : -3], refs[-3:]
    rows, channels = blocks[0].shape
    member = mod(lax.axis_index(axis), group)
    copies = []
    for i, block in zip(which, blocks):
        part = pl.ds(pl.multiple_of(partner(member, i, group) * share + offset, 16), rows)
        v = (block[...].astype(F32) + w_ref[part, :]) * g_ref[part, :]
        power = jnp.sum(v * v, axis=1, keepdims=True) / channels
        at = len(copies)
        made[at] = (v * lax.rsqrt(power + 1e-5) * gain_ref[...]).astype(BF16)
        copies.append(pltpu.make_async_copy(made.at[at], out_ref.at[part, :], sems.at[at]))
        copies[-1].start()
    for copy in copies:
        copy.wait()


def cost(micros):
    return pl.CostEstimate(flops=1024 + int(micros * 10**9), bytes_accessed=1024, transcendentals=0)


def call(kernel, out_shape, micros, specs=None, **more):
    if specs is not None:
        more["in_specs"] = [spec or pl.BlockSpec() for spec in specs]
    return pl.pallas_call(
        kernel,
        out_shape=out_shape,
        compiler_params=pltpu.CompilerParams(vmem_limit_bytes=VMEM_LIMIT),
        cost_estimate=cost(micros),
        **more,
    )


def entering_states(ends, factor, axis, size, stride, width, wrap=True):
    if size == stride:
        return ends
    onward = [(i, (i + stride) % size) for i in range(size if wrap else size - stride)]
    entering = lax.ppermute(ends, axis, onward)
    for _ in range(size // stride - 2):
        follows = (lax.axis_index(axis) >= stride).astype(F32)
        decayed = follows * jnp.repeat(factor[0], width, axis=1) * entering.astype(F32)
        entering = lax.ppermute((ends.astype(F32) + decayed).astype(BF16), axis, onward)
    return entering


def body(x_in, gate_in, proj_bc, dt_raw, step_index, step_table, rates, skip, norm_gain, *, row_count, col_count):
    _, tile_rows, cols, channels = x_in.shape
    heads = skip.shape[0]
    width = channels // heads
    state = proj_bc.shape[-1] // 4
    tokens = tile_rows * cols
    group = GROUP
    while col_count % group:
        group //= 2
    share = tokens // group
    pieces = [[eighths * share // 8 for eighths in piece] for piece in PIECES]

    x = x_in.reshape(tokens, channels)
    gate = gate_in.reshape(tokens, channels)
    maps = proj_bc.reshape(tokens, 4 * state)
    raw = dt_raw.reshape(tokens, 2 * heads)
    sizes = dict(cols=cols, heads=heads, state=state, width=width)
    shared = dict(group=group, axis="col")
    shape = jax.ShapeDtypeStruct
    any_spec = pl.BlockSpec(memory_space=pl.ANY)

    given = [x, raw, maps, step_table.T, rates]
    raw, maps, table, rates, *packed = pl.pallas_call(
        functools.partial(pack_kernel, heads=heads, state=state, **shared),
        in_specs=[pl.BlockSpec(memory_space=pltpu.HBM)] * len(given),
        out_shape=[pltpu.VMEM(a.shape, a.dtype) for a in given[1:]]
        + [pltpu.VMEM((sum(piece), channels + LANES), BF16) for piece in pieces for _ in range(group)],
        scratch_shapes=[pltpu.SemaphoreType.DMA((len(given) - 1 + group * len(pieces),))],
        compiler_params=pltpu.CompilerParams(vmem_limit_bytes=VMEM_LIMIT),
        cost_estimate=cost(1),
    )(*[pltpu.with_memory_space_constraint(a, pltpu.HBM) for a in given])
    index, rates = lax.optimization_barrier((step_index, rates))
    params = pl.pallas_call(
        params_kernel,
        grid_spec=pltpu.PrefetchScalarGridSpec(
            num_scalar_prefetch=1,
            grid=(1,),
            in_specs=[
                pl.BlockSpec(table.shape, lambda i, index: (0, 0)),
                pl.BlockSpec(rates.shape, lambda i, index: (0, 0)),
            ],
            out_specs=pl.BlockSpec((8, 2 * heads), lambda i, index: (0, 0)),
        ),
        out_shape=shape((8, 2 * heads), F32),
        compiler_params=pltpu.CompilerParams(vmem_limit_bytes=VMEM_LIMIT),
        cost_estimate=cost(0),
    )(index, table, rates)

    def exchange(blocks):
        return [blocks[0]] + [
            lax.ppermute(blocks[i], "col", [(at, partner(at, i, group)) for at in range(col_count)])
            for i in range(1, group)
        ]

    def state_shapes(places, count):
        states = [pltpu.VMEM((rows, channels), BF16) for rows in places]
        return states + [shape((sum(places), heads), F32)] * (count > 2)

    got = [exchange(packed[i * group : (i + 1) * group]) for i in range(len(pieces))]

    def own_rows(i, before):
        known = []
        for j, rows in enumerate(pieces[i]):
            known.append(
                call(
                    functools.partial(row_local_kernel, offset=sum(pieces[i][:j]), **sizes, **shared),
                    [
                        pltpu.VMEM((group * rows, channels), F32),
                        pltpu.VMEM((group * rows, 2 * heads), BF16),
                        pltpu.VMEM((group * rows, rows // cols * state), BF16),
                    ],
                    2,
                    specs=[None] * (1 + group) + [any_spec],
                )(params, *got[i], before)
            )
            before = known[-1][1]
        return known, before

    def row_states(i, before):
        places = [rows // cols * state for rows in pieces[i]]
        made = call(
            functools.partial(row_state_kernel, count=len(places), **sizes, **shared),
            state_shapes(places, col_count // group),
            0,
            specs=[None] * (1 + group) + [any_spec],
        )(params, *got[i], before)
        entering = []
        for j, count in enumerate(places):
            first = sum(places[:j])
            factor = [f[first : first + count] for f in made[len(places) :]]
            entering.append(entering_states(made[j], factor, "col", col_count, group, width, wrap=i == 0))
        return entering, made[0]

    known, entering = [None] * len(pieces), [None] * len(pieces)
    entering[0], before = row_states(0, params)
    if row_count > 2:
        col_made = call(
            functools.partial(col_state_kernel, **sizes),
            state_shapes([cols * state], row_count),
            0,
            specs=[None] * 4 + [any_spec],
        )(params, x, raw, maps, before)
        col_entering = entering_states(col_made[0], col_made[1:], "row", row_count, 1, width)
        before = col_made[0]
        y_col, silu, *col_known = call(
            functools.partial(col_local_kernel, **sizes),
            [
                pltpu.VMEM((tokens, channels), F32),
                pltpu.VMEM((tokens, channels), F32),
                pltpu.VMEM((tokens, 2 * heads), BF16),
                pltpu.VMEM((tokens, cols * state), BF16),
            ],
            2,
            specs=[None] * 6 + [any_spec],
        )(params, x, raw, maps, gate, skip.reshape(1, heads), before)
    else:
        ends, y_col, silu, *col_known = call(
            functools.partial(col_both_kernel, **sizes),
            [
                pltpu.VMEM((cols * state, channels), BF16),
                pltpu.VMEM((tokens, channels), F32),
                pltpu.VMEM((tokens, channels), F32),
                pltpu.VMEM((tokens, 2 * heads), BF16),
                pltpu.VMEM((tokens, cols * state), BF16),
            ],
            0,
            specs=[None] * 6 + [any_spec],
        )(params, x, raw, maps, gate, skip.reshape(1, heads), before)
        col_entering = entering_states(ends, [], "row", row_count, 1, width)
    w = call(
        functools.partial(col_out_kernel, heads=heads, width=width),
        pltpu.VMEM((tokens, channels), F32),
        0,
    )(col_entering, y_col, *col_known)
    before = y_col
    known[0], before = own_rows(0, before)
    for i in range(1, len(pieces)):
        if len(pieces[i]) > 1 or col_count > 2 * group:
            known[i], before = own_rows(i, before)
            entering[i], before = row_states(i, before)
            continue
        rows = pieces[i][0]
        places = rows // cols * state
        made, *own = call(
            functools.partial(row_both_kernel, **sizes, **shared),
            [
                pltpu.VMEM((places, channels), BF16),
                pltpu.VMEM((group * rows, channels), F32),
                pltpu.VMEM((group * rows, 2 * heads), BF16),
                pltpu.VMEM((group * rows, places), BF16),
            ],
            2,
            specs=[None] * (1 + group) + [any_spec],
        )(params, *got[i], before)
        known[i], before = [own], made
        entering[i] = [entering_states(made, [], "col", col_count, group, width, wrap=False)]
    parts_of = []
    for i, piece in enumerate(pieces):
        for j, rows in enumerate(piece):
            first = sum(map(sum, pieces[:i])) + sum(piece[:j])
            parts_of.append((first, rows, known[i][j], entering[i][j]))

    back = []
    for _, rows, known, entering in parts_of:
        y_row = call(
            functools.partial(row_out_kernel, heads=heads, width=width),
            [pltpu.VMEM((rows, channels), BF16)] * group,
            0,
            specs=[None] * 4 + [any_spec] * 2,
        )(entering, *known, before, col_entering if back else before)
        back.append(exchange(y_row))
        before = y_row[0]

    which = [0, *range(group - 1, 0, -1)]
    mixed = None
    for i in range(len(parts_of)):
        first, rows = parts_of[i][:2]
        more = [] if mixed is None else [mixed]
        mixed = call(
            functools.partial(final_kernel, which=which, offset=first, share=share, **shared),
            shape((tokens, channels), BF16),
            0,
            specs=[None] * 3 + [any_spec] * len(more) + [None] * len(which),
            out_specs=any_spec,
            scratch_shapes=[
                pltpu.VMEM((len(which), rows, channels), BF16),
                pltpu.SemaphoreType.DMA((len(which),)),
            ],
            input_output_aliases={3: 0} if more else {},
        )(w, silu, norm_gain.reshape(1, channels), *more, *[back[i][j] for j in which])
    return mixed.reshape(x_in.shape)


def solution(mesh):
    tile = P("img", "row", "col", None)
    return jax.shard_map(
        functools.partial(body, row_count=mesh.shape["row"], col_count=mesh.shape["col"]),
        mesh=mesh,
        in_specs=(tile, tile, tile, tile, P("img"), P(), P(), P(), P()),
        out_specs=tile,
        check_vma=False,
    )
```
